32 devices in a mesh: seq: 4 (over x, core), fsdp: 8 (over z, y).
Axes of the slice: x: 2, y: 2, z: 4, core: 2. Of those that a mesh axis runs over, the one named last changes fastest.
Arguments:
- tokens: bfloat16 [8, 512, 2048], P('fsdp', 'seq'), may hold values from -6 to 6
- segments: int32 [8, 512], P('fsdp'), may hold values from 0 to 4, as said below
- positions: int32 [8, 512], P('fsdp', 'seq'), may hold values from 0 to 510, as said below
- gain_one: bfloat16 [2048], P(('seq', 'fsdp')), may hold values from 0.5 to 1.5
- w_query: bfloat16 [2048, 2048], P(('seq', 'fsdp')), may hold values from -0.125 to 0.125
- w_key: bfloat16 [2048, 128], P(('seq', 'fsdp')), may hold values from -0.125 to 0.125
- w_value: bfloat16 [2048, 128], P(('seq', 'fsdp')), may hold values from -0.125 to 0.125
- w_out: bfloat16 [2048, 2048], P(('seq', 'fsdp')), may hold values from -1 to 1
- gain_two: bfloat16 [2048], P(('seq', 'fsdp')), may hold values from 0.5 to 1.5
- w_gate: bfloat16 [2048, 5632], P(('seq', 'fsdp')), may hold values from -0.125 to 0.125
- w_up: bfloat16 [2048, 5632], P(('seq', 'fsdp')), may hold values from -0.125 to 0.125
- w_down: bfloat16 [5632, 2048], P(('seq', 'fsdp')), may hold values from -0.078125 to 0.078125
- cotangent: bfloat16 [8, 512, 2048], P('fsdp', 'seq'), may hold values from -6 to 6
Outputs:
- output: bfloat16 [8, 512, 2048], P('fsdp', 'seq')
- keys_out: bfloat16 [8, 512, 128], P('fsdp', 'seq')
- values_out: bfloat16 [8, 512, 128], P('fsdp', 'seq')
- grad_tokens: float32 [8, 512, 2048], P('fsdp', 'seq')
- grad_gain_one: float32 [2048], P(('seq', 'fsdp'))
- grad_w_query: float32 [2048, 2048], P(('seq', 'fsdp'))
- grad_w_key: float32 [2048, 128], P(('seq', 'fsdp'))
- grad_w_value: float32 [2048, 128], P(('seq', 'fsdp'))
- grad_w_out: float32 [2048, 2048], P(('seq', 'fsdp'))
- grad_gain_two: float32 [2048], P(('seq', 'fsdp'))
- grad_w_gate: float32 [2048, 5632], P(('seq', 'fsdp'))
- grad_w_up: float32 [2048, 5632], P(('seq', 'fsdp'))
- grad_w_down: float32 [5632, 2048], P(('seq', 'fsdp'))
The draws below stay inside these ranges and needn't reach their ends.
Inputs may be any that keep to these rules, and one draw needn't show every extreme that they name: `segments`: segment ids never fall along a row; in every row one segment runs from the first block of 128 tokens into the last. `positions`: a token's position counts its place from the start of its segment.
All inputs are finite; a program needn't handle non-finite values.
Results may differ from the reference program's by a relative error of at most 0.013.
Values may be sent and summed in bfloat16 or wider, within the bound.
A program may use at most 448 MiB of HBM per device.

```python
import jax
import jax.numpy as jnp
from jax import lax

D = 2048
HEADS = 16
HEAD = 128
FF = 5632
SEQ_DEV = 128
ROWS = 8
ROW_LEN = 512


def document_bounds(key):
    key_a, key_b, key_c, key_d = jax.random.split(key, 4)
    begin_long = jax.random.randint(key_a, (ROWS, 1), 1, SEQ_DEV)
    end_long = ROW_LEN - jax.random.randint(key_b, (ROWS, 1), 1, SEQ_DEV)
    early_cut = jax.random.randint(key_c, (ROWS, 1), 0, begin_long)
    late_cut = jax.random.randint(key_d, (ROWS, 1), end_long + 1, ROW_LEN + 1)
    token_index = jnp.arange(ROW_LEN, dtype=jnp.int32)[None, :]
    segment_ids = (token_index >= early_cut).astype(jnp.int32) + (token_index >= begin_long).astype(jnp.int32) + (token_index >= end_long).astype(jnp.int32) + (token_index >= late_cut).astype(jnp.int32)
    zero_start = jnp.zeros_like(token_index)
    start_of = jnp.where(token_index >= early_cut, early_cut, zero_start)
    start_of = jnp.where(token_index >= begin_long, begin_long, start_of)
    start_of = jnp.where(token_index >= end_long, end_long, start_of)
    start_of = jnp.where(token_index >= late_cut, late_cut, start_of)
    return (segment_ids.astype(jnp.int32), (token_index - start_of).astype(jnp.int32))


def draw_segments(key, part):
    return document_bounds(key)[0]


def draw_positions(key, part):
    return document_bounds(key)[1]


def level_of(own_key, shape, pieces, smallest, top_value):
    loudness, own = 1.0, jax.random.fold_in(own_key, 6)
    for dim, shards_of in pieces:
        heights = jnp.exp(jax.random.uniform(jax.random.fold_in(own, dim), (shards_of,), jnp.float32, smallest / len(pieces), top_value / len(pieces)))
        loudness = loudness * jnp.repeat(heights, shape[dim] // shards_of).reshape([-1 if axis == dim else 1 for axis in range(len(shape))])
    return loudness


def gaussian(rng, dims, scale, bound, cuts=(), kind=jnp.bfloat16):
    array = scale * jax.random.normal(rng, dims, jnp.float32)
    if cuts:
        array = array * level_of(rng, dims, cuts, -0.22, 0.18)
    return jnp.clip(array, -bound, bound).astype(kind)


def setup_inputs(seed: int = 0) -> dict:
    key_of = jax.random.split(jax.random.key(seed), 14)
    return {
        "tokens": gaussian(key_of[0], (ROWS, ROW_LEN, D), 1.0, 6.0, ((0, 8), (1, 4))),
        "segments": draw_segments(jax.random.fold_in(key_of[13], 71), 0),
        "positions": draw_positions(jax.random.fold_in(key_of[13], 71), 0),
        "gain_one": jnp.clip(1.0 + 0.1 * jax.random.normal(key_of[3], (D,), jnp.float32), 0.5, 1.5).astype(jnp.bfloat16),
        "w_query": gaussian(key_of[4], (D, HEADS * HEAD), D ** -0.5, 0.125, ((0, 32),)),
        "w_key": gaussian(key_of[5], (D, HEAD), D ** -0.5, 0.125, ((0, 32),)),
        "w_value": gaussian(key_of[6], (D, HEAD), D ** -0.5, 0.125, ((0, 32),)),
        "w_out": gaussian(key_of[7], (HEADS * HEAD, D), (HEADS * HEAD // 64) ** -0.5, 1.0, ((0, 32),)),
        "gain_two": jnp.clip(1.0 + 0.1 * jax.random.normal(key_of[8], (D,), jnp.float32), 0.5, 1.5).astype(jnp.bfloat16),
        "w_gate": gaussian(key_of[9], (D, FF), D ** -0.5, 0.125, ((0, 32),)),
        "w_up": gaussian(key_of[10], (D, FF), D ** -0.5, 0.125, ((0, 32),)),
        "w_down": gaussian(key_of[11], (FF, D), FF ** -0.5, 0.078125, ((0, 32),)),
        "cotangent": gaussian(key_of[12], (ROWS, ROW_LEN, D), 1.0, 6.0, ((0, 8), (1, 4))),
    }


epsilon = 1e-05
highest = lax.Precision.HIGHEST

@jax.custom_vjp
def low(v):
    return lax.optimization_barrier(v.astype(jnp.bfloat16)).astype(jnp.float32)

@jax.custom_vjp
def low_back(v):
    return v

def low_keep(v):
    return (low(v), None)

def low_pass(kept, grad):
    return (grad,)

def back_keep(v):
    return (v, None)

def back_low(kept, grad):
    return (low(grad),)
low.defvjp(low_keep, low_pass)
low_back.defvjp(back_keep, back_low)

def angle_tables(position_row):
    half_head = HEAD // 2
    frequency = 10000.0 ** (-jnp.arange(half_head, dtype=jnp.float32) * 2.0 / HEAD)
    phase_angle = position_row.astype(jnp.float32)[:, None] * frequency[None, :]
    return (jnp.cos(phase_angle)[:, None, :], jnp.sin(phase_angle)[:, None, :])

def rotate(tensor_in, cosine, sine):
    half_head = tensor_in.shape[-1] // 2
    first_half = tensor_in[..., :half_head]
    second_half = tensor_in[..., half_head:]
    return jnp.concatenate([first_half * cosine - second_half * sine, second_half * cosine + first_half * sine], -1)

def block_forward(row_input, gain_one, w_query, w_key, w_value, w_out, gain_two, w_gate, w_up, w_down, segment_row, position_row):
    row_length = row_input.shape[0]
    cosine, sine = angle_tables(position_row)
    inverse_one = lax.rsqrt(lax.optimization_barrier(jnp.mean(row_input * row_input, -1, keepdims=True)) + epsilon)
    normed_one = low(row_input * inverse_one * gain_one)
    queries = low_back(jnp.dot(normed_one, w_query, precision=highest)).reshape(row_length, HEADS, HEAD)
    key_proj = low_back(jnp.dot(normed_one, w_key, precision=highest))
    value_rows = low(low_back(jnp.dot(normed_one, w_value, precision=highest)))
    query_rot = low(rotate(queries, cosine, sine))
    key_rows = low(rotate(key_proj[:, None, :], cosine, sine)[:, 0, :])
    scores = low_back(jnp.einsum('qhd,kd->hqk', query_rot, key_rows, precision=highest) * HEAD ** (-0.5))
    token_index = jnp.arange(row_length)
    allowed = (token_index[None, :] <= token_index[:, None]) & (segment_row[None, :] == segment_row[:, None])
    scores = jnp.where(allowed[None], scores, -1e+30)
    weights_soft = low(jax.nn.softmax(scores, axis=-1))
    attended = jnp.einsum('hqk,kd->qhd', weights_soft, value_rows, precision=highest).reshape(row_length, HEADS * HEAD)
    attended = low(low_back(attended))
    residual = row_input + low_back(jnp.dot(attended, w_out, precision=highest))
    inverse_two = lax.rsqrt(lax.optimization_barrier(jnp.mean(residual * residual, -1, keepdims=True)) + epsilon)
    normed_two = low(residual * inverse_two * gain_two)
    gate_proj = low_back(jnp.dot(normed_two, w_gate, precision=highest))
    up_proj = low_back(jnp.dot(normed_two, w_up, precision=highest))
    inner_act = low(jax.nn.silu(gate_proj) * up_proj)
    output_row = residual + low_back(jnp.dot(inner_act, w_down, precision=highest))
    return (output_row, (key_rows, value_rows))

def reference(tokens, segments, positions, gain_one, w_query, w_key, w_value, w_out, gain_two, w_gate, w_up, w_down, cotangent):
    params = tuple((item.astype(jnp.float32) for item in (gain_one, w_query, w_key, w_value, w_out, gain_two, w_gate, w_up, w_down)))

    def one_row(totals, row_data):
        row_tokens, segment_row, position_row, grad_row = row_data

        def forward_pass(row_input, *weights_in):
            return block_forward(row_input, *weights_in, segment_row, position_row)
        output_row, pullback, shared = jax.vjp(forward_pass, row_tokens.astype(jnp.float32), *params, has_aux=True)
        gradient = pullback(grad_row.astype(jnp.float32))
        totals = tuple((left + right for left, right in zip(totals, gradient[1:])))
        return (totals, (output_row.astype(jnp.bfloat16), shared[0].astype(jnp.bfloat16), shared[1].astype(jnp.bfloat16), gradient[0]))
    zeros_init = tuple((jnp.zeros(item.shape, jnp.float32) for item in params))
    totals, (outputs, key_rows, value_rows, grad_input) = lax.scan(one_row, zeros_init, (tokens, segments, positions, cotangent))
    return (outputs, key_rows, value_rows, grad_input, totals[0], totals[1], totals[2], totals[3], totals[4], totals[5], totals[6], totals[7], totals[8])
```

```python
import functools

import jax
import jax.numpy as jnp
from jax import lax
from jax.experimental import pallas as pl
from jax.experimental.pallas import tpu as pltpu
from jax.sharding import PartitionSpec as P

epsilon = 1e-05
MESH = pl.DeviceIdType.MESH
VMEM_LIMIT = 60 * 2**20
bf16 = jnp.bfloat16
f32 = jnp.float32


def dot(left, right):
    return jnp.dot(left, right, preferred_element_type=f32)


def contract_last(left, right):
    return lax.dot_general(left, right, (((1,), (1,)), ((), ())), preferred_element_type=f32)


def contract_first(left, right):
    return lax.dot_general(left, right, (((0,), (0,)), ((), ())), preferred_element_type=f32)


class Arrival:
    def __init__(self, copy):
        self.copy, self.waited = copy, False

    def wait(self):
        if not self.waited:
            self.waited = True
            self.copy.wait_recv()


class Links:
    def __init__(self, send, recv):
        self.send, self.recv, self.sent = send, recv, []
        self.s, self.f = lax.axis_index("seq"), lax.axis_index("fsdp")

    def greet(self, masks):
        barrier = pltpu.get_barrier_semaphore()
        for a, b in masks:
            pl.semaphore_signal(
                barrier, inc=1, device_id=(self.s ^ a, self.f ^ b), device_id_type=MESH
            )
        pl.semaphore_wait(barrier, len(masks))

    def start(self, source, target, mask):
        i = len(self.sent)
        copy = pltpu.make_async_remote_copy(
            src_ref=source,
            dst_ref=target,
            send_sem=self.send.at[i],
            recv_sem=self.recv.at[i],
            device_id=(self.s ^ mask[0], self.f ^ mask[1]),
            device_id_type=MESH,
        )
        copy.start()
        self.sent.append(Arrival(copy))
        return self.sent[-1]

    def pass_on(self, block, mask):
        return self.start(block, block, mask)

    def finish(self):
        for arrival in self.sent:
            arrival.wait()
        for arrival in self.sent:
            arrival.copy.wait_send()


class Group:
    def __init__(self, links, own, full, FQ):
        self.links, self.full, self.FQ = links, full, FQ
        self.s, self.tb = links.s, links.f // FQ
        self.there = links.start(own, full.at[self.s, self.tb], (0, FQ))
        self.across = links.start(own, full.at[self.s, self.tb], (2, 0))
        links.start(own, full.at[self.s, self.tb], (1, 0))

    def relay(self):
        s, tb, full = self.s, self.tb, self.full
        self.there.wait()
        across_two = self.links.pass_on(full.at[s, 1 - tb], (2, 0))
        self.links.pass_on(full.at[s, 1 - tb], (1, 0))
        self.across.wait()
        self.links.pass_on(full.at[s ^ 2, tb], (1, 0))
        across_two.wait()
        self.links.pass_on(full.at[s ^ 2, 1 - tb], (1, 0))


class Local:
    def __init__(self, sems, pairs):
        self.copies = [pltpu.make_async_copy(a, b, sems.at[i]) for i, (a, b) in enumerate(pairs)]
        self.open = set(range(len(pairs)))
        for copy in self.copies:
            copy.start()

    def wait(self, *which):
        for i in which or sorted(self.open):
            self.open.discard(i)
            self.copies[i].wait()


def row_loop(rows, step, body):
    if rows % step:
        body(slice(0, rows))
        return

    @pl.loop(0, rows // step)
    def _(i):
        body(pl.ds(pl.multiple_of(i * step, step), step))


def communicate(
    body, args, outs, copies, collective_id, in_vmem=False, out_vmem=False, scratch=(), kept=1
):
    def spec(inside):
        return pl.BlockSpec(memory_space=pltpu.VMEM if inside else pl.ANY)

    return pl.pallas_call(
        body,
        out_shape=outs,
        in_specs=[spec(in_vmem)] * len(args),
        out_specs=[spec(out_vmem)] * len(outs),
        scratch_shapes=[
            pltpu.SemaphoreType.DMA((copies,)),
            pltpu.SemaphoreType.DMA((copies,)),
            pltpu.SemaphoreType.DMA((kept,)),
            *scratch,
        ],
        compiler_params=pltpu.CompilerParams(
            collective_id=collective_id, has_side_effects=True, vmem_limit_bytes=VMEM_LIMIT
        ),
    )(*args)


def shape(dims, kind=bf16):
    return jax.ShapeDtypeStruct(dims, kind)


def group_masks(FQ):
    return [(a, b) for a in range(4) for b in (0, FQ) if (a, b) != (0, 0)]


def gather_all_kernel(FH, FQ, *refs):
    tok, pos, wq, kvg, wo, gate, up, down, cot = refs[:9]
    tok_g, pos_g, q_g, kv_g, o_g, gate_g, up_g, down_g, cot_g = refs[9:18]
    send, recv, here = refs[18:]
    links = Links(send, recv)
    s, f = links.s, links.f
    tb, q = f // FQ, f % FQ
    t = 2 * s + tb
    evens = [2 * k for k in range(1, FH)]
    evens_q = [b for b in evens if b < FQ]
    links.greet([(a, 0) for a in (1, 2, 3)] + [(0, 1)] + [(0, b) for b in evens] + [(a, FQ) for a in (1, 2, 3)])
    local = Local(
        here,
        [
            (wq.at[s], q_g.at[s, f]),
            (kvg, kv_g.at[s, f]),
            (gate.at[t], gate_g.at[t, q]),
            (up.at[t], up_g.at[t, q]),
            (tok, tok_g.at[s]),
            (pos, pos_g.at[s]),
            (wo, o_g.at[f]),
            (down, down_g.at[q]),
            (cot, cot_g.at[s, tb]),
        ],
    )
    first = []
    for a in (1, 2, 3):
        first.append(links.start(wq.at[s ^ a], q_g.at[s, f], (a, 0)))
        first.append(links.start(kvg, kv_g.at[s, f], (a, 0)))
    tok_x = links.start(tok, tok_g.at[s], (2, 0))
    links.start(tok, tok_g.at[s], (1, 0))
    for a in (1, 2, 3):
        links.start(pos, pos_g.at[s], (a, 0))
    links.start(wo, o_g.at[f], (0, 1))
    o_z = [links.start(wo, o_g.at[f], (0, b)) for b in evens]
    local.wait(0, 1)
    for arrival in first:
        arrival.wait()
    for r in (q_g, kv_g):
        links.pass_on(r.at[:, f], (0, 1))
    qk_z = [[links.pass_on(r.at[:, f], (0, b)) for r in (q_g, kv_g)] for b in evens]
    ffn = []
    for a, b in group_masks(FQ):
        to = 2 * (s ^ a) + (tb ^ (b // FQ))
        ffn.append(links.start(gate.at[to], gate_g.at[t, q], (a, b)))
        ffn.append(links.start(up.at[to], up_g.at[t, q], (a, b)))
    cot_group = Group(links, cot, cot_g, FQ)
    for k, b in enumerate(evens):
        o_z[k].wait()
        links.pass_on(o_g.at[f ^ b], (0, 1))
        for r, arrival in zip((q_g, kv_g), qk_z[k]):
            arrival.wait()
            links.pass_on(r.at[:, f ^ b], (0, 1))
    tok_x.wait()
    links.pass_on(tok_g.at[s ^ 2], (1, 0))
    down_y = links.start(down, down_g.at[q], (0, 1))
    down_z = [links.start(down, down_g.at[q], (0, b)) for b in evens_q]
    local.wait(2, 3)
    for arrival in ffn:
        arrival.wait()
    gu_y = [links.pass_on(r.at[:, q], (0, 1)) for r in (gate_g, up_g)]
    gu_z = [[links.pass_on(r.at[:, q], (0, b)) for r in (gate_g, up_g)] for b in evens_q]
    cot_group.relay()
    half = down_g.shape[2] // 2
    low_half, high_half = pl.ds(0, half), pl.ds(half, half)
    low_t, high_t = pl.ds(0, 4), pl.ds(4, 4)
    down_y.wait()
    for b in evens_q:
        links.pass_on(down_g.at[q ^ 1, :, high_half], (0, b))
    for arrival, b in zip(down_z, evens_q):
        arrival.wait()
        links.pass_on(down_g.at[q ^ b, :, low_half], (0, 1))
    for r, arrival in zip((gate_g, up_g), gu_y):
        arrival.wait()
        for b in evens_q:
            links.pass_on(r.at[high_t, q ^ 1], (0, b))
    for arrivals, b in zip(gu_z, evens_q):
        for r, arrival in zip((gate_g, up_g), arrivals):
            arrival.wait()
            links.pass_on(r.at[low_t, q ^ b], (0, 1))
    links.finish()
    local.wait()


def gather_group_kernel(FQ, own, full, send, recv, here):
    links = Links(send, recv)
    links.greet([(1, 0), (2, 0), (0, FQ)])
    local = Local(here, [(own, full.at[links.s, links.f // FQ])])
    Group(links, own, full, FQ).relay()
    links.finish()
    local.wait()


def gather_row_kernel(own, full, send, recv, here):
    links = Links(send, recv)
    links.greet([(1, 0), (2, 0)])
    s = links.s
    local = Local(here, [(own, full.at[s])])
    across = links.start(own, full.at[s], (2, 0))
    links.start(own, full.at[s], (1, 0))
    across.wait()
    links.pass_on(full.at[s ^ 2], (1, 0))
    links.finish()
    local.wait()


class RowSum:
    def __init__(self, links, parts, from_core, from_x, to_x):
        self.links, self.parts = links, parts
        self.from_core, self.from_x, self.to_x = from_core, from_x, to_x
        self.x, self.core = links.s // 2, links.s % 2
        self.far = links.start(parts.at[1 - self.x, 1 - self.core], from_core.at[0], (1, 0))
        self.near = links.start(parts.at[self.x, 1 - self.core], from_core.at[1], (1, 0))

    def middle(self):
        self.far.wait()
        x, core = self.x, self.core

        def add(rows):
            total = self.parts[1 - x, core, rows].astype(f32) + self.from_core[0, rows].astype(f32)
            self.to_x[rows] = total.astype(bf16)

        row_loop(self.to_x.shape[0], 16, add)
        self.across = self.links.start(self.to_x, self.from_x, (2, 0))

    def total(self, rows):
        return (
            self.parts[self.x, self.core, rows].astype(f32)
            + self.from_core[1, rows].astype(f32)
            + self.from_x[rows].astype(f32)
        )

    def last(self, out):
        self.near.wait()
        self.across.wait()

        def add(rows):
            out[rows] = self.total(rows)

        row_loop(out.shape[0], 16, add)


def sum_row_kernel(parts, out, send, recv, here, from_core, from_x, to_x):
    links = Links(send, recv)
    links.greet([(1, 0), (2, 0)])
    total = RowSum(links, parts, from_core, from_x, to_x)
    total.middle()
    total.last(out)
    links.finish()


class GroupSum:
    def __init__(self, links, parts, bufs, FQ):
        self.links, self.parts, self.FQ = links, parts, FQ
        self.from_core, self.from_x, self.to_x, self.from_t, self.to_t = bufs
        self.x, self.core, self.tb = links.s // 2, links.s % 2, links.f // FQ
        self.far = links.start(parts.at[1 - self.x, 1 - self.core], self.from_core.at[0], (1, 0))
        self.near = links.start(parts.at[self.x, 1 - self.core], self.from_core.at[1], (1, 0))

    def to_other_x(self):
        self.far.wait()
        x, core = self.x, self.core

        def add(rows):
            for j in (0, 1):
                total = self.parts[1 - x, core, j, rows].astype(f32)
                self.to_x[j, rows] = (total + self.from_core[0, j, rows].astype(f32)).astype(bf16)

        row_loop(self.to_x.shape[1], 16, add)
        self.across = self.links.start(self.to_x, self.from_x, (2, 0))

    def total(self, j, rows):
        return (
            self.parts[self.x, self.core, j, rows].astype(f32)
            + self.from_core[1, j, rows].astype(f32)
            + self.from_x[j, rows].astype(f32)
        )

    def to_other_t(self):
        self.near.wait()
        self.across.wait()

        def add(rows):
            self.to_t[rows] = self.total(1 - self.tb, rows).astype(bf16)

        row_loop(self.to_t.shape[0], 16, add)
        self.there = self.links.start(self.to_t, self.from_t, (0, self.FQ))

    def last(self, out):
        self.there.wait()

        def add(rows):
            out[rows] = self.total(self.tb, rows) + self.from_t[rows].astype(f32)

        row_loop(out.shape[0], 16, add)


def group_sum_scratch(seq_len, width):
    block = (seq_len, width)
    return [
        pltpu.VMEM((2, 2, *block), bf16),
        pltpu.VMEM((2, *block), bf16),
        pltpu.VMEM((2, *block), bf16),
        pltpu.VMEM(block, bf16),
        pltpu.VMEM(block, bf16),
    ]


class WeightSum:
    def __init__(self, links, parts, total, bufs, first):
        self.links, self.parts, self.total = links, parts, total
        self.low_l, self.low_mid, self.low_w, self.high_w, self.high_mid, self.high_l = bufs
        leads, self.W = parts.shape[:2]
        self.rows = parts.shape[3]
        self.low, self.high = range(first), range(first, leads)
        self.l = links.f % 2
        self.w = (links.f // 2) % self.W
        if self.low:
            source = parts.at[pl.ds(0, first), :, 1 - self.l]
            self.by_l = links.start(source, self.low_l, (0, 1))
        if self.high:
            self.by_w = [
                links.start(
                    parts.at[pl.ds(first, leads - first), self.w ^ k], self.high_w.at[k - 1], (0, 2 * k)
                )
                for k in range(1, self.W)
            ]

    def middle(self):
        parts, w, l = self.parts, self.w, self.l
        if self.low:
            self.by_l.wait()
            for k in range(1, self.W):
                for i in self.low:

                    def add(rows, k=k, i=i):
                        total = parts[i, w ^ k, l, rows].astype(f32)
                        total += self.low_l[i, w ^ k, rows].astype(f32)
                        self.low_mid[k - 1, i, rows] = total.astype(bf16)

                    row_loop(self.rows, 16, add)
            self.low_end = [
                self.links.start(self.low_mid.at[k - 1], self.low_w.at[k - 1], (0, 2 * k))
                for k in range(1, self.W)
            ]
        if self.high:
            for arrival in self.by_w:
                arrival.wait()
            for j, i in enumerate(self.high):

                def add(rows, i=i, j=j):
                    total = parts[i, w, 1 - l, rows].astype(f32)
                    for k in range(1, self.W):
                        total += self.high_w[k - 1, j, 1 - l, rows].astype(f32)
                    self.high_mid[j, rows] = total.astype(bf16)

                row_loop(self.rows, 16, add)
            self.high_end = self.links.start(self.high_mid, self.high_l, (0, 1))

    def last(self):
        parts, w, l = self.parts, self.w, self.l
        if self.low:
            for arrival in self.low_end:
                arrival.wait()
            for i in self.low:

                def add(rows, i=i):
                    total = parts[i, w, l, rows].astype(f32) + self.low_l[i, w, rows].astype(f32)
                    for k in range(1, self.W):
                        total += self.low_w[k - 1, i, rows].astype(f32)
                    self.total[i, rows] = total.astype(self.total.dtype)

                row_loop(self.rows, 16, add)
        if self.high:
            self.high_end.wait()
            for j, i in enumerate(self.high):

                def add(rows, i=i, j=j):
                    total = parts[i, w, l, rows].astype(f32) + self.high_l[j, rows].astype(f32)
                    for k in range(1, self.W):
                        total += self.high_w[k - 1, j, l, rows].astype(f32)
                    self.total[i, rows] = total.astype(self.total.dtype)

                row_loop(self.rows, 16, add)


def weight_sum_scratch(parts, first):
    leads, W, _, rows, width = parts
    block = (rows, width)
    high = leads - first
    return [
        pltpu.VMEM((max(first, 1), W, *block), bf16),
        pltpu.VMEM((max(W - 1, 1), max(first, 1), *block), bf16),
        pltpu.VMEM((max(W - 1, 1), max(first, 1), *block), bf16),
        pltpu.VMEM((max(W - 1, 1), max(high, 1), 2, *block) if high else (8, 128), bf16),
        pltpu.VMEM((max(high, 1), *block) if high else (8, 128), bf16),
        pltpu.VMEM((max(high, 1), *block) if high else (8, 128), bf16),
    ]


def sum_ffn_kernel(FQ, *refs):
    back, out, gate, up, down = refs[:5]
    back_sum, out_sum, gate_own, up_own, down_sum = refs[5:10]
    send, recv, here = refs[10:13]
    refs = refs[13:]
    back_bufs, out_bufs, gate_bufs, up_bufs, down_bufs = refs[:5], refs[5:10], refs[10:16], refs[16:22], refs[22:28]
    gate_sum, up_sum = refs[28:]
    links = Links(send, recv)
    W = gate.shape[1]
    links.greet([(0, 1)] + [(0, 2 * k) for k in range(1, W)] + group_masks(FQ))
    t = 2 * links.s + links.f // FQ
    back_total = GroupSum(links, back, back_bufs, FQ)
    sums = [
        WeightSum(links, gate, gate_sum, gate_bufs, 4),
        WeightSum(links, up, up_sum, up_bufs, 4),
        WeightSum(links, down, down_sum, down_bufs, 1),
    ]
    out_total = GroupSum(links, out, out_bufs, FQ)
    back_total.to_other_x()
    out_total.to_other_x()
    back_total.to_other_t()
    out_total.to_other_t()
    back_total.last(back_sum)
    out_total.last(out_sum)
    for weight in sums:
        weight.middle()
    for weight in sums:
        weight.last()
    for a, b in group_masks(FQ):
        to = 2 * (links.s ^ a) + ((links.f // FQ) ^ (b // FQ))
        links.start(gate_sum.at[to], gate_own.at[t], (a, b))
        links.start(up_sum.at[to], up_own.at[t], (a, b))
    gate_own[t] = gate_sum[t]
    up_own[t] = up_sum[t]
    links.finish()


def sum_attention_kernel(FH, *refs):
    back, qo, kv = refs[:3]
    back_sum, q_own, o_sum, kv_sum = refs[3:7]
    send, recv, here, from_core, from_x, to_x = refs[7:13]
    qo_bufs, kv_bufs, qo_total, kv_total, kv_own = refs[13:19], refs[19:25], refs[25], refs[26], refs[27]
    links = Links(send, recv)
    links.greet([(1, 0), (2, 0), (3, 0), (0, 1)] + [(0, 2 * k) for k in range(1, FH)])
    s = links.s
    back_total = RowSum(links, back, from_core, from_x, to_x)
    kv_weight = WeightSum(links, kv, kv_total, kv_bufs, 4)
    qo_weight = WeightSum(links, qo, qo_total, qo_bufs, 8)
    back_total.middle()
    kv_weight.middle()
    qo_weight.middle()
    back_total.last(back_sum)
    kv_weight.last()
    for a in (1, 2, 3):
        links.start(kv_total.at[s ^ a], kv_own.at[s], (a, 0))
    qo_weight.last()
    for a in (1, 2, 3):
        links.start(qo_total.at[s ^ a], q_own.at[s], (a, 0))
    q_own[s] = qo_total[s]
    kv_own[s] = kv_total[s]
    for i in range(4):
        o_sum[i] = qo_total[4 + i].astype(f32)
    links.finish()

    def add(rows):
        total = kv_own[0, rows].astype(f32)
        for i in range(1, 4):
            total += kv_own[i, rows].astype(f32)
        kv_sum[rows] = total

    row_loop(kv_sum.shape[0], 16, add)


def angle_tables(position_row, head_size):
    half_head = head_size // 2
    frequency = 10000.0 ** (-jnp.arange(half_head, dtype=f32) * 2.0 / head_size)
    phase_angle = position_row.astype(f32)[:, None] * frequency[None, :]
    return (jnp.cos(phase_angle), jnp.sin(phase_angle))


def rotate(tensor_in, cosine, sine):
    half_head = tensor_in.shape[-1] // 2
    first_half = tensor_in[..., :half_head]
    second_half = tensor_in[..., half_head:]
    return jnp.concatenate(
        [first_half * cosine - second_half * sine, second_half * cosine + first_half * sine], -1
    )


def norm_back(grad_normed, inputs, inverse_rms, gain_full):
    scaled = grad_normed * gain_full
    width = inputs.shape[-1]
    inner_sum = jnp.sum(scaled * inputs, -1, keepdims=True)
    return inverse_rms * scaled - inputs * inverse_rms**3 * inner_sum / width


def per_device(
    S,
    F,
    tokens,
    segments,
    positions,
    gain_one,
    w_query,
    w_key,
    w_value,
    w_out,
    gain_two,
    w_gate,
    w_up,
    w_down,
    cotangent,
):
    T, D = tokens.shape[1:]
    head = w_key.shape[1]
    row_len = segments.shape[1]
    rows = w_query.shape[0]
    down_rows = w_down.shape[0]
    FF = w_gate.shape[1]
    FH, FQ = F // 2, F // 2
    W = FQ // 2
    TG = 2 * S
    HC = w_query.shape[1] // S
    heads = HC // head
    FC = FF // TG
    s = lax.axis_index("seq")

    def column_blocks(weight, n):
        return weight.reshape(rows, n, -1).transpose(1, 0, 2)

    gains = jnp.stack([gain_one, gain_two], 1)
    kvg = jnp.concatenate([w_key, w_value, gains, jnp.zeros((rows, head - 2), bf16)], 1)
    KV = kvg.shape[1]
    pos_block = jnp.broadcast_to(positions, (8, T))
    args = (
        tokens[0],
        pos_block,
        column_blocks(w_query, S),
        kvg,
        w_out,
        column_blocks(w_gate, TG),
        column_blocks(w_up, TG),
        w_down,
        cotangent[0],
    )
    outs = [
        shape((S, T, D)),
        shape((S, 8, T), jnp.int32),
        shape((S, F, rows, HC)),
        shape((S, F, rows, KV)),
        shape((F, rows, D)),
        shape((TG, FQ, rows, FC)),
        shape((TG, FQ, rows, FC)),
        shape((FQ, down_rows, D)),
        shape((S, 2, T, D)),
    ]
    tok, pos, wq, kvg, wo, gate_w, up_w, down_w, cot = communicate(
        functools.partial(gather_all_kernel, FH, FQ), args, outs, 120 + 24 * F, 0, kept=9
    )
    wq = wq.reshape(D, HC)
    kvg = kvg.reshape(D, KV)
    w_kv = kvg[:, : 2 * head]
    gain_one = kvg[:, 2 * head].astype(f32)
    gain_two = kvg[:, 2 * head + 1].astype(f32)
    wo = wo.reshape(HC, D)
    gate_w, up_w = gate_w.reshape(D, FC), up_w.reshape(D, FC)
    down_w = down_w.reshape(FC, D)
    cot = cot.reshape(TG * T, D)

    cosine, sine = angle_tables(pos[:, 0].reshape(row_len), head)
    row_in = tok.reshape(row_len, D).astype(f32)
    inverse_one = lax.rsqrt(jnp.mean(row_in * row_in, -1, keepdims=True) + epsilon)
    normed_one = (row_in * inverse_one * gain_one).astype(bf16)
    queries = dot(normed_one, wq)
    kv = dot(normed_one, w_kv)
    query_rot = rotate(
        queries.reshape(row_len, heads, head).transpose(1, 0, 2), cosine, sine
    ).astype(bf16)
    key_rot = rotate(kv[:, :head], cosine, sine).astype(bf16)
    value_low = kv[:, head:].astype(bf16)
    scale = head ** (-0.5)
    segment = segments[0]
    index = jnp.arange(row_len)
    allowed = (index[None, :] <= index[:, None]) & (segment[None, :] == segment[:, None])
    scores = jnp.einsum("htd,ud->htu", query_rot, key_rot, preferred_element_type=f32) * scale
    scores = jnp.where(allowed[None], scores, -1e30)
    row_max = jnp.max(scores, -1, keepdims=True)
    exp_scores = jnp.exp(scores - row_max)
    probs = exp_scores / jnp.sum(exp_scores, -1, keepdims=True)
    probs_low = probs.astype(bf16)
    attended = jnp.einsum("htu,ud->thd", probs_low, value_low, preferred_element_type=f32)
    attended = attended.reshape(row_len, HC).astype(bf16)
    part = dot(attended, wo).astype(bf16)

    def sum_row(parts, collective_id):
        block = (T, D)
        return communicate(
            sum_row_kernel,
            (parts.reshape(2, 2, T, D),),
            [shape(block, f32)],
            8,
            collective_id,
            in_vmem=True,
            out_vmem=True,
            scratch=[
                pltpu.VMEM((2, *block), bf16),
                pltpu.VMEM(block, bf16),
                pltpu.VMEM(block, bf16),
            ],
        )[0]

    inputs = tokens[0].astype(f32)
    residual = inputs + sum_row(part, 1)
    inverse_two = lax.rsqrt(jnp.mean(residual * residual, -1, keepdims=True) + epsilon)
    normed_two = (residual * inverse_two * gain_two).astype(bf16)
    (normed_all,) = communicate(
        functools.partial(gather_group_kernel, FQ), (normed_two,), [shape((S, 2, T, D))], 8, 2
    )
    normed_all = normed_all.reshape(TG * T, D)

    gate_proj = dot(normed_all, gate_w)
    up_proj = dot(normed_all, up_w)
    sig = jax.nn.sigmoid(gate_proj)
    inner = (gate_proj * sig * up_proj).astype(bf16)
    out_part = dot(inner, down_w).astype(bf16)
    grad_inner = contract_last(cot, down_w)
    grad_gate = (grad_inner * up_proj * sig * (1.0 + gate_proj * (1.0 - sig))).astype(bf16)
    grad_up = (grad_inner * gate_proj * sig).astype(bf16)
    back_part = (contract_last(grad_gate, gate_w) + contract_last(grad_up, up_w)).astype(bf16)
    half = D // 2
    grad_down_part = jnp.stack(
        [contract_first(inner, cot[:, :half]), contract_first(inner, cot[:, half:])]
    ).astype(bf16)
    grad_gate_part = contract_first(normed_all, grad_gate).astype(bf16)
    grad_up_part = contract_first(normed_all, grad_up).astype(bf16)

    gu_shape = (TG, W, 2, rows, FC)
    down_shape = (2, W, 2, down_rows, half)
    back_two, out_sum, grad_gate_own, grad_up_own, grad_down = communicate(
        functools.partial(sum_ffn_kernel, FQ),
        (
            back_part.reshape(2, 2, 2, T, D),
            out_part.reshape(2, 2, 2, T, D),
            grad_gate_part.reshape(gu_shape),
            grad_up_part.reshape(gu_shape),
            grad_down_part.reshape(down_shape),
        ),
        [
            shape((T, D), f32),
            shape((T, D), f32),
            shape((TG, rows, FC)),
            shape((TG, rows, FC)),
            shape((2, down_rows, half), f32),
        ],
        40 + 6 * F,
        3,
        in_vmem=True,
        out_vmem=True,
        scratch=group_sum_scratch(T, D) * 2
        + weight_sum_scratch(gu_shape, 4) * 2
        + weight_sum_scratch(down_shape, 1)
        + [pltpu.VMEM((TG, rows, FC), bf16)] * 2,
    )
    output = (residual + out_sum).astype(bf16)
    grad_w_gate = grad_gate_own.transpose(1, 0, 2).reshape(rows, FF).astype(f32)
    grad_w_up = grad_up_own.transpose(1, 0, 2).reshape(rows, FF).astype(f32)
    grad_w_down = grad_down.transpose(1, 0, 2).reshape(down_rows, D)

    grad_residual = cotangent[0].astype(f32) + norm_back(back_two, residual, inverse_two, gain_two)
    grad_gain_two = jnp.sum(back_two * residual * inverse_two, 0)
    (grad_row,) = communicate(
        gather_row_kernel, (grad_residual.astype(bf16),), [shape((S, T, D))], 4, 4
    )
    grad_row = grad_row.reshape(row_len, D)
    grad_attended = contract_last(grad_row, wo).astype(bf16)
    grad_att = grad_attended.reshape(row_len, heads, head).transpose(1, 0, 2)
    grad_probs = jnp.einsum("htd,ud->htu", grad_att, value_low, preferred_element_type=f32)
    delta = jnp.sum(probs * grad_probs, -1, keepdims=True)
    grad_scores = (probs * (grad_probs - delta)).astype(bf16)
    grad_query_rot = jnp.einsum("htu,ud->htd", grad_scores, key_rot, preferred_element_type=f32)
    grad_key_rot = jnp.einsum("htu,htd->ud", grad_scores, query_rot, preferred_element_type=f32)
    grad_value = jnp.einsum("htu,htd->ud", probs_low, grad_att, preferred_element_type=f32)
    grad_query = rotate(grad_query_rot * scale, cosine, -sine)
    grad_query = grad_query.transpose(1, 0, 2).reshape(row_len, HC).astype(bf16)
    grad_key = rotate(grad_key_rot * scale, cosine, -sine)
    grad_kv = jnp.concatenate([grad_key, grad_value], 1).astype(bf16)
    back_one_part = contract_last(grad_query, wq) + contract_last(grad_kv, w_kv)
    grad_gain_one = jnp.sum(back_one_part * row_in * inverse_one, 0)
    grad_wq_part = contract_first(normed_one, grad_query).astype(bf16)
    grad_wo_part = contract_first(attended, grad_row).astype(bf16)
    grad_wkv_part = contract_first(normed_one, grad_kv).astype(bf16)
    grad_gains = jnp.stack([grad_gain_one, grad_gain_two], 1).astype(bf16)
    grad_kvg_part = jnp.concatenate([grad_wkv_part, grad_gains, jnp.zeros((D, head - 2), bf16)], 1)
    qo_part = jnp.concatenate(
        [
            grad_wq_part.reshape(S, FH, 2, rows, HC),
            grad_wo_part.reshape(FH, 2, rows, S, HC).transpose(3, 0, 1, 2, 4),
        ]
    )
    kv_shape = (S, FH, 2, rows, KV)
    back_one, grad_wq_own, grad_wo, grad_kvg = communicate(
        functools.partial(sum_attention_kernel, FH),
        (
            back_one_part.astype(bf16).reshape(2, 2, T, D),
            qo_part,
            grad_kvg_part.reshape(kv_shape),
        ),
        [
            shape((T, D), f32),
            shape((S, rows, HC)),
            shape((S, rows, HC), f32),
            shape((rows, KV), f32),
        ],
        24 + 4 * F,
        5,
        in_vmem=True,
        out_vmem=True,
        scratch=[
            pltpu.VMEM((2, T, D), bf16),
            pltpu.VMEM((T, D), bf16),
            pltpu.VMEM((T, D), bf16),
            *weight_sum_scratch(qo_part.shape, 2 * S),
            *weight_sum_scratch(kv_shape, S),
            pltpu.VMEM((2 * S, rows, HC), bf16),
            pltpu.VMEM((S, rows, KV), bf16),
            pltpu.VMEM((S, rows, KV), bf16),
        ],
    )
    own_inverse = lax.rsqrt(jnp.mean(inputs * inputs, -1, keepdims=True) + epsilon)
    grad_tokens = grad_residual + norm_back(back_one, inputs, own_inverse, gain_one)
    grad_w_query = grad_wq_own.transpose(1, 0, 2).reshape(rows, S * HC).astype(f32)
    grad_w_out = grad_wo.transpose(1, 0, 2).reshape(rows, D)
    offset = s * T
    return (
        output[None],
        lax.dynamic_slice_in_dim(key_rot, offset, T)[None],
        lax.dynamic_slice_in_dim(value_low, offset, T)[None],
        grad_tokens[None],
        grad_kvg[:, 2 * head],
        grad_w_query,
        grad_kvg[:, :head],
        grad_kvg[:, head : 2 * head],
        grad_w_out,
        grad_kvg[:, 2 * head + 1],
        grad_w_gate,
        grad_w_up,
        grad_w_down,
    )


def solution(mesh):
    token_spec = P("fsdp", "seq", None)
    flat, matrix = P(("seq", "fsdp")), P(("seq", "fsdp"), None)
    return jax.shard_map(
        functools.partial(per_device, mesh.shape["seq"], mesh.shape["fsdp"]),
        mesh=mesh,
        in_specs=(
            token_spec,
            P("fsdp", None),
            P("fsdp", "seq"),
            flat,
            matrix,
            matrix,
            matrix,
            matrix,
            flat,
            matrix,
            matrix,
            matrix,
            token_spec,
        ),
        out_specs=(
            token_spec,
            token_spec,
            token_spec,
            token_spec,
            flat,
            matrix,
            matrix,
            matrix,
            matrix,
            flat,
            matrix,
            matrix,
            matrix,
        ),
        check_vma=False,
    )
```

```python
import functools

import jax
import jax.numpy as jnp
from jax import lax
from jax.experimental import pallas as pl
from jax.experimental.pallas import tpu as pltpu
from jax.sharding import PartitionSpec as P

epsilon = 1e-05
MESH = pl.DeviceIdType.MESH
VMEM_LIMIT = 60 * 2**20
bf16 = jnp.bfloat16
f32 = jnp.float32


def dot(left, right):
    return jnp.dot(left, right, preferred_element_type=f32)


def contract_last(left, right):
    return lax.dot_general(left, right, (((1,), (1,)), ((), ())), preferred_element_type=f32)


def contract_first(left, right):
    return lax.dot_general(left, right, (((0,), (0,)), ((), ())), preferred_element_type=f32)


class Arrival:
    def __init__(self, copy):
        self.copy, self.waited = copy, False

    def wait(self):
        if not self.waited:
            self.waited = True
            self.copy.wait_recv()


class Links:
    def __init__(self, send, recv):
        self.send, self.recv, self.sent, self.count = send, recv, [], 0
        self.s, self.f = lax.axis_index("seq"), lax.axis_index("fsdp")

    def greet(self, masks):
        barrier = pltpu.get_barrier_semaphore()
        for a, b in masks:
            pl.semaphore_signal(
                barrier, inc=1, device_id=(self.s ^ a, self.f ^ b), device_id_type=MESH
            )
        pl.semaphore_wait(barrier, len(masks))

    def copy(self, source, target, device):
        self.count += 1
        return pltpu.make_async_remote_copy(
            src_ref=source,
            dst_ref=target,
            send_sem=self.send.at[self.count - 1],
            recv_sem=self.recv.at[self.count - 1],
            device_id=device,
            device_id_type=MESH,
        )

    def start(self, source, target, mask):
        copy = self.copy(source, target, (self.s ^ mask[0], self.f ^ mask[1]))
        copy.start()
        self.sent.append(Arrival(copy))
        return self.sent[-1]

    def pass_on(self, block, mask):
        return self.start(block, block, mask)

    def finish(self):
        for arrival in self.sent:
            arrival.wait()
        for arrival in self.sent:
            arrival.copy.wait_send()


class Group:
    def __init__(self, links, own, full, FQ):
        self.links, self.full, self.FQ = links, full, FQ
        self.s, self.tb = links.s, links.f // FQ
        self.there = links.start(own, full.at[self.s, self.tb], (0, FQ))
        self.across = links.start(own, full.at[self.s, self.tb], (2, 0))
        links.start(own, full.at[self.s, self.tb], (1, 0))

    def relay(self):
        s, tb, full = self.s, self.tb, self.full
        self.there.wait()
        across_two = self.links.pass_on(full.at[s, 1 - tb], (2, 0))
        self.links.pass_on(full.at[s, 1 - tb], (1, 0))
        self.across.wait()
        self.links.pass_on(full.at[s ^ 2, tb], (1, 0))
        across_two.wait()
        self.links.pass_on(full.at[s ^ 2, 1 - tb], (1, 0))


class Local:
    def __init__(self, sems, pairs):
        self.copies = [pltpu.make_async_copy(a, b, sems.at[i]) for i, (a, b) in enumerate(pairs)]
        self.open = set(range(len(pairs)))
        for copy in self.copies:
            copy.start()

    def wait(self, *which):
        for i in which or sorted(self.open):
            self.open.discard(i)
            self.copies[i].wait()


def row_loop(rows, step, body):
    if rows % step:
        body(slice(0, rows))
        return

    @pl.loop(0, rows // step)
    def _(i):
        body(pl.ds(pl.multiple_of(i * step, step), step))


def communicate(
    body, args, outs, copies, collective_id, in_vmem=False, out_vmem=False, scratch=(), kept=1
):
    def specs(inside, n):
        inside = [inside] * n if isinstance(inside, bool) else inside
        return [pl.BlockSpec(memory_space=pltpu.VMEM if i else pl.ANY) for i in inside]

    return pl.pallas_call(
        body,
        out_shape=outs,
        in_specs=specs(in_vmem, len(args)),
        out_specs=specs(out_vmem, len(outs)),
        scratch_shapes=[
            pltpu.SemaphoreType.DMA((copies,)),
            pltpu.SemaphoreType.DMA((copies,)),
            pltpu.SemaphoreType.DMA((kept,)),
            *scratch,
        ],
        compiler_params=pltpu.CompilerParams(
            collective_id=collective_id, has_side_effects=True, vmem_limit_bytes=VMEM_LIMIT
        ),
    )(*args)


def shape(dims, kind=bf16):
    return jax.ShapeDtypeStruct(dims, kind)


def group_masks(FQ):
    return [(a, b) for a in range(4) for b in (0, FQ) if (a, b) != (0, 0)]


class Line:
    def __init__(self, links, views, FH):
        self.links, self.views, self.FH = links, views, FH
        self.h, self.l = links.f // 2, links.f % 2
        self.right, self.left, self.pending = [], [], []

    def here(self, h):
        return self.views(2 * h + self.l)

    def step(self, j):
        h, FH = self.h, self.FH
        rights = [
            self.links.copy(block, block, (self.links.s, self.links.f + 2))
            for block in self.here(lax.max(h - j, 0))
        ]
        lefts = [
            self.links.copy(block, block, (self.links.s, self.links.f - 2))
            for block in self.here(lax.min(h + j, FH - 1))
        ]
        for i in range(len(rights)):

            @pl.when((h >= j) & (h < FH - 1))
            def _():
                rights[i].start()

            @pl.when((h + j < FH) & (h > 0))
            def _():
                lefts[i].start()

        self.right.append(rights)
        self.left.append(lefts)

    def arrived(self, j):
        h, FH = self.h, self.FH
        up = self.here(lax.max(h - 1 - j, 0))
        down = self.here(lax.min(h + 1 + j, FH - 1))
        for i in range(len(up)):
            for blocks, copies, there in (
                (up, self.right[j], h - 1 - j >= 0),
                (down, self.left[j], h + 1 + j < FH),
            ):
                on = self.links.copy(
                    blocks[i], blocks[i], (self.links.s, self.links.f ^ 1)
                )
                self.pending.append((on, there))

                @pl.when(there)
                def _():
                    copies[i].wait_recv()
                    on.start()

    def finish(self):
        h, FH = self.h, self.FH
        for on, there in self.pending:

            @pl.when(there)
            def _():
                on.wait_recv()
                on.wait_send()

        for j in range(FH - 1):
            for i in range(len(self.right[j])):

                @pl.when((h >= j) & (h < FH - 1))
                def _():
                    self.right[j][i].wait_send()

                @pl.when((h + j < FH) & (h > 0))
                def _():
                    self.left[j][i].wait_send()


def rows_of(ref):
    return ref[...].reshape(-1, ref.shape[-1])


def rotation(table):
    half = table.shape[-1] // 2
    swapped = pltpu.roll(table, half, 1)
    first = lax.broadcasted_iota(jnp.int32, table.shape, 1) < half
    return jnp.where(first, table, swapped), jnp.where(first, -swapped, table)


def turn(vector, factors):
    return vector * factors[0] + pltpu.roll(vector, vector.shape[-1] // 2, 1) * factors[1]


def forward_kernel(FH, FQ, *refs):
    tok, tab, wq, kvg, wo, gate, up, down, cot, bias = refs[:10]
    (q_g, kv_g, o_g, gate_g, up_g, down_g, cot_g) = refs[10:17]
    (tab_g, normed_one, q_rot, k_rot, v_low, attended, keys, values) = refs[17:25]
    residual, normed_all, tok_g = refs[25:28]
    send, recv, here, part, from_core, from_x, to_x, normed_two = refs[28:]
    T = residual.shape[0]
    D = residual.shape[1]
    HC = attended.shape[1]
    head = k_rot.shape[1]
    row_len = k_rot.shape[0]
    links = Links(send, recv)
    s, f = links.s, links.f
    x, core = s // 2, s % 2
    tb, q = f // FQ, f % FQ
    t = 2 * s + tb
    evens_q = [2 * k for k in range(1, FQ // 2)]
    links.greet(
        [(a, 0) for a in (1, 2, 3)]
        + [(0, 1)]
        + [(0, 2 * k) for k in range(1, FH)]
        + [(a, FQ) for a in (1, 2, 3)]
    )
    local = Local(
        here,
        [
            (wq.at[s], q_g.at[s, f]),
            (kvg, kv_g.at[s, f]),
            (gate.at[t], gate_g.at[t, q]),
            (up.at[t], up_g.at[t, q]),
            (wo, o_g.at[f]),
            (tok, tok_g.at[s]),
            (tab, tab_g.at[s]),
            (down, down_g.at[q]),
            (cot, cot_g.at[s, tb]),
        ],
    )
    first = []
    for a in (1, 2, 3):
        first.append(links.start(wq.at[s ^ a], q_g.at[s, f], (a, 0)))
        first.append(links.start(kvg, kv_g.at[s, f], (a, 0)))
    local.wait(4)
    o_line = Line(links, lambda place: [o_g.at[place]], FH)
    qk_line = Line(links, lambda place: [q_g.at[:, place], kv_g.at[:, place]], FH)
    o_line.step(0)
    needed = [links.pass_on(o_g.at[f], (0, 1))]
    tok_x = links.start(tok, tok_g.at[s], (2, 0))
    needed.append(links.start(tok, tok_g.at[s], (1, 0)))
    needed += [links.start(tab, tab_g.at[s], (a, 0)) for a in (1, 2, 3)]
    local.wait(0, 1)
    for arrival in first:
        arrival.wait()
    qk_line.step(0)
    needed += [links.pass_on(r.at[:, f], (0, 1)) for r in (q_g, kv_g)]
    ffn = []
    for a, b in group_masks(FQ):
        to = 2 * (s ^ a) + (tb ^ (b // FQ))
        ffn.append(links.start(gate.at[to], gate_g.at[t, q], (a, b)))
        ffn.append(links.start(up.at[to], up_g.at[t, q], (a, b)))
    tok_x.wait()
    needed.append(links.pass_on(tok_g.at[s ^ 2], (1, 0)))
    for j in range(FH - 1):
        o_line.arrived(j)
        if j + 1 < FH - 1:
            o_line.step(j + 1)
        qk_line.arrived(j)
        if j + 1 < FH - 1:
            qk_line.step(j + 1)
    down_y = links.start(down, down_g.at[q], (0, 1))
    down_z = [links.start(down, down_g.at[q], (0, b)) for b in evens_q]
    local.wait(2, 3)
    for arrival in ffn:
        arrival.wait()
    gu_y = [links.pass_on(r.at[:, q], (0, 1)) for r in (gate_g, up_g)]
    gu_z = [[links.pass_on(r.at[:, q], (0, b)) for r in (gate_g, up_g)] for b in evens_q]
    cot_group = Group(links, cot, cot_g, FQ)
    for arrival in needed:
        arrival.wait()
    o_line.finish()
    qk_line.finish()
    local.wait(5, 6)

    place = lax.broadcasted_iota(jnp.int32, (8, head), 0)
    lane = lax.broadcasted_iota(jnp.int32, (8, head), 1)
    pick = (place == lane).astype(bf16)
    kv_full = rows_of(kv_g)
    gains = contract_last(pick, kv_full[:, 2 * head :])
    gain_one, gain_two = gains[0:1], gains[1:2]

    @pl.loop(0, row_len // 16)
    def _(i):
        rows = pl.ds(pl.multiple_of(i * 16, 16), 16)
        inner = pl.ds(pl.multiple_of(lax.rem(i, T // 16) * 16, 16), 16)
        value = tok_g[i // (T // 16), inner].astype(f32)
        inverse = lax.rsqrt(jnp.mean(value * value, -1, keepdims=True) + epsilon)
        normed_one[rows] = (value * inverse * gain_one).astype(bf16)

    factors = rotation(rows_of(tab_g))
    kv = dot(normed_one[...], kv_full[:, : 2 * head])
    k_rot[...] = turn(kv[:, :head], factors).astype(bf16)
    v_low[...] = kv[:, head:].astype(bf16)
    heads = HC // head
    for n in range(0, heads, 2):
        columns = slice(n * head, (n + 2) * head)
        both = dot(normed_one[...], q_g[:, :, :, columns].reshape(D, 2 * head))
        for j in (0, 1):
            q_rot[n + j] = turn(both[:, j * head : (j + 1) * head], factors).astype(bf16)
    keys[...] = k_rot[pl.ds(pl.multiple_of(s * T, T), T)]
    values[...] = v_low[pl.ds(pl.multiple_of(s * T, T), T)]
    scale = head ** (-0.5)
    for r in range(row_len // T):
        rows, seen = slice(r * T, (r + 1) * T), slice(0, (r + 1) * T)
        for n in range(heads):
            scores = contract_last(q_rot[n, rows], k_rot[seen]) * scale + bias[rows, seen]
            scores = jnp.exp(scores - jnp.max(scores, -1, keepdims=True))
            probs = (scores / jnp.sum(scores, -1, keepdims=True)).astype(bf16)
            attended[rows, n * head : (n + 1) * head] = dot(probs, v_low[seen]).astype(bf16)

    def project(x_to, core_to):
        rows = attended[pl.ds(pl.multiple_of((2 * x_to + core_to) * T, T), T)]
        for n in range(0, D, HC):
            columns = slice(n, n + HC)
            full = o_g[:, :, columns].reshape(HC, HC)
            part[x_to, core_to, :, columns] = dot(rows, full).astype(bf16)

    project(1 - x, 1 - core)
    far = links.start(part.at[1 - x, 1 - core], from_core.at[0], (1, 0))
    project(1 - x, core)
    project(x, 1 - core)
    near = links.start(part.at[x, 1 - core], from_core.at[1], (1, 0))
    far.wait()

    def add_x(rows):
        total = part[1 - x, core, rows].astype(f32) + from_core[0, rows].astype(f32)
        to_x[rows] = total.astype(bf16)

    row_loop(T, 16, add_x)
    across = links.start(to_x, from_x, (2, 0))
    project(x, core)
    near.wait()
    across.wait()

    def add_last(rows):
        total = tok_g[s, rows].astype(f32) + part[x, core, rows].astype(f32)
        total += from_core[1, rows].astype(f32) + from_x[rows].astype(f32)
        residual[rows] = total
        inverse = lax.rsqrt(jnp.mean(total * total, -1, keepdims=True) + epsilon)
        normed_two[rows] = (total * inverse * gain_two).astype(bf16)

    row_loop(T, 16, add_last)
    normed_group = Group(links, normed_two, normed_all, FQ)
    mine = pltpu.make_async_copy(normed_two, normed_all.at[s, tb], here.at[9])
    mine.start()
    half = down_g.shape[2] // 2
    low_half, high_half = pl.ds(0, half), pl.ds(half, half)
    low_t, high_t = pl.ds(0, 4), pl.ds(4, 4)
    down_y.wait()
    for b in evens_q:
        links.pass_on(down_g.at[q ^ 1, :, high_half], (0, b))
    for arrival, b in zip(down_z, evens_q):
        arrival.wait()
        links.pass_on(down_g.at[q ^ b, :, low_half], (0, 1))
    for r, arrival in zip((gate_g, up_g), gu_y):
        arrival.wait()
        for b in evens_q:
            links.pass_on(r.at[high_t, q ^ 1], (0, b))
    for arrivals, b in zip(gu_z, evens_q):
        for r, arrival in zip((gate_g, up_g), arrivals):
            arrival.wait()
            links.pass_on(r.at[low_t, q ^ b], (0, 1))
    cot_group.relay()
    normed_group.relay()
    links.finish()
    local.wait()
    mine.wait()


def gather_row_kernel(own, full, send, recv, here):
    links = Links(send, recv)
    links.greet([(1, 0), (2, 0)])
    s = links.s
    local = Local(here, [(own, full.at[s])])
    across = links.start(own, full.at[s], (2, 0))
    links.start(own, full.at[s], (1, 0))
    across.wait()
    links.pass_on(full.at[s ^ 2], (1, 0))
    links.finish()
    local.wait()


class RowSum:
    def __init__(self, links, parts, from_core, from_x, to_x):
        self.links, self.parts = links, parts
        self.from_core, self.from_x, self.to_x = from_core, from_x, to_x
        self.x, self.core = links.s // 2, links.s % 2
        self.far = links.start(parts.at[1 - self.x, 1 - self.core], from_core.at[0], (1, 0))
        self.near = links.start(parts.at[self.x, 1 - self.core], from_core.at[1], (1, 0))

    def middle(self):
        self.far.wait()
        x, core = self.x, self.core

        def add(rows):
            total = self.parts[1 - x, core, rows].astype(f32) + self.from_core[0, rows].astype(f32)
            self.to_x[rows] = total.astype(bf16)

        row_loop(self.to_x.shape[0], 16, add)
        self.across = self.links.start(self.to_x, self.from_x, (2, 0))

    def total(self, rows):
        return (
            self.parts[self.x, self.core, rows].astype(f32)
            + self.from_core[1, rows].astype(f32)
            + self.from_x[rows].astype(f32)
        )

    def last(self, out):
        self.near.wait()
        self.across.wait()

        def add(rows):
            out[rows] = self.total(rows)

        row_loop(out.shape[0], 16, add)


class GroupSum:
    def __init__(self, links, parts, bufs, FQ):
        self.links, self.parts, self.FQ = links, parts, FQ
        self.from_core, self.from_x, self.to_x, self.from_t, self.to_t = bufs
        self.x, self.core, self.tb = links.s // 2, links.s % 2, links.f // FQ
        self.far = links.start(parts.at[1 - self.x, 1 - self.core], self.from_core.at[0], (1, 0))
        self.near = links.start(parts.at[self.x, 1 - self.core], self.from_core.at[1], (1, 0))

    def to_other_x(self):
        self.far.wait()
        x, core = self.x, self.core

        def add(rows):
            for j in (0, 1):
                total = self.parts[1 - x, core, j, rows].astype(f32)
                self.to_x[j, rows] = (total + self.from_core[0, j, rows].astype(f32)).astype(bf16)

        row_loop(self.to_x.shape[1], 16, add)
        self.across = self.links.start(self.to_x, self.from_x, (2, 0))

    def total(self, j, rows):
        return (
            self.parts[self.x, self.core, j, rows].astype(f32)
            + self.from_core[1, j, rows].astype(f32)
            + self.from_x[j, rows].astype(f32)
        )

    def to_other_t(self):
        self.near.wait()
        self.across.wait()

        def add(rows):
            self.to_t[rows] = self.total(1 - self.tb, rows).astype(bf16)

        row_loop(self.to_t.shape[0], 16, add)
        self.there = self.links.start(self.to_t, self.from_t, (0, self.FQ))

    def last(self, out):
        self.there.wait()

        def add(rows):
            out[rows] = self.total(self.tb, rows) + self.from_t[rows].astype(f32)

        row_loop(out.shape[0], 16, add)


def group_sum_scratch(seq_len, width):
    block = (seq_len, width)
    return [
        pltpu.VMEM((2, 2, *block), bf16),
        pltpu.VMEM((2, *block), bf16),
        pltpu.VMEM((2, *block), bf16),
        pltpu.VMEM(block, bf16),
        pltpu.VMEM(block, bf16),
    ]


class WeightSum:
    def __init__(self, links, parts, total, bufs, first):
        self.links, self.parts, self.total = links, parts, total
        self.low_l, self.low_mid, self.low_w, self.high_w, self.high_mid, self.high_l = bufs
        leads, self.W = parts.shape[:2]
        self.rows = parts.shape[3]
        self.low, self.high = range(first), range(first, leads)
        self.l = links.f % 2
        self.w = (links.f // 2) % self.W
        if self.low:
            source = parts.at[pl.ds(0, first), :, 1 - self.l]
            self.by_l = links.start(source, self.low_l, (0, 1))
        if self.high:
            self.by_w = [
                links.start(
                    parts.at[pl.ds(first, leads - first), self.w ^ k], self.high_w.at[k - 1], (0, 2 * k)
                )
                for k in range(1, self.W)
            ]

    def middle(self):
        parts, w, l = self.parts, self.w, self.l
        if self.low:
            self.by_l.wait()
            for k in range(1, self.W):
                for i in self.low:

                    def add(rows, k=k, i=i):
                        total = parts[i, w ^ k, l, rows].astype(f32)
                        total += self.low_l[i, w ^ k, rows].astype(f32)
                        self.low_mid[k - 1, i, rows] = total.astype(bf16)

                    row_loop(self.rows, 16, add)
            self.low_end = [
                self.links.start(self.low_mid.at[k - 1], self.low_w.at[k - 1], (0, 2 * k))
                for k in range(1, self.W)
            ]
        if self.high:
            for arrival in self.by_w:
                arrival.wait()
            for j, i in enumerate(self.high):

                def add(rows, i=i, j=j):
                    total = parts[i, w, 1 - l, rows].astype(f32)
                    for k in range(1, self.W):
                        total += self.high_w[k - 1, j, 1 - l, rows].astype(f32)
                    self.high_mid[j, rows] = total.astype(bf16)

                row_loop(self.rows, 16, add)
            self.high_end = self.links.start(self.high_mid, self.high_l, (0, 1))

    def last(self):
        parts, w, l = self.parts, self.w, self.l
        if self.low:
            for arrival in self.low_end:
                arrival.wait()
            for i in self.low:

                def add(rows, i=i):
                    total = parts[i, w, l, rows].astype(f32) + self.low_l[i, w, rows].astype(f32)
                    for k in range(1, self.W):
                        total += self.low_w[k - 1, i, rows].astype(f32)
                    self.total[i, rows] = total.astype(self.total.dtype)

                row_loop(self.rows, 16, add)
        if self.high:
            self.high_end.wait()
            for j, i in enumerate(self.high):

                def add(rows, i=i, j=j):
                    total = parts[i, w, l, rows].astype(f32) + self.high_l[j, rows].astype(f32)
                    for k in range(1, self.W):
                        total += self.high_w[k - 1, j, l, rows].astype(f32)
                    self.total[i, rows] = total.astype(self.total.dtype)

                row_loop(self.rows, 16, add)


def weight_sum_scratch(parts, first):
    leads, W, _, rows, width = parts
    block = (rows, width)
    high = leads - first
    return [
        pltpu.VMEM((max(first, 1), W, *block), bf16),
        pltpu.VMEM((max(W - 1, 1), max(first, 1), *block), bf16),
        pltpu.VMEM((max(W - 1, 1), max(first, 1), *block), bf16),
        pltpu.VMEM((max(W - 1, 1), max(high, 1), 2, *block) if high else (8, 128), bf16),
        pltpu.VMEM((max(high, 1), *block) if high else (8, 128), bf16),
        pltpu.VMEM((max(high, 1), *block) if high else (8, 128), bf16),
    ]


def sum_ffn_kernel(FQ, *refs):
    back, out, gate, up, down = refs[:5]
    back_sum, out_sum, gate_own, up_own, down_sum = refs[5:10]
    send, recv, here = refs[10:13]
    refs = refs[13:]
    back_bufs, out_bufs, gate_bufs, up_bufs, down_bufs = refs[:5], refs[5:10], refs[10:16], refs[16:22], refs[22:28]
    gate_sum, up_sum = refs[28:]
    links = Links(send, recv)
    W = gate.shape[1]
    links.greet([(0, 1)] + [(0, 2 * k) for k in range(1, W)] + group_masks(FQ))
    t = 2 * links.s + links.f // FQ
    back_total = GroupSum(links, back, back_bufs, FQ)
    sums = [
        WeightSum(links, gate, gate_sum, gate_bufs, 4),
        WeightSum(links, up, up_sum, up_bufs, 4),
        WeightSum(links, down, down_sum, down_bufs, 1),
    ]
    out_total = GroupSum(links, out, out_bufs, FQ)
    back_total.to_other_x()
    out_total.to_other_x()
    back_total.to_other_t()
    out_total.to_other_t()
    back_total.last(back_sum)
    out_total.last(out_sum)
    for weight in sums:
        weight.middle()
    for weight in sums:
        weight.last()
    for a, b in group_masks(FQ):
        to = 2 * (links.s ^ a) + ((links.f // FQ) ^ (b // FQ))
        links.start(gate_sum.at[to], gate_own.at[t], (a, b))
        links.start(up_sum.at[to], up_own.at[t], (a, b))
    gate_own[t] = gate_sum[t]
    up_own[t] = up_sum[t]
    links.finish()


def sum_attention_kernel(FH, *refs):
    back, qo, kv = refs[:3]
    back_sum, q_own, o_sum, kv_sum = refs[3:7]
    send, recv, here, from_core, from_x, to_x = refs[7:13]
    qo_bufs, kv_bufs, qo_total, kv_total, kv_own = refs[13:19], refs[19:25], refs[25], refs[26], refs[27]
    links = Links(send, recv)
    links.greet([(1, 0), (2, 0), (3, 0), (0, 1)] + [(0, 2 * k) for k in range(1, FH)])
    s = links.s
    back_total = RowSum(links, back, from_core, from_x, to_x)
    kv_weight = WeightSum(links, kv, kv_total, kv_bufs, 4)
    qo_weight = WeightSum(links, qo, qo_total, qo_bufs, 8)
    back_total.middle()
    kv_weight.middle()
    qo_weight.middle()
    back_total.last(back_sum)
    kv_weight.last()
    for a in (1, 2, 3):
        links.start(kv_total.at[s ^ a], kv_own.at[s], (a, 0))
    qo_weight.last()
    for a in (1, 2, 3):
        links.start(qo_total.at[s ^ a], q_own.at[s], (a, 0))
    q_own[s] = qo_total[s]
    kv_own[s] = kv_total[s]
    for i in range(4):
        o_sum[i] = qo_total[4 + i].astype(f32)
    links.finish()

    def add(rows):
        total = kv_own[0, rows].astype(f32)
        for i in range(1, 4):
            total += kv_own[i, rows].astype(f32)
        kv_sum[rows] = total

    row_loop(kv_sum.shape[0], 16, add)


def angle_tables(position_row, head_size):
    half_head = head_size // 2
    frequency = 10000.0 ** (-jnp.arange(half_head, dtype=f32) * 2.0 / head_size)
    phase_angle = position_row.astype(f32)[:, None] * frequency[None, :]
    return (jnp.cos(phase_angle), jnp.sin(phase_angle))


def rotate(tensor_in, cosine, sine):
    half_head = tensor_in.shape[-1] // 2
    first_half = tensor_in[..., :half_head]
    second_half = tensor_in[..., half_head:]
    return jnp.concatenate(
        [first_half * cosine - second_half * sine, second_half * cosine + first_half * sine], -1
    )


def norm_back(grad_normed, inputs, inverse_rms, gain_full):
    scaled = grad_normed * gain_full
    width = inputs.shape[-1]
    inner_sum = jnp.sum(scaled * inputs, -1, keepdims=True)
    return inverse_rms * scaled - inputs * inverse_rms**3 * inner_sum / width


def per_device(
    S,
    F,
    tokens,
    segments,
    positions,
    gain_one,
    w_query,
    w_key,
    w_value,
    w_out,
    gain_two,
    w_gate,
    w_up,
    w_down,
    cotangent,
):
    T, D = tokens.shape[1:]
    head = w_key.shape[1]
    row_len = segments.shape[1]
    rows = w_query.shape[0]
    down_rows = w_down.shape[0]
    FF = w_gate.shape[1]
    FH, FQ = F // 2, F // 2
    W = FQ // 2
    TG = 2 * S
    HC = w_query.shape[1] // S
    heads = HC // head
    FC = FF // TG
    s = lax.axis_index("seq")

    def column_blocks(weight, n):
        return weight.reshape(rows, n, -1).transpose(1, 0, 2)

    gains = jnp.stack([gain_one, gain_two], 1)
    kvg = jnp.concatenate([w_key, w_value, gains, jnp.zeros((rows, head - 2), bf16)], 1)
    KV = kvg.shape[1]
    table = jnp.concatenate(angle_tables(positions[0], head), 1)
    segment = segments[0]
    index = jnp.arange(row_len)
    allowed = (index[None, :] <= index[:, None]) & (segment[None, :] == segment[:, None])
    bias = jnp.where(allowed, 0.0, -1e30)
    outs = [
        (True, (S, F, rows, HC), bf16),
        (True, (S, F, rows, KV), bf16),
        (True, (F, rows, D), bf16),
        (False, (TG, FQ, rows, FC), bf16),
        (False, (TG, FQ, rows, FC), bf16),
        (False, (FQ, down_rows, D), bf16),
        (False, (S, 2, T, D), bf16),
        (True, (S, T, head), f32),
        (True, (row_len, D), bf16),
        (True, (heads, row_len, head), bf16),
        (True, (row_len, head), bf16),
        (True, (row_len, head), bf16),
        (True, (row_len, HC), bf16),
        (True, (T, head), bf16),
        (True, (T, head), bf16),
        (True, (T, D), f32),
        (False, (S, 2, T, D), bf16),
        (True, (S, T, D), bf16),
    ]
    (wq, kvg, wo, gate_w, up_w, down_w, cot, table, normed_one, query_rot, key_rot, value_low, attended, keys, values, residual, normed_all, tok) = communicate(
        functools.partial(forward_kernel, FH, FQ),
        (
            tokens[0],
            table,
            column_blocks(w_query, S),
            kvg,
            w_out,
            column_blocks(w_gate, TG),
            column_blocks(w_up, TG),
            w_down,
            cotangent[0],
            bias,
        ),
        [shape(dims, kind) for _, dims, kind in outs],
        120 + 18 * F,
        0,
        in_vmem=[False] * 9 + [True],
        out_vmem=[inside for inside, _, _ in outs],
        kept=10,
        scratch=[
            pltpu.VMEM((2, 2, T, D), bf16),
            pltpu.VMEM((2, T, D), bf16),
            pltpu.VMEM((T, D), bf16),
            pltpu.VMEM((T, D), bf16),
            pltpu.VMEM((T, D), bf16),
        ],
    )
    wq = wq.reshape(D, HC)
    kvg = kvg.reshape(D, KV)
    w_kv = kvg[:, : 2 * head]
    gain_one = kvg[:, 2 * head].astype(f32)
    gain_two = kvg[:, 2 * head + 1].astype(f32)
    wo = wo.reshape(HC, D)
    gate_w, up_w = gate_w.reshape(D, FC), up_w.reshape(D, FC)
    down_w = down_w.reshape(FC, D)
    cot = cot.reshape(TG * T, D)
    normed_all = normed_all.reshape(TG * T, D)
    cosine, sine = jnp.split(table.reshape(row_len, head), 2, 1)
    inputs = tokens[0].astype(f32)
    row_in = tok.reshape(row_len, D).astype(f32)
    inverse_one = lax.rsqrt(jnp.mean(row_in * row_in, -1, keepdims=True) + epsilon)
    inverse_two = lax.rsqrt(jnp.mean(residual * residual, -1, keepdims=True) + epsilon)

    gate_proj = dot(normed_all, gate_w)
    up_proj = dot(normed_all, up_w)
    sig = jax.nn.sigmoid(gate_proj)
    inner = (gate_proj * sig * up_proj).astype(bf16)
    out_part = dot(inner, down_w).astype(bf16)
    grad_inner = contract_last(cot, down_w)
    grad_gate = (grad_inner * up_proj * sig * (1.0 + gate_proj * (1.0 - sig))).astype(bf16)
    grad_up = (grad_inner * gate_proj * sig).astype(bf16)
    back_part = (contract_last(grad_gate, gate_w) + contract_last(grad_up, up_w)).astype(bf16)
    half = D // 2
    grad_down_part = jnp.stack(
        [contract_first(inner, cot[:, :half]), contract_first(inner, cot[:, half:])]
    ).astype(bf16)
    grad_gate_part = contract_first(normed_all, grad_gate).astype(bf16)
    grad_up_part = contract_first(normed_all, grad_up).astype(bf16)

    gu_shape = (TG, W, 2, rows, FC)
    down_shape = (2, W, 2, down_rows, half)
    back_two, out_sum, grad_gate_own, grad_up_own, grad_down = communicate(
        functools.partial(sum_ffn_kernel, FQ),
        (
            back_part.reshape(2, 2, 2, T, D),
            out_part.reshape(2, 2, 2, T, D),
            grad_gate_part.reshape(gu_shape),
            grad_up_part.reshape(gu_shape),
            grad_down_part.reshape(down_shape),
        ),
        [
            shape((T, D), f32),
            shape((T, D), f32),
            shape((TG, rows, FC)),
            shape((TG, rows, FC)),
            shape((2, down_rows, half), f32),
        ],
        40 + 6 * F,
        3,
        in_vmem=True,
        out_vmem=True,
        scratch=group_sum_scratch(T, D) * 2
        + weight_sum_scratch(gu_shape, 4) * 2
        + weight_sum_scratch(down_shape, 1)
        + [pltpu.VMEM((TG, rows, FC), bf16)] * 2,
    )
    output = (residual + out_sum).astype(bf16)
    grad_w_gate = grad_gate_own.transpose(1, 0, 2).reshape(rows, FF).astype(f32)
    grad_w_up = grad_up_own.transpose(1, 0, 2).reshape(rows, FF).astype(f32)
    grad_w_down = grad_down.transpose(1, 0, 2).reshape(down_rows, D)

    grad_residual = cotangent[0].astype(f32) + norm_back(back_two, residual, inverse_two, gain_two)
    grad_gain_two = jnp.sum(back_two * residual * inverse_two, 0)
    (grad_row,) = communicate(
        gather_row_kernel, (grad_residual.astype(bf16),), [shape((S, T, D))], 4, 4
    )
    grad_row = grad_row.reshape(row_len, D)
    grad_attended = contract_last(grad_row, wo).astype(bf16)
    grad_att = grad_attended.reshape(row_len, heads, head).transpose(1, 0, 2)
    grad_probs = jnp.einsum("htd,ud->htu", grad_att, value_low, preferred_element_type=f32)
    scale = head ** (-0.5)
    scores = jnp.einsum("htd,ud->htu", query_rot, key_rot, preferred_element_type=f32) * scale
    exp_scores = jnp.exp(scores + bias - jnp.max(scores + bias, -1, keepdims=True))
    probs = exp_scores / jnp.sum(exp_scores, -1, keepdims=True)
    probs_low = probs.astype(bf16)
    delta = jnp.sum(probs * grad_probs, -1, keepdims=True)
    grad_scores = (probs * (grad_probs - delta)).astype(bf16)
    grad_query_rot = jnp.einsum("htu,ud->htd", grad_scores, key_rot, preferred_element_type=f32)
    grad_key_rot = jnp.einsum("htu,htd->ud", grad_scores, query_rot, preferred_element_type=f32)
    grad_value = jnp.einsum("htu,htd->ud", probs_low, grad_att, preferred_element_type=f32)
    grad_query = rotate(grad_query_rot * scale, cosine, -sine)
    grad_query = grad_query.transpose(1, 0, 2).reshape(row_len, HC).astype(bf16)
    grad_key = rotate(grad_key_rot * scale, cosine, -sine)
    grad_kv = jnp.concatenate([grad_key, grad_value], 1).astype(bf16)
    back_one_part = contract_last(grad_query, wq) + contract_last(grad_kv, w_kv)
    grad_gain_one = jnp.sum(back_one_part * row_in * inverse_one, 0)
    grad_wq_part = contract_first(normed_one, grad_query).astype(bf16)
    grad_wo_part = contract_first(attended, grad_row).astype(bf16)
    grad_wkv_part = contract_first(normed_one, grad_kv).astype(bf16)
    grad_gains = jnp.stack([grad_gain_one, grad_gain_two], 1).astype(bf16)
    grad_kvg_part = jnp.concatenate([grad_wkv_part, grad_gains, jnp.zeros((D, head - 2), bf16)], 1)
    qo_part = jnp.concatenate(
        [
            grad_wq_part.reshape(S, FH, 2, rows, HC),
            grad_wo_part.reshape(FH, 2, rows, S, HC).transpose(3, 0, 1, 2, 4),
        ]
    )
    kv_shape = (S, FH, 2, rows, KV)
    back_one, grad_wq_own, grad_wo, grad_kvg = communicate(
        functools.partial(sum_attention_kernel, FH),
        (
            back_one_part.astype(bf16).reshape(2, 2, T, D),
            qo_part,
            grad_kvg_part.reshape(kv_shape),
        ),
        [
            shape((T, D), f32),
            shape((S, rows, HC)),
            shape((S, rows, HC), f32),
            shape((rows, KV), f32),
        ],
        24 + 4 * F,
        5,
        in_vmem=True,
        out_vmem=True,
        scratch=[
            pltpu.VMEM((2, T, D), bf16),
            pltpu.VMEM((T, D), bf16),
            pltpu.VMEM((T, D), bf16),
            *weight_sum_scratch(qo_part.shape, 2 * S),
            *weight_sum_scratch(kv_shape, S),
            pltpu.VMEM((2 * S, rows, HC), bf16),
            pltpu.VMEM((S, rows, KV), bf16),
            pltpu.VMEM((S, rows, KV), bf16),
        ],
    )
    own_inverse = lax.rsqrt(jnp.mean(inputs * inputs, -1, keepdims=True) + epsilon)
    grad_tokens = grad_residual + norm_back(back_one, inputs, own_inverse, gain_one)
    grad_w_query = grad_wq_own.transpose(1, 0, 2).reshape(rows, S * HC).astype(f32)
    grad_w_out = grad_wo.transpose(1, 0, 2).reshape(rows, D)
    return (
        output[None],
        keys[None],
        values[None],
        grad_tokens[None],
        grad_kvg[:, 2 * head],
        grad_w_query,
        grad_kvg[:, :head],
        grad_kvg[:, head : 2 * head],
        grad_w_out,
        grad_kvg[:, 2 * head + 1],
        grad_w_gate,
        grad_w_up,
        grad_w_down,
    )


def solution(mesh):
    token_spec = P("fsdp", "seq", None)
    flat, matrix = P(("seq", "fsdp")), P(("seq", "fsdp"), None)
    return jax.shard_map(
        functools.partial(per_device, mesh.shape["seq"], mesh.shape["fsdp"]),
        mesh=mesh,
        in_specs=(
            token_spec,
            P("fsdp", None),
            P("fsdp", "seq"),
            flat,
            matrix,
            matrix,
            matrix,
            matrix,
            flat,
            matrix,
            matrix,
            matrix,
            token_spec,
        ),
        out_specs=(
            token_spec,
            token_spec,
            token_spec,
            token_spec,
            flat,
            matrix,
            matrix,
            matrix,
            matrix,
            flat,
            matrix,
            matrix,
            matrix,
        ),
        check_vma=False,
    )
```

```python
import functools

import jax
import jax.numpy as jnp
from jax import lax
from jax.experimental import pallas as pl
from jax.experimental.pallas import tpu as pltpu
from jax.sharding import PartitionSpec as P

epsilon = 1e-05
MESH = pl.DeviceIdType.MESH
VMEM_LIMIT = 64 * 2**20 - 2**18
bf16 = jnp.bfloat16
f32 = jnp.float32


def dot(left, right):
    return jnp.dot(left, right, preferred_element_type=f32)


def contract_last(left, right):
    return lax.dot_general(left, right, (((1,), (1,)), ((), ())), preferred_element_type=f32)


def contract_first(left, right):
    return lax.dot_general(left, right, (((0,), (0,)), ((), ())), preferred_element_type=f32)


class Arrival:
    def __init__(self, copy):
        self.copy, self.waited, self.left = copy, False, False

    def wait(self):
        if not self.waited:
            self.waited = True
            self.copy.wait_recv()

    def wait_sent(self):
        if not self.left:
            self.left = True
            self.copy.wait_send()


class Links:
    def __init__(self, send, recv):
        self.send, self.recv, self.sent, self.count = send, recv, [], 0
        self.s, self.f = lax.axis_index("seq"), lax.axis_index("fsdp")

    def greet(self, masks):
        barrier = pltpu.get_barrier_semaphore()
        for a, b in masks:
            pl.semaphore_signal(
                barrier, inc=1, device_id=(self.s ^ a, self.f ^ b), device_id_type=MESH
            )
        pl.semaphore_wait(barrier, len(masks))

    def copy(self, source, target, device):
        self.count += 1
        return pltpu.make_async_remote_copy(
            src_ref=source,
            dst_ref=target,
            send_sem=self.send.at[self.count - 1],
            recv_sem=self.recv.at[self.count - 1],
            device_id=device,
            device_id_type=MESH,
        )

    def start(self, source, target, mask):
        copy = self.copy(source, target, (self.s ^ mask[0], self.f ^ mask[1]))
        copy.start()
        self.sent.append(Arrival(copy))
        return self.sent[-1]

    def pass_on(self, block, mask):
        return self.start(block, block, mask)

    def finish(self):
        for arrival in self.sent:
            arrival.wait()
        for arrival in self.sent:
            arrival.wait_sent()


class Group:
    def __init__(self, links, own, full, FQ):
        self.links, self.full = links, full
        self.x, self.core, self.tb = links.s // 2, links.s % 2, links.f // FQ
        place = full.at[self.x, self.tb, self.core]
        self.there = links.start(own, place, (0, FQ))
        self.across = links.start(own, place, (2, 0))
        links.start(own, place, (1, 0))

    def relay(self):
        x, tb, core, full = self.x, self.tb, self.core, self.full
        self.there.wait()
        across_two = self.links.pass_on(full.at[x, 1 - tb, core], (2, 0))
        self.links.pass_on(full.at[x, 1 - tb, core], (1, 0))
        self.across.wait()
        self.links.pass_on(full.at[1 - x, tb, core], (1, 0))
        across_two.wait()
        self.links.pass_on(full.at[1 - x, 1 - tb, core], (1, 0))


class Local:
    def __init__(self, sems, pairs, base=0):
        self.copies = [
            pltpu.make_async_copy(a, b, sems.at[base + i]) for i, (a, b) in enumerate(pairs)
        ]
        self.open = set(range(len(pairs)))
        for copy in self.copies:
            copy.start()

    def wait(self, *which):
        for i in which or sorted(self.open):
            self.open.discard(i)
            self.copies[i].wait()


def row_loop(rows, step, body):
    block_loop(1, rows, step, lambda i, part: body(part))


def block_loop(n, rows, step, body):
    if rows % step:
        for i in range(n):
            body(i, slice(0, rows))
        return
    steps = rows // step

    @pl.loop(0, n * steps)
    def _(k):
        body(k // steps, pl.ds(pl.multiple_of(lax.rem(k, steps) * step, step), step))


def communicate(
    body, args, outs, copies, collective_id, in_vmem=False, out_vmem=False, scratch=(), kept=1
):
    def specs(inside, n):
        inside = [inside] * n if isinstance(inside, bool) else inside
        return [pl.BlockSpec(memory_space=pltpu.VMEM if i else pl.ANY) for i in inside]

    return pl.pallas_call(
        body,
        out_shape=outs,
        in_specs=specs(in_vmem, len(args)),
        out_specs=specs(out_vmem, len(outs)),
        scratch_shapes=[
            pltpu.SemaphoreType.DMA((copies,)),
            pltpu.SemaphoreType.DMA((copies,)),
            pltpu.SemaphoreType.DMA((kept,)),
            *scratch,
        ],
        compiler_params=pltpu.CompilerParams(
            collective_id=collective_id, has_side_effects=True, vmem_limit_bytes=VMEM_LIMIT
        ),
    )(*args)


def shape(dims, kind=bf16):
    return jax.ShapeDtypeStruct(dims, kind)


def group_masks(FQ):
    return [(a, b) for a in range(4) for b in (0, FQ) if (a, b) != (0, 0)]


class Line:
    def __init__(self, links, views, FH):
        self.links, self.views, self.FH = links, views, FH
        self.h, self.l = links.f // 2, links.f % 2
        self.right, self.left, self.pending = [], [], []

    def here(self, h):
        return self.views(2 * h + self.l)

    def step(self, j):
        h, FH = self.h, self.FH
        rights = [
            self.links.copy(block, block, (self.links.s, self.links.f + 2))
            for block in self.here(lax.max(h - j, 0))
        ]
        lefts = [
            self.links.copy(block, block, (self.links.s, self.links.f - 2))
            for block in self.here(lax.min(h + j, FH - 1))
        ]
        for i in range(len(rights)):

            @pl.when((h >= j) & (h < FH - 1))
            def _():
                rights[i].start()

            @pl.when((h + j < FH) & (h > 0))
            def _():
                lefts[i].start()

        self.right.append(rights)
        self.left.append(lefts)

    def arrived(self, j):
        h, FH = self.h, self.FH
        up = self.here(lax.max(h - 1 - j, 0))
        down = self.here(lax.min(h + 1 + j, FH - 1))
        for i in range(len(up)):
            for blocks, copies, there in (
                (up, self.right[j], h - 1 - j >= 0),
                (down, self.left[j], h + 1 + j < FH),
            ):
                on = self.links.copy(
                    blocks[i], blocks[i], (self.links.s, self.links.f ^ 1)
                )
                self.pending.append((on, there))

                @pl.when(there)
                def _():
                    copies[i].wait_recv()
                    on.start()

    def finish(self):
        h, FH = self.h, self.FH
        for on, there in self.pending:

            @pl.when(there)
            def _():
                on.wait_recv()
                on.wait_send()

        for j in range(FH - 1):
            for i in range(len(self.right[j])):

                @pl.when((h >= j) & (h < FH - 1))
                def _():
                    self.right[j][i].wait_send()

                @pl.when((h + j < FH) & (h > 0))
                def _():
                    self.left[j][i].wait_send()


def rows_of(ref):
    return ref[...].reshape(-1, ref.shape[-1])


def rotation(table):
    half = table.shape[-1] // 2
    swapped = pltpu.roll(table, half, 1)
    first = lax.broadcasted_iota(jnp.int32, table.shape, 1) < half
    return jnp.where(first, table, swapped), jnp.where(first, -swapped, table)


def turn(vector, factors):
    return vector * factors[0] + pltpu.roll(vector, vector.shape[-1] // 2, 1) * factors[1]


def forward_kernel(FH, FQ, *refs):
    tok, tab, wq, kvg, wo, gate, up, down, cot, bias = refs[:10]
    (q_g, kv_g, o_g, gate_g, up_g, down_g, cot_g) = refs[10:17]
    (tab_g, normed_one, q_rot, k_rot, v_low, attended, keys, values) = refs[17:25]
    residual, normed_all, gains = refs[25:28]
    send, recv, here, tok_g, part, from_core, from_x, to_x, normed_two = refs[28:]
    T = residual.shape[0]
    D = residual.shape[1]
    HC = attended.shape[1]
    head = k_rot.shape[1]
    row_len = k_rot.shape[0]
    links = Links(send, recv)
    s, f = links.s, links.f
    x, core = s // 2, s % 2
    tb, q = f // FQ, f % FQ
    t = 2 * s + tb
    evens_q = [2 * k for k in range(1, FQ // 2)]
    links.greet(
        [(a, 0) for a in (1, 2, 3)]
        + [(0, 1)]
        + [(0, 2 * k) for k in range(1, FH)]
        + [(a, FQ) for a in (1, 2, 3)]
    )
    local = Local(
        here,
        [
            (wq.at[s], q_g.at[s, f]),
            (kvg, kv_g.at[s, f]),
            (gate.at[t], gate_g.at[t, q]),
            (up.at[t], up_g.at[t, q]),
            (wo, o_g.at[f]),
            (tok, tok_g.at[s]),
            (tab, tab_g.at[s]),
            (down, down_g.at[q]),
            (cot, cot_g.at[x, tb, core]),
        ],
    )
    first = []
    for a in (1, 2, 3):
        first.append(links.start(wq.at[s ^ a], q_g.at[s, f], (a, 0)))
        first.append(links.start(kvg, kv_g.at[s, f], (a, 0)))
    local.wait(4)
    o_line = Line(links, lambda place: [o_g.at[place]], FH)
    qk_line = Line(links, lambda place: [q_g.at[:, place], kv_g.at[:, place]], FH)
    o_line.step(0)
    needed = [links.pass_on(o_g.at[f], (0, 1))]
    tok_x = links.start(tok, tok_g.at[s], (2, 0))
    needed.append(links.start(tok, tok_g.at[s], (1, 0)))
    needed += [links.start(tab, tab_g.at[s], (a, 0)) for a in (1, 2, 3)]
    local.wait(0, 1)
    for arrival in first:
        arrival.wait()
    qk_line.step(0)
    needed += [links.pass_on(r.at[:, f], (0, 1)) for r in (q_g, kv_g)]
    ffn = []
    for a, b in group_masks(FQ):
        to = 2 * (s ^ a) + (tb ^ (b // FQ))
        ffn.append(links.start(gate.at[to], gate_g.at[t, q], (a, b)))
        ffn.append(links.start(up.at[to], up_g.at[t, q], (a, b)))
    tok_x.wait()
    needed.append(links.pass_on(tok_g.at[s ^ 2], (1, 0)))
    for j in range(FH - 1):
        o_line.arrived(j)
        if j + 1 < FH - 1:
            o_line.step(j + 1)
        qk_line.arrived(j)
        if j + 1 < FH - 1:
            qk_line.step(j + 1)
    down_y = links.start(down, down_g.at[q], (0, 1))
    down_z = [links.start(down, down_g.at[q], (0, b)) for b in evens_q]
    local.wait(2, 3)
    for arrival in ffn:
        arrival.wait()
    gu_y = [links.pass_on(r.at[:, q], (0, 1)) for r in (gate_g, up_g)]
    gu_z = [[links.pass_on(r.at[:, q], (0, b)) for r in (gate_g, up_g)] for b in evens_q]
    cot_group = Group(links, cot, cot_g, FQ)
    for arrival in needed:
        arrival.wait()
    o_line.finish()
    qk_line.finish()
    local.wait(5, 6)

    place = lax.broadcasted_iota(jnp.int32, (8, head), 0)
    lane = lax.broadcasted_iota(jnp.int32, (8, head), 1)
    pick = (place == lane).astype(bf16)
    kv_full = rows_of(kv_g)
    gains[...] = contract_last(pick, kv_full[:, 2 * head :])
    gain_one, gain_two = gains[0:1], gains[1:2]

    @pl.loop(0, row_len // 16)
    def _(i):
        rows = pl.ds(pl.multiple_of(i * 16, 16), 16)
        inner = pl.ds(pl.multiple_of(lax.rem(i, T // 16) * 16, 16), 16)
        value = tok_g[i // (T // 16), inner].astype(f32)
        inverse = lax.rsqrt(jnp.mean(value * value, -1, keepdims=True) + epsilon)
        normed_one[rows] = (value * inverse * gain_one).astype(bf16)

    factors = rotation(rows_of(tab_g))
    kv = dot(normed_one[...], kv_full[:, : 2 * head])
    k_rot[...] = turn(kv[:, :head], factors).astype(bf16)
    v_low[...] = kv[:, head:].astype(bf16)
    heads = HC // head
    for n in range(0, heads, 2):
        columns = slice(n * head, (n + 2) * head)
        both = dot(normed_one[...], q_g[:, :, :, columns].reshape(D, 2 * head))
        for j in (0, 1):
            q_rot[n + j] = turn(both[:, j * head : (j + 1) * head], factors).astype(bf16)
    keys[...] = k_rot[pl.ds(pl.multiple_of(s * T, T), T)]
    values[...] = v_low[pl.ds(pl.multiple_of(s * T, T), T)]
    scale = head ** (-0.5)
    for r in range(row_len // T):
        rows, seen = slice(r * T, (r + 1) * T), slice(0, (r + 1) * T)
        for n in range(heads):
            scores = contract_last(q_rot[n, rows], k_rot[seen]) * scale + bias[rows, seen].astype(f32)
            scores = jnp.exp(scores - jnp.max(scores, -1, keepdims=True))
            probs = (scores / jnp.sum(scores, -1, keepdims=True)).astype(bf16)
            attended[rows, n * head : (n + 1) * head] = dot(probs, v_low[seen]).astype(bf16)

    def project(x_to, core_to):
        rows = attended[pl.ds(pl.multiple_of((2 * x_to + core_to) * T, T), T)]
        for n in range(0, D, HC):
            columns = slice(n, n + HC)
            full = o_g[:, :, columns].reshape(HC, HC)
            part[x_to, core_to, :, columns] = dot(rows, full).astype(bf16)

    project(1 - x, 1 - core)
    far = links.start(part.at[1 - x, 1 - core], from_core.at[0], (1, 0))
    project(1 - x, core)
    project(x, 1 - core)
    near = links.start(part.at[x, 1 - core], from_core.at[1], (1, 0))
    far.wait()

    def add_x(rows):
        total = part[1 - x, core, rows].astype(f32) + from_core[0, rows].astype(f32)
        to_x[rows] = total.astype(bf16)

    row_loop(T, 16, add_x)
    across = links.start(to_x, from_x, (2, 0))
    project(x, core)
    near.wait()
    across.wait()

    def add_last(rows):
        total = tok_g[s, rows].astype(f32) + part[x, core, rows].astype(f32)
        total += from_core[1, rows].astype(f32) + from_x[rows].astype(f32)
        residual[rows] = total
        inverse = lax.rsqrt(jnp.mean(total * total, -1, keepdims=True) + epsilon)
        normed_two[rows] = (total * inverse * gain_two).astype(bf16)

    row_loop(T, 16, add_last)
    normed_group = Group(links, normed_two, normed_all, FQ)
    mine = pltpu.make_async_copy(normed_two, normed_all.at[x, tb, core], here.at[9])
    mine.start()
    half = down_g.shape[2] // 2
    low_half, high_half = pl.ds(0, half), pl.ds(half, half)
    low_t, high_t = pl.ds(0, 4), pl.ds(4, 4)
    down_y.wait()
    for b in evens_q:
        links.pass_on(down_g.at[q ^ 1, :, high_half], (0, b))
    for arrival, b in zip(down_z, evens_q):
        arrival.wait()
        links.pass_on(down_g.at[q ^ b, :, low_half], (0, 1))
    for r, arrival in zip((gate_g, up_g), gu_y):
        arrival.wait()
        for b in evens_q:
            links.pass_on(r.at[high_t, q ^ 1], (0, b))
    for arrivals, b in zip(gu_z, evens_q):
        for r, arrival in zip((gate_g, up_g), arrivals):
            arrival.wait()
            links.pass_on(r.at[low_t, q ^ b], (0, 1))
    cot_group.relay()
    normed_group.relay()
    links.finish()
    local.wait()
    mine.wait()


class RowSum:
    def __init__(self, links, parts, from_core, from_x):
        self.links, self.parts, self.from_core, self.from_x = links, parts, from_core, from_x
        self.x, self.core = links.s // 2, links.s % 2

    def far(self):
        x, core = 1 - self.x, 1 - self.core
        self.to_far = self.links.start(self.parts.at[x, core], self.from_core.at[x], (1, 0))

    def near(self):
        x, core = self.x, 1 - self.core
        self.to_near = self.links.start(self.parts.at[x, core], self.from_core.at[x], (1, 0))

    def middle(self):
        self.to_far.wait()
        x, core = 1 - self.x, self.core

        def add(rows):
            total = self.parts[x, core, rows].astype(f32) + self.from_core[x, rows].astype(f32)
            self.parts[x, core, rows] = total.astype(bf16)

        row_loop(self.from_x.shape[0], 16, add)
        self.across = self.links.start(self.parts.at[x, core], self.from_x, (2, 0))

    def arrive(self):
        self.to_near.wait()
        self.across.wait()

    def total(self, rows):
        return (
            self.parts[self.x, self.core, rows].astype(f32)
            + self.from_core[self.x, rows].astype(f32)
            + self.from_x[rows].astype(f32)
        )


class GroupSum:
    def __init__(self, links, parts, from_core, from_x, from_t, FQ):
        self.links, self.parts, self.FQ = links, parts, FQ
        self.from_core, self.from_x, self.from_t = from_core, from_x, from_t
        self.x, self.core, self.tb = links.s // 2, links.s % 2, links.f // FQ
        self.T = from_t.shape[0]
        self.by_core, self.by_x, self.sent = {}, {}, []

    def send_core(self, name, x, tb):
        arrival = self.links.start(
            self.parts.at[x, tb, 1 - self.core], self.from_core.at[x, tb], (1, 0)
        )
        self.by_core[name] = arrival
        self.sent.append(arrival)

    def far(self, name, tb):
        self.by_core[name].wait()
        x, core = 1 - self.x, self.core

        def add(rows):
            total = self.parts[x, tb, core, rows].astype(f32)
            total += self.from_core[x, tb, rows].astype(f32)
            self.parts[x, tb, core, rows] = total.astype(bf16)

        row_loop(self.T, 16, add)
        arrival = self.links.start(self.parts.at[x, tb, core], self.from_x.at[tb], (2, 0))
        self.by_x[name] = arrival
        self.sent.append(arrival)

    def partial(self, tb, rows):
        return (
            self.parts[self.x, tb, self.core, rows].astype(f32)
            + self.from_core[self.x, tb, rows].astype(f32)
            + self.from_x[tb, rows].astype(f32)
        )

    def to_t(self, core_name, x_name):
        self.by_core[core_name].wait()
        self.by_x[x_name].wait()
        tb = 1 - self.tb

        def add(rows):
            self.parts[self.x, tb, self.core, rows] = self.partial(tb, rows).astype(bf16)

        row_loop(self.T, 16, add)
        self.there = self.links.start(
            self.parts.at[self.x, tb, self.core], self.from_t, (0, self.FQ)
        )
        self.sent.append(self.there)

    def arrive(self, core_name, x_name):
        self.by_core[core_name].wait()
        self.by_x[x_name].wait()
        self.there.wait()

    def total(self, rows):
        return self.partial(self.tb, rows) + self.from_t[rows].astype(f32)


class PieceByL:
    def __init__(self, links, parts, by_l, by_w):
        self.links, self.parts, self.by_l, self.by_w = links, parts, by_l, by_w
        self.n, self.W, _, self.rows = parts.shape[:4]
        self.l = links.f % 2
        self.w = (links.f // 2) % self.W
        self.first = links.start(parts.at[:, :, 1 - self.l], by_l, (0, 1))

    def middle(self):
        self.first.wait()
        l, self.second = self.l, []
        for k in range(1, self.W):
            w = self.w ^ k

            def add(i, rows, w=w):
                total = self.parts[i, w, l, rows].astype(f32) + self.by_l[i, w, rows].astype(f32)
                self.parts[i, w, l, rows] = total.astype(bf16)

            block_loop(self.n, self.rows, 16, add)
            self.second.append(
                self.links.start(self.parts.at[:, w, l], self.by_w.at[k - 1], (0, 2 * k))
            )

    def last(self, store=None):
        for arrival in self.second:
            arrival.wait()

        def add(i, rows):
            total = self.parts[i, self.w, self.l, rows].astype(f32)
            total += self.by_l[i, self.w, rows].astype(f32)
            for k in range(1, self.W):
                total += self.by_w[k - 1, i, rows].astype(f32)
            if store is None:
                self.parts[i, self.w, self.l, rows] = total.astype(bf16)
            else:
                store(i, rows, total)

        block_loop(self.n, self.rows, 16, add)


class PieceByW:
    def __init__(self, links, parts, by_l, by_w):
        self.links, self.parts, self.by_l, self.by_w = links, parts, by_l, by_w
        self.n, self.W, _, self.rows = parts.shape[:4]
        self.l = links.f % 2
        self.w = (links.f // 2) % self.W
        self.first = [
            links.start(parts.at[:, self.w ^ k], by_w.at[k - 1], (0, 2 * k))
            for k in range(1, self.W)
        ]

    def partial(self, i, l, rows):
        total = self.parts[i, self.w, l, rows].astype(f32)
        for k in range(1, self.W):
            total += self.by_w[k - 1, i, l, rows].astype(f32)
        return total

    def middle(self):
        for arrival in self.first:
            arrival.wait()
        l = 1 - self.l

        def add(i, rows):
            self.parts[i, self.w, l, rows] = self.partial(i, l, rows).astype(bf16)

        block_loop(self.n, self.rows, 16, add)
        self.second = self.links.start(self.parts.at[:, self.w, l], self.by_l, (0, 1))

    def last(self, store=None):
        self.second.wait()

        def add(i, rows):
            total = self.partial(i, self.l, rows) + self.by_l[i, rows].astype(f32)
            if store is None:
                self.parts[i, self.w, self.l, rows] = total.astype(bf16)
            else:
                store(i, rows, total)

        block_loop(self.n, self.rows, 16, add)


def by_l_scratch(n, W, rows, width):
    return [pltpu.VMEM((n, W, rows, width), bf16), pltpu.VMEM((W - 1, n, rows, width), bf16)]


def by_w_scratch(n, W, rows, width):
    return [pltpu.VMEM((n, rows, width), bf16), pltpu.VMEM((W - 1, n, 2, rows, width), bf16)]


def norm_back(grad_normed, inputs, gain):
    inverse = lax.rsqrt(jnp.mean(inputs * inputs, -1, keepdims=True) + epsilon)
    scaled = grad_normed * gain
    inner_sum = jnp.sum(scaled * inputs, -1, keepdims=True)
    grad = inverse * scaled - inputs * (inverse**3 * inner_sum / inputs.shape[-1])
    return grad, inputs * inverse


def backward_kernel(FH, FQ, *refs):
    (normed_in, cot_in, gate_in, up_in, down_in, q_in, kv_in, o_in) = refs[:8]
    (normed_one_in, q_rot_in, k_rot_in, v_in, attended_in, tab_in) = refs[8:14]
    tok_in, bias, residual, gains = refs[14:18]
    output, grad_tokens, gate_own, up_own, grad_down, q_own, o_sum, kv_sum = refs[18:26]
    send, recv, here, gate, up, down, q_w, kv_w, o_w = refs[26:35]
    grad_row, kv_own, gain_sums = refs[35:38]
    back_bufs, out_bufs = refs[38:42], refs[42:46]
    normed, cot, grad_gate, grad_up, tab, grad_k, grad_v = refs[46:53]
    bufs = refs[53:]
    links = Links(send, recv)
    s, f = links.s, links.f
    x, core = s // 2, s % 2
    tb, q = f // FQ, f % FQ
    t = 2 * s + tb
    T, D = residual.shape
    S, F, rows_w, HC = q_w.shape
    head = grad_k.shape[1]
    row_len = grad_k.shape[0]
    heads = HC // head
    TG, W, _, _, FC = gate.shape
    two = 2 * T
    links.greet(
        [(a, 0) for a in (1, 2, 3)]
        + [(0, 1)]
        + [(0, 2 * k) for k in range(1, FH)]
        + [(a, FQ) for a in (1, 2, 3)]
    )
    back = GroupSum(links, *back_bufs, FQ)
    out = GroupSum(links, *out_bufs, FQ)
    back_parts, out_parts = back.parts, out.parts
    ffn = {}

    def feed_forward():
        order = [(1 - x, 1 - tb), (1 - x, tb), (x, 1 - tb), (x, tb)]
        pairs = [(gate_in, gate), (up_in, up), (down_in, down)]
        for place in order:
            pairs += [(normed_in.at[place], normed.at[place]), (cot_in.at[place], cot.at[place])]
        loads = Local(here, pairs)
        slot = D // 2
        tiles = [slice(n, min(n + 256, FC)) for n in range(0, FC, 256)]
        for j, (cx, ct) in enumerate(order):
            if j == 0:
                loads.wait(0, 1, 2)
            loads.wait(3 + 2 * j, 4 + 2 * j)
            n = normed[cx, ct].reshape(two, D)
            c = cot[cx, ct].reshape(two, D)
            for tile in tiles:
                gate_proj = dot(n, gate[:, :, :, :, tile].reshape(D, -1))
                up_proj = dot(n, up[:, :, :, :, tile].reshape(D, -1))
                grad_inner = contract_last(c, down[...].reshape(FC, D)[tile])
                sig = jax.nn.sigmoid(gate_proj)
                silu = gate_proj * sig
                place = pl.ds(pl.multiple_of(cx * slot + tile.start, 128), tile.stop - tile.start)
                hidden = (silu * up_proj).astype(bf16)
                o_w[pl.ds(ct * (F // 2), F // 2), :, place] = hidden.reshape(F // 2, rows_w, -1)
                grad_up[cx, ct, :, tile] = (grad_inner * silu).astype(bf16)
                slope = sig * (1.0 + gate_proj * (1.0 - sig))
                grad_gate[cx, ct, :, tile] = (grad_inner * up_proj * slope).astype(bf16)
            for i in range(0, TG, 2):
                columns = slice(i * FQ * rows_w, (i + 2) * FQ * rows_w)
                total = contract_last(grad_gate[cx, ct], gate[i : i + 2].reshape(-1, FC))
                total += contract_last(grad_up[cx, ct], up[i : i + 2].reshape(-1, FC))
                back_parts[cx, ct, :, :, columns] = total.astype(bf16).reshape(2, T, -1)
            back.send_core(j, cx, ct)
            inner_columns = pl.ds(pl.multiple_of(cx * slot, 128), FC)
            for i in range(0, D, 512):
                columns = slice(i, i + 512)
                hidden = o_w[pl.ds(ct * (F // 2), F // 2), :, inner_columns].reshape(two, FC)
                total = dot(hidden, down[:, :, :, :, columns].reshape(FC, 512))
                out_parts[cx, ct, :, :, columns] = total.astype(bf16).reshape(2, T, -1)
            out.send_core(j, cx, ct)
            if j == 1:
                back.far(0, 1 - tb)
            if j == 2:
                back.far(1, tb)
        back.to_t(2, 0)
        inner = [o_w[:, :, i * slot : i * slot + FC].reshape(2 * two, FC) for i in (0, 1)]
        for i in range(0, D, 256):
            columns = slice(i, i + 256)
            total = contract_first(inner[0], cot[0, :, :, :, columns].reshape(2 * two, 256))
            total += contract_first(inner[1], cot[1, :, :, :, columns].reshape(2 * two, 256))
            down[:, :, :, :, columns] = total.astype(bf16).reshape(1, W, 2, -1, 256)
            if 2 * (i + 256) == D:
                ffn["down_low"] = PieceByL(
                    links, down.at[:, :, :, :, pl.ds(0, D // 2)], *bufs[0:2]
                )
        ffn["down_high"] = PieceByW(links, down.at[:, :, :, :, pl.ds(D // 2, D // 2)], *bufs[2:4])
        width = FQ * rows_w
        for i in range(TG):
            turned = normed[:, :, :, :, i * width : (i + 1) * width].reshape(4 * two, width)
            for grad, target in ((grad_gate, gate), (grad_up, up)):
                total = contract_first(turned, grad[...].reshape(4 * two, FC))
                target[i] = total.astype(bf16).reshape(W, 2, rows_w, FC)
            if i + 1 == TG // 2:
                low = pl.ds(0, TG // 2)
                ffn["gate_low"] = PieceByL(links, gate.at[low], *bufs[4:6])
                ffn["up_low"] = PieceByL(links, up.at[low], *bufs[6:8])
        high = pl.ds(TG // 2, TG // 2)
        ffn["gate_high"] = PieceByW(links, gate.at[high], *bufs[8:10])
        ffn["up_high"] = PieceByW(links, up.at[high], *bufs[10:12])

    feed_forward()

    cot_own, tok = normed.at[1, 0, 0], normed.at[1, 0, 1]
    own = Local(here, [(cot_in.at[x, tb, core], cot_own), (tok_in, tok)], 26)
    back.arrive(3, 1)
    own.wait()
    gain_sums[...] = jnp.zeros_like(gain_sums)

    def second_norm(rows):
        grad_normed = back.total(rows)
        grad, unit = norm_back(grad_normed, residual[rows], gains[1:2])
        grad = grad + cot_own[rows].astype(f32)
        grad_tokens[rows] = grad
        grad_row[s, rows] = grad.astype(bf16)
        gain_sums[1:2] += jnp.sum(grad_normed * unit, 0, keepdims=True)

    row_loop(T, 16, second_norm)
    row_x = links.pass_on(grad_row.at[s], (2, 0))
    row_c = links.pass_on(grad_row.at[s], (1, 0))

    normed_one = normed.at[0]
    spots = {}
    for name, width in (("attended", HC), ("q", HC), ("k", head), ("v", head), ("grad", HC)):
        base = sum(w for _, w in spots.values())
        spots[name] = (base, width)

    def column(name, first=0, width=None):
        base, full_width = spots[name]
        return pl.ds(base + first, width or full_width)

    def block(name, r, first=0, width=None):
        return cot[0, r // 2, r % 2, :, column(name, first, width)]

    def whole(name, first=0, width=None):
        return cot[0, :, :, :, column(name, first, width)].reshape(row_len, -1)

    def attention():
        loads = Local(
            here,
            [
                (o_in, o_w),
                (attended_in, cot.at[0, :, :, :, column("attended")]),
                (k_rot_in, cot.at[0, :, :, :, column("k")]),
                (v_in, cot.at[0, :, :, :, column("v")]),
                (tab_in, tab),
                (q_in, q_w),
                (kv_in, kv_w),
                (normed_one_in, normed_one),
            ]
            + [
                (q_rot_in.at[n], cot.at[0, :, :, :, column("q", n * head, head)])
                for n in range(heads)
            ],
            12,
        )
        out.far(0, 1 - tb)
        out.far(1, tb)
        row_x.wait()
        row_cc = links.pass_on(grad_row.at[s ^ 2], (1, 0))
        ffn["down_low"].middle()
        ffn["down_high"].middle()
        row_c.wait()
        row_cc.wait()
        loads.wait()
        full = rows_of(grad_row)
        wo = rows_of(o_w)
        for n in range(0, heads, 2):
            both = contract_last(full, wo[n * head : (n + 2) * head]).astype(bf16)
            cot[0, :, :, :, column("grad", n * head, 2 * head)] = both.reshape(2, 2, T, 2 * head)
        for i in range(0, D, HC):
            columns = slice(i, i + HC)
            total = contract_first(whole("attended"), full[:, columns])
            o_w[:, :, columns] = total.astype(bf16).reshape(F, rows_w, HC)
        o_view = o_w.reshape(1, FH, 2, rows_w, D)
        o_piece = PieceByL(links, o_view, *bufs[12:14])
        grad_k[...] = jnp.zeros_like(grad_k)
        grad_v[...] = jnp.zeros_like(grad_v)
        scale = head ** (-0.5)
        factors = rotation(rows_of(tab))
        back_turn = (factors[0], -factors[1])
        for r in range(row_len // T):
            rows, seen = slice(r * T, (r + 1) * T), slice(0, (r + 1) * T)
            keys, values = whole("k")[seen], whole("v")[seen]
            for n in range(heads):
                query, grad_att = block("q", r, n * head, head), block("grad", r, n * head, head)
                scores = contract_last(query, keys) * scale + bias[rows, seen].astype(f32)
                scores = jnp.exp(scores - jnp.max(scores, -1, keepdims=True))
                probs = scores / jnp.sum(scores, -1, keepdims=True)
                grad_probs = contract_last(grad_att, values)
                delta = jnp.sum(probs * grad_probs, -1, keepdims=True)
                grad_scores = (probs * (grad_probs - delta)).astype(bf16)
                grad_q = dot(grad_scores, keys) * scale
                grad_q = turn(grad_q, (back_turn[0][rows], back_turn[1][rows])).astype(bf16)
                cot[1, r // 2, r % 2, :, n * head : (n + 1) * head] = grad_q
                grad_k[seen] += contract_first(grad_scores, query)
                grad_v[seen] += contract_first(probs.astype(bf16), grad_att)
        grad_key = turn(grad_k[...] * scale, back_turn).astype(bf16)
        cot[1, :, :, :, HC : HC + head] = grad_key.reshape(2, 2, T, head)
        cot[1, :, :, :, HC + head : HC + 2 * head] = grad_v[...].astype(bf16).reshape(2, 2, T, head)
        grad_qkv = slice(0, HC + 2 * head)
        for arrival in back.sent:
            arrival.wait_sent()
        row = RowSum(links, back_parts.at[:, 0], back.from_core.at[:, 0], back.from_x.at[0])
        for cx, go in ((1 - x, row.far), (x, row.near)):
            for i in range(S):
                total = contract_last(
                    cot[1, cx, :, :, :HC].reshape(two, HC), q_w[i].reshape(-1, HC)
                )
                total += contract_last(
                    cot[1, cx, :, :, HC : HC + 2 * head].reshape(two, 2 * head),
                    kv_w[i, :, :, : 2 * head].reshape(-1, 2 * head),
                )
                columns = slice(i * F * rows_w, (i + 1) * F * rows_w)
                back_parts[cx, 0, :, :, columns] = total.astype(bf16).reshape(2, T, -1)
            go()
        row.middle()
        pieces = []
        q_view = q_w.reshape(S, FH, 2, rows_w, HC)
        kv_view = kv_w.reshape(S, FH, 2, rows_w, kv_w.shape[3])
        for i in range(S):
            columns = slice(i * F * rows_w, (i + 1) * F * rows_w)
            turned = normed[0, :, :, :, columns].reshape(row_len, -1)
            total = contract_first(turned, cot[1, :, :, :, grad_qkv].reshape(row_len, -1))
            total = total.astype(bf16)
            q_w[i] = total[:, :HC].reshape(F, rows_w, HC)
            kv_w[i, :, :, : 2 * head] = total[:, HC:].reshape(F, rows_w, 2 * head)
            pieces.append(
                PieceByL(
                    links, q_view.at[pl.ds(i, 1)], bufs[14].at[pl.ds(i, 1)], bufs[15].at[:, pl.ds(i, 1)]
                )
            )
        ffn["gate_low"].middle()
        ffn["up_low"].middle()
        ffn["gate_high"].middle()
        ffn["up_high"].middle()
        out.to_t(2, 0)
        o_piece.middle()
        row.arrive()

        def first_norm(rows):
            grad_normed = row.total(rows)
            grad, unit = norm_back(grad_normed, tok[rows].astype(f32), gains[0:1])
            grad_tokens[rows] += grad
            gain_sums[0:1] += jnp.sum(grad_normed * unit, 0, keepdims=True)

        row_loop(T, 16, first_norm)
        place = lax.broadcasted_iota(jnp.int32, (8, head), 0)
        lane = lax.broadcasted_iota(jnp.int32, (8, head), 1)
        pick = jnp.where((place == lane) & (place < 2), 1.0, 0.0)
        columns = contract_first(gain_sums[...], pick).astype(bf16)
        kv_w[:, :, :, 2 * head :] = columns.reshape(S, F, rows_w, head)
        kv_piece = PieceByL(links, kv_view, *bufs[16:18])
        for piece in pieces:
            piece.middle()
        for name in ("gate_low", "up_low", "gate_high", "up_high"):
            ffn[name].last()
        w, l = q // 2, q % 2
        for a, b in group_masks(FQ):
            to = 2 * (s ^ a) + (tb ^ (b // FQ))
            links.start(gate.at[to, w, l], gate_own.at[t], (a, b))
            links.start(up.at[to, w, l], up_own.at[t], (a, b))
        pairs = [(gate.at[t, w, l], gate_own.at[t]), (up.at[t, w, l], up_own.at[t])]
        mine = Local(here, pairs, 24)
        kv_piece.middle()

        def store_down(base):
            def store(i, rows, total):
                grad_down[rows, base : base + D // 2] = total

            return store

        ffn["down_low"].last(store_down(0))
        ffn["down_high"].last(store_down(D // 2))

        def store_o(i, rows, total):
            o_sum[rows] = total

        o_piece.last(store_o)
        out.arrive(3, 1)

        def finish_output(rows):
            output[rows] = (residual[rows] + out.total(rows)).astype(bf16)

        row_loop(T, 16, finish_output)
        h = f // 2
        for piece in pieces:
            piece.last()
        for a in (1, 2, 3):
            links.start(q_view.at[s ^ a, h, l], q_own.at[s], (a, 0))
        q_own[s] = q_view[s, h, l]
        kv_piece.last()
        for a in (1, 2, 3):
            links.start(kv_view.at[s ^ a, h, l], kv_own.at[s], (a, 0))
        kv_own[s] = kv_view[s, h, l]
        links.finish()
        mine.wait()

        def add_kv(rows):
            total = kv_own[0, rows].astype(f32)
            for i in range(1, S):
                total += kv_own[i, rows].astype(f32)
            kv_sum[rows] = total

        row_loop(kv_sum.shape[0], 16, add_kv)

    attention()


def angle_tables(position_row, head_size):
    half_head = head_size // 2
    frequency = 10000.0 ** (-jnp.arange(half_head, dtype=f32) * 2.0 / head_size)
    phase_angle = position_row.astype(f32)[:, None] * frequency[None, :]
    return (jnp.cos(phase_angle), jnp.sin(phase_angle))


def per_device(
    S,
    F,
    tokens,
    segments,
    positions,
    gain_one,
    w_query,
    w_key,
    w_value,
    w_out,
    gain_two,
    w_gate,
    w_up,
    w_down,
    cotangent,
):
    T, D = tokens.shape[1:]
    head = w_key.shape[1]
    row_len = segments.shape[1]
    rows = w_query.shape[0]
    down_rows = w_down.shape[0]
    FF = w_gate.shape[1]
    FH, FQ = F // 2, F // 2
    W = FQ // 2
    TG = 2 * S
    HC = w_query.shape[1] // S
    heads = HC // head
    FC = FF // TG

    def column_blocks(weight, n):
        return weight.reshape(rows, n, -1).transpose(1, 0, 2)

    gains = jnp.stack([gain_one, gain_two], 1)
    kvg = jnp.concatenate([w_key, w_value, gains, jnp.zeros((rows, head - 2), bf16)], 1)
    KV = kvg.shape[1]
    table = jnp.concatenate(angle_tables(positions[0], head), 1)
    segment = segments[0]
    index = jnp.arange(row_len)
    allowed = (index[None, :] <= index[:, None]) & (segment[None, :] == segment[:, None])
    bias = jnp.where(allowed, 0.0, -1e30).astype(bf16)
    outs = [
        (True, (S, F, rows, HC), bf16),
        (True, (S, F, rows, KV), bf16),
        (True, (F, rows, D), bf16),
        (False, (TG, FQ, rows, FC), bf16),
        (False, (TG, FQ, rows, FC), bf16),
        (False, (FQ, down_rows, D), bf16),
        (False, (2, 2, 2, T, D), bf16),
        (True, (S, T, head), f32),
        (True, (row_len, D), bf16),
        (True, (heads, row_len, head), bf16),
        (True, (row_len, head), bf16),
        (True, (row_len, head), bf16),
        (True, (row_len, HC), bf16),
        (True, (T, head), bf16),
        (True, (T, head), bf16),
        (True, (T, D), f32),
        (False, (2, 2, 2, T, D), bf16),
        (True, (8, D), f32),
    ]
    (wq, kvg, wo, gate_w, up_w, down_w, cot, table, normed_one, query_rot, key_rot, value_low, attended, keys, values, residual, normed_all, gains) = communicate(
        functools.partial(forward_kernel, FH, FQ),
        (
            tokens[0],
            table,
            column_blocks(w_query, S),
            kvg,
            w_out,
            column_blocks(w_gate, TG),
            column_blocks(w_up, TG),
            w_down,
            cotangent[0],
            bias,
        ),
        [shape(dims, kind) for _, dims, kind in outs],
        120 + 18 * F,
        0,
        in_vmem=[False] * 9 + [True],
        out_vmem=[inside for inside, _, _ in outs],
        kept=10,
        scratch=[
            pltpu.VMEM((S, T, D), bf16),
            pltpu.VMEM((2, 2, T, D), bf16),
            pltpu.VMEM((2, T, D), bf16),
            pltpu.VMEM((T, D), bf16),
            pltpu.VMEM((T, D), bf16),
            pltpu.VMEM((T, D), bf16),
        ],
    )
    group = [pltpu.VMEM((2, 2, 2, T, D), bf16), pltpu.VMEM((2, 2, T, D), bf16)]
    group += [pltpu.VMEM((2, T, D), bf16), pltpu.VMEM((T, D), bf16)]
    half = (1, W, down_rows, D // 2)
    block = (TG // 2, W, rows, FC)
    outs = [
        (True, (T, D), bf16),
        (True, (T, D), f32),
        (False, (TG, rows, FC), bf16),
        (False, (TG, rows, FC), bf16),
        (True, (down_rows, D), f32),
        (True, (S, rows, HC), bf16),
        (True, (rows, D), f32),
        (True, (rows, KV), f32),
    ]
    output, grad_tokens, gate_own, up_own, grad_w_down, q_own, grad_w_out, grad_kvg = communicate(
        functools.partial(backward_kernel, FH, FQ),
        (
            normed_all,
            cot,
            gate_w.reshape(TG, W, 2, rows, FC),
            up_w.reshape(TG, W, 2, rows, FC),
            down_w.reshape(1, W, 2, down_rows, D),
            wq,
            kvg,
            wo,
            normed_one.reshape(2, 2, T, D),
            query_rot.reshape(heads, 2, 2, T, head),
            key_rot.reshape(2, 2, T, head),
            value_low.reshape(2, 2, T, head),
            attended.reshape(2, 2, T, HC),
            table,
            tokens[0],
            bias,
            residual,
            gains,
        ),
        [shape(dims, kind) for _, dims, kind in outs],
        100 + 4 * F,
        1,
        in_vmem=[False] * 15 + [True] * 3,
        out_vmem=[inside for inside, _, _ in outs],
        kept=28,
        scratch=[
            pltpu.VMEM((TG, W, 2, rows, FC), bf16),
            pltpu.VMEM((TG, W, 2, rows, FC), bf16),
            pltpu.VMEM((1, W, 2, down_rows, D), bf16),
            pltpu.VMEM((S, F, rows, HC), bf16),
            pltpu.VMEM((S, F, rows, KV), bf16),
            pltpu.VMEM((F, rows, D), bf16),
            pltpu.VMEM((S, T, D), bf16),
            pltpu.VMEM((S, rows, KV), bf16),
            pltpu.VMEM((8, D), f32),
            *group,
            *group,
            pltpu.VMEM((2, 2, 2, T, D), bf16),
            pltpu.VMEM((2, 2, 2, T, D), bf16),
            pltpu.VMEM((2, 2, 2 * T, FC), bf16),
            pltpu.VMEM((2, 2, 2 * T, FC), bf16),
            pltpu.VMEM((S, T, head), f32),
            pltpu.VMEM((row_len, head), f32),
            pltpu.VMEM((row_len, head), f32),
            *by_l_scratch(*half),
            *by_w_scratch(*half),
            *by_l_scratch(*block),
            *by_l_scratch(*block),
            *by_w_scratch(*block),
            *by_w_scratch(*block),
            *by_l_scratch(1, FH, rows, D),
            *by_l_scratch(S, FH, rows, HC),
            *by_l_scratch(S, FH, rows, KV),
        ],
    )
    grad_w_gate = gate_own.transpose(1, 0, 2).reshape(rows, FF).astype(f32)
    grad_w_up = up_own.transpose(1, 0, 2).reshape(rows, FF).astype(f32)
    grad_w_query = q_own.transpose(1, 0, 2).reshape(rows, S * HC).astype(f32)
    return (
        output[None],
        keys[None],
        values[None],
        grad_tokens[None],
        grad_kvg[:, 2 * head],
        grad_w_query,
        grad_kvg[:, :head],
        grad_kvg[:, head : 2 * head],
        grad_w_out,
        grad_kvg[:, 2 * head + 1],
        grad_w_gate,
        grad_w_up,
        grad_w_down,
    )


def solution(mesh):
    token_spec = P("fsdp", "seq", None)
    flat, matrix = P(("seq", "fsdp")), P(("seq", "fsdp"), None)
    return jax.shard_map(
        functools.partial(per_device, mesh.shape["seq"], mesh.shape["fsdp"]),
        mesh=mesh,
        in_specs=(
            token_spec,
            P("fsdp", None),
            P("fsdp", "seq"),
            flat,
            matrix,
            matrix,
            matrix,
            matrix,
            flat,
            matrix,
            matrix,
            matrix,
            token_spec,
        ),
        out_specs=(
            token_spec,
            token_spec,
            token_spec,
            token_spec,
            flat,
            matrix,
            matrix,
            matrix,
            matrix,
            flat,
            matrix,
            matrix,
            matrix,
        ),
        check_vma=False,
    )
```

```python
import functools

import jax
import jax.numpy as jnp
from jax import lax
from jax.experimental import pallas as pl
from jax.experimental.pallas import tpu as pltpu
from jax.sharding import PartitionSpec as P

epsilon = 1e-05
MESH = pl.DeviceIdType.MESH
VMEM_LIMIT = 64 * 2**20 - 2**18
bf16 = jnp.bfloat16
f32 = jnp.float32


def dot(left, right):
    return jnp.dot(left, right, preferred_element_type=f32)


def contract_last(left, right):
    return lax.dot_general(left, right, (((1,), (1,)), ((), ())), preferred_element_type=f32)


def contract_first(left, right):
    return lax.dot_general(left, right, (((0,), (0,)), ((), ())), preferred_element_type=f32)


class Arrival:
    def __init__(self, copy):
        self.copy, self.waited, self.left = copy, False, False

    def wait(self):
        if not self.waited:
            self.waited = True
            self.copy.wait_recv()

    def wait_sent(self):
        if not self.left:
            self.left = True
            self.copy.wait_send()


class Links:
    def __init__(self, send, recv):
        self.send, self.recv, self.sent, self.count = send, recv, [], 0
        self.s, self.f = lax.axis_index("seq"), lax.axis_index("fsdp")

    def greet(self, masks):
        barrier = pltpu.get_barrier_semaphore()
        for a, b in masks:
            pl.semaphore_signal(
                barrier, inc=1, device_id=(self.s ^ a, self.f ^ b), device_id_type=MESH
            )
        pl.semaphore_wait(barrier, len(masks))

    def copy(self, source, target, device):
        self.count += 1
        return pltpu.make_async_remote_copy(
            src_ref=source,
            dst_ref=target,
            send_sem=self.send.at[self.count - 1],
            recv_sem=self.recv.at[self.count - 1],
            device_id=device,
            device_id_type=MESH,
        )

    def start(self, source, target, mask):
        copy = self.copy(source, target, (self.s ^ mask[0], self.f ^ mask[1]))
        copy.start()
        self.sent.append(Arrival(copy))
        return self.sent[-1]

    def pass_on(self, block, mask):
        return self.start(block, block, mask)

    def finish(self):
        for arrival in self.sent:
            arrival.wait()
        for arrival in self.sent:
            arrival.wait_sent()


class Group:
    def __init__(self, links, own, full, FQ):
        self.links, self.full, self.FQ, self.own = links, full, FQ, own
        self.x, self.core, self.tb = links.s // 2, links.s % 2, links.f // FQ
        place = full.at[self.x, self.tb, self.core]
        self.there = links.start(own, place, (0, FQ))
        self.across = links.start(own, place, (2, 0))
        self.beside = links.start(own, place, (1, 0))

    def pass_core(self, x, tb):
        return self.links.pass_on(self.full.at[x, tb, self.core], (1, 0))

    def near(self):
        self.beside.wait()

    def other_x(self):
        self.across.wait()
        self.beside_x = self.pass_core(1 - self.x, self.tb)

    def other_t(self):
        self.there.wait()
        self.across_t = self.links.pass_on(self.full.at[self.x, 1 - self.tb, self.core], (2, 0))
        self.beside_t = self.pass_core(self.x, 1 - self.tb)

    def far(self):
        self.across_t.wait()
        self.beside_far = self.pass_core(1 - self.x, 1 - self.tb)

    def relay(self):
        self.other_x()
        self.other_t()
        self.far()


class Local:
    def __init__(self, sems, pairs, base=0):
        self.copies = [
            pltpu.make_async_copy(a, b, sems.at[base + i]) for i, (a, b) in enumerate(pairs)
        ]
        self.open = set(range(len(pairs)))
        for copy in self.copies:
            copy.start()

    def wait(self, *which):
        for i in which or sorted(self.open):
            self.open.discard(i)
            self.copies[i].wait()


def row_loop(rows, step, body):
    block_loop(1, rows, step, lambda i, part: body(part))


def block_loop(n, rows, step, body):
    if rows % step:
        for i in range(n):
            body(i, slice(0, rows))
        return
    steps = rows // step

    @pl.loop(0, n * steps)
    def _(k):
        body(k // steps, pl.ds(pl.multiple_of(lax.rem(k, steps) * step, step), step))


def communicate(
    body, args, outs, copies, collective_id, in_vmem=False, out_vmem=False, scratch=(), kept=1
):
    def specs(inside, n):
        inside = [inside] * n if isinstance(inside, bool) else inside
        return [pl.BlockSpec(memory_space=pltpu.VMEM if i else pl.ANY) for i in inside]

    return pl.pallas_call(
        body,
        out_shape=outs,
        in_specs=specs(in_vmem, len(args)),
        out_specs=specs(out_vmem, len(outs)),
        scratch_shapes=[
            pltpu.SemaphoreType.DMA((copies,)),
            pltpu.SemaphoreType.DMA((copies,)),
            pltpu.SemaphoreType.DMA((kept,)),
            *scratch,
        ],
        compiler_params=pltpu.CompilerParams(
            collective_id=collective_id, has_side_effects=True, vmem_limit_bytes=VMEM_LIMIT
        ),
    )(*args)


def shape(dims, kind=bf16):
    return jax.ShapeDtypeStruct(dims, kind)


def group_masks(FQ):
    return [(a, b) for a in range(4) for b in (0, FQ) if (a, b) != (0, 0)]


class Line:
    def __init__(self, links, views, FH):
        self.links, self.views, self.FH = links, views, FH
        self.h, self.l = links.f // 2, links.f % 2
        self.right, self.left, self.pending = [], [], []

    def here(self, h):
        return self.views(2 * h + self.l)

    def step(self, j):
        h, FH = self.h, self.FH
        rights = [
            self.links.copy(block, block, (self.links.s, self.links.f + 2))
            for block in self.here(lax.max(h - j, 0))
        ]
        lefts = [
            self.links.copy(block, block, (self.links.s, self.links.f - 2))
            for block in self.here(lax.min(h + j, FH - 1))
        ]
        for i in range(len(rights)):

            @pl.when((h >= j) & (h < FH - 1))
            def _():
                rights[i].start()

            @pl.when((h + j < FH) & (h > 0))
            def _():
                lefts[i].start()

        self.right.append(rights)
        self.left.append(lefts)

    def arrived(self, j):
        h, FH = self.h, self.FH
        up = self.here(lax.max(h - 1 - j, 0))
        down = self.here(lax.min(h + 1 + j, FH - 1))
        for i in range(len(up)):
            for blocks, copies, there in (
                (up, self.right[j], h - 1 - j >= 0),
                (down, self.left[j], h + 1 + j < FH),
            ):
                on = self.links.copy(
                    blocks[i], blocks[i], (self.links.s, self.links.f ^ 1)
                )
                self.pending.append((on, there))

                @pl.when(there)
                def _():
                    copies[i].wait_recv()
                    on.start()

    def finish(self):
        h, FH = self.h, self.FH
        for on, there in self.pending:

            @pl.when(there)
            def _():
                on.wait_recv()
                on.wait_send()

        for j in range(FH - 1):
            for i in range(len(self.right[j])):

                @pl.when((h >= j) & (h < FH - 1))
                def _():
                    self.right[j][i].wait_send()

                @pl.when((h + j < FH) & (h > 0))
                def _():
                    self.left[j][i].wait_send()


def rows_of(ref):
    return ref[...].reshape(-1, ref.shape[-1])


def rotation(table):
    half = table.shape[-1] // 2
    swapped = pltpu.roll(table, half, 1)
    first = lax.broadcasted_iota(jnp.int32, table.shape, 1) < half
    return jnp.where(first, table, swapped), jnp.where(first, -swapped, table)


def turn(vector, factors):
    return vector * factors[0] + pltpu.roll(vector, vector.shape[-1] // 2, 1) * factors[1]


class RowSum:
    def __init__(self, links, parts, from_core, from_x):
        self.links, self.parts, self.from_core, self.from_x = links, parts, from_core, from_x
        self.x, self.core, self.sent = links.s // 2, links.s % 2, []

    def far(self):
        x, core = 1 - self.x, 1 - self.core
        self.to_far = self.links.start(self.parts.at[x, core], self.from_core.at[x], (1, 0))
        self.sent.append(self.to_far)

    def near(self):
        x, core = self.x, 1 - self.core
        self.to_near = self.links.start(self.parts.at[x, core], self.from_core.at[x], (1, 0))
        self.sent.append(self.to_near)

    def middle(self):
        self.to_far.wait()
        x, core = 1 - self.x, self.core

        def add(rows):
            total = self.parts[x, core, rows].astype(f32) + self.from_core[x, rows].astype(f32)
            self.parts[x, core, rows] = total.astype(bf16)

        row_loop(self.from_x.shape[0], 16, add)
        self.across = self.links.start(self.parts.at[x, core], self.from_x, (2, 0))
        self.sent.append(self.across)

    def arrive(self):
        self.to_near.wait()
        self.across.wait()

    def total(self, rows):
        return (
            self.parts[self.x, self.core, rows].astype(f32)
            + self.from_core[self.x, rows].astype(f32)
            + self.from_x[rows].astype(f32)
        )


class GroupSum:
    def __init__(self, links, parts, from_core, from_x, from_t, FQ):
        self.links, self.parts, self.FQ = links, parts, FQ
        self.from_core, self.from_x, self.from_t = from_core, from_x, from_t
        self.x, self.core, self.tb = links.s // 2, links.s % 2, links.f // FQ
        self.T = from_t.shape[0]
        self.by_core, self.by_x, self.sent = {}, {}, []

    def send_core(self, name, x, tb):
        arrival = self.links.start(
            self.parts.at[x, tb, 1 - self.core], self.from_core.at[x, tb], (1, 0)
        )
        self.by_core[name] = arrival
        self.sent.append(arrival)

    def far(self, name, tb):
        self.by_core[name].wait()
        x, core = 1 - self.x, self.core

        def add(rows):
            total = self.parts[x, tb, core, rows].astype(f32)
            total += self.from_core[x, tb, rows].astype(f32)
            self.parts[x, tb, core, rows] = total.astype(bf16)

        row_loop(self.T, 16, add)
        arrival = self.links.start(self.parts.at[x, tb, core], self.from_x.at[tb], (2, 0))
        self.by_x[name] = arrival
        self.sent.append(arrival)

    def partial(self, tb, rows):
        return (
            self.parts[self.x, tb, self.core, rows].astype(f32)
            + self.from_core[self.x, tb, rows].astype(f32)
            + self.from_x[tb, rows].astype(f32)
        )

    def to_t(self, core_name, x_name):
        self.by_core[core_name].wait()
        self.by_x[x_name].wait()
        tb = 1 - self.tb

        def add(rows):
            self.parts[self.x, tb, self.core, rows] = self.partial(tb, rows).astype(bf16)

        row_loop(self.T, 16, add)
        self.there = self.links.start(
            self.parts.at[self.x, tb, self.core], self.from_t, (0, self.FQ)
        )
        self.sent.append(self.there)

    def arrive(self, core_name, x_name):
        self.by_core[core_name].wait()
        self.by_x[x_name].wait()
        self.there.wait()

    def total(self, rows):
        return self.partial(self.tb, rows) + self.from_t[rows].astype(f32)


class PieceByL:
    def __init__(self, links, parts, by_l, by_w):
        self.links, self.parts, self.by_l, self.by_w = links, parts, by_l, by_w
        self.n, self.W, _, self.rows = parts.shape[:4]
        self.l = links.f % 2
        self.w = (links.f // 2) % self.W
        self.first = links.start(parts.at[:, :, 1 - self.l], by_l, (0, 1))

    def middle(self):
        self.first.wait()
        l, self.second = self.l, []
        for k in range(1, self.W):
            w = self.w ^ k

            def add(i, rows, w=w):
                total = self.parts[i, w, l, rows].astype(f32) + self.by_l[i, w, rows].astype(f32)
                self.parts[i, w, l, rows] = total.astype(bf16)

            block_loop(self.n, self.rows, 16, add)
            self.second.append(
                self.links.start(self.parts.at[:, w, l], self.by_w.at[k - 1], (0, 2 * k))
            )

    def last(self, store=None):
        for arrival in self.second:
            arrival.wait()

        def add(i, rows):
            total = self.parts[i, self.w, self.l, rows].astype(f32)
            total += self.by_l[i, self.w, rows].astype(f32)
            for k in range(1, self.W):
                total += self.by_w[k - 1, i, rows].astype(f32)
            if store is None:
                self.parts[i, self.w, self.l, rows] = total.astype(bf16)
            else:
                store(i, rows, total)

        block_loop(self.n, self.rows, 16, add)


class PieceByW:
    def __init__(self, links, parts, by_l, by_w):
        self.links, self.parts, self.by_l, self.by_w = links, parts, by_l, by_w
        self.n, self.W, _, self.rows = parts.shape[:4]
        self.l = links.f % 2
        self.w = (links.f // 2) % self.W
        self.first = [
            links.start(parts.at[:, self.w ^ k], by_w.at[k - 1], (0, 2 * k))
            for k in range(1, self.W)
        ]

    def partial(self, i, l, rows):
        total = self.parts[i, self.w, l, rows].astype(f32)
        for k in range(1, self.W):
            total += self.by_w[k - 1, i, l, rows].astype(f32)
        return total

    def middle(self):
        for arrival in self.first:
            arrival.wait()
        l = 1 - self.l

        def add(i, rows):
            self.parts[i, self.w, l, rows] = self.partial(i, l, rows).astype(bf16)

        block_loop(self.n, self.rows, 16, add)
        self.second = self.links.start(self.parts.at[:, self.w, l], self.by_l, (0, 1))

    def last(self, store=None):
        self.second.wait()

        def add(i, rows):
            total = self.partial(i, self.l, rows) + self.by_l[i, rows].astype(f32)
            if store is None:
                self.parts[i, self.w, self.l, rows] = total.astype(bf16)
            else:
                store(i, rows, total)

        block_loop(self.n, self.rows, 16, add)


def low_part(n):
    return n * 5 // 8


def by_l_scratch(n, W, rows, width):
    return [pltpu.VMEM((n, W, rows, width), bf16), pltpu.VMEM((W - 1, n, rows, width), bf16)]


def by_w_scratch(n, W, rows, width):
    return [pltpu.VMEM((n, rows, width), bf16), pltpu.VMEM((W - 1, n, 2, rows, width), bf16)]


def norm_back(grad_normed, inputs, gain):
    inverse = lax.rsqrt(jnp.mean(inputs * inputs, -1, keepdims=True) + epsilon)
    scaled = grad_normed * gain
    inner_sum = jnp.sum(scaled * inputs, -1, keepdims=True)
    grad = inverse * scaled - inputs * (inverse**3 * inner_sum / inputs.shape[-1])
    return grad, inputs * inverse


def layer_kernel(FH, FQ, *refs):
    tok, tab_in, wq_in, kvg_in, wo_in, gate_in, up_in, down_in, cot_in, bias = refs[:10]
    output, keys, values, grad_tokens, gate_own, up_own, grad_down = refs[10:17]
    q_own, o_sum, kv_sum, normed_kept, side_kept, o_kept = refs[17:23]
    send, recv, here, gate, up, down, q_w, kv_w, o_w = refs[23:32]
    residual, gains, gain_sums, grad_row = refs[32:36]
    back_bufs, out_bufs = refs[36:40], refs[40:44]
    normed, cot, grad_gate, grad_up, tab, grad_k, grad_v = refs[44:51]
    bufs = refs[51:]
    links = Links(send, recv)
    s, f = links.s, links.f
    x, core = s // 2, s % 2
    tb, q = f // FQ, f % FQ
    w, l = q // 2, q % 2
    t = 2 * s + tb
    T, D = residual.shape
    S, F, rows_w, HC = q_w.shape
    row_len, head = grad_k.shape
    heads = HC // head
    TG, W, _, _, FC = gate.shape
    two = 2 * T
    cut, lead_cut = low_part(D), low_part(TG)
    scale = head ** (-0.5)
    evens_q = [2 * k for k in range(1, W)]
    back = GroupSum(links, *back_bufs, FQ)
    out = GroupSum(links, *out_bufs, FQ)
    back_parts, out_parts = back.parts, out.parts
    tok_g = grad_row
    spots = {}
    for name, width in (("attended", HC), ("q", HC), ("k", head), ("v", head), ("grad", HC)):
        base = sum(n for _, n in spots.values())
        spots[name] = (base, width)
    side_width = spots["grad"][0]

    def column(name, first=0, width=None):
        base, full_width = spots[name]
        return pl.ds(base + first, width or full_width)

    def block(where, name, r, first=0, width=None):
        return where[r // 2, r % 2, :, column(name, first, width)]

    def whole(where, name, first=0, width=None):
        return where[:, :, :, column(name, first, width)].reshape(row_len, -1)

    links.greet(
        [(a, 0) for a in (1, 2, 3)]
        + [(0, 1)]
        + [(0, 2 * k) for k in range(1, FH)]
        + [(a, FQ) for a in (1, 2, 3)]
    )
    local = Local(
        here,
        [
            (wq_in.at[s], q_w.at[s, f]),
            (kvg_in, kv_w.at[s, f]),
            (gate_in.at[t], gate.at[t, w, l]),
            (up_in.at[t], up.at[t, w, l]),
            (wo_in, o_w.at[f]),
            (tok, tok_g.at[s]),
            (tab_in, tab.at[s]),
            (down_in, down.at[0, w, l]),
            (cot_in, cot.at[x, tb, core]),
        ],
    )
    first = [links.start(wq_in.at[s ^ a], q_w.at[s, f], (a, 0)) for a in (1, 2, 3)]
    local.wait(1, 4)
    kv_line = Line(links, lambda place: [kv_w.at[s, place]], FH)
    o_line = Line(links, lambda place: [o_w.at[place]], FH)
    q_line = Line(links, lambda place: [q_w.at[:, place]], FH)
    kv_line.step(0)
    kv_y = links.pass_on(kv_w.at[s, f], (0, 1))
    o_line.step(0)
    needed = [links.pass_on(o_w.at[f], (0, 1))]
    local.wait(0)
    for arrival in first:
        arrival.wait()
    q_line.step(0)
    needed.append(links.pass_on(q_w.at[:, f], (0, 1)))
    tok_x = links.start(tok, tok_g.at[s], (2, 0))
    needed.append(links.start(tok, tok_g.at[s], (1, 0)))
    needed += [links.start(tab_in, tab.at[s], (a, 0)) for a in (1, 2, 3)]
    ffn_in = []

    def to_group(masks):
        for a, b in masks:
            to = 2 * (s ^ a) + (tb ^ (b // FQ))
            ffn_in.append(links.start(gate_in.at[to], gate.at[t, w, l], (a, b)))
            ffn_in.append(links.start(up_in.at[to], up.at[t, w, l], (a, b)))

    to_group([(a, 0) for a in (1, 2, 3)])
    for j in range(FH - 1):
        for way in (kv_line, o_line, q_line):
            way.arrived(j)
            if j + 1 < FH - 1:
                way.step(j + 1)
        if j == 0:
            tok_x.wait()
            needed.append(links.pass_on(tok_g.at[s ^ 2], (1, 0)))
    kv_y.wait()
    kv_line.finish()
    kv_x = links.pass_on(kv_w.at[s], (2, 0))
    needed.append(links.pass_on(kv_w.at[s], (1, 0)))
    same_tb = len(ffn_in)
    to_group([(a, FQ) for a in range(4)])
    down_y = links.start(down_in, down.at[0, w, l], (0, 1))
    down_z = [links.start(down_in, down.at[0, w, l], (0, b)) for b in evens_q]

    class Spread:
        def __init__(self, view, low):
            self.view, self.low, self.high = view, pl.ds(0, low), pl.ds(low, S - low)
            self.by_y = links.pass_on(view.at[:, w, l], (0, 1))
            self.by_z = [links.pass_on(view.at[:, w, l], (0, b)) for b in evens_q]

        def second(self):
            self.by_y.wait()
            hops = [links.pass_on(self.view.at[self.high, w, 1 - l], (0, b)) for b in evens_q]
            for arrival, b in zip(self.by_z, evens_q):
                arrival.wait()
                hops.append(links.pass_on(self.view.at[self.low, w ^ (b // 2), l], (0, 1)))
            return hops

    gate_by_tb = gate.reshape(S, 2, W, 2, rows_w, FC)
    up_by_tb = up.reshape(S, 2, W, 2, rows_w, FC)
    local.wait(2, 3)
    for arrival in ffn_in[:same_tb]:
        arrival.wait()
    spreads = [Spread(r.at[:, tb], 3) for r in (gate_by_tb, up_by_tb)]
    kv_x.wait()
    needed.append(links.pass_on(kv_w.at[s ^ 2], (1, 0)))
    for arrival in needed:
        arrival.wait()
    o_line.finish()
    q_line.finish()
    local.wait(5, 6)
    kept_o = Local(here, [(o_w, o_kept)], 9)

    normed_one, side = out_parts.at[0], out_parts.at[1]
    place = lax.broadcasted_iota(jnp.int32, (8, head), 0)
    lane = lax.broadcasted_iota(jnp.int32, (8, head), 1)
    pick = (place == lane).astype(bf16)
    kv_full = rows_of(kv_w)
    gains[...] = contract_last(pick, kv_full[:, 2 * head :])

    def norm_one(i, rows):
        value = tok_g[i, rows].astype(f32)
        inverse = lax.rsqrt(jnp.mean(value * value, -1, keepdims=True) + epsilon)
        normed_one[i // 2, lax.rem(i, 2), rows] = (value * inverse * gains[0:1]).astype(bf16)

    block_loop(S, T, 16, norm_one)
    factors = rotation(rows_of(tab))

    def put(name, first, value):
        columns = column(name, first, value.shape[1])
        side[:, :, :, columns] = value.astype(bf16).reshape(2, 2, T, -1)

    kv = dot(rows_of(normed_one), kv_full[:, : 2 * head])
    put("k", 0, turn(kv[:, :head], factors))
    put("v", 0, kv[:, head:])
    for n in range(0, heads, 2):
        columns = slice(n * head, (n + 2) * head)
        both = dot(rows_of(normed_one), q_w[:, :, :, columns].reshape(D, 2 * head))
        for j in (0, 1):
            put("q", (n + j) * head, turn(both[:, j * head : (j + 1) * head], factors))
    keys[...] = side[x, core, :, column("k")]
    values[...] = side[x, core, :, column("v")]
    for r in range(S):
        rows, seen = slice(r * T, (r + 1) * T), slice(0, (r + 1) * T)
        keys_seen, values_seen = whole(side, "k")[seen], whole(side, "v")[seen]
        for n in range(heads):
            query = block(side, "q", r, n * head, head)
            scores = contract_last(query, keys_seen) * scale + bias[rows, seen].astype(f32)
            scores = jnp.exp(scores - jnp.max(scores, -1, keepdims=True))
            probs = (scores / jnp.sum(scores, -1, keepdims=True)).astype(bf16)
            side[r // 2, r % 2, :, column("attended", n * head, head)] = dot(
                probs, values_seen
            ).astype(bf16)
    low_half, high_half = pl.ds(0, cut), pl.ds(cut, D - cut)
    arriving = []
    down_y.wait()
    for b in evens_q:
        arriving.append(links.pass_on(down.at[0, w, 1 - l, :, high_half], (0, b)))
    for arrival, b in zip(down_z, evens_q):
        arrival.wait()
        arriving.append(links.pass_on(down.at[0, w ^ (b // 2), l, :, low_half], (0, 1)))

    parts = RowSum(links, back_parts.at[:, 0], back.from_core.at[:, 0], back.from_x.at[0])

    def project(x_to):
        rows = side[x_to, :, :, column("attended")].reshape(two, HC)
        for n in range(0, D, HC):
            columns = slice(n, n + HC)
            total = dot(rows, o_w[:, :, columns].reshape(HC, HC))
            parts.parts[x_to, :, :, columns] = total.astype(bf16).reshape(2, T, HC)

    project(1 - x)
    parts.far()
    project(x)
    parts.near()
    parts.middle()
    for arrival in ffn_in[same_tb:]:
        arrival.wait()
    spreads += [Spread(r.at[:, 1 - tb], 2) for r in (gate_by_tb, up_by_tb)]
    cot_group = Group(links, cot_in, cot, FQ)
    for spread in spreads[:2]:
        arriving += spread.second()
    kept = Local(
        here, [(normed_one, normed_kept), (side.at[:, :, :, pl.ds(0, side_width)], side_kept)], 10
    )
    parts.arrive()

    def norm_two(rows):
        total = tok_g[s, rows].astype(f32) + parts.total(rows)
        residual[rows] = total
        inverse = lax.rsqrt(jnp.mean(total * total, -1, keepdims=True) + epsilon)
        normed[x, tb, core, rows] = (total * inverse * gains[1:2]).astype(bf16)

    row_loop(T, 16, norm_two)
    group_start = len(links.sent)
    group = Group(links, normed.at[x, tb, core], normed, FQ)
    for spread in spreads[2:]:
        arriving += spread.second()
    cot_group.other_x()
    cot_group.other_t()
    local.wait(7, 8)
    kept_o.wait()
    kept.wait()
    for arrival in arriving:
        arrival.wait()
    weights_sent = links.sent[:group_start]
    for arrival in weights_sent:
        arrival.wait_sent()

    slot = D // 2
    tiles = [slice(n, min(n + 256, FC)) for n in range(0, FC, 256)]

    def feed_forward(name, cx, ct):
        n = normed[cx, ct].reshape(two, D)
        c = cot[cx, ct].reshape(two, D)
        for tile in tiles:
            gate_proj = dot(n, gate[:, :, :, :, tile].reshape(D, -1))
            up_proj = dot(n, up[:, :, :, :, tile].reshape(D, -1))
            grad_inner = contract_last(c, down[...].reshape(FC, D)[tile])
            sig = jax.nn.sigmoid(gate_proj)
            silu = gate_proj * sig
            spot = pl.ds(pl.multiple_of(cx * slot + tile.start, 128), tile.stop - tile.start)
            hidden = (silu * up_proj).astype(bf16)
            o_w[pl.ds(ct * (F // 2), F // 2), :, spot] = hidden.reshape(F // 2, rows_w, -1)
            grad_up[cx, ct, :, tile] = (grad_inner * silu).astype(bf16)
            slope = sig * (1.0 + gate_proj * (1.0 - sig))
            grad_gate[cx, ct, :, tile] = (grad_inner * up_proj * slope).astype(bf16)
        for i in range(0, TG, 2):
            columns = slice(i * FQ * rows_w, (i + 2) * FQ * rows_w)
            total = contract_last(grad_gate[cx, ct], gate[i : i + 2].reshape(-1, FC))
            total += contract_last(grad_up[cx, ct], up[i : i + 2].reshape(-1, FC))
            back_parts[cx, ct, :, :, columns] = total.astype(bf16).reshape(2, T, -1)
        back.send_core(name, cx, ct)
        inner_columns = pl.ds(pl.multiple_of(cx * slot, 128), FC)
        hidden = o_w[pl.ds(ct * (F // 2), F // 2), :, inner_columns].reshape(two, FC)
        for i in range(0, D, 512):
            columns = slice(i, i + 512)
            total = dot(hidden, down[:, :, :, :, columns].reshape(FC, 512))
            out_parts[cx, ct, :, :, columns] = total.astype(bf16).reshape(2, T, -1)
        out.send_core(name, cx, ct)

    group.near()
    cot_group.near()
    feed_forward("near", x, tb)
    group.other_x()
    group.beside_x.wait()
    cot_group.beside_x.wait()
    feed_forward("x", 1 - x, tb)
    group.other_t()
    back.far("x", tb)
    group.beside_t.wait()
    cot_group.beside_t.wait()
    feed_forward("t", x, 1 - tb)
    group.far()
    cot_group.far()
    group.beside_far.wait()
    cot_group.beside_far.wait()
    feed_forward("far", 1 - x, 1 - tb)
    back.far("far", 1 - tb)
    out.far("x", tb)
    for arrival in links.sent[group_start:]:
        if arrival not in back.sent and arrival not in out.sent:
            arrival.wait_sent()
    ffn = {}
    inner = [o_w[:, :, i * slot : i * slot + FC].reshape(2 * two, FC) for i in (0, 1)]
    for i in range(0, D, 256):
        columns = slice(i, i + 256)
        total = contract_first(inner[0], cot[0, :, :, :, columns].reshape(2 * two, 256))
        total += contract_first(inner[1], cot[1, :, :, :, columns].reshape(2 * two, 256))
        down[:, :, :, :, columns] = total.astype(bf16).reshape(1, W, 2, -1, 256)
        if i + 256 == cut:
            ffn["down_low"] = PieceByL(links, down.at[:, :, :, :, pl.ds(0, cut)], *bufs[0:2])
    ffn["down_high"] = PieceByW(links, down.at[:, :, :, :, pl.ds(cut, D - cut)], *bufs[2:4])
    out.far("far", 1 - tb)
    width = FQ * rows_w
    for i in range(TG):
        turned = normed[:, :, :, :, i * width : (i + 1) * width].reshape(4 * two, width)
        for grad, target in ((grad_gate, gate), (grad_up, up)):
            total = contract_first(turned, grad[...].reshape(4 * two, FC))
            target[i] = total.astype(bf16).reshape(W, 2, rows_w, FC)
        if i + 1 == lead_cut:
            low = pl.ds(0, lead_cut)
            ffn["gate_low"] = PieceByL(links, gate.at[low], *bufs[4:6])
            ffn["up_low"] = PieceByL(links, up.at[low], *bufs[6:8])
            back.to_t("t", "far")
    high = pl.ds(lead_cut, TG - lead_cut)
    ffn["gate_high"] = PieceByW(links, gate.at[high], *bufs[8:10])
    ffn["up_high"] = PieceByW(links, up.at[high], *bufs[10:12])
    ffn["down_low"].middle()
    ffn["down_high"].middle()
    out.to_t("t", "far")

    cot_own, tok_own = normed.at[1, 0, 0], normed.at[1, 0, 1]
    own = Local(here, [(cot_in, cot_own), (tok, tok_own)], 12)
    gain_sums[...] = jnp.zeros_like(gain_sums)
    own.wait()
    back.arrive("near", "x")

    def second_norm(rows):
        grad_normed = back.total(rows)
        grad, unit = norm_back(grad_normed, residual[rows], gains[1:2])
        grad = grad + cot_own[rows].astype(f32)
        grad_tokens[rows] = grad
        grad_row[s, rows] = grad.astype(bf16)
        gain_sums[1:2] += jnp.sum(grad_normed * unit, 0, keepdims=True)

    row_loop(T, 16, second_norm)
    row_x = links.pass_on(grad_row.at[s], (2, 0))
    row_c = links.pass_on(grad_row.at[s], (1, 0))

    side = cot.at[0]
    normed_one = normed.at[0]
    loads = Local(
        here,
        [
            (o_kept, o_w),
            (side_kept, cot.at[0, :, :, :, pl.ds(0, side_width)]),
            (normed_kept, normed_one),
        ],
        14,
    )
    ffn["gate_low"].middle()
    row_x.wait()
    row_cc = links.pass_on(grad_row.at[s ^ 2], (1, 0))
    ffn["gate_high"].middle()
    ffn["up_high"].middle()
    row_c.wait()
    row_cc.wait()
    loads.wait()
    full = rows_of(grad_row)
    wo = rows_of(o_w)
    for n in range(0, heads, 2):
        both = contract_last(full, wo[n * head : (n + 2) * head]).astype(bf16)
        side[:, :, :, column("grad", n * head, 2 * head)] = both.reshape(2, 2, T, 2 * head)
    for i in range(0, D, HC):
        columns = slice(i, i + HC)
        total = contract_first(whole(side, "attended"), full[:, columns])
        o_w[:, :, columns] = total.astype(bf16).reshape(F, rows_w, HC)
    o_piece = PieceByL(links, o_w.reshape(1, FH, 2, rows_w, D), *bufs[12:14])
    grad_k[...] = jnp.zeros_like(grad_k)
    grad_v[...] = jnp.zeros_like(grad_v)
    factors = rotation(rows_of(tab))
    back_turn = (factors[0], -factors[1])
    for r in range(S):
        rows, seen = slice(r * T, (r + 1) * T), slice(0, (r + 1) * T)
        keys_seen, values_seen = whole(side, "k")[seen], whole(side, "v")[seen]
        for n in range(heads):
            query = block(side, "q", r, n * head, head)
            grad_att = block(side, "grad", r, n * head, head)
            scores = contract_last(query, keys_seen) * scale + bias[rows, seen].astype(f32)
            scores = jnp.exp(scores - jnp.max(scores, -1, keepdims=True))
            probs = scores / jnp.sum(scores, -1, keepdims=True)
            grad_probs = contract_last(grad_att, values_seen)
            delta = jnp.sum(probs * grad_probs, -1, keepdims=True)
            grad_scores = (probs * (grad_probs - delta)).astype(bf16)
            grad_q = dot(grad_scores, keys_seen) * scale
            grad_q = turn(grad_q, (back_turn[0][rows], back_turn[1][rows])).astype(bf16)
            cot[1, r // 2, r % 2, :, n * head : (n + 1) * head] = grad_q
            grad_k[seen] += contract_first(grad_scores, query)
            grad_v[seen] += contract_first(probs.astype(bf16), grad_att)
    grad_key = turn(grad_k[...] * scale, back_turn).astype(bf16)
    cot[1, :, :, :, HC : HC + head] = grad_key.reshape(2, 2, T, head)
    cot[1, :, :, :, HC + head : HC + 2 * head] = grad_v[...].astype(bf16).reshape(2, 2, T, head)
    grad_qkv = slice(0, HC + 2 * head)
    for arrival in back.sent:
        arrival.wait_sent()
    row = RowSum(links, back_parts.at[:, 0], back.from_core.at[:, 0], back.from_x.at[0])
    for cx, go in ((1 - x, row.far), (x, row.near)):
        for i in range(S):
            total = contract_last(cot[1, cx, :, :, :HC].reshape(two, HC), q_w[i].reshape(-1, HC))
            total += contract_last(
                cot[1, cx, :, :, HC : HC + 2 * head].reshape(two, 2 * head),
                kv_w[i, :, :, : 2 * head].reshape(-1, 2 * head),
            )
            columns = slice(i * F * rows_w, (i + 1) * F * rows_w)
            back_parts[cx, 0, :, :, columns] = total.astype(bf16).reshape(2, T, -1)
        go()
    row.middle()
    ffn["up_low"].middle()
    pieces = []
    q_view = q_w.reshape(S, FH, 2, rows_w, HC)
    kv_view = kv_w.reshape(S, FH, 2, rows_w, kv_w.shape[3])
    for i in range(S):
        columns = slice(i * F * rows_w, (i + 1) * F * rows_w)
        turned = normed[0, :, :, :, columns].reshape(row_len, -1)
        total = contract_first(turned, cot[1, :, :, :, grad_qkv].reshape(row_len, -1))
        total = total.astype(bf16)
        q_w[i] = total[:, :HC].reshape(F, rows_w, HC)
        kv_w[i, :, :, : 2 * head] = total[:, HC:].reshape(F, rows_w, 2 * head)
        one = pl.ds(i, 1)
        pieces.append(PieceByL(links, q_view.at[one], bufs[14].at[one], bufs[15].at[:, one]))
    def to_owners(target, own):
        for a, b in group_masks(FQ):
            to = 2 * (s ^ a) + (tb ^ (b // FQ))
            links.start(target.at[to, w, l], own.at[t], (a, b))

    ffn["gate_low"].last()
    ffn["gate_high"].last()
    to_owners(gate, gate_own)
    row.arrive()

    def first_norm(rows):
        grad_normed = row.total(rows)
        grad, unit = norm_back(grad_normed, tok_own[rows].astype(f32), gains[0:1])
        grad_tokens[rows] += grad
        gain_sums[0:1] += jnp.sum(grad_normed * unit, 0, keepdims=True)

    row_loop(T, 16, first_norm)
    pick = jnp.where((place == lane) & (place < 2), 1.0, 0.0)
    columns = contract_first(gain_sums[...], pick).astype(bf16)
    kv_w[:, :, :, 2 * head :] = columns.reshape(S, F, rows_w, head)
    kv_row = RowSum(links, kv_w.reshape(2, 2, F * rows_w, kv_w.shape[3]), *bufs[16:18])
    kv_row.far()
    kv_row.near()
    kv_row.middle()
    ffn["up_low"].last()
    ffn["up_high"].last()
    to_owners(up, up_own)
    mine = Local(here, [(gate.at[t, w, l], gate_own.at[t]), (up.at[t, w, l], up_own.at[t])], 17)
    o_piece.middle()
    pieces[0].middle()
    kv_row.arrive()

    def keep_kv(rows):
        kv_row.parts[x, core, rows] = kv_row.total(rows).astype(bf16)

    row_loop(F * rows_w, 16, keep_kv)
    kv_piece = PieceByL(links, kv_view.at[pl.ds(s, 1)], *bufs[18:20])
    for piece in pieces[1:]:
        piece.middle()
    kv_piece.middle()

    def store_down(base):
        def store(i, rows, total):
            grad_down[rows, base : base + total.shape[1]] = total

        return store

    ffn["down_low"].last(store_down(0))
    ffn["down_high"].last(store_down(cut))

    def store_o(i, rows, total):
        o_sum[rows] = total

    o_piece.last(store_o)
    out.arrive("near", "x")

    def finish_output(rows):
        output[rows] = (residual[rows] + out.total(rows)).astype(bf16)

    row_loop(T, 16, finish_output)
    h = f // 2
    for piece in pieces:
        piece.last()
    for a in (1, 2, 3):
        links.start(q_view.at[s ^ a, h, l], q_own.at[s], (a, 0))
    q_own[s] = q_view[s, h, l]

    def store_kv(i, rows, total):
        kv_sum[rows] = total

    kv_piece.last(store_kv)
    links.finish()
    mine.wait()


def angle_tables(position_row, head_size):
    half_head = head_size // 2
    frequency = 10000.0 ** (-jnp.arange(half_head, dtype=f32) * 2.0 / head_size)
    phase_angle = position_row.astype(f32)[:, None] * frequency[None, :]
    return (jnp.cos(phase_angle), jnp.sin(phase_angle))


def per_device(
    S,
    F,
    tokens,
    segments,
    positions,
    gain_one,
    w_query,
    w_key,
    w_value,
    w_out,
    gain_two,
    w_gate,
    w_up,
    w_down,
    cotangent,
):
    T, D = tokens.shape[1:]
    head = w_key.shape[1]
    row_len = segments.shape[1]
    rows = w_query.shape[0]
    down_rows = w_down.shape[0]
    FF = w_gate.shape[1]
    FH, FQ = F // 2, F // 2
    W = FQ // 2
    TG = 2 * S
    HC = w_query.shape[1] // S
    heads = HC // head
    FC = FF // TG

    def column_blocks(weight, n):
        return weight.reshape(rows, n, -1).transpose(1, 0, 2)

    gains = jnp.stack([gain_one, gain_two], 1)
    kvg = jnp.concatenate([w_key, w_value, gains, jnp.zeros((rows, head - 2), bf16)], 1)
    KV = kvg.shape[1]
    table = jnp.concatenate(angle_tables(positions[0], head), 1)
    segment = segments[0]
    index = jnp.arange(row_len)
    allowed = (index[None, :] <= index[:, None]) & (segment[None, :] == segment[:, None])
    bias = jnp.where(allowed, 0.0, -1e30).astype(bf16)
    group = [pltpu.VMEM((2, 2, 2, T, D), bf16), pltpu.VMEM((2, 2, T, D), bf16)]
    group += [pltpu.VMEM((2, T, D), bf16), pltpu.VMEM((T, D), bf16)]
    low, low_columns = low_part(TG), low_part(D)
    outs = [
        (True, (T, D), bf16),
        (True, (T, head), bf16),
        (True, (T, head), bf16),
        (True, (T, D), f32),
        (False, (TG, rows, FC), bf16),
        (False, (TG, rows, FC), bf16),
        (True, (down_rows, D), f32),
        (True, (S, rows, HC), bf16),
        (True, (rows, D), f32),
        (True, (rows, KV), f32),
        (False, (2, 2, T, D), bf16),
        (False, (2, 2, T, 2 * HC + 2 * head), bf16),
        (False, (F, rows, D), bf16),
    ]
    results = communicate(
        functools.partial(layer_kernel, FH, FQ),
        (
            tokens[0],
            table,
            column_blocks(w_query, S),
            kvg,
            w_out,
            column_blocks(w_gate, TG),
            column_blocks(w_up, TG),
            w_down,
            cotangent[0],
            bias,
        ),
        [shape(dims, kind) for _, dims, kind in outs],
        220 + 20 * F,
        0,
        in_vmem=[False] * 9 + [True],
        out_vmem=[inside for inside, _, _ in outs],
        kept=24,
        scratch=[
            pltpu.VMEM((TG, W, 2, rows, FC), bf16),
            pltpu.VMEM((TG, W, 2, rows, FC), bf16),
            pltpu.VMEM((1, W, 2, down_rows, D), bf16),
            pltpu.VMEM((S, F, rows, HC), bf16),
            pltpu.VMEM((S, F, rows, KV), bf16),
            pltpu.VMEM((F, rows, D), bf16),
            pltpu.VMEM((T, D), f32),
            pltpu.VMEM((8, D), f32),
            pltpu.VMEM((8, D), f32),
            pltpu.VMEM((S, T, D), bf16),
            *group,
            *group,
            pltpu.VMEM((2, 2, 2, T, D), bf16),
            pltpu.VMEM((2, 2, 2, T, D), bf16),
            pltpu.VMEM((2, 2, 2 * T, FC), bf16),
            pltpu.VMEM((2, 2, 2 * T, FC), bf16),
            pltpu.VMEM((S, T, head), f32),
            pltpu.VMEM((row_len, head), f32),
            pltpu.VMEM((row_len, head), f32),
            *by_l_scratch(1, W, down_rows, low_columns),
            *by_w_scratch(1, W, down_rows, D - low_columns),
            *by_l_scratch(low, W, rows, FC),
            *by_l_scratch(low, W, rows, FC),
            *by_w_scratch(TG - low, W, rows, FC),
            *by_w_scratch(TG - low, W, rows, FC),
            *by_l_scratch(1, FH, rows, D),
            *by_l_scratch(S, FH, rows, HC),
            pltpu.VMEM((2, F * rows, KV), bf16),
            pltpu.VMEM((F * rows, KV), bf16),
            *by_l_scratch(1, FH, rows, KV),
        ],
    )
    output, keys, values, grad_tokens, gate_own, up_own, grad_w_down, q_own, grad_w_out, grad_kvg = results[:10]
    grad_w_gate = gate_own.transpose(1, 0, 2).reshape(rows, FF).astype(f32)
    grad_w_up = up_own.transpose(1, 0, 2).reshape(rows, FF).astype(f32)
    grad_w_query = q_own.transpose(1, 0, 2).reshape(rows, S * HC).astype(f32)
    return (
        output[None],
        keys[None],
        values[None],
        grad_tokens[None],
        grad_kvg[:, 2 * head],
        grad_w_query,
        grad_kvg[:, :head],
        grad_kvg[:, head : 2 * head],
        grad_w_out,
        grad_kvg[:, 2 * head + 1],
        grad_w_gate,
        grad_w_up,
        grad_w_down,
    )


def solution(mesh):
    token_spec = P("fsdp", "seq", None)
    flat, matrix = P(("seq", "fsdp")), P(("seq", "fsdp"), None)
    return jax.shard_map(
        functools.partial(per_device, mesh.shape["seq"], mesh.shape["fsdp"]),
        mesh=mesh,
        in_specs=(
            token_spec,
            P("fsdp", None),
            P("fsdp", "seq"),
            flat,
            matrix,
            matrix,
            matrix,
            matrix,
            flat,
            matrix,
            matrix,
            matrix,
            token_spec,
        ),
        out_specs=(
            token_spec,
            token_spec,
            token_spec,
            token_spec,
            flat,
            matrix,
            matrix,
            matrix,
            matrix,
            flat,
            matrix,
            matrix,
            matrix,
        ),
        check_vma=False,
    )
```

```python
import functools

import jax
import jax.numpy as jnp
from jax import lax
from jax.experimental import pallas as pl
from jax.experimental.pallas import tpu as pltpu
from jax.sharding import PartitionSpec as P

epsilon = 1e-05
MESH = pl.DeviceIdType.MESH
Z = 4
VMEM_LIMIT = 64 * 2**20 - 2**18
bf16 = jnp.bfloat16
f32 = jnp.float32


def dot(left, right):
    return jnp.dot(left, right, preferred_element_type=f32)


def contract_last(left, right):
    return lax.dot_general(left, right, (((1,), (1,)), ((), ())), preferred_element_type=f32)


def contract_first(left, right):
    return lax.dot_general(left, right, (((0,), (0,)), ((), ())), preferred_element_type=f32)


class Arrival:
    def __init__(self, copy):
        self.copy, self.waited, self.left = copy, False, False

    def wait(self):
        if not self.waited:
            self.waited = True
            self.copy.wait_recv()

    def wait_sent(self):
        if not self.left:
            self.left = True
            self.copy.wait_send()


class Links:
    def __init__(self, send, recv):
        self.send, self.recv, self.sent, self.count = send, recv, [], 0
        self.s, self.f = lax.axis_index("seq"), lax.axis_index("fsdp")

    def greet(self, masks):
        barrier = pltpu.get_barrier_semaphore()
        for a, b in masks:
            pl.semaphore_signal(
                barrier, inc=1, device_id=(self.s ^ a, self.f ^ b), device_id_type=MESH
            )
        pl.semaphore_wait(barrier, len(masks))

    def copy(self, source, target, device):
        self.count += 1
        return pltpu.make_async_remote_copy(
            src_ref=source,
            dst_ref=target,
            send_sem=self.send.at[self.count - 1],
            recv_sem=self.recv.at[self.count - 1],
            device_id=device,
            device_id_type=MESH,
        )

    def start(self, source, target, mask):
        copy = self.copy(source, target, (self.s ^ mask[0], self.f ^ mask[1]))
        copy.start()
        self.sent.append(Arrival(copy))
        return self.sent[-1]

    def pass_on(self, block, mask):
        return self.start(block, block, mask)

    def finish(self):
        for arrival in self.sent:
            arrival.wait()
        for arrival in self.sent:
            arrival.wait_sent()


class Local:
    def __init__(self, sems, pairs, base=0):
        self.copies = [
            pltpu.make_async_copy(a, b, sems.at[base + i]) for i, (a, b) in enumerate(pairs)
        ]
        self.open = set(range(len(pairs)))
        for copy in self.copies:
            copy.start()

    def wait(self, *which):
        for i in which or sorted(self.open):
            self.open.discard(i)
            self.copies[i].wait()


def row_loop(rows, step, body):
    block_loop(1, rows, step, lambda i, part: body(part))


def block_loop(n, rows, step, body):
    if rows % step:
        for i in range(n):
            body(i, slice(0, rows))
        return
    steps = rows // step

    @pl.loop(0, n * steps)
    def _(k):
        body(k // steps, pl.ds(pl.multiple_of(lax.rem(k, steps) * step, step), step))


def communicate(
    body, args, outs, copies, collective_id, in_vmem=False, out_vmem=False, scratch=(), kept=1
):
    def specs(inside, n):
        inside = [inside] * n if isinstance(inside, bool) else inside
        return [pl.BlockSpec(memory_space=pltpu.VMEM if i else pl.ANY) for i in inside]

    return pl.pallas_call(
        body,
        out_shape=outs,
        in_specs=specs(in_vmem, len(args)),
        out_specs=specs(out_vmem, len(outs)),
        scratch_shapes=[
            pltpu.SemaphoreType.DMA((copies,)),
            pltpu.SemaphoreType.DMA((copies,)),
            pltpu.SemaphoreType.DMA((kept,)),
            *scratch,
        ],
        compiler_params=pltpu.CompilerParams(
            collective_id=collective_id, has_side_effects=True, vmem_limit_bytes=VMEM_LIMIT
        ),
    )(*args)


def shape(dims, kind=bf16):
    return jax.ShapeDtypeStruct(dims, kind)


class Line:
    def __init__(self, links, here, h, FH, forward):
        self.links, self.here, self.h, self.FH, self.forward = links, here, h, FH, forward
        self.right, self.left, self.pending = [], [], []
        self.settled = set()

    def step(self, j):
        h, FH = self.h, self.FH
        rights = [
            self.links.copy(block, block, (self.links.s, self.links.f + 2))
            for block in self.here(lax.max(h - j, 0))
        ]
        lefts = [
            self.links.copy(block, block, (self.links.s, self.links.f - 2))
            for block in self.here(lax.min(h + j, FH - 1))
        ]
        for i in range(len(rights)):

            @pl.when((h >= j) & (h < FH - 1))
            def _():
                rights[i].start()

            @pl.when((h + j < FH) & (h > 0))
            def _():
                lefts[i].start()

        self.right.append(rights)
        self.left.append(lefts)

    def arrived(self, j):
        h, FH = self.h, self.FH
        up = self.here(lax.max(h - 1 - j, 0))
        down = self.here(lax.min(h + 1 + j, FH - 1))
        for i in range(len(up)):
            for blocks, copies, there in (
                (up, self.right[j], h - 1 - j >= 0),
                (down, self.left[j], h + 1 + j < FH),
            ):
                a, b = self.forward
                on = self.links.copy(blocks[i], blocks[i], (self.links.s ^ a, self.links.f ^ b))
                self.pending.append((j, on, there))

                @pl.when(there)
                def _():
                    copies[i].wait_recv()
                    on.start()

    def came(self, j):
        self.settled.add(j)
        for step, on, there in self.pending:
            if step == j:

                @pl.when(there)
                def _():
                    on.wait_recv()

    def finish(self):
        h, FH = self.h, self.FH
        for j in range(FH - 1):
            if j not in self.settled:
                self.came(j)
        for _, on, there in self.pending:

            @pl.when(there)
            def _():
                on.wait_send()

        for j in range(FH - 1):
            for i in range(len(self.right[j])):

                @pl.when((h >= j) & (h < FH - 1))
                def _():
                    self.right[j][i].wait_send()

                @pl.when((h + j < FH) & (h > 0))
                def _():
                    self.left[j][i].wait_send()


def rows_of(ref):
    return ref[...].reshape(-1, ref.shape[-1])


def rotation(table):
    half = table.shape[-1] // 2
    swapped = pltpu.roll(table, half, 1)
    first = lax.broadcasted_iota(jnp.int32, table.shape, 1) < half
    return jnp.where(first, table, swapped), jnp.where(first, -swapped, table)


def turn(vector, factors):
    return vector * factors[0] + pltpu.roll(vector, vector.shape[-1] // 2, 1) * factors[1]


class RowSum:
    def __init__(self, links, parts, from_core, from_x):
        self.links, self.parts, self.from_core, self.from_x = links, parts, from_core, from_x
        self.x, self.core, self.sent = links.s // 2, links.s % 2, []

    def far(self):
        x, core = 1 - self.x, 1 - self.core
        self.to_far = self.links.start(self.parts.at[x, core], self.from_core.at[x], (1, 0))
        self.sent.append(self.to_far)

    def near(self):
        x, core = self.x, 1 - self.core
        self.to_near = self.links.start(self.parts.at[x, core], self.from_core.at[x], (1, 0))
        self.sent.append(self.to_near)

    def middle(self):
        self.to_far.wait()
        x, core = 1 - self.x, self.core

        def add(rows):
            total = self.parts[x, core, rows].astype(f32) + self.from_core[x, rows].astype(f32)
            self.parts[x, core, rows] = total.astype(bf16)

        row_loop(self.from_x.shape[0], 16, add)
        self.across = self.links.start(self.parts.at[x, core], self.from_x, (2, 0))
        self.sent.append(self.across)

    def arrive(self):
        self.to_near.wait()
        self.across.wait()

    def total(self, rows):
        return (
            self.parts[self.x, self.core, rows].astype(f32)
            + self.from_core[self.x, rows].astype(f32)
            + self.from_x[rows].astype(f32)
        )


class LineSum:
    def __init__(self, links, h, parts, from_core, chain, extra):
        self.links, self.h, self.parts = links, h, parts
        self.from_core, self.chain, self.extra = from_core, chain, extra
        self.core, self.T = links.s % 2, extra.shape[0]
        self.by_core, self.right, self.left, self.end = {}, {}, {}, {}
        s, f = links.s, links.f
        for d in range(Z):
            block = parts.at[d, self.core]
            self.right[d] = links.copy(block, chain.at[d], (s, f + 2))
            self.left[d] = links.copy(block, chain.at[d], (s, f - 2))
            self.end[d] = links.copy(block, extra, (s, f - 2))

    def send_core(self, d):
        self.by_core[d] = self.links.start(
            self.parts.at[d, 1 - self.core], self.from_core.at[d], (1, 0)
        )

    def add(self, d, chained):
        def add(rows):
            total = self.parts[d, self.core, rows].astype(f32)
            total += self.from_core[d, rows].astype(f32)
            if chained:
                total += self.chain[d, rows].astype(f32)
            self.parts[d, self.core, rows] = total.astype(bf16)

        row_loop(self.T, 16, add)

    def stage(self, k, places):
        h = self.h
        for d in places:
            self.by_core[d].wait()
            rightward, leftward = (h < d) & (h == k), (h > d) & (h == Z - 1 - k)

            @pl.when(rightward)
            def _():
                if k:
                    self.right[d].wait_recv()
                self.add(d, k > 0)
                self.right[d].start()

            @pl.when(leftward)
            def _():
                if k:
                    self.left[d].wait_recv()
                self.add(d, k > 0)

            @pl.when(leftward & (h > d + 1))
            def _():
                self.left[d].start()

            @pl.when(leftward & (h == d + 1))
            def _():
                self.end[d].start()

    def arrive(self):
        h = self.h
        for d in range(Z):
            self.by_core[d].wait()
            if d > 0:

                @pl.when(h == d)
                def _():
                    self.right[d].wait_recv()

            else:

                @pl.when(h == 0)
                def _():
                    self.chain[0] = jnp.zeros_like(self.chain[0])

            if d < Z - 1:

                @pl.when(h == d)
                def _():
                    self.end[d].wait_recv()

            else:

                @pl.when(h == Z - 1)
                def _():
                    self.extra[...] = jnp.zeros_like(self.extra)

    def total(self, rows):
        return (
            self.parts[self.h, self.core, rows].astype(f32)
            + self.from_core[self.h, rows].astype(f32)
            + self.chain[self.h, rows].astype(f32)
            + self.extra[rows].astype(f32)
        )

    def settle(self):
        h = self.h
        for d in range(Z):
            self.by_core[d].wait_sent()

            @pl.when(h < d)
            def _():
                self.right[d].wait_send()

            @pl.when(h > d + 1)
            def _():
                self.left[d].wait_send()

            @pl.when(h == d + 1)
            def _():
                self.end[d].wait_send()


class LeadFirst:
    def __init__(self, ref):
        self.ref, self.n, self.rows = ref, ref.shape[0], ref.shape[3]

    def half(self, l):
        return self.ref.at[:, :, l]

    def both(self, w):
        return self.ref.at[:, w]

    def part(self, w, l):
        return self.ref.at[:, w, l]

    def item(self, i, w, l):
        return self.ref.at[i, w, l]

    def got(self, ref, i, w):
        return ref.at[i, w]


class Natural:
    def __init__(self, ref):
        self.ref, self.n, self.rows = ref, ref.shape[2], ref.shape[4]

    def half(self, l):
        return self.ref.at[:, :, :, l]

    def both(self, w):
        return self.ref.at[w % 2, w // 2]

    def part(self, w, l):
        return self.ref.at[w % 2, w // 2, :, l]

    def item(self, i, w, l):
        return self.ref.at[w % 2, w // 2, i, l]

    def got(self, ref, i, w):
        return ref.at[w % 2, w // 2, i]


class PieceByL:
    def __init__(self, links, view, by_l, by_w, w, masks):
        self.links, self.view, self.by_l, self.by_w = links, view, by_l, by_w
        self.w, self.masks, self.l = w, masks, links.f % 2
        self.first = links.start(view.half(1 - self.l), by_l, (0, 1))

    def partial(self, i, w, rows):
        total = self.view.item(i, w, self.l)[rows].astype(f32)
        return total + self.view.got(self.by_l, i, w)[rows].astype(f32)

    def middle(self):
        self.first.wait()
        self.second = []
        for k in range(1, len(self.masks)):
            w = self.w ^ k

            def add(i, rows, w=w):
                self.view.item(i, w, self.l)[rows] = self.partial(i, w, rows).astype(bf16)

            block_loop(self.view.n, self.view.rows, 16, add)
            self.second.append(
                self.links.start(self.view.part(w, self.l), self.by_w.at[k - 1], self.masks[k])
            )

    def last(self, store=None):
        for arrival in self.second:
            arrival.wait()

        def add(i, rows):
            total = self.partial(i, self.w, rows)
            for k in range(1, len(self.masks)):
                total += self.by_w[k - 1, i, rows].astype(f32)
            if store is None:
                self.view.item(i, self.w, self.l)[rows] = total.astype(bf16)
            else:
                store(i, rows, total)

        block_loop(self.view.n, self.view.rows, 16, add)


class PieceByW:
    def __init__(self, links, view, by_l, by_w, w, masks):
        self.links, self.view, self.by_l, self.by_w = links, view, by_l, by_w
        self.w, self.masks, self.l = w, masks, links.f % 2
        self.first = [
            links.start(view.both(w ^ k), by_w.at[k - 1], masks[k]) for k in range(1, len(masks))
        ]

    def partial(self, i, l, rows):
        total = self.view.item(i, self.w, l)[rows].astype(f32)
        for k in range(1, len(self.masks)):
            total += self.by_w[k - 1, i, l, rows].astype(f32)
        return total

    def middle(self):
        for arrival in self.first:
            arrival.wait()
        l = 1 - self.l

        def add(i, rows):
            self.view.item(i, self.w, l)[rows] = self.partial(i, l, rows).astype(bf16)

        block_loop(self.view.n, self.view.rows, 16, add)
        self.second = self.links.start(self.view.part(self.w, l), self.by_l, (0, 1))

    def last(self, store=None):
        self.second.wait()

        def add(i, rows):
            total = self.partial(i, self.l, rows) + self.by_l[i, rows].astype(f32)
            if store is None:
                self.view.item(i, self.w, self.l)[rows] = total.astype(bf16)
            else:
                store(i, rows, total)

        block_loop(self.view.n, self.view.rows, 16, add)


def by_l_scratch(n, W, rows, width):
    return [pltpu.VMEM((n, W, rows, width), bf16), pltpu.VMEM((W - 1, n, rows, width), bf16)]


def by_w_scratch(n, W, rows, width):
    return [pltpu.VMEM((n, rows, width), bf16), pltpu.VMEM((W - 1, n, 2, rows, width), bf16)]


def norm_back(grad_normed, inputs, gain):
    inverse = lax.rsqrt(jnp.mean(inputs * inputs, -1, keepdims=True) + epsilon)
    scaled = grad_normed * gain
    inner_sum = jnp.sum(scaled * inputs, -1, keepdims=True)
    grad = inverse * scaled - inputs * (inverse**3 * inner_sum / inputs.shape[-1])
    return grad, inputs * inverse


def layer_kernel(FH, *refs):
    tok, tab_in, wq_in, wk_in, wv_in, gains_in, wo_in = refs[:7]
    gate_in, up_in, down_in, cot_in, bias = refs[7:12]
    output, keys, values, grad_tokens, gate_out, up_out, down_out = refs[12:19]
    wq_out, wo_out, wk_out, wv_out, gains_out = refs[19:24]
    both_own, normed_kept, side_kept, o_kept = refs[24:28]
    send, recv, here, both, down, q_w, kv_w, o_w = refs[28:36]
    residual, grad_in, gains, gain_sums, grad_row = refs[36:41]
    grad_down, o_sum, kv_sum, q_own = refs[41:45]
    back_bufs, out_bufs = refs[45:49], refs[49:53]
    normed, cot, grad_both, tab, grad_k, grad_v = refs[53:59]
    bufs = refs[59:]
    links = Links(send, recv)
    s, f = links.s, links.f
    x, core = s // 2, s % 2
    e, h, l = f // 8, (f // 2) % Z, f % 2
    t = 2 * h + core
    T, D = residual.shape
    S, F, rows_w, HC = q_w.shape
    row_len, head = grad_k.shape
    heads = HC // head
    E, FC = both.shape[2], both.shape[6] // 2
    W, TG = 2 * E, 2 * Z
    w = 2 * e + x
    two = 2 * T
    cut = D // 4 * 3
    scale = head ** (-0.5)
    group_masks = [(a, 2 * m) for m in range(Z) for a in (0, 1)][1:]
    w_masks = [(2 * (j % 2), 8 * (j // 2)) for j in range(W)]
    back = LineSum(links, h, *back_bufs)
    out = LineSum(links, h, *out_bufs)
    back_parts, out_parts = back.parts, out.parts
    tok_g = grad_row
    spots = {}
    for name, width in (("attended", HC), ("q", HC), ("k", head), ("v", head), ("grad", HC)):
        base = sum(n for _, n in spots.values())
        spots[name] = (base, width)
    side_width = spots["grad"][0]

    def column(name, first=0, width=None):
        base, full_width = spots[name]
        return pl.ds(base + first, width or full_width)

    def block(where, name, r, first=0, width=None):
        return where[r // 2, r % 2, :, column(name, first, width)]

    def to_x(ref, j):
        return ref.at[(w ^ j) % 2, :, (w ^ j) // 2]

    def whole(where, name, first=0, width=None):
        return where[:, :, :, column(name, first, width)].reshape(row_len, -1)

    links.greet(
        [(a, 0) for a in (1, 2, 3)]
        + [(0, 1)]
        + [(0, 2 * k) for k in range(1, FH)]
        + [(1, 2 * m) for m in range(1, Z)]
        + [mask for mask in w_masks if mask[0] and mask[1]]
    )
    local = Local(
        here,
        [
            (wq_in.at[:, pl.ds(pl.multiple_of(s * HC, HC), HC)], q_w.at[s, f]),
            (wk_in, kv_w.at[s, f, :, pl.ds(0, head)]),
            (wv_in, kv_w.at[s, f, :, pl.ds(head, head)]),
            (gains_in, kv_w.at[s, f, :, pl.ds(2 * head, head)]),
            (wo_in, o_w.at[f]),
            (tok, tok_g.at[s]),
            (tab_in, tab.at[s]),
            (down_in, down.at[0, w, l]),
            (cot_in, cot.at[h, core]),
        ],
    )
    first = [
        links.start(
            wq_in.at[:, pl.ds(pl.multiple_of((s ^ a) * HC, HC), HC)], q_w.at[s, f], (a, 0)
        )
        for a in (1, 2, 3)
    ]
    quarter = FC * TG // S
    natural = Local(
        here,
        [
            (r.at[:, pl.ds(i * quarter, quarter)], back_parts.at[i, j, pl.ds(0, rows_w), pl.ds(0, quarter)])
            for j, r in enumerate((gate_in, up_in))
            for i in range(S)
        ],
        9,
    )
    local.wait(1, 2, 3, 4)
    along_z = (f // 2, FH, (0, 1))
    kv_line = Line(links, lambda place: [kv_w.at[s, 2 * place + l]], *along_z)
    o_line = Line(links, lambda place: [o_w.at[2 * place + l]], *along_z)
    q_line = Line(links, lambda place: [q_w.at[:, 2 * place + l]], *along_z)
    kv_line.step(0)
    kv_y = links.pass_on(kv_w.at[s, f], (0, 1))
    o_line.step(0)
    needed = [links.pass_on(o_w.at[f], (0, 1))]
    local.wait(0)
    for arrival in first:
        arrival.wait()
    q_line.step(0)
    needed.append(links.pass_on(q_w.at[:, f], (0, 1)))
    tok_x = links.start(tok, tok_g.at[s], (2, 0))
    needed.append(links.start(tok, tok_g.at[s], (1, 0)))
    needed += [links.start(tab_in, tab.at[s], (a, 0)) for a in (1, 2, 3)]
    ffn_in = {}
    lanes = 128
    whole_tiles = FC // lanes

    def blocks_of(ref, at_h, c):
        width = 2 * FC // W // 2
        parts = []
        for at_e in range(E):
            for at_x in (0, 1):
                base = (at_e * Z + at_h) * width
                parts.append(ref(2 * at_x + c)[:, base : base + width])
        return jnp.concatenate(parts, 1)

    def side_by_side(gate_units, up_units):
        tiles = []
        for j in range(whole_tiles):
            part = slice(j * lanes, (j + 1) * lanes)
            tiles += [gate_units[:, part], up_units[:, part]]
        rest = slice(whole_tiles * lanes, FC)
        return jnp.concatenate(tiles + [gate_units[:, rest], up_units[:, rest]], 1)

    def sent_blocks(at_h, c):
        return grad_both.at[at_h, pl.ds(pl.multiple_of(c * rows_w, rows_w), rows_w)]

    natural.wait()
    columns_of = [
        [back_parts[i, j, :rows_w, :quarter].astype(f32) for i in range(S)] for j in (0, 1)
    ]
    for at_h in range(Z):
        for c in (0, 1):
            units = [blocks_of(lambda i: columns_of[j][i], at_h, c) for j in (0, 1)]
            grad_both[at_h, c * rows_w : (c + 1) * rows_w] = side_by_side(*units).astype(bf16)
    own_block = Local(here, [(sent_blocks(h, core), both.at[x, core, e, h, l])], 17)

    def to_group(m):
        for a in (0, 1):
            if (a, m) != (0, 0):
                place = (x, core, e, h, l)
                source = sent_blocks(h ^ m, core ^ a)
                ffn_in[a, m] = links.start(source, both.at[place], (a, 2 * m))

    arriving = []

    class Spread:
        def __init__(self, near, second_w, second_y):
            self.near, self.second_w, self.second_y = near, second_w, second_y

        def by_w(self):
            self.came_w = [links.pass_on(self.near, mask) for mask in w_masks[1:]]

        def by_y(self):
            self.came_y = links.pass_on(self.near, (0, 1))

        def on_w(self):
            self.came_y.wait()
            arriving.extend(links.pass_on(self.second_w, mask) for mask in w_masks[1:])

        def on_y(self):
            for j, arrival in enumerate(self.came_w):
                arrival.wait()
                arriving.append(links.pass_on(self.second_y(j + 1), (0, 1)))

    def spread_of(m):
        def second_y(j):
            return to_x(both, j).at[0, h ^ m, l]

        here_q = to_x(both, 0)
        return Spread(here_q.at[:, h ^ m, l], here_q.at[1, h ^ m, 1 - l], second_y)

    low_half, high_half = pl.ds(0, cut), pl.ds(cut, D - cut)
    spread_down = Spread(
        down.at[0, w, l],
        down.at[0, w, 1 - l, :, high_half],
        lambda j: down.at[0, w ^ j, l, :, low_half],
    )
    to_group(0)
    local.wait(7)
    spread_down.by_w()
    for j in range(FH - 1):
        for way in (kv_line, o_line, q_line):
            way.arrived(j)
            if j + 1 < FH - 1:
                way.step(j + 1)
        if j == 0:
            tok_x.wait()
            needed.append(links.pass_on(tok_g.at[s ^ 2], (1, 0)))
            own_block.wait()
            ffn_in[1, 0].wait()
            spreads = [spread_of(m) for m in range(Z)]
            spreads[0].by_w()
    kv_y.wait()
    kv_line.finish()
    kv_x = links.pass_on(kv_w.at[s], (2, 0))
    needed.append(links.pass_on(kv_w.at[s], (1, 0)))
    for m in range(1, Z):
        to_group(m)
    spread_down.by_y()
    spreads[0].by_y()
    cot_line = Line(links, lambda place: [cot.at[place, core]], h, Z, (1, 0))
    kv_x.wait()
    needed.append(links.pass_on(kv_w.at[s ^ 2], (1, 0)))
    for arrival in needed:
        arrival.wait()
    o_line.finish()
    q_line.finish()
    local.wait(5, 6)
    kept_o = Local(here, [(o_w, o_kept)], 18)

    normed_one, side = out_parts.at[pl.ds(0, 2)], out_parts.at[pl.ds(2, 2)]
    place = lax.broadcasted_iota(jnp.int32, (8, head), 0)
    lane = lax.broadcasted_iota(jnp.int32, (8, head), 1)
    pick = (place == lane).astype(bf16)
    kv_full = rows_of(kv_w)
    gains[...] = contract_last(pick, kv_full[:, 2 * head :])

    def norm_one(i, rows):
        value = tok_g[i, rows].astype(f32)
        inverse = lax.rsqrt(jnp.mean(value * value, -1, keepdims=True) + epsilon)
        normed_one[i // 2, lax.rem(i, 2), rows] = (value * inverse * gains[0:1]).astype(bf16)

    block_loop(S, T, 16, norm_one)
    local.wait(8)
    cot_line.step(0)
    arriving.append(links.pass_on(cot.at[h, core], (1, 0)))
    factors = rotation(rows_of(tab))

    def put(name, first, value):
        columns = column(name, first, value.shape[1])
        side[:, :, :, columns] = value.astype(bf16).reshape(2, 2, T, -1)

    kv = dot(rows_of(normed_one), kv_full[:, : 2 * head])
    put("k", 0, turn(kv[:, :head], factors))
    put("v", 0, kv[:, head:])
    for n in range(0, heads, 2):
        columns = slice(n * head, (n + 2) * head)
        pair = dot(rows_of(normed_one), q_w[:, :, :, columns].reshape(D, 2 * head))
        for j in (0, 1):
            put("q", (n + j) * head, turn(pair[:, j * head : (j + 1) * head], factors))
    results = [
        Local(
            here,
            [
                (side.at[x, core, :, column("k")], keys),
                (side.at[x, core, :, column("v")], values),
            ],
            21,
        )
    ]
    for r in range(S):
        rows, seen = slice(r * T, (r + 1) * T), slice(0, (r + 1) * T)
        keys_seen, values_seen = whole(side, "k")[seen], whole(side, "v")[seen]
        for n in range(heads):
            query = block(side, "q", r, n * head, head)
            scores = contract_last(query, keys_seen) * scale + bias[rows, seen].astype(f32)
            scores = jnp.exp(scores - jnp.max(scores, -1, keepdims=True))
            probs = (scores / jnp.sum(scores, -1, keepdims=True)).astype(bf16)
            side[r // 2, r % 2, :, column("attended", n * head, head)] = dot(
                probs, values_seen
            ).astype(bf16)
    spread_down.on_y()
    spread_down.on_w()

    first_two = pl.ds(0, 2)
    row_bufs = (back_parts.at[first_two], back.from_core.at[first_two], back.chain.at[0])
    parts = RowSum(links, *row_bufs)

    def project(x_to):
        rows = side[x_to, :, :, column("attended")].reshape(two, HC)
        for n in range(0, D, HC):
            columns = slice(n, n + HC)
            total = dot(rows, o_w[:, :, columns].reshape(HC, HC))
            parts.parts[x_to, :, :, columns] = total.astype(bf16).reshape(2, T, HC)

    project(1 - x)
    parts.far()
    project(x)
    parts.near()
    parts.middle()
    spreads[0].on_y()
    spreads[0].on_w()
    for m in range(1, Z):
        for a in (0, 1):
            ffn_in[a, m].wait()
        spreads[m].by_y()
        spreads[m].by_w()
    cot_line.arrived(0)
    cot_line.step(1)
    kept = Local(
        here, [(normed_one, normed_kept), (side.at[:, :, :, pl.ds(0, side_width)], side_kept)], 19
    )
    parts.arrive()

    def norm_two(rows):
        total = tok_g[s, rows].astype(f32) + parts.total(rows)
        residual[rows] = total
        inverse = lax.rsqrt(jnp.mean(total * total, -1, keepdims=True) + epsilon)
        normed[h, core, rows] = (total * inverse * gains[1:2]).astype(bf16)

    row_loop(T, 16, norm_two)
    normed_line = Line(links, lambda place: [normed.at[place, core]], h, Z, (1, 0))
    normed_line.step(0)
    beside = [links.pass_on(normed.at[h, core], (1, 0))]
    cot_line.arrived(1)
    cot_line.step(2)
    for m in range(1, Z):
        spreads[m].on_y()
        spreads[m].on_w()
        if m < Z - 1:
            normed_line.arrived(m - 1)
            normed_line.step(m)
    results[0].wait()
    kept_o.wait()
    kept.wait()
    for arrival in arriving:
        arrival.wait()
    for arrival in links.sent:
        arrival.wait_sent()

    slot = D // 2
    lane_is_low = lax.broadcasted_iota(jnp.int32, (two, lanes), 1) < lanes // 2

    def hidden_of(d):
        n = normed[d].reshape(two, D)
        c = cot[d].reshape(two, D)
        weights = down[...].reshape(FC, D)

        def units(first, width, gate_proj, up_proj, grad_inner):
            sig = jax.nn.sigmoid(gate_proj)
            silu = gate_proj * sig
            spot = pl.ds(pl.multiple_of(d // 2 * slot + first, lanes), width)
            hidden = (silu * up_proj).astype(bf16)[:, :width]
            o_w[pl.ds(d % 2 * (F // 2), F // 2), :, spot] = hidden.reshape(F // 2, rows_w, width)
            slope = sig * (1.0 + gate_proj * (1.0 - sig))
            return (grad_inner * up_proj * slope).astype(bf16), (grad_inner * silu).astype(bf16)

        for first in range(0, FC, 2 * lanes):
            width = min(2 * lanes, FC - first)
            rows = weights[first : first + width]
            if width % lanes:
                rows = jnp.concatenate([rows, rows[width - lanes // 2 :]], 0)
            grad_inner = contract_last(c, rows)
            for i in range(0, width, lanes):
                base = 2 * (first + i)
                columns = (slice(None),) * 6 + (slice(base, min(base + 2 * lanes, 2 * FC)),)
                proj = dot(n, both[columns].reshape(D, -1))
                part = slice(i, i + lanes)
                if i + lanes <= width:
                    grad_gate, grad_up = units(
                        first + i,
                        lanes,
                        proj[:, :lanes],
                        proj[:, lanes:],
                        grad_inner[:, part],
                    )
                    grad_both[d, :, base : base + lanes] = grad_gate
                    grad_both[d, :, base + lanes : base + 2 * lanes] = grad_up
                else:
                    mixed = proj
                    turned = pltpu.roll(mixed, lanes // 2, 1)
                    grad_gate, grad_up = units(
                        first + i,
                        lanes // 2,
                        jnp.where(lane_is_low, mixed, turned),
                        jnp.where(lane_is_low, turned, mixed),
                        grad_inner[:, part],
                    )
                    grad_both[d, :, base : base + lanes] = jnp.where(
                        lane_is_low, grad_gate, grad_up
                    )

    def back_of(d):
        for i in range(S):
            columns = slice(i * F * rows_w, (i + 1) * F * rows_w)
            total = contract_last(grad_both[d], both[i // 2, i % 2].reshape(-1, 2 * FC))
            back_parts[d, :, :, columns] = total.astype(bf16).reshape(2, T, -1)
        back.send_core(d)

    def out_of(d):
        spot = slice(d // 2 * slot, d // 2 * slot + FC)
        hidden = o_w[pl.ds(d % 2 * (F // 2), F // 2), :, spot].reshape(two, FC)
        for i in range(0, D, 512):
            columns = slice(i, i + 512)
            total = dot(hidden, down[:, :, :, :, columns].reshape(FC, 512))
            out_parts[d, :, :, columns] = total.astype(bf16).reshape(2, T, -1)
        out.send_core(d)

    for arrival in beside:
        arrival.wait()
    hidden_of(h)
    for line in (cot_line, normed_line):
        line.came(0)
    hidden_of(h ^ 1)
    for line in (cot_line, normed_line):
        line.came(1)
    hidden_of(h ^ 2)
    for line in (cot_line, normed_line):
        line.arrived(2)
    for line in (cot_line, normed_line):
        line.came(2)
    hidden_of(h ^ 3)
    back_of(3)
    back_of(0)
    back.stage(0, (3, 0))
    back_of(2)
    back_of(1)
    back.stage(0, (2, 1))
    for line in (cot_line, normed_line):
        line.finish()
    for d in (3, 0, 2, 1):
        out_of(d)
    ffn = {}
    inner = [o_w[:, :, i * slot : i * slot + FC].reshape(2 * two, FC) for i in (0, 1)]
    for i in range(0, D, 256):
        columns = slice(i, i + 256)
        total = contract_first(inner[0], cot[0:2, :, :, columns].reshape(2 * two, 256))
        total += contract_first(inner[1], cot[2:4, :, :, columns].reshape(2 * two, 256))
        down[:, :, :, :, columns] = total.astype(bf16).reshape(1, W, 2, -1, 256)
        if i + 256 == cut:
            ffn["down_low"] = PieceByL(
                links, LeadFirst(down.at[:, :, :, :, low_half]), *bufs[0:2], w, w_masks
            )
    ffn["down_high"] = PieceByW(
        links, LeadFirst(down.at[:, :, :, :, high_half]), *bufs[2:4], w, w_masks
    )
    back.stage(1, (3, 0))
    width = F * rows_w
    for c in (0, 1):
        for i in (0, 1):
            base = (2 * i + c) * width
            turned = normed[:, :, :, base : base + width].reshape(4 * two, width)
            for columns in [slice(n, min(n + 3 * lanes, 2 * FC)) for n in range(0, 2 * FC, 3 * lanes)]:
                total = contract_first(turned, grad_both[:, :, columns].reshape(4 * two, -1))
                both[i, c, :, :, :, :, columns] = total.astype(bf16).reshape(E, Z, 2, rows_w, -1)
        if c == 0:
            ffn["both", 0] = PieceByL(links, Natural(both.at[:, 0]), *bufs[4:6], w, w_masks)
            back.stage(1, (2, 1))
            back.stage(2, (3, 0))
    ffn["both", 1] = PieceByL(
        links, Natural(both.at[:, 1, :, first_two]), *bufs[6:8], w, w_masks
    )
    ffn["both", 2] = PieceByW(
        links, Natural(both.at[:, 1, :, pl.ds(2, 2)]), *bufs[8:10], w, w_masks
    )
    out.stage(0, (3, 0, 2, 1))
    ffn["down_low"].middle()
    ffn["down_high"].middle()

    cot_own, tok_own = normed.at[2, 0], normed.at[2, 1]
    own = Local(here, [(cot_in, cot_own), (tok, tok_own)], 23)
    gain_sums[...] = jnp.zeros_like(gain_sums)
    own.wait()
    back.arrive()

    def second_norm(rows):
        grad_normed = back.total(rows)
        grad, unit = norm_back(grad_normed, residual[rows], gains[1:2])
        grad = grad + cot_own[rows].astype(f32)
        grad_in[rows] = grad
        grad_row[s, rows] = grad.astype(bf16)
        gain_sums[1:2] += jnp.sum(grad_normed * unit, 0, keepdims=True)

    row_loop(T, 16, second_norm)
    row_x = links.pass_on(grad_row.at[s], (2, 0))
    row_c = links.pass_on(grad_row.at[s], (1, 0))

    last_two = pl.ds(2, 2)
    side = cot.at[first_two]
    normed_one = normed.at[first_two]
    grad_side = cot.at[last_two]
    loads = Local(
        here,
        [
            (o_kept, o_w),
            (side_kept, cot.at[first_two, :, :, pl.ds(0, side_width)]),
            (normed_kept, normed_one),
        ],
        25,
    )
    ffn["both", 2].middle()
    row_x.wait()
    row_cc = links.pass_on(grad_row.at[s ^ 2], (1, 0))
    out.stage(1, (3, 0, 2, 1))
    row_c.wait()
    row_cc.wait()
    loads.wait()
    per = 2 * head // rows_w
    for n in range(0, heads, 2):
        wo = o_w[n // 2 * per : (n // 2 + 1) * per].reshape(2 * head, D)
        pair = contract_last(rows_of(grad_row), wo).astype(bf16)
        side[:, :, :, column("grad", n * head, 2 * head)] = pair.reshape(2, 2, T, 2 * head)
    for i in range(0, D, HC):
        columns = slice(i, i + HC)
        grad_columns = grad_row[:, :, columns].reshape(row_len, HC)
        total = contract_first(whole(side, "attended"), grad_columns)
        o_w[:, :, columns] = total.astype(bf16).reshape(F, rows_w, HC)
    place_z, z_masks = f // 2, [(0, 2 * j) for j in range(FH)]
    o_view = LeadFirst(o_w.reshape(1, FH, 2, rows_w, D))
    o_piece = PieceByL(links, o_view, *bufs[10:12], place_z, z_masks)
    ffn["both", 0].middle()
    grad_k[...] = jnp.zeros_like(grad_k)
    grad_v[...] = jnp.zeros_like(grad_v)
    factors = rotation(rows_of(tab))
    back_turn = (factors[0], -factors[1])
    for r in range(S):
        rows, seen = slice(r * T, (r + 1) * T), slice(0, (r + 1) * T)
        keys_seen, values_seen = whole(side, "k")[seen], whole(side, "v")[seen]
        for n in range(heads):
            query = block(side, "q", r, n * head, head)
            grad_att = block(side, "grad", r, n * head, head)
            scores = contract_last(query, keys_seen) * scale + bias[rows, seen].astype(f32)
            scores = jnp.exp(scores - jnp.max(scores, -1, keepdims=True))
            probs = scores / jnp.sum(scores, -1, keepdims=True)
            grad_probs = contract_last(grad_att, values_seen)
            delta = jnp.sum(probs * grad_probs, -1, keepdims=True)
            grad_scores = (probs * (grad_probs - delta)).astype(bf16)
            grad_q = dot(grad_scores, keys_seen) * scale
            grad_q = turn(grad_q, (back_turn[0][rows], back_turn[1][rows])).astype(bf16)
            grad_side[r // 2, r % 2, :, n * head : (n + 1) * head] = grad_q
            grad_k[seen] += contract_first(grad_scores, query)
            grad_v[seen] += contract_first(probs.astype(bf16), grad_att)
    grad_key = turn(grad_k[...] * scale, back_turn).astype(bf16)
    grad_side[:, :, :, HC : HC + head] = grad_key.reshape(2, 2, T, head)
    grad_side[:, :, :, HC + head : HC + 2 * head] = grad_v[...].astype(bf16).reshape(2, 2, T, head)
    grad_qkv = slice(0, HC + 2 * head)
    back.settle()
    row = RowSum(links, *row_bufs)
    for cx, go in ((1 - x, row.far), (x, row.near)):
        for i in range(S):
            total = contract_last(grad_side[cx, :, :, :HC].reshape(two, HC), q_w[i].reshape(-1, HC))
            total += contract_last(
                grad_side[cx, :, :, HC : HC + 2 * head].reshape(two, 2 * head),
                kv_w[i, :, :, : 2 * head].reshape(-1, 2 * head),
            )
            columns = slice(i * F * rows_w, (i + 1) * F * rows_w)
            row.parts[cx, :, :, columns] = total.astype(bf16).reshape(2, T, -1)
        go()
    row.middle()
    ffn["both", 1].middle()
    out.stage(2, (3, 0))
    pieces = []
    q_view = q_w.reshape(S, FH, 2, rows_w, HC)
    kv_view = kv_w.reshape(S, FH, 2, rows_w, kv_w.shape[3])
    for i in range(S):
        columns = slice(i * F * rows_w, (i + 1) * F * rows_w)
        turned = normed_one[:, :, :, columns].reshape(row_len, -1)
        total = contract_first(turned, grad_side[:, :, :, grad_qkv].reshape(row_len, -1))
        total = total.astype(bf16)
        q_w[i] = total[:, :HC].reshape(F, rows_w, HC)
        kv_w[i, :, :, : 2 * head] = total[:, HC:].reshape(F, rows_w, 2 * head)
        one = pl.ds(i, 1)
        spare = (bufs[12].at[one], bufs[13].at[:, one])
        pieces.append(PieceByL(links, LeadFirst(q_view.at[one]), *spare, place_z, z_masks))
    for i in range(3):
        ffn["both", i].last()
    owners = [
        links.start(both.at[x, core ^ a, e, h ^ (b // 2), l], both_own.at[t], (a, b))
        for a, b in group_masks
    ]
    mine = Local(here, [(both.at[x, core, e, h, l], both_own.at[t])], 28)
    row.arrive()

    def first_norm(rows):
        grad_normed = row.total(rows)
        grad, unit = norm_back(grad_normed, tok_own[rows].astype(f32), gains[0:1])
        grad_in[rows] += grad
        gain_sums[0:1] += jnp.sum(grad_normed * unit, 0, keepdims=True)

    row_loop(T, 16, first_norm)
    results = [Local(here, [(grad_in, grad_tokens)], 29)]
    pick = jnp.where((place == lane) & (place < 2), 1.0, 0.0)
    columns = contract_first(gain_sums[...], pick).astype(bf16)
    kv_w[:, :, :, 2 * head :] = columns.reshape(S, F, rows_w, head)
    kv_row = RowSum(links, kv_w.reshape(2, 2, F * rows_w, kv_w.shape[3]), *bufs[14:16])
    kv_row.far()
    kv_row.near()
    kv_row.middle()
    o_piece.middle()
    pieces[0].middle()
    kv_row.arrive()

    def keep_kv(rows):
        kv_row.parts[x, core, rows] = kv_row.total(rows).astype(bf16)

    row_loop(F * rows_w, 16, keep_kv)
    kv_mine = LeadFirst(kv_view.at[pl.ds(s, 1)])
    kv_piece = PieceByL(links, kv_mine, *bufs[16:18], place_z, z_masks)
    for piece in pieces[1:]:
        piece.middle()
    kv_piece.middle()

    def store_down(base):
        def store(i, rows, total):
            grad_down[rows, base : base + total.shape[1]] = total

        return store

    ffn["down_low"].last(store_down(0))
    ffn["down_high"].last(store_down(cut))
    results.append(Local(here, [(grad_down, down_out)], 30))

    def store_o(i, rows, total):
        o_sum[rows] = total

    o_piece.last(store_o)
    results.append(Local(here, [(o_sum, wo_out)], 31))
    out.arrive()

    out_rows = back_parts.at[3, 0]

    def finish_output(rows):
        out_rows[rows] = (residual[rows] + out.total(rows)).astype(bf16)

    row_loop(T, 16, finish_output)
    results.append(Local(here, [(out_rows, output)], 32))
    grad_own = grad_both.reshape(Z, two // rows_w, rows_w, 2 * FC)
    for arrival in owners:
        arrival.wait()
    mine.wait()
    came = Local(
        here, [(both_own.at[pl.ds(2 * i, 2)], grad_own.at[i, pl.ds(0, 2)]) for i in range(Z)], 33
    )
    came.wait()
    results[0].wait()
    stores = [
        r.at[pl.ds(j * rows_w, rows_w), pl.ds(0, quarter)]
        for r in (residual, grad_in)
        for j in (0, 1)
    ]
    leaving = [None] * len(stores)
    count = 0
    for i, target in enumerate((gate_out, up_out)):
        units = []
        for at_h in range(Z):
            for c in (0, 1):
                block = grad_own[at_h, c].astype(f32)
                tiles = [
                    block[:, (2 * j + i) * lanes : (2 * j + i + 1) * lanes]
                    for j in range(whole_tiles)
                ]
                base = 2 * whole_tiles * lanes + i * (FC - whole_tiles * lanes)
                tiles.append(block[:, base : base + FC - whole_tiles * lanes])
                units.append(jnp.concatenate(tiles, 1))
        width = FC // W
        for at_x in (0, 1):
            for c in (0, 1):
                parts = [
                    units[2 * at_h + c][:, (2 * at_e + at_x) * width : (2 * at_e + at_x + 1) * width]
                    for at_e in range(E)
                    for at_h in range(Z)
                ]
                slot_now = count % len(stores)
                if leaving[slot_now] is not None:
                    leaving[slot_now].wait()
                stores[slot_now][...] = jnp.concatenate(parts, 1)
                columns = pl.ds((2 * at_x + c) * quarter, quarter)
                leaving[slot_now] = Local(
                    here, [(stores[slot_now], target.at[:, columns])], 37 + slot_now
                )
                count += 1
    for piece in pieces:
        piece.last()
    for a in (1, 2, 3):
        links.start(q_view.at[s ^ a, place_z, l], q_own.at[s], (a, 0))
    q_own[s] = q_view[s, place_z, l]
    q_came = links.sent[-3:]

    def store_kv(i, rows, total):
        kv_sum[rows] = total

    kv_piece.last(store_kv)
    names = (wk_out, wv_out, gains_out)
    results.append(
        Local(here, [(kv_sum.at[:, pl.ds(i * head, head)], r) for i, r in enumerate(names)], 41)
    )
    for arrival in q_came:
        arrival.wait()
    for i in leaving:
        i.wait()
    q_rows = residual.at[pl.ds(0, rows_w)]
    for i in range(S):
        q_rows[:, i * HC : (i + 1) * HC] = q_own[i].astype(f32)
    results.append(Local(here, [(q_rows, wq_out)], 44))
    out.settle()
    links.finish()
    for result in results[1:]:
        result.wait()


def angle_tables(position_row, head_size):
    half_head = head_size // 2
    frequency = 10000.0 ** (-jnp.arange(half_head, dtype=f32) * 2.0 / head_size)
    phase_angle = position_row.astype(f32)[:, None] * frequency[None, :]
    return (jnp.cos(phase_angle), jnp.sin(phase_angle))


def per_device(
    S,
    F,
    tokens,
    segments,
    positions,
    gain_one,
    w_query,
    w_key,
    w_value,
    w_out,
    gain_two,
    w_gate,
    w_up,
    w_down,
    cotangent,
):
    T, D = tokens.shape[1:]
    head = w_key.shape[1]
    row_len = segments.shape[1]
    rows = w_query.shape[0]
    down_rows = w_down.shape[0]
    FF = w_gate.shape[1]
    FH, E = F // 2, F // 8
    W, TG = 2 * E, 2 * Z
    HC = w_query.shape[1] // S
    heads = HC // head
    FC = FF // TG

    gains = jnp.stack([gain_one, gain_two], 1)
    gains = jnp.concatenate([gains, jnp.zeros((rows, head - 2), bf16)], 1)
    KV = 3 * head
    table = jnp.concatenate(angle_tables(positions[0], head), 1)
    segment = segments[0]
    index = jnp.arange(row_len)
    allowed = (index[None, :] <= index[:, None]) & (segment[None, :] == segment[:, None])
    bias = jnp.where(allowed, 0.0, -1e30).astype(bf16)
    group = [pltpu.VMEM((Z, 2, T, D), bf16), pltpu.VMEM((Z, T, D), bf16)]
    group += [pltpu.VMEM((Z, T, D), bf16), pltpu.VMEM((T, D), bf16)]
    weight = pltpu.VMEM((2, 2, E, Z, 2, rows, 2 * FC), bf16)

    def natural_by_l(n):
        block = (n, rows, 2 * FC)
        return [pltpu.VMEM((2, E, *block), bf16), pltpu.VMEM((W - 1, *block), bf16)]

    outs = [
        ((T, D), bf16),
        ((T, head), bf16),
        ((T, head), bf16),
        ((T, D), f32),
        ((rows, FF), f32),
        ((rows, FF), f32),
        ((down_rows, D), f32),
        ((rows, D), f32),
        ((rows, D), f32),
        ((rows, head), f32),
        ((rows, head), f32),
        ((rows, head), f32),
        ((TG, rows, 2 * FC), bf16),
        ((2, 2, T, D), bf16),
        ((2, 2, T, 2 * HC + 2 * head), bf16),
        ((F, rows, D), bf16),
    ]
    results = communicate(
        functools.partial(layer_kernel, FH),
        (
            tokens[0],
            table,
            w_query,
            w_key,
            w_value,
            gains,
            w_out,
            w_gate,
            w_up,
            w_down,
            cotangent[0],
            bias,
        ),
        [shape(dims, kind) for dims, kind in outs],
        300 + 40 * F,
        0,
        in_vmem=[False] * 11 + [True],
        kept=48,
        scratch=[
            weight,
            pltpu.VMEM((1, W, 2, down_rows, D), bf16),
            pltpu.VMEM((S, F, rows, HC), bf16),
            pltpu.VMEM((S, F, rows, KV), bf16),
            pltpu.VMEM((F, rows, D), bf16),
            pltpu.VMEM((T, D), f32),
            pltpu.VMEM((T, D), f32),
            pltpu.VMEM((8, D), f32),
            pltpu.VMEM((8, D), f32),
            pltpu.VMEM((S, T, D), bf16),
            pltpu.VMEM((down_rows, D), f32),
            pltpu.VMEM((rows, D), f32),
            pltpu.VMEM((rows, KV), f32),
            pltpu.VMEM((S, rows, HC), bf16),
            *group,
            *group,
            pltpu.VMEM((Z, 2, T, D), bf16),
            pltpu.VMEM((Z, 2, T, D), bf16),
            pltpu.VMEM((Z, 2 * T, 2 * FC), bf16),
            pltpu.VMEM((S, T, head), f32),
            pltpu.VMEM((row_len, head), f32),
            pltpu.VMEM((row_len, head), f32),
            *by_l_scratch(1, W, down_rows, D // 4 * 3),
            *by_w_scratch(1, W, down_rows, D // 4),
            *natural_by_l(Z),
            *natural_by_l(2),
            *by_w_scratch(2, W, rows, 2 * FC),
            *by_l_scratch(1, FH, rows, D),
            *by_l_scratch(S, FH, rows, HC),
            pltpu.VMEM((2, F * rows, KV), bf16),
            pltpu.VMEM((F * rows, KV), bf16),
            *by_l_scratch(1, FH, rows, KV),
        ],
    )
    output, keys, values, grad_tokens, gate, up, down, query, out, key, value, gains = results[:12]
    return (
        output[None],
        keys[None],
        values[None],
        grad_tokens[None],
        gains[:, 0],
        query,
        key,
        value,
        out,
        gains[:, 1],
        gate,
        up,
        down,
    )


def solution(mesh):
    token_spec = P("fsdp", "seq", None)
    flat, matrix = P(("seq", "fsdp")), P(("seq", "fsdp"), None)
    return jax.shard_map(
        functools.partial(per_device, mesh.shape["seq"], mesh.shape["fsdp"]),
        mesh=mesh,
        in_specs=(
            token_spec,
            P("fsdp", None),
            P("fsdp", "seq"),
            flat,
            matrix,
            matrix,
            matrix,
            matrix,
            flat,
            matrix,
            matrix,
            matrix,
            token_spec,
        ),
        out_specs=(
            token_spec,
            token_spec,
            token_spec,
            token_spec,
            flat,
            matrix,
            matrix,
            matrix,
            matrix,
            flat,
            matrix,
            matrix,
            matrix,
        ),
        check_vma=False,
    )
```

```python
import functools

import jax
import jax.numpy as jnp
from jax import lax
from jax.experimental import pallas as pl
from jax.experimental.pallas import tpu as pltpu
from jax.sharding import PartitionSpec as P

epsilon = 1e-05
MESH = pl.DeviceIdType.MESH
Z = 4
VMEM_LIMIT = 64 * 2**20 - 2**18
bf16 = jnp.bfloat16
f32 = jnp.float32


def dot(left, right):
    return jnp.dot(left, right, preferred_element_type=f32)


def contract_last(left, right):
    return lax.dot_general(left, right, (((1,), (1,)), ((), ())), preferred_element_type=f32)


def contract_first(left, right):
    return lax.dot_general(left, right, (((0,), (0,)), ((), ())), preferred_element_type=f32)


class Arrival:
    def __init__(self, copy):
        self.copy, self.waited, self.left = copy, False, False

    def wait(self):
        if not self.waited:
            self.waited = True
            self.copy.wait_recv()

    def wait_sent(self):
        if not self.left:
            self.left = True
            self.copy.wait_send()


class Links:
    def __init__(self, send, recv):
        self.send, self.recv, self.sent, self.count = send, recv, [], 0
        self.s, self.f = lax.axis_index("seq"), lax.axis_index("fsdp")

    def greet(self, masks):
        barrier = pltpu.get_barrier_semaphore()
        for a, b in masks:
            pl.semaphore_signal(
                barrier, inc=1, device_id=(self.s ^ a, self.f ^ b), device_id_type=MESH
            )
        pl.semaphore_wait(barrier, len(masks))

    def copy(self, source, target, device):
        self.count += 1
        return pltpu.make_async_remote_copy(
            src_ref=source,
            dst_ref=target,
            send_sem=self.send.at[self.count - 1],
            recv_sem=self.recv.at[self.count - 1],
            device_id=device,
            device_id_type=MESH,
        )

    def start(self, source, target, mask):
        copy = self.copy(source, target, (self.s ^ mask[0], self.f ^ mask[1]))
        copy.start()
        self.sent.append(Arrival(copy))
        return self.sent[-1]

    def pass_on(self, block, mask):
        return self.start(block, block, mask)

    def finish(self):
        for arrival in self.sent:
            arrival.wait()
        for arrival in self.sent:
            arrival.wait_sent()


class Local:
    def __init__(self, sems, pairs, base=0):
        self.copies = [
            pltpu.make_async_copy(a, b, sems.at[base + i]) for i, (a, b) in enumerate(pairs)
        ]
        self.open = set(range(len(pairs)))
        for copy in self.copies:
            copy.start()

    def wait(self, *which):
        for i in which or sorted(self.open):
            self.open.discard(i)
            self.copies[i].wait()


def row_loop(rows, step, body):
    block_loop(1, rows, step, lambda i, part: body(part))


def block_loop(n, rows, step, body):
    if rows % step:
        for i in range(n):
            body(i, slice(0, rows))
        return
    steps = rows // step

    @pl.loop(0, n * steps)
    def _(k):
        body(k // steps, pl.ds(pl.multiple_of(lax.rem(k, steps) * step, step), step))


def communicate(
    body, args, outs, copies, collective_id, in_vmem=False, out_vmem=False, scratch=(), kept=1
):
    def specs(inside, n):
        inside = [inside] * n if isinstance(inside, bool) else inside
        return [pl.BlockSpec(memory_space=pltpu.VMEM if i else pl.ANY) for i in inside]

    return pl.pallas_call(
        body,
        out_shape=outs,
        in_specs=specs(in_vmem, len(args)),
        out_specs=specs(out_vmem, len(outs)),
        scratch_shapes=[
            pltpu.SemaphoreType.DMA((copies,)),
            pltpu.SemaphoreType.DMA((copies,)),
            pltpu.SemaphoreType.DMA((kept,)),
            *scratch,
        ],
        compiler_params=pltpu.CompilerParams(
            collective_id=collective_id, has_side_effects=True, vmem_limit_bytes=VMEM_LIMIT
        ),
    )(*args)


def shape(dims, kind=bf16):
    return jax.ShapeDtypeStruct(dims, kind)


class Line:
    def __init__(self, links, here, h, FH, forward):
        self.links, self.here, self.h, self.FH, self.forward = links, here, h, FH, forward
        self.right, self.left, self.pending = [], [], []
        self.settled = set()

    def step(self, j):
        h, FH = self.h, self.FH
        rights = [
            self.links.copy(block, block, (self.links.s, self.links.f + 2))
            for block in self.here(lax.max(h - j, 0))
        ]
        lefts = [
            self.links.copy(block, block, (self.links.s, self.links.f - 2))
            for block in self.here(lax.min(h + j, FH - 1))
        ]
        for i in range(len(rights)):

            @pl.when((h >= j) & (h < FH - 1))
            def _():
                rights[i].start()

            @pl.when((h + j < FH) & (h > 0))
            def _():
                lefts[i].start()

        self.right.append(rights)
        self.left.append(lefts)

    def arrived(self, j):
        h, FH = self.h, self.FH
        up = self.here(lax.max(h - 1 - j, 0))
        down = self.here(lax.min(h + 1 + j, FH - 1))
        for i in range(len(up)):
            for blocks, copies, there in (
                (up, self.right[j], h - 1 - j >= 0),
                (down, self.left[j], h + 1 + j < FH),
            ):
                a, b = self.forward
                on = self.links.copy(blocks[i], blocks[i], (self.links.s ^ a, self.links.f ^ b))
                self.pending.append((j, on, there))

                @pl.when(there)
                def _():
                    copies[i].wait_recv()
                    on.start()

    def came(self, j):
        self.settled.add(j)
        for step, on, there in self.pending:
            if step == j:

                @pl.when(there)
                def _():
                    on.wait_recv()

    def finish(self):
        h, FH = self.h, self.FH
        for j in range(FH - 1):
            if j not in self.settled:
                self.came(j)
        for _, on, there in self.pending:

            @pl.when(there)
            def _():
                on.wait_send()

        for j in range(FH - 1):
            for i in range(len(self.right[j])):

                @pl.when((h >= j) & (h < FH - 1))
                def _():
                    self.right[j][i].wait_send()

                @pl.when((h + j < FH) & (h > 0))
                def _():
                    self.left[j][i].wait_send()


def rows_of(ref):
    return ref[...].reshape(-1, ref.shape[-1])


def rotation(table):
    half = table.shape[-1] // 2
    swapped = pltpu.roll(table, half, 1)
    first = lax.broadcasted_iota(jnp.int32, table.shape, 1) < half
    return jnp.where(first, table, swapped), jnp.where(first, -swapped, table)


def turn(vector, factors):
    return vector * factors[0] + pltpu.roll(vector, vector.shape[-1] // 2, 1) * factors[1]


class RowSum:
    def __init__(self, links, parts, from_core, from_x):
        self.links, self.parts, self.from_core, self.from_x = links, parts, from_core, from_x
        self.x, self.core, self.sent = links.s // 2, links.s % 2, []

    def far(self):
        x, core = 1 - self.x, 1 - self.core
        self.to_far = self.links.start(self.parts.at[x, core], self.from_core.at[x], (1, 0))
        self.sent.append(self.to_far)

    def near(self):
        x, core = self.x, 1 - self.core
        self.to_near = self.links.start(self.parts.at[x, core], self.from_core.at[x], (1, 0))
        self.sent.append(self.to_near)

    def middle(self):
        self.to_far.wait()
        x, core = 1 - self.x, self.core

        def add(rows):
            total = self.parts[x, core, rows].astype(f32) + self.from_core[x, rows].astype(f32)
            self.parts[x, core, rows] = total.astype(bf16)

        row_loop(self.from_x.shape[0], 16, add)
        self.across = self.links.start(self.parts.at[x, core], self.from_x, (2, 0))
        self.sent.append(self.across)

    def arrive(self):
        self.to_near.wait()
        self.across.wait()

    def total(self, rows):
        return (
            self.parts[self.x, self.core, rows].astype(f32)
            + self.from_core[self.x, rows].astype(f32)
            + self.from_x[rows].astype(f32)
        )


class LineSum:
    def __init__(self, links, h, parts, from_core, chain, extra):
        self.links, self.h, self.parts = links, h, parts
        self.from_core, self.chain, self.extra = from_core, chain, extra
        self.core, self.T = links.s % 2, extra.shape[0]
        self.by_core, self.right, self.left, self.end = {}, {}, {}, {}
        s, f = links.s, links.f
        for d in range(Z):
            block = parts.at[d, self.core]
            self.right[d] = links.copy(block, chain.at[d], (s, f + 2))
            self.left[d] = links.copy(block, chain.at[d], (s, f - 2))
            self.end[d] = links.copy(block, extra, (s, f - 2))

    def send_core(self, d):
        self.by_core[d] = self.links.start(
            self.parts.at[d, 1 - self.core], self.from_core.at[d], (1, 0)
        )

    def add(self, d, chained):
        def add(rows):
            total = self.parts[d, self.core, rows].astype(f32)
            total += self.from_core[d, rows].astype(f32)
            if chained:
                total += self.chain[d, rows].astype(f32)
            self.parts[d, self.core, rows] = total.astype(bf16)

        row_loop(self.T, 16, add)

    def stage(self, k, places):
        h = self.h
        for d in places:
            self.by_core[d].wait()
            rightward, leftward = (h < d) & (h == k), (h > d) & (h == Z - 1 - k)

            @pl.when(rightward)
            def _():
                if k:
                    self.right[d].wait_recv()
                self.add(d, k > 0)
                self.right[d].start()

            @pl.when(leftward)
            def _():
                if k:
                    self.left[d].wait_recv()
                self.add(d, k > 0)

            @pl.when(leftward & (h > d + 1))
            def _():
                self.left[d].start()

            @pl.when(leftward & (h == d + 1))
            def _():
                self.end[d].start()

    def arrive(self):
        h = self.h
        for d in range(Z):
            self.by_core[d].wait()
            if d > 0:

                @pl.when(h == d)
                def _():
                    self.right[d].wait_recv()

            else:

                @pl.when(h == 0)
                def _():
                    self.chain[0] = jnp.zeros_like(self.chain[0])

            if d < Z - 1:

                @pl.when(h == d)
                def _():
                    self.end[d].wait_recv()

            else:

                @pl.when(h == Z - 1)
                def _():
                    self.extra[...] = jnp.zeros_like(self.extra)

    def total(self, rows):
        return (
            self.parts[self.h, self.core, rows].astype(f32)
            + self.from_core[self.h, rows].astype(f32)
            + self.chain[self.h, rows].astype(f32)
            + self.extra[rows].astype(f32)
        )

    def settle(self):
        h = self.h
        for d in range(Z):
            self.by_core[d].wait_sent()

            @pl.when(h < d)
            def _():
                self.right[d].wait_send()

            @pl.when(h > d + 1)
            def _():
                self.left[d].wait_send()

            @pl.when(h == d + 1)
            def _():
                self.end[d].wait_send()


class LeadFirst:
    def __init__(self, ref):
        self.ref, self.n, self.rows = ref, ref.shape[0], ref.shape[3]

    def half(self, l):
        return self.ref.at[:, :, l]

    def both(self, w):
        return self.ref.at[:, w]

    def part(self, w, l):
        return self.ref.at[:, w, l]

    def item(self, i, w, l):
        return self.ref.at[i, w, l]

    def got(self, ref, i, w):
        return ref.at[i, w]


class Natural:
    def __init__(self, ref):
        self.ref, self.n, self.rows = ref, ref.shape[2], ref.shape[4]

    def half(self, l):
        return self.ref.at[:, :, :, l]

    def both(self, w):
        return self.ref.at[w % 2, w // 2]

    def part(self, w, l):
        return self.ref.at[w % 2, w // 2, :, l]

    def item(self, i, w, l):
        return self.ref.at[w % 2, w // 2, i, l]

    def got(self, ref, i, w):
        return ref.at[w % 2, w // 2, i]


class PieceByL:
    def __init__(self, links, view, by_l, by_w, w, masks):
        self.links, self.view, self.by_l, self.by_w = links, view, by_l, by_w
        self.w, self.masks, self.l = w, masks, links.f % 2
        self.first = links.start(view.half(1 - self.l), by_l, (0, 1))

    def partial(self, i, w, rows):
        total = self.view.item(i, w, self.l)[rows].astype(f32)
        return total + self.view.got(self.by_l, i, w)[rows].astype(f32)

    def place(self, k, slot=None):
        w = self.w ^ k

        def add(i, rows):
            total = self.partial(i, w, rows)
            if slot is not None:
                total += self.by_w[slot, i, rows].astype(f32)
            self.view.item(i, w, self.l)[rows] = total.astype(bf16)

        block_loop(self.view.n, self.view.rows, 16, add)

    def middle(self):
        self.first.wait()
        self.second = []
        for k in range(1, len(self.masks)):
            self.place(k)
            block = self.view.part(self.w ^ k, self.l)
            self.second.append(self.links.start(block, self.by_w.at[k - 1], self.masks[k]))

    def arrive(self):
        for arrival in self.second:
            arrival.wait()

    def last(self, store=None):
        self.arrive()

        def add(i, rows):
            total = self.partial(i, self.w, rows)
            for k in self.slots():
                total += self.by_w[k, i, rows].astype(f32)
            if store is None:
                self.view.item(i, self.w, self.l)[rows] = total.astype(bf16)
            else:
                store(i, rows, total)

        block_loop(self.view.n, self.view.rows, 16, add)

    def slots(self):
        return range(len(self.masks) - 1)

    def inner(self):
        pass

    def settle(self):
        pass


class PieceAlongZ(PieceByL):
    def __init__(self, links, view, by_l, by_w, w, masks):
        super().__init__(links, view, by_l, by_w, w, masks)
        self.is_inner = (w == 1) | (w == 2)
        device = [(links.s ^ a, links.f ^ b) for a, b in masks]

        def copy(k, slot, to):
            return links.copy(view.part(w ^ k, self.l), by_w.at[slot], device[to])

        self.out = [copy(k, k - 1, 1) for k in (1, 2, 3)]
        self.over = [copy(3, 3, 3), copy(2, 3, 2)]
        self.beside = copy(1, 0, 1)

    def middle(self):
        self.first.wait()

        @pl.when(self.is_inner)
        def _():
            self.place(1)
            self.beside.start()

        @pl.when(jnp.logical_not(self.is_inner))
        def _():
            for k in (2, 3, 1):
                self.place(k)
                self.out[k - 1].start()

    def inner(self):
        @pl.when(self.is_inner)
        def _():
            for k, over in zip((3, 2), self.over):
                self.out[4 - k].wait_recv()
                self.place(k, 4 - k)
                over.start()

    def arrive(self):
        @pl.when(self.is_inner)
        def _():
            self.out[0].wait_recv()
            self.over[0].wait_recv()

        @pl.when(jnp.logical_not(self.is_inner))
        def _():
            self.beside.wait_recv()
            self.over[1].wait_recv()

    def slots(self):
        return (0, 3)

    def settle(self):
        @pl.when(self.is_inner)
        def _():
            for copy in [self.beside] + self.over:
                copy.wait_send()

        @pl.when(jnp.logical_not(self.is_inner))
        def _():
            for copy in self.out:
                copy.wait_send()


def z_piece(links, view, by_l, by_w, w, masks):
    kind = PieceAlongZ if len(masks) == 4 else PieceByL
    return kind(links, view, by_l, by_w, w, masks)


class PieceByW:
    def __init__(self, links, view, by_l, by_w, w, masks):
        self.links, self.view, self.by_l, self.by_w = links, view, by_l, by_w
        self.w, self.masks, self.l = w, masks, links.f % 2
        self.first = [
            links.start(view.both(w ^ k), by_w.at[k - 1], masks[k]) for k in range(1, len(masks))
        ]

    def partial(self, i, l, rows):
        total = self.view.item(i, self.w, l)[rows].astype(f32)
        for k in range(1, len(self.masks)):
            total += self.by_w[k - 1, i, l, rows].astype(f32)
        return total

    def middle(self):
        for arrival in self.first:
            arrival.wait()
        l = 1 - self.l

        def add(i, rows):
            self.view.item(i, self.w, l)[rows] = self.partial(i, l, rows).astype(bf16)

        block_loop(self.view.n, self.view.rows, 16, add)
        self.second = self.links.start(self.view.part(self.w, l), self.by_l, (0, 1))

    def last(self, store=None):
        self.second.wait()

        def add(i, rows):
            total = self.partial(i, self.l, rows) + self.by_l[i, rows].astype(f32)
            if store is None:
                self.view.item(i, self.w, self.l)[rows] = total.astype(bf16)
            else:
                store(i, rows, total)

        block_loop(self.view.n, self.view.rows, 16, add)


def by_l_scratch(n, W, rows, width):
    return [pltpu.VMEM((n, W, rows, width), bf16), pltpu.VMEM((W - 1, n, rows, width), bf16)]


def z_scratch(n, W, rows, width):
    slots = 4 if W == 4 else W - 1
    return [pltpu.VMEM((n, W, rows, width), bf16), pltpu.VMEM((slots, n, rows, width), bf16)]


def by_w_scratch(n, W, rows, width):
    return [pltpu.VMEM((n, rows, width), bf16), pltpu.VMEM((W - 1, n, 2, rows, width), bf16)]


def norm_back(grad_normed, inputs, gain):
    inverse = lax.rsqrt(jnp.mean(inputs * inputs, -1, keepdims=True) + epsilon)
    scaled = grad_normed * gain
    inner_sum = jnp.sum(scaled * inputs, -1, keepdims=True)
    grad = inverse * scaled - inputs * (inverse**3 * inner_sum / inputs.shape[-1])
    return grad, inputs * inverse


def layer_kernel(FH, copies, *refs):
    tok, tab_in, wq_in, wk_in, wv_in, gains_in, wo_in = refs[:7]
    gate_in, up_in, down_in, cot_in, bias = refs[7:12]
    output, keys, values, grad_tokens, gate_out, up_out, down_out = refs[12:19]
    wq_out, wo_out, wk_out, wv_out, gains_out = refs[19:24]
    both_own, normed_kept, side_kept, o_kept = refs[24:28]
    send, recv, here, both, down, q_w, kv_w, o_w = refs[28:36]
    residual, grad_in, gains, gain_sums, grad_row = refs[36:41]
    grad_down, o_sum, kv_sum, q_own = refs[41:45]
    back_bufs, out_bufs = refs[45:49], refs[49:53]
    normed, cot, grad_both, tab, grad_k, grad_v = refs[53:59]
    bufs = refs[59:]
    links = Links(send, recv)
    s, f = links.s, links.f
    x, core = s // 2, s % 2
    e, h, l = f // 8, (f // 2) % Z, f % 2
    t = 2 * h + core
    T, D = residual.shape
    S, F, rows_w, HC = q_w.shape
    row_len, head = grad_k.shape
    heads = HC // head
    E, FC = both.shape[2], both.shape[6] // 2
    W, TG = 2 * E, 2 * Z
    w = 2 * e + x
    two = 2 * T
    cut = D // 4 * 3
    scale = head ** (-0.5)
    group_masks = [(a, 2 * m) for m in range(Z) for a in (0, 1)][1:]
    w_masks = [(2 * (j % 2), 8 * (j // 2)) for j in range(W)]
    back = LineSum(links, h, *back_bufs)
    out = LineSum(links, h, *out_bufs)
    back_parts, out_parts = back.parts, out.parts
    tok_g = grad_row
    spots = {}
    for name, width in (("attended", HC), ("q", HC), ("k", head), ("v", head), ("grad", HC)):
        base = sum(n for _, n in spots.values())
        spots[name] = (base, width)
    side_width = spots["grad"][0]

    def column(name, first=0, width=None):
        base, full_width = spots[name]
        return pl.ds(base + first, width or full_width)

    def block(where, name, r, first=0, width=None):
        return where[r // 2, r % 2, :, column(name, first, width)]

    def to_x(ref, j):
        return ref.at[(w ^ j) % 2, :, (w ^ j) // 2]

    def whole(where, name, first=0, width=None):
        return where[:, :, :, column(name, first, width)].reshape(row_len, -1)

    links.greet(
        [(a, 0) for a in (1, 2, 3)]
        + [(0, 1)]
        + [(0, 2 * k) for k in range(1, FH)]
        + [(1, 2 * m) for m in range(1, Z)]
        + [mask for mask in w_masks if mask[0] and mask[1]]
    )
    local = Local(
        here,
        [
            (wq_in.at[:, pl.ds(pl.multiple_of(s * HC, HC), HC)], q_w.at[s, f]),
            (wk_in, kv_w.at[s, f, :, pl.ds(0, head)]),
            (wv_in, kv_w.at[s, f, :, pl.ds(head, head)]),
            (gains_in, kv_w.at[s, f, :, pl.ds(2 * head, head)]),
            (wo_in, o_w.at[f]),
            (tok, tok_g.at[s]),
            (tab_in, tab.at[s]),
            (down_in, down.at[0, w, l]),
            (cot_in, cot.at[h, core]),
        ],
    )
    first = [
        links.start(
            wq_in.at[:, pl.ds(pl.multiple_of((s ^ a) * HC, HC), HC)], q_w.at[s, f], (a, 0)
        )
        for a in (1, 2, 3)
    ]
    quarter = FC * TG // S
    natural = Local(
        here,
        [
            (r.at[:, pl.ds(i * quarter, quarter)], back_parts.at[i, j, pl.ds(0, rows_w), pl.ds(0, quarter)])
            for j, r in enumerate((gate_in, up_in))
            for i in range(S)
        ],
        9,
    )
    local.wait(1, 2, 3, 4)
    along_z = (f // 2, FH, (0, 1))
    kv_line = Line(links, lambda place: [kv_w.at[s, 2 * place + l]], *along_z)
    o_line = Line(links, lambda place: [o_w.at[2 * place + l]], *along_z)
    q_line = Line(links, lambda place: [q_w.at[:, 2 * place + l]], *along_z)
    kv_line.step(0)
    kv_y = links.pass_on(kv_w.at[s, f], (0, 1))
    o_line.step(0)
    needed = [links.pass_on(o_w.at[f], (0, 1))]
    local.wait(0)
    for arrival in first:
        arrival.wait()
    q_line.step(0)
    needed.append(links.pass_on(q_w.at[:, f], (0, 1)))
    tok_x = links.start(tok, tok_g.at[s], (2, 0))
    needed.append(links.start(tok, tok_g.at[s], (1, 0)))
    needed += [links.start(tab_in, tab.at[s], (a, 0)) for a in (1, 2, 3)]
    ffn_in = {}
    lanes = 128
    whole_tiles = FC // lanes

    def blocks_of(ref, at_h, c):
        width = 2 * FC // W // 2
        parts = []
        for at_e in range(E):
            for at_x in (0, 1):
                base = (at_e * Z + at_h) * width
                parts.append(ref(2 * at_x + c)[:, base : base + width])
        return jnp.concatenate(parts, 1)

    def side_by_side(gate_units, up_units):
        tiles = []
        for j in range(whole_tiles):
            part = slice(j * lanes, (j + 1) * lanes)
            tiles += [gate_units[:, part], up_units[:, part]]
        rest = slice(whole_tiles * lanes, FC)
        return jnp.concatenate(tiles + [gate_units[:, rest], up_units[:, rest]], 1)

    def sent_blocks(at_h, c):
        return grad_both.at[at_h, pl.ds(pl.multiple_of(c * rows_w, rows_w), rows_w)]

    natural.wait()
    columns_of = [
        [back_parts[i, j, :rows_w, :quarter].astype(f32) for i in range(S)] for j in (0, 1)
    ]
    for at_h in range(Z):
        for c in (0, 1):
            units = [blocks_of(lambda i: columns_of[j][i], at_h, c) for j in (0, 1)]
            grad_both[at_h, c * rows_w : (c + 1) * rows_w] = side_by_side(*units).astype(bf16)
    own_block = Local(here, [(sent_blocks(h, core), both.at[x, core, e, h, l])], 17)

    def to_group(m):
        for a in (0, 1):
            if (a, m) != (0, 0):
                place = (x, core, e, h, l)
                source = sent_blocks(h ^ m, core ^ a)
                ffn_in[a, m] = links.start(source, both.at[place], (a, 2 * m))

    arriving = []

    class Spread:
        def __init__(self, near, second_w, second_y):
            self.near, self.second_w, self.second_y = near, second_w, second_y

        def by_w(self):
            self.came_w = [links.pass_on(self.near, mask) for mask in w_masks[1:]]

        def by_y(self):
            self.came_y = links.pass_on(self.near, (0, 1))

        def on_w(self):
            self.came_y.wait()
            arriving.extend(links.pass_on(self.second_w, mask) for mask in w_masks[1:])

        def on_y(self):
            for j, arrival in enumerate(self.came_w):
                arrival.wait()
                arriving.append(links.pass_on(self.second_y(j + 1), (0, 1)))

    def spread_of(m):
        def second_y(j):
            return to_x(both, j).at[0, h ^ m, l]

        here_q = to_x(both, 0)
        return Spread(here_q.at[:, h ^ m, l], here_q.at[1, h ^ m, 1 - l], second_y)

    low_half, high_half = pl.ds(0, cut), pl.ds(cut, D - cut)
    spread_down = Spread(
        down.at[0, w, l],
        down.at[0, w, 1 - l, :, high_half],
        lambda j: down.at[0, w ^ j, l, :, low_half],
    )
    to_group(0)
    local.wait(7)
    spread_down.by_w()
    for j in range(FH - 1):
        for way in (kv_line, o_line, q_line):
            way.arrived(j)
            if j + 1 < FH - 1:
                way.step(j + 1)
        if j == 0:
            tok_x.wait()
            needed.append(links.pass_on(tok_g.at[s ^ 2], (1, 0)))
            own_block.wait()
            ffn_in[1, 0].wait()
            spreads = [spread_of(m) for m in range(Z)]
            spreads[0].by_w()
    kv_y.wait()
    kv_line.finish()
    kv_x = links.pass_on(kv_w.at[s], (2, 0))
    needed.append(links.pass_on(kv_w.at[s], (1, 0)))
    for m in range(1, Z):
        to_group(m)
    spread_down.by_y()
    spreads[0].by_y()
    cot_line = Line(links, lambda place: [cot.at[place, core]], h, Z, (1, 0))
    kv_x.wait()
    needed.append(links.pass_on(kv_w.at[s ^ 2], (1, 0)))
    for arrival in needed:
        arrival.wait()
    o_line.finish()
    q_line.finish()
    local.wait(5, 6)
    kept_o = Local(here, [(o_w, o_kept)], 18)

    normed_one, side = out_parts.at[pl.ds(0, 2)], out_parts.at[pl.ds(2, 2)]
    place = lax.broadcasted_iota(jnp.int32, (8, head), 0)
    lane = lax.broadcasted_iota(jnp.int32, (8, head), 1)
    pick = (place == lane).astype(bf16)
    kv_full = rows_of(kv_w)
    gains[...] = contract_last(pick, kv_full[:, 2 * head :])

    def norm_one(i, rows):
        value = tok_g[i, rows].astype(f32)
        inverse = lax.rsqrt(jnp.mean(value * value, -1, keepdims=True) + epsilon)
        normed_one[i // 2, lax.rem(i, 2), rows] = (value * inverse * gains[0:1]).astype(bf16)

    block_loop(S, T, 16, norm_one)
    local.wait(8)
    cot_line.step(0)
    arriving.append(links.pass_on(cot.at[h, core], (1, 0)))
    factors = rotation(rows_of(tab))

    def put(name, first, value):
        columns = column(name, first, value.shape[1])
        side[:, :, :, columns] = value.astype(bf16).reshape(2, 2, T, -1)

    kv = dot(rows_of(normed_one), kv_full[:, : 2 * head])
    put("k", 0, turn(kv[:, :head], factors))
    put("v", 0, kv[:, head:])
    for n in range(0, heads, 2):
        columns = slice(n * head, (n + 2) * head)
        pair = dot(rows_of(normed_one), q_w[:, :, :, columns].reshape(D, 2 * head))
        for j in (0, 1):
            put("q", (n + j) * head, turn(pair[:, j * head : (j + 1) * head], factors))
    results = [
        Local(
            here,
            [
                (side.at[x, core, :, column("k")], keys),
                (side.at[x, core, :, column("v")], values),
            ],
            21,
        )
    ]
    for r in range(S):
        rows, seen = slice(r * T, (r + 1) * T), slice(0, (r + 1) * T)
        keys_seen, values_seen = whole(side, "k")[seen], whole(side, "v")[seen]
        for n in range(heads):
            query = block(side, "q", r, n * head, head)
            scores = contract_last(query, keys_seen) * scale + bias[rows, seen].astype(f32)
            scores = jnp.exp(scores - jnp.max(scores, -1, keepdims=True))
            probs = (scores / jnp.sum(scores, -1, keepdims=True)).astype(bf16)
            side[r // 2, r % 2, :, column("attended", n * head, head)] = dot(
                probs, values_seen
            ).astype(bf16)
    spread_down.on_y()
    spread_down.on_w()

    first_two = pl.ds(0, 2)
    row_bufs = (back_parts.at[first_two], back.from_core.at[first_two], back.chain.at[0])
    parts = RowSum(links, *row_bufs)

    def project(x_to):
        rows = side[x_to, :, :, column("attended")].reshape(two, HC)
        for n in range(0, D, HC):
            columns = slice(n, n + HC)
            total = dot(rows, o_w[:, :, columns].reshape(HC, HC))
            parts.parts[x_to, :, :, columns] = total.astype(bf16).reshape(2, T, HC)

    project(1 - x)
    parts.far()
    project(x)
    parts.near()
    parts.middle()
    spreads[0].on_y()
    spreads[0].on_w()
    for m in range(1, Z):
        for a in (0, 1):
            ffn_in[a, m].wait()
        spreads[m].by_y()
        spreads[m].by_w()
    cot_line.arrived(0)
    cot_line.step(1)
    kept = Local(
        here, [(normed_one, normed_kept), (side.at[:, :, :, pl.ds(0, side_width)], side_kept)], 19
    )
    parts.arrive()

    def norm_two(rows):
        total = tok_g[s, rows].astype(f32) + parts.total(rows)
        residual[rows] = total
        inverse = lax.rsqrt(jnp.mean(total * total, -1, keepdims=True) + epsilon)
        normed[h, core, rows] = (total * inverse * gains[1:2]).astype(bf16)

    row_loop(T, 16, norm_two)
    normed_line = Line(links, lambda place: [normed.at[place, core]], h, Z, (1, 0))
    normed_line.step(0)
    beside = [links.pass_on(normed.at[h, core], (1, 0))]
    cot_line.arrived(1)
    cot_line.step(2)
    spreads[1].on_y()
    spreads[1].on_w()
    normed_line.arrived(0)
    normed_line.step(1)
    for m in range(2, Z):
        spreads[m].on_y()
        spreads[m].on_w()
    results[0].wait()
    kept_o.wait()
    kept.wait()
    for arrival in arriving:
        arrival.wait()
    for arrival in links.sent:
        arrival.wait_sent()

    slot = D // 2
    lane_is_low = lax.broadcasted_iota(jnp.int32, (two, lanes), 1) < lanes // 2

    def hidden_of(d):
        n = normed[d].reshape(two, D)
        c = cot[d].reshape(two, D)
        weights = down[...].reshape(FC, D)

        def units(first, width, gate_proj, up_proj, grad_inner):
            sig = jax.nn.sigmoid(gate_proj)
            silu = gate_proj * sig
            spot = pl.ds(pl.multiple_of(d // 2 * slot + first, lanes), width)
            hidden = (silu * up_proj).astype(bf16)[:, :width]
            o_w[pl.ds(d % 2 * (F // 2), F // 2), :, spot] = hidden.reshape(F // 2, rows_w, width)
            slope = sig * (1.0 + gate_proj * (1.0 - sig))
            return (grad_inner * up_proj * slope).astype(bf16), (grad_inner * silu).astype(bf16)

        for first in range(0, FC, 2 * lanes):
            width = min(2 * lanes, FC - first)
            rows = weights[first : first + width]
            if width % lanes:
                rows = jnp.concatenate([rows, rows[width - lanes // 2 :]], 0)
            grad_inner = contract_last(c, rows)
            for i in range(0, width, lanes):
                base = 2 * (first + i)
                columns = (slice(None),) * 6 + (slice(base, min(base + 2 * lanes, 2 * FC)),)
                proj = dot(n, both[columns].reshape(D, -1))
                part = slice(i, i + lanes)
                if i + lanes <= width:
                    grad_gate, grad_up = units(
                        first + i,
                        lanes,
                        proj[:, :lanes],
                        proj[:, lanes:],
                        grad_inner[:, part],
                    )
                    grad_both[d, :, base : base + lanes] = grad_gate
                    grad_both[d, :, base + lanes : base + 2 * lanes] = grad_up
                else:
                    mixed = proj
                    turned = pltpu.roll(mixed, lanes // 2, 1)
                    grad_gate, grad_up = units(
                        first + i,
                        lanes // 2,
                        jnp.where(lane_is_low, mixed, turned),
                        jnp.where(lane_is_low, turned, mixed),
                        grad_inner[:, part],
                    )
                    grad_both[d, :, base : base + lanes] = jnp.where(
                        lane_is_low, grad_gate, grad_up
                    )

    def back_of(d):
        for i in range(S):
            columns = slice(i * F * rows_w, (i + 1) * F * rows_w)
            total = contract_last(grad_both[d], both[i // 2, i % 2].reshape(-1, 2 * FC))
            back_parts[d, :, :, columns] = total.astype(bf16).reshape(2, T, -1)
        back.send_core(d)

    def out_of(d):
        spot = slice(d // 2 * slot, d // 2 * slot + FC)
        hidden = o_w[pl.ds(d % 2 * (F // 2), F // 2), :, spot].reshape(two, FC)
        for i in range(0, D, 512):
            columns = slice(i, i + 512)
            total = dot(hidden, down[:, :, :, :, columns].reshape(FC, 512))
            out_parts[d, :, :, columns] = total.astype(bf16).reshape(2, T, -1)
        out.send_core(d)

    for arrival in beside:
        arrival.wait()
    hidden_of(h)
    for line in (cot_line, normed_line):
        line.came(0)
    hidden_of(h ^ 1)
    normed_line.arrived(1)
    normed_line.step(2)
    for line in (cot_line, normed_line):
        line.came(1)
    hidden_of(h ^ 2)
    for line in (cot_line, normed_line):
        line.arrived(2)
    for line in (cot_line, normed_line):
        line.came(2)
    hidden_of(h ^ 3)
    back_of(3)
    back_of(0)
    back.stage(0, (3, 0))
    back_of(2)
    back_of(1)
    back.stage(0, (2, 1))
    for line in (cot_line, normed_line):
        line.finish()
    for d in (3, 0, 2, 1):
        out_of(d)
    ffn = {}
    width = F * rows_w
    for c in (0, 1):
        for i in (0, 1):
            base = (2 * i + c) * width
            turned = normed[:, :, :, base : base + width].reshape(4 * two, width)
            for columns in [slice(n, min(n + 3 * lanes, 2 * FC)) for n in range(0, 2 * FC, 3 * lanes)]:
                total = contract_first(turned, grad_both[:, :, columns].reshape(4 * two, -1))
                both[i, c, :, :, :, :, columns] = total.astype(bf16).reshape(E, Z, 2, rows_w, -1)
        if c == 0:
            ffn["both", 0] = PieceByL(links, Natural(both.at[:, 0]), *bufs[4:6], w, w_masks)
            back.stage(1, (3, 0))
    ffn["both", 1] = PieceByL(
        links, Natural(both.at[:, 1, :, first_two]), *bufs[6:8], w, w_masks
    )
    ffn["both", 2] = PieceByW(
        links, Natural(both.at[:, 1, :, pl.ds(2, 2)]), *bufs[8:10], w, w_masks
    )
    inner = [o_w[:, :, i * slot : i * slot + FC].reshape(2 * two, FC) for i in (0, 1)]
    for i in range(0, D, 256):
        columns = slice(i, i + 256)
        total = contract_first(inner[0], cot[0:2, :, :, columns].reshape(2 * two, 256))
        total += contract_first(inner[1], cot[2:4, :, :, columns].reshape(2 * two, 256))
        down[:, :, :, :, columns] = total.astype(bf16).reshape(1, W, 2, -1, 256)
        if i + 256 == cut:
            ffn["down_low"] = PieceByL(
                links, LeadFirst(down.at[:, :, :, :, low_half]), *bufs[0:2], w, w_masks
            )
    ffn["down_high"] = PieceByW(
        links, LeadFirst(down.at[:, :, :, :, high_half]), *bufs[2:4], w, w_masks
    )
    back.stage(1, (2, 1))
    back.stage(2, (3, 0))
    out.stage(0, (3, 0, 2, 1))

    cot_own, tok_own = normed.at[2, 0], normed.at[2, 1]
    own = Local(here, [(cot_in, cot_own), (tok, tok_own)], 23)
    gain_sums[...] = jnp.zeros_like(gain_sums)
    own.wait()
    back.arrive()

    def second_norm(rows):
        grad_normed = back.total(rows)
        grad, unit = norm_back(grad_normed, residual[rows], gains[1:2])
        grad = grad + cot_own[rows].astype(f32)
        grad_in[rows] = grad
        grad_row[s, rows] = grad.astype(bf16)
        gain_sums[1:2] += jnp.sum(grad_normed * unit, 0, keepdims=True)

    row_loop(T, 16, second_norm)
    row_x = links.pass_on(grad_row.at[s], (3, 0))
    row_c = links.pass_on(grad_row.at[s], (1, 0))

    last_two = pl.ds(2, 2)
    side = cot.at[first_two]
    normed_one = normed.at[first_two]
    grad_side = cot.at[last_two]
    loads = Local(
        here,
        [
            (o_kept, o_w),
            (side_kept, cot.at[first_two, :, :, pl.ds(0, side_width)]),
            (normed_kept, normed_one),
        ],
        25,
    )
    ffn["both", 2].middle()
    ffn["both", 0].middle()
    ffn["down_high"].middle()
    row_x.wait()
    row_cc = links.pass_on(grad_row.at[s ^ 3], (1, 0))
    out.stage(1, (3, 0, 2, 1))
    row_c.wait()
    row_cc.wait()
    loads.wait()
    per = 2 * head // rows_w
    for n in range(0, heads, 2):
        wo = o_w[n // 2 * per : (n // 2 + 1) * per].reshape(2 * head, D)
        pair = contract_last(rows_of(grad_row), wo).astype(bf16)
        side[:, :, :, column("grad", n * head, 2 * head)] = pair.reshape(2, 2, T, 2 * head)
    for i in range(0, D, HC):
        columns = slice(i, i + HC)
        grad_columns = grad_row[:, :, columns].reshape(row_len, HC)
        total = contract_first(whole(side, "attended"), grad_columns)
        o_w[:, :, columns] = total.astype(bf16).reshape(F, rows_w, HC)
    place_z, z_masks = f // 2, [(0, 2 * j) for j in range(FH)]
    o_view = LeadFirst(o_w.reshape(1, FH, 2, rows_w, D))
    o_piece = z_piece(links, o_view, *bufs[10:12], place_z, z_masks)
    ffn["both", 1].middle()
    grad_k[...] = jnp.zeros_like(grad_k)
    grad_v[...] = jnp.zeros_like(grad_v)
    factors = rotation(rows_of(tab))
    back_turn = (factors[0], -factors[1])
    for r in range(S):
        rows, seen = slice(r * T, (r + 1) * T), slice(0, (r + 1) * T)
        keys_seen, values_seen = whole(side, "k")[seen], whole(side, "v")[seen]
        for n in range(heads):
            query = block(side, "q", r, n * head, head)
            grad_att = block(side, "grad", r, n * head, head)
            scores = contract_last(query, keys_seen) * scale + bias[rows, seen].astype(f32)
            scores = jnp.exp(scores - jnp.max(scores, -1, keepdims=True))
            probs = scores / jnp.sum(scores, -1, keepdims=True)
            grad_probs = contract_last(grad_att, values_seen)
            delta = jnp.sum(probs * grad_probs, -1, keepdims=True)
            grad_scores = (probs * (grad_probs - delta)).astype(bf16)
            grad_q = dot(grad_scores, keys_seen) * scale
            grad_q = turn(grad_q, (back_turn[0][rows], back_turn[1][rows])).astype(bf16)
            grad_side[r // 2, r % 2, :, n * head : (n + 1) * head] = grad_q
            grad_k[seen] += contract_first(grad_scores, query)
            grad_v[seen] += contract_first(probs.astype(bf16), grad_att)
    grad_key = turn(grad_k[...] * scale, back_turn).astype(bf16)
    grad_side[:, :, :, HC : HC + head] = grad_key.reshape(2, 2, T, head)
    grad_side[:, :, :, HC + head : HC + 2 * head] = grad_v[...].astype(bf16).reshape(2, 2, T, head)
    grad_qkv = slice(0, HC + 2 * head)
    back.settle()
    row = RowSum(links, *row_bufs)
    for cx, go in ((1 - x, row.far), (x, row.near)):
        for i in range(S):
            total = contract_last(grad_side[cx, :, :, :HC].reshape(two, HC), q_w[i].reshape(-1, HC))
            total += contract_last(
                grad_side[cx, :, :, HC : HC + 2 * head].reshape(two, 2 * head),
                kv_w[i, :, :, : 2 * head].reshape(-1, 2 * head),
            )
            columns = slice(i * F * rows_w, (i + 1) * F * rows_w)
            row.parts[cx, :, :, columns] = total.astype(bf16).reshape(2, T, -1)
        go()
    row.middle()
    for i in range(3):
        ffn["both", i].last()
    owners = [
        links.start(both.at[x, core ^ a, e, h ^ (b // 2), l], both_own.at[t], (a, b))
        for a, b in group_masks
    ]
    mine = Local(here, [(both.at[x, core, e, h, l], both_own.at[t])], 28)
    out.stage(2, (3, 0))
    pieces = []
    q_view = q_w.reshape(S, FH, 2, rows_w, HC)
    kv_view = kv_w.reshape(S, FH, 2, rows_w, kv_w.shape[3])
    for i in range(S):
        columns = slice(i * F * rows_w, (i + 1) * F * rows_w)
        turned = normed_one[:, :, :, columns].reshape(row_len, -1)
        total = contract_first(turned, grad_side[:, :, :, grad_qkv].reshape(row_len, -1))
        total = total.astype(bf16)
        q_w[i] = total[:, :HC].reshape(F, rows_w, HC)
        kv_w[i, :, :, : 2 * head] = total[:, HC:].reshape(F, rows_w, 2 * head)
        one = pl.ds(i, 1)
        spare = (bufs[12].at[one], bufs[13].at[:, one])
        pieces.append(z_piece(links, LeadFirst(q_view.at[one]), *spare, place_z, z_masks))
    ffn["down_low"].middle()
    row.arrive()

    def first_norm(rows):
        grad_normed = row.total(rows)
        grad, unit = norm_back(grad_normed, tok_own[rows].astype(f32), gains[0:1])
        grad_in[rows] += grad
        gain_sums[0:1] += jnp.sum(grad_normed * unit, 0, keepdims=True)

    row_loop(T, 16, first_norm)
    results = [Local(here, [(grad_in, grad_tokens)], 29)]
    pick = jnp.where((place == lane) & (place < 2), 1.0, 0.0)
    columns = contract_first(gain_sums[...], pick).astype(bf16)
    kv_w[:, :, :, 2 * head :] = columns.reshape(S, F, rows_w, head)
    kv_row = RowSum(links, kv_w.reshape(2, 2, F * rows_w, kv_w.shape[3]), *bufs[14:16])
    kv_row.far()
    kv_row.near()
    kv_row.middle()
    o_piece.middle()
    pieces[0].middle()
    o_piece.inner()
    kv_row.arrive()

    def keep_kv(rows):
        kv_row.parts[x, core, rows] = kv_row.total(rows).astype(bf16)

    row_loop(F * rows_w, 16, keep_kv)
    kv_mine = LeadFirst(kv_view.at[pl.ds(s, 1)])
    kv_piece = z_piece(links, kv_mine, *bufs[16:18], place_z, z_masks)
    for i in range(1, S):
        pieces[i].middle()
        pieces[i - 1].inner()
    kv_piece.middle()
    pieces[S - 1].inner()

    def store_down(base):
        def store(i, rows, total):
            grad_down[rows, base : base + total.shape[1]] = total

        return store

    kv_piece.inner()
    ffn["down_low"].last(store_down(0))
    ffn["down_high"].last(store_down(cut))
    results.append(Local(here, [(grad_down, down_out)], 30))

    def store_o(i, rows, total):
        o_sum[rows] = total

    o_piece.last(store_o)
    results.append(Local(here, [(o_sum, wo_out)], 31))
    out.arrive()

    out_rows = back_parts.at[3, 0]

    def finish_output(rows):
        out_rows[rows] = (residual[rows] + out.total(rows)).astype(bf16)

    row_loop(T, 16, finish_output)
    results.append(Local(here, [(out_rows, output)], 32))
    grad_own = grad_both.reshape(Z, two // rows_w, rows_w, 2 * FC)
    for arrival in owners:
        arrival.wait()
    mine.wait()
    came = Local(
        here, [(both_own.at[pl.ds(2 * i, 2)], grad_own.at[i, pl.ds(0, 2)]) for i in range(Z)], 33
    )
    came.wait()
    results[0].wait()
    stores = [
        r.at[pl.ds(j * rows_w, rows_w), pl.ds(0, quarter)]
        for r in (residual, grad_in)
        for j in (0, 1)
    ]
    leaving = [None] * len(stores)
    count = 0
    for i, target in enumerate((gate_out, up_out)):
        units = []
        for at_h in range(Z):
            for c in (0, 1):
                block = grad_own[at_h, c].astype(f32)
                tiles = [
                    block[:, (2 * j + i) * lanes : (2 * j + i + 1) * lanes]
                    for j in range(whole_tiles)
                ]
                base = 2 * whole_tiles * lanes + i * (FC - whole_tiles * lanes)
                tiles.append(block[:, base : base + FC - whole_tiles * lanes])
                units.append(jnp.concatenate(tiles, 1))
        width = FC // W
        for at_x in (0, 1):
            for c in (0, 1):
                parts = [
                    units[2 * at_h + c][:, (2 * at_e + at_x) * width : (2 * at_e + at_x + 1) * width]
                    for at_e in range(E)
                    for at_h in range(Z)
                ]
                slot_now = count % len(stores)
                if leaving[slot_now] is not None:
                    leaving[slot_now].wait()
                stores[slot_now][...] = jnp.concatenate(parts, 1)
                columns = pl.ds((2 * at_x + c) * quarter, quarter)
                leaving[slot_now] = Local(
                    here, [(stores[slot_now], target.at[:, columns])], 37 + slot_now
                )
                count += 1
    for piece in pieces:
        piece.last()
    for a in (1, 2, 3):
        links.start(q_view.at[s ^ a, place_z, l], q_own.at[s], (a, 0))
    q_own[s] = q_view[s, place_z, l]
    q_came = links.sent[-3:]

    def store_kv(i, rows, total):
        kv_sum[rows] = total

    kv_piece.last(store_kv)
    names = (wk_out, wv_out, gains_out)
    results.append(
        Local(here, [(kv_sum.at[:, pl.ds(i * head, head)], r) for i, r in enumerate(names)], 41)
    )
    for arrival in q_came:
        arrival.wait()
    for i in leaving:
        i.wait()
    q_rows = residual.at[pl.ds(0, rows_w)]
    for i in range(S):
        q_rows[:, i * HC : (i + 1) * HC] = q_own[i].astype(f32)
    results.append(Local(here, [(q_rows, wq_out)], 44))
    out.settle()
    for piece in [o_piece, kv_piece] + pieces:
        piece.settle()
    links.finish()
    assert links.count == copies, links.count
    for result in results[1:]:
        result.wait()


def hand_over_kernel(n, *refs):
    inputs, outputs, rooms, sems = refs[:n], refs[n : 2 * n], refs[2 * n : 3 * n], refs[3 * n]
    loads = [pltpu.make_async_copy(inputs[i], rooms[i], sems.at[i]) for i in range(n)]
    stores = [pltpu.make_async_copy(rooms[i], outputs[i], sems.at[n + i]) for i in range(n)]
    for load in loads:
        load.start()
    for load, store in zip(loads, stores):
        load.wait()
        store.start()
    for store in stores:
        store.wait()


def hand_over(arrays):
    n = len(arrays)
    anywhere = [pl.BlockSpec(memory_space=pl.ANY)] * n
    return pl.pallas_call(
        functools.partial(hand_over_kernel, n),
        out_shape=[shape(a.shape, a.dtype) for a in arrays],
        in_specs=anywhere,
        out_specs=anywhere,
        scratch_shapes=[pltpu.VMEM(a.shape, a.dtype) for a in arrays]
        + [pltpu.SemaphoreType.DMA((2 * n,))],
        compiler_params=pltpu.CompilerParams(vmem_limit_bytes=VMEM_LIMIT),
    )(*arrays)


def angle_tables(position_row, head_size):
    half_head = head_size // 2
    frequency = 10000.0 ** (-jnp.arange(half_head, dtype=f32) * 2.0 / head_size)
    phase_angle = position_row.astype(f32)[:, None] * frequency[None, :]
    return (jnp.cos(phase_angle), jnp.sin(phase_angle))


def per_device(
    S,
    F,
    tokens,
    segments,
    positions,
    gain_one,
    w_query,
    w_key,
    w_value,
    w_out,
    gain_two,
    w_gate,
    w_up,
    w_down,
    cotangent,
):
    T, D = tokens.shape[1:]
    head = w_key.shape[1]
    row_len = segments.shape[1]
    rows = w_query.shape[0]
    down_rows = w_down.shape[0]
    FF = w_gate.shape[1]
    FH, E = F // 2, F // 8
    W, TG = 2 * E, 2 * Z
    HC = w_query.shape[1] // S
    heads = HC // head
    FC = FF // TG

    gains = jnp.stack([gain_one, gain_two], 1)
    gains = jnp.concatenate([gains, jnp.zeros((rows, head - 2), bf16)], 1)
    KV = 3 * head
    table = jnp.concatenate(angle_tables(positions[0], head), 1)
    segment = segments[0]
    index = jnp.arange(row_len)
    allowed = (index[None, :] <= index[:, None]) & (segment[None, :] == segment[:, None])
    bias = jnp.where(allowed, 0.0, -1e30).astype(bf16)
    group = [pltpu.VMEM((Z, 2, T, D), bf16), pltpu.VMEM((Z, T, D), bf16)]
    group += [pltpu.VMEM((Z, T, D), bf16), pltpu.VMEM((T, D), bf16)]
    weight = pltpu.VMEM((2, 2, E, Z, 2, rows, 2 * FC), bf16)

    def natural_by_l(n):
        block = (n, rows, 2 * FC)
        return [pltpu.VMEM((2, E, *block), bf16), pltpu.VMEM((W - 1, *block), bf16)]

    outs = [
        ((T, D), bf16),
        ((T, head), bf16),
        ((T, head), bf16),
        ((T, D), f32),
        ((rows, FF), f32),
        ((rows, FF), f32),
        ((down_rows, D), f32),
        ((rows, D), f32),
        ((rows, D), f32),
        ((rows, head), f32),
        ((rows, head), f32),
        ((rows, head), f32),
        ((TG, rows, 2 * FC), bf16),
        ((2, 2, T, D), bf16),
        ((2, 2, T, 2 * HC + 2 * head), bf16),
        ((F, rows, D), bf16),
    ]
    copies = 112 + 12 * (FH - 1) + 20 * (W - 1) + 6 * (1 + (6 if FH == 4 else FH - 1))
    results = communicate(
        functools.partial(layer_kernel, FH, copies),
        (
            tokens[0],
            table,
            w_query,
            w_key,
            w_value,
            gains,
            w_out,
            w_gate,
            w_up,
            w_down,
            cotangent[0],
            bias,
        ),
        [shape(dims, kind) for dims, kind in outs],
        copies,
        0,
        in_vmem=[False] * 11 + [True],
        kept=45,
        scratch=[
            weight,
            pltpu.VMEM((1, W, 2, down_rows, D), bf16),
            pltpu.VMEM((S, F, rows, HC), bf16),
            pltpu.VMEM((S, F, rows, KV), bf16),
            pltpu.VMEM((F, rows, D), bf16),
            pltpu.VMEM((T, D), f32),
            pltpu.VMEM((T, D), f32),
            pltpu.VMEM((8, D), f32),
            pltpu.VMEM((8, D), f32),
            pltpu.VMEM((S, T, D), bf16),
            pltpu.VMEM((down_rows, D), f32),
            pltpu.VMEM((rows, D), f32),
            pltpu.VMEM((rows, KV), f32),
            pltpu.VMEM((S, rows, HC), bf16),
            *group,
            *group,
            pltpu.VMEM((Z, 2, T, D), bf16),
            pltpu.VMEM((Z, 2, T, D), bf16),
            pltpu.VMEM((Z, 2 * T, 2 * FC), bf16),
            pltpu.VMEM((S, T, head), f32),
            pltpu.VMEM((row_len, head), f32),
            pltpu.VMEM((row_len, head), f32),
            *by_l_scratch(1, W, down_rows, D // 4 * 3),
            *by_w_scratch(1, W, down_rows, D // 4),
            *natural_by_l(Z),
            *natural_by_l(2),
            *by_w_scratch(2, W, rows, 2 * FC),
            *z_scratch(1, FH, rows, D),
            *z_scratch(S, FH, rows, HC),
            pltpu.VMEM((2, F * rows, KV), bf16),
            pltpu.VMEM((F * rows, KV), bf16),
            *z_scratch(1, FH, rows, KV),
        ],
    )
    output, keys, values, grad_tokens, gate, up, down, query, out, key, value, gains = hand_over(
        results[:12]
    )
    return (
        output[None],
        keys[None],
        values[None],
        grad_tokens[None],
        gains[:, 0],
        query,
        key,
        value,
        out,
        gains[:, 1],
        gate,
        up,
        down,
    )


def solution(mesh):
    token_spec = P("fsdp", "seq", None)
    flat, matrix = P(("seq", "fsdp")), P(("seq", "fsdp"), None)
    return jax.shard_map(
        functools.partial(per_device, mesh.shape["seq"], mesh.shape["fsdp"]),
        mesh=mesh,
        in_specs=(
            token_spec,
            P("fsdp", None),
            P("fsdp", "seq"),
            flat,
            matrix,
            matrix,
            matrix,
            matrix,
            flat,
            matrix,
            matrix,
            matrix,
            token_spec,
        ),
        out_specs=(
            token_spec,
            token_spec,
            token_spec,
            token_spec,
            flat,
            matrix,
            matrix,
            matrix,
            matrix,
            flat,
            matrix,
            matrix,
            matrix,
        ),
        check_vma=False,
    )
```

```python
import functools

import jax
import jax.numpy as jnp
from jax import lax
from jax.experimental import pallas as pl
from jax.experimental.pallas import tpu as pltpu
from jax.sharding import PartitionSpec as P

epsilon = 1e-05
MESH = pl.DeviceIdType.MESH
Z = 4
VMEM_LIMIT = 64 * 2**20 - 2**18
bf16 = jnp.bfloat16
f32 = jnp.float32


def dot(left, right):
    return jnp.dot(left, right, preferred_element_type=f32)


def contract_last(left, right):
    return lax.dot_general(left, right, (((1,), (1,)), ((), ())), preferred_element_type=f32)


def contract_first(left, right):
    return lax.dot_general(left, right, (((0,), (0,)), ((), ())), preferred_element_type=f32)


class Arrival:
    def __init__(self, copy):
        self.copy, self.waited, self.left = copy, False, False

    def wait(self):
        if not self.waited:
            self.waited = True
            self.copy.wait_recv()

    def wait_sent(self):
        if not self.left:
            self.left = True
            self.copy.wait_send()


class Links:
    def __init__(self, send, recv):
        self.send, self.recv, self.sent, self.count = send, recv, [], 0
        self.s, self.f = lax.axis_index("seq"), lax.axis_index("fsdp")

    def greet(self, masks):
        barrier = pltpu.get_barrier_semaphore()
        for a, b in masks:
            pl.semaphore_signal(
                barrier, inc=1, device_id=(self.s ^ a, self.f ^ b), device_id_type=MESH
            )
        pl.semaphore_wait(barrier, len(masks))

    def copy(self, source, target, device):
        self.count += 1
        return pltpu.make_async_remote_copy(
            src_ref=source,
            dst_ref=target,
            send_sem=self.send.at[self.count - 1],
            recv_sem=self.recv.at[self.count - 1],
            device_id=device,
            device_id_type=MESH,
        )

    def start(self, source, target, mask):
        copy = self.copy(source, target, (self.s ^ mask[0], self.f ^ mask[1]))
        copy.start()
        self.sent.append(Arrival(copy))
        return self.sent[-1]

    def pass_on(self, block, mask):
        return self.start(block, block, mask)

    def finish(self):
        for arrival in self.sent:
            arrival.wait()
        for arrival in self.sent:
            arrival.wait_sent()


class Local:
    def __init__(self, sems, pairs, base=0):
        self.copies = [
            pltpu.make_async_copy(a, b, sems.at[base + i]) for i, (a, b) in enumerate(pairs)
        ]
        self.open = set(range(len(pairs)))
        for copy in self.copies:
            copy.start()

    def wait(self, *which):
        for i in which or sorted(self.open):
            self.open.discard(i)
            self.copies[i].wait()


def row_loop(rows, step, body):
    block_loop(1, rows, step, lambda i, part: body(part))


def block_loop(n, rows, step, body):
    if rows % step:
        for i in range(n):
            body(i, slice(0, rows))
        return
    steps = rows // step

    @pl.loop(0, n * steps)
    def _(k):
        body(k // steps, pl.ds(pl.multiple_of(lax.rem(k, steps) * step, step), step))


def communicate(
    body, args, outs, copies, collective_id, in_vmem=False, out_vmem=False, scratch=(), kept=1
):
    def specs(inside, n):
        inside = [inside] * n if isinstance(inside, bool) else inside
        return [pl.BlockSpec(memory_space=pltpu.VMEM if i else pl.ANY) for i in inside]

    return pl.pallas_call(
        body,
        out_shape=outs,
        in_specs=specs(in_vmem, len(args)),
        out_specs=specs(out_vmem, len(outs)),
        scratch_shapes=[
            pltpu.SemaphoreType.DMA((copies,)),
            pltpu.SemaphoreType.DMA((copies,)),
            pltpu.SemaphoreType.DMA((kept,)),
            *scratch,
        ],
        compiler_params=pltpu.CompilerParams(
            collective_id=collective_id, has_side_effects=True, vmem_limit_bytes=VMEM_LIMIT
        ),
    )(*args)


def shape(dims, kind=bf16):
    return jax.ShapeDtypeStruct(dims, kind)


class Line:
    def __init__(self, links, here, h, FH, forward):
        self.links, self.here, self.h, self.FH, self.forward = links, here, h, FH, forward
        self.right, self.left, self.pending = [], [], []
        self.settled = set()

    def step(self, j):
        h, FH = self.h, self.FH
        rights = [
            self.links.copy(block, block, (self.links.s, self.links.f + 2))
            for block in self.here(lax.max(h - j, 0))
        ]
        lefts = [
            self.links.copy(block, block, (self.links.s, self.links.f - 2))
            for block in self.here(lax.min(h + j, FH - 1))
        ]
        for i in range(len(rights)):

            @pl.when((h >= j) & (h < FH - 1))
            def _():
                rights[i].start()

            @pl.when((h + j < FH) & (h > 0))
            def _():
                lefts[i].start()

        self.right.append(rights)
        self.left.append(lefts)

    def arrived(self, j):
        h, FH = self.h, self.FH
        up = self.here(lax.max(h - 1 - j, 0))
        down = self.here(lax.min(h + 1 + j, FH - 1))
        for i in range(len(up)):
            for blocks, copies, there in (
                (up, self.right[j], h - 1 - j >= 0),
                (down, self.left[j], h + 1 + j < FH),
            ):
                a, b = self.forward
                on = self.links.copy(blocks[i], blocks[i], (self.links.s ^ a, self.links.f ^ b))
                self.pending.append((j, on, there))

                @pl.when(there)
                def _():
                    copies[i].wait_recv()
                    on.start()

    def came(self, j):
        self.settled.add(j)
        for step, on, there in self.pending:
            if step == j:

                @pl.when(there)
                def _():
                    on.wait_recv()

    def finish(self):
        h, FH = self.h, self.FH
        for j in range(FH - 1):
            if j not in self.settled:
                self.came(j)
        for _, on, there in self.pending:

            @pl.when(there)
            def _():
                on.wait_send()

        for j in range(FH - 1):
            for i in range(len(self.right[j])):

                @pl.when((h >= j) & (h < FH - 1))
                def _():
                    self.right[j][i].wait_send()

                @pl.when((h + j < FH) & (h > 0))
                def _():
                    self.left[j][i].wait_send()


def rows_of(ref):
    return ref[...].reshape(-1, ref.shape[-1])


def rotation(table):
    half = table.shape[-1] // 2
    swapped = pltpu.roll(table, half, 1)
    first = lax.broadcasted_iota(jnp.int32, table.shape, 1) < half
    return jnp.where(first, table, swapped), jnp.where(first, -swapped, table)


def turn(vector, factors):
    return vector * factors[0] + pltpu.roll(vector, vector.shape[-1] // 2, 1) * factors[1]


class RowSum:
    def __init__(self, links, parts, from_core, from_x):
        self.links, self.parts, self.from_core, self.from_x = links, parts, from_core, from_x
        self.x, self.core, self.sent = links.s // 2, links.s % 2, []

    def far(self):
        x, core = 1 - self.x, 1 - self.core
        self.to_far = self.links.start(self.parts.at[x, core], self.from_core.at[x], (1, 0))
        self.sent.append(self.to_far)

    def near(self):
        x, core = self.x, 1 - self.core
        self.to_near = self.links.start(self.parts.at[x, core], self.from_core.at[x], (1, 0))
        self.sent.append(self.to_near)

    def middle(self):
        self.to_far.wait()
        x, core = 1 - self.x, self.core

        def add(rows):
            total = self.parts[x, core, rows].astype(f32) + self.from_core[x, rows].astype(f32)
            self.parts[x, core, rows] = total.astype(bf16)

        row_loop(self.from_x.shape[0], 16, add)
        self.across = self.links.start(self.parts.at[x, core], self.from_x, (2, 0))
        self.sent.append(self.across)

    def arrive(self):
        self.to_near.wait()
        self.across.wait()

    def total(self, rows):
        return (
            self.parts[self.x, self.core, rows].astype(f32)
            + self.from_core[self.x, rows].astype(f32)
            + self.from_x[rows].astype(f32)
        )


class LineSum:
    def __init__(self, links, h, parts, from_core, chain, extra):
        self.links, self.h, self.parts = links, h, parts
        self.from_core, self.chain, self.extra = from_core, chain, extra
        self.core, self.T = links.s % 2, extra.shape[0]
        self.by_core, self.right, self.left, self.end = {}, {}, {}, {}
        s, f = links.s, links.f
        for d in range(Z):
            block = parts.at[d, self.core]
            self.right[d] = links.copy(block, chain.at[d], (s, f + 2))
            self.left[d] = links.copy(block, chain.at[d], (s, f - 2))
            self.end[d] = links.copy(block, extra, (s, f - 2))

    def send_core(self, d):
        self.by_core[d] = self.links.start(
            self.parts.at[d, 1 - self.core], self.from_core.at[d], (1, 0)
        )

    def add(self, d, chained):
        def add(rows):
            total = self.parts[d, self.core, rows].astype(f32)
            total += self.from_core[d, rows].astype(f32)
            if chained:
                total += self.chain[d, rows].astype(f32)
            self.parts[d, self.core, rows] = total.astype(bf16)

        row_loop(self.T, 16, add)

    def stage(self, k, places):
        h = self.h
        for d in places:
            self.by_core[d].wait()
            rightward, leftward = (h < d) & (h == k), (h > d) & (h == Z - 1 - k)

            @pl.when(rightward)
            def _():
                if k:
                    self.right[d].wait_recv()
                self.add(d, k > 0)
                self.right[d].start()

            @pl.when(leftward)
            def _():
                if k:
                    self.left[d].wait_recv()
                self.add(d, k > 0)

            @pl.when(leftward & (h > d + 1))
            def _():
                self.left[d].start()

            @pl.when(leftward & (h == d + 1))
            def _():
                self.end[d].start()

    def arrive(self):
        h = self.h
        for d in range(Z):
            self.by_core[d].wait()
            if d > 0:

                @pl.when(h == d)
                def _():
                    self.right[d].wait_recv()

            else:

                @pl.when(h == 0)
                def _():
                    self.chain[0] = jnp.zeros_like(self.chain[0])

            if d < Z - 1:

                @pl.when(h == d)
                def _():
                    self.end[d].wait_recv()

            else:

                @pl.when(h == Z - 1)
                def _():
                    self.extra[...] = jnp.zeros_like(self.extra)

    def total(self, rows):
        return (
            self.parts[self.h, self.core, rows].astype(f32)
            + self.from_core[self.h, rows].astype(f32)
            + self.chain[self.h, rows].astype(f32)
            + self.extra[rows].astype(f32)
        )

    def settle(self):
        h = self.h
        for d in range(Z):
            self.by_core[d].wait_sent()

            @pl.when(h < d)
            def _():
                self.right[d].wait_send()

            @pl.when(h > d + 1)
            def _():
                self.left[d].wait_send()

            @pl.when(h == d + 1)
            def _():
                self.end[d].wait_send()


class LeadFirst:
    def __init__(self, ref):
        self.ref, self.n, self.rows = ref, ref.shape[0], ref.shape[3]

    def half(self, l):
        return self.ref.at[:, :, l]

    def both(self, w):
        return self.ref.at[:, w]

    def part(self, w, l):
        return self.ref.at[:, w, l]

    def item(self, i, w, l):
        return self.ref.at[i, w, l]

    def got(self, ref, i, w):
        return ref.at[i, w]


class Natural:
    def __init__(self, ref):
        self.ref, self.n, self.rows = ref, ref.shape[2], ref.shape[4]

    def half(self, l):
        return self.ref.at[:, :, :, l]

    def both(self, w):
        return self.ref.at[w % 2, w // 2]

    def part(self, w, l):
        return self.ref.at[w % 2, w // 2, :, l]

    def item(self, i, w, l):
        return self.ref.at[w % 2, w // 2, i, l]

    def got(self, ref, i, w):
        return ref.at[w % 2, w // 2, i]


class PieceByL:
    def __init__(self, links, view, by_l, by_w, w, masks):
        self.links, self.view, self.by_l, self.by_w = links, view, by_l, by_w
        self.w, self.masks, self.l = w, masks, links.f % 2
        self.first = links.start(view.half(1 - self.l), by_l, (0, 1))

    def partial(self, i, w, rows):
        total = self.view.item(i, w, self.l)[rows].astype(f32)
        return total + self.view.got(self.by_l, i, w)[rows].astype(f32)

    def place(self, k, slot=None):
        w = self.w ^ k

        def add(i, rows):
            total = self.partial(i, w, rows)
            if slot is not None:
                total += self.by_w[slot, i, rows].astype(f32)
            self.view.item(i, w, self.l)[rows] = total.astype(bf16)

        block_loop(self.view.n, self.view.rows, 16, add)

    def middle(self):
        self.first.wait()
        self.second = []
        for k in range(1, len(self.masks)):
            self.place(k)
            block = self.view.part(self.w ^ k, self.l)
            self.second.append(self.links.start(block, self.by_w.at[k - 1], self.masks[k]))

    def arrive(self):
        for arrival in self.second:
            arrival.wait()

    def last(self, store=None):
        self.arrive()

        def add(i, rows):
            total = self.partial(i, self.w, rows)
            for k in self.slots():
                total += self.by_w[k, i, rows].astype(f32)
            if store is None:
                self.view.item(i, self.w, self.l)[rows] = total.astype(bf16)
            else:
                store(i, rows, total)

        block_loop(self.view.n, self.view.rows, 16, add)

    def slots(self):
        return range(len(self.masks) - 1)

    def inner(self):
        pass

    def settle(self):
        pass


class PieceAlongZ(PieceByL):
    def __init__(self, links, view, by_l, by_w, w, masks):
        super().__init__(links, view, by_l, by_w, w, masks)
        self.is_inner = (w == 1) | (w == 2)
        device = [(links.s ^ a, links.f ^ b) for a, b in masks]

        def copy(k, slot, to):
            return links.copy(view.part(w ^ k, self.l), by_w.at[slot], device[to])

        self.out = [copy(k, k - 1, 1) for k in (1, 2, 3)]
        self.over = [copy(3, 3, 3), copy(2, 3, 2)]
        self.beside = copy(1, 0, 1)

    def middle(self):
        self.first.wait()

        @pl.when(self.is_inner)
        def _():
            self.place(1)
            self.beside.start()

        @pl.when(jnp.logical_not(self.is_inner))
        def _():
            for k in (2, 3, 1):
                self.place(k)
                self.out[k - 1].start()

    def inner(self):
        @pl.when(self.is_inner)
        def _():
            for k, over in zip((3, 2), self.over):
                self.out[4 - k].wait_recv()
                self.place(k, 4 - k)
                over.start()

    def arrive(self):
        @pl.when(self.is_inner)
        def _():
            self.out[0].wait_recv()
            self.over[0].wait_recv()

        @pl.when(jnp.logical_not(self.is_inner))
        def _():
            self.beside.wait_recv()
            self.over[1].wait_recv()

    def slots(self):
        return (0, 3)

    def settle(self):
        @pl.when(self.is_inner)
        def _():
            for copy in [self.beside] + self.over:
                copy.wait_send()

        @pl.when(jnp.logical_not(self.is_inner))
        def _():
            for copy in self.out:
                copy.wait_send()


def z_piece(links, view, by_l, by_w, w, masks):
    kind = PieceAlongZ if len(masks) == 4 else PieceByL
    return kind(links, view, by_l, by_w, w, masks)


class PieceByW:
    def __init__(self, links, view, by_l, by_w, w, masks):
        self.links, self.view, self.by_l, self.by_w = links, view, by_l, by_w
        self.w, self.masks, self.l = w, masks, links.f % 2
        self.first = [
            links.start(view.both(w ^ k), by_w.at[k - 1], masks[k]) for k in range(1, len(masks))
        ]

    def partial(self, i, l, rows):
        total = self.view.item(i, self.w, l)[rows].astype(f32)
        for k in range(1, len(self.masks)):
            total += self.by_w[k - 1, i, l, rows].astype(f32)
        return total

    def middle(self):
        for arrival in self.first:
            arrival.wait()
        l = 1 - self.l

        def add(i, rows):
            self.view.item(i, self.w, l)[rows] = self.partial(i, l, rows).astype(bf16)

        block_loop(self.view.n, self.view.rows, 16, add)
        self.second = self.links.start(self.view.part(self.w, l), self.by_l, (0, 1))

    def last(self, store=None):
        self.second.wait()

        def add(i, rows):
            total = self.partial(i, self.l, rows) + self.by_l[i, rows].astype(f32)
            if store is None:
                self.view.item(i, self.w, self.l)[rows] = total.astype(bf16)
            else:
                store(i, rows, total)

        block_loop(self.view.n, self.view.rows, 16, add)


def by_l_scratch(n, W, rows, width):
    return [pltpu.VMEM((n, W, rows, width), bf16), pltpu.VMEM((W - 1, n, rows, width), bf16)]


def z_scratch(n, W, rows, width):
    slots = 4 if W == 4 else W - 1
    return [pltpu.VMEM((n, W, rows, width), bf16), pltpu.VMEM((slots, n, rows, width), bf16)]


def by_w_scratch(n, W, rows, width):
    return [pltpu.VMEM((n, rows, width), bf16), pltpu.VMEM((W - 1, n, 2, rows, width), bf16)]


def norm_back(grad_normed, inputs, gain):
    inverse = lax.rsqrt(jnp.mean(inputs * inputs, -1, keepdims=True) + epsilon)
    scaled = grad_normed * gain
    inner_sum = jnp.sum(scaled * inputs, -1, keepdims=True)
    grad = inverse * scaled - inputs * (inverse**3 * inner_sum / inputs.shape[-1])
    return grad, inputs * inverse


def layer_kernel(FH, copies, *refs):
    tok, tab_in, wq_in, wk_in, wv_in, gains_in, wo_in = refs[:7]
    gate_in, up_in, down_in, cot_in, segments = refs[7:12]
    output, keys, values, grad_tokens, gate_out, up_out, down_out = refs[12:19]
    wq_out, wo_out, wk_out, wv_out, gains_out = refs[19:24]
    both_own, normed_kept, side_kept, o_kept = refs[24:28]
    send, recv, here, both, down, q_w, kv_w, o_w = refs[28:36]
    residual, grad_in, gains, gain_sums, grad_row = refs[36:41]
    grad_down, o_sum, kv_sum, q_own = refs[41:45]
    back_bufs, out_bufs = refs[45:49], refs[49:53]
    normed, cot, grad_both, tab, grad_k, grad_v, bias = refs[53:60]
    bufs = refs[60:]
    links = Links(send, recv)
    s, f = links.s, links.f
    x, core = s // 2, s % 2
    e, h, l = f // 8, (f // 2) % Z, f % 2
    t = 2 * h + core
    T, D = residual.shape
    S, F, rows_w, HC = q_w.shape
    row_len, head = grad_k.shape
    heads = HC // head
    E, FC = both.shape[2], both.shape[6] // 2
    W, TG = 2 * E, 2 * Z
    w = 2 * e + x
    two = 2 * T
    cut = D // 2
    scale = head ** (-0.5)
    group_masks = [(a, 2 * m) for m in range(Z) for a in (0, 1)][1:]
    w_masks = [(2 * (j % 2), 8 * (j // 2)) for j in range(W)]
    back = LineSum(links, h, *back_bufs)
    out = LineSum(links, h, *out_bufs)
    back_parts, out_parts = back.parts, out.parts
    tok_g = grad_row
    spots = {}
    for name, width in (("attended", HC), ("q", HC), ("k", head), ("v", head), ("grad", HC)):
        base = sum(n for _, n in spots.values())
        spots[name] = (base, width)
    side_width = spots["grad"][0]

    def column(name, first=0, width=None):
        base, full_width = spots[name]
        return pl.ds(base + first, width or full_width)

    def block(where, name, r, first=0, width=None):
        return where[r // 2, r % 2, :, column(name, first, width)]

    def to_x(ref, j):
        return ref.at[(w ^ j) % 2, :, (w ^ j) // 2]

    def whole(where, name, first=0, width=None):
        return where[:, :, :, column(name, first, width)].reshape(row_len, -1)

    links.greet(
        [(a, 0) for a in (1, 2, 3)]
        + [(0, 1)]
        + [(0, 2 * k) for k in range(1, FH)]
        + [(1, 2 * m) for m in range(1, Z)]
        + [mask for mask in w_masks if mask[0] and mask[1]]
    )
    local = Local(
        here,
        [
            (wq_in.at[:, pl.ds(pl.multiple_of(s * HC, HC), HC)], q_w.at[s, f]),
            (wk_in, kv_w.at[s, f, :, pl.ds(0, head)]),
            (wv_in, kv_w.at[s, f, :, pl.ds(head, head)]),
            (gains_in, kv_w.at[s, f, :, pl.ds(2 * head, head)]),
            (wo_in, o_w.at[f]),
            (tok, tok_g.at[s]),
            (tab_in, tab.at[s]),
            (down_in, down.at[0, w, l]),
            (cot_in, cot.at[h, core]),
        ],
    )
    first = [
        links.start(
            wq_in.at[:, pl.ds(pl.multiple_of((s ^ a) * HC, HC), HC)], q_w.at[s, f], (a, 0)
        )
        for a in (1, 2, 3)
    ]
    quarter = FC * TG // S
    natural = Local(
        here,
        [
            (r.at[:, pl.ds(i * quarter, quarter)], back_parts.at[i, j, pl.ds(0, rows_w), pl.ds(0, quarter)])
            for j, r in enumerate((gate_in, up_in))
            for i in range(S)
        ],
        9,
    )
    local.wait(1, 2, 3, 4)
    along_z = (f // 2, FH, (0, 1))
    kv_line = Line(links, lambda place: [kv_w.at[s, 2 * place + l]], *along_z)
    o_line = Line(links, lambda place: [o_w.at[2 * place + l]], *along_z)
    q_line = Line(links, lambda place: [q_w.at[:, 2 * place + l]], *along_z)
    kv_line.step(0)
    kv_y = links.pass_on(kv_w.at[s, f], (0, 1))
    o_line.step(0)
    needed = [links.pass_on(o_w.at[f], (0, 1))]
    local.wait(0)
    for arrival in first:
        arrival.wait()
    q_line.step(0)
    needed.append(links.pass_on(q_w.at[:, f], (0, 1)))
    tok_x = links.start(tok, tok_g.at[s], (2, 0))
    needed.append(links.start(tok, tok_g.at[s], (1, 0)))
    needed += [links.start(tab_in, tab.at[s], (a, 0)) for a in (1, 2, 3)]
    ffn_in = {}
    lanes = 128
    whole_tiles = FC // lanes

    def blocks_of(ref, at_h, c):
        width = 2 * FC // W // 2
        parts = []
        for at_e in range(E):
            for at_x in (0, 1):
                base = (at_e * Z + at_h) * width
                parts.append(ref(2 * at_x + c)[:, base : base + width])
        return jnp.concatenate(parts, 1)

    def side_by_side(gate_units, up_units):
        tiles = []
        for j in range(whole_tiles):
            part = slice(j * lanes, (j + 1) * lanes)
            tiles += [gate_units[:, part], up_units[:, part]]
        rest = slice(whole_tiles * lanes, FC)
        return jnp.concatenate(tiles + [gate_units[:, rest], up_units[:, rest]], 1)

    def sent_blocks(at_h, c):
        return grad_both.at[at_h, pl.ds(pl.multiple_of(c * rows_w, rows_w), rows_w)]

    ids = jnp.broadcast_to(segments[...].astype(f32), (lanes, row_len))
    own_ids = jnp.transpose(ids)[:, :1]
    for r in range(S):
        rows = slice(r * T, (r + 1) * T)
        mine_at = lax.broadcasted_iota(jnp.int32, (T, row_len), 0) + r * T
        seen_at = lax.broadcasted_iota(jnp.int32, (T, row_len), 1)
        allowed = (seen_at <= mine_at) & (ids[:1] == own_ids[rows])
        bias[rows] = jnp.where(allowed, 0.0, -1e30).astype(bf16)
    natural.wait()
    columns_of = [
        [back_parts[i, j, :rows_w, :quarter].astype(f32) for i in range(S)] for j in (0, 1)
    ]
    for at_h in range(Z):
        for c in (0, 1):
            units = [blocks_of(lambda i: columns_of[j][i], at_h, c) for j in (0, 1)]
            grad_both[at_h, c * rows_w : (c + 1) * rows_w] = side_by_side(*units).astype(bf16)
    own_block = Local(here, [(sent_blocks(h, core), both.at[x, core, e, h, l])], 17)

    def to_group(m):
        for a in (0, 1):
            if (a, m) != (0, 0):
                place = (x, core, e, h, l)
                source = sent_blocks(h ^ m, core ^ a)
                ffn_in[a, m] = links.start(source, both.at[place], (a, 2 * m))

    arriving = []

    class Spread:
        def __init__(self, near, second_w, second_y):
            self.near, self.second_w, self.second_y = near, second_w, second_y

        def by_w(self):
            self.came_w = [links.pass_on(self.near, mask) for mask in w_masks[1:]]

        def by_y(self):
            self.came_y = links.pass_on(self.near, (0, 1))

        def on_w(self):
            self.came_y.wait()
            arriving.extend(links.pass_on(self.second_w, mask) for mask in w_masks[1:])

        def on_y(self):
            for j, arrival in enumerate(self.came_w):
                arrival.wait()
                arriving.append(links.pass_on(self.second_y(j + 1), (0, 1)))

    def spread_of(m):
        def second_y(j):
            return to_x(both, j).at[0, h ^ m, l]

        here_q = to_x(both, 0)
        return Spread(here_q.at[:, h ^ m, l], here_q.at[1, h ^ m, 1 - l], second_y)

    low_half, high_half = pl.ds(0, cut), pl.ds(cut, D - cut)
    spread_down = Spread(
        down.at[0, w, l],
        down.at[0, w, 1 - l, :, high_half],
        lambda j: down.at[0, w ^ j, l, :, low_half],
    )
    to_group(0)
    local.wait(7)
    spread_down.by_w()
    for j in range(FH - 1):
        for way in (kv_line, o_line, q_line):
            way.arrived(j)
            if j + 1 < FH - 1:
                way.step(j + 1)
        if j == 0:
            tok_x.wait()
            needed.append(links.pass_on(tok_g.at[s ^ 2], (1, 0)))
            own_block.wait()
            ffn_in[1, 0].wait()
            spreads = [spread_of(m) for m in range(Z)]
            spreads[0].by_w()
    kv_y.wait()
    kv_line.finish()
    kv_x = links.pass_on(kv_w.at[s], (2, 0))
    needed.append(links.pass_on(kv_w.at[s], (1, 0)))
    for m in range(1, Z):
        to_group(m)
    spread_down.by_y()
    spreads[0].by_y()
    cot_line = Line(links, lambda place: [cot.at[place, core]], h, Z, (1, 0))
    kv_x.wait()
    needed.append(links.pass_on(kv_w.at[s ^ 2], (1, 0)))
    for arrival in needed:
        arrival.wait()
    o_line.finish()
    q_line.finish()
    local.wait(5, 6)
    kept_o = Local(here, [(o_w, o_kept)], 18)

    normed_one, side = out_parts.at[pl.ds(0, 2)], out_parts.at[pl.ds(2, 2)]
    place = lax.broadcasted_iota(jnp.int32, (8, head), 0)
    lane = lax.broadcasted_iota(jnp.int32, (8, head), 1)
    pick = (place == lane).astype(bf16)
    kv_full = rows_of(kv_w)
    gains[...] = contract_last(pick, kv_full[:, 2 * head :])

    def norm_one(i, rows):
        value = tok_g[i, rows].astype(f32)
        inverse = lax.rsqrt(jnp.mean(value * value, -1, keepdims=True) + epsilon)
        normed_one[i // 2, lax.rem(i, 2), rows] = (value * inverse * gains[0:1]).astype(bf16)

    block_loop(S, T, 16, norm_one)
    local.wait(8)
    cot_line.step(0)
    arriving.append(links.pass_on(cot.at[h, core], (1, 0)))
    factors = rotation(rows_of(tab))

    def put(name, first, value):
        columns = column(name, first, value.shape[1])
        side[:, :, :, columns] = value.astype(bf16).reshape(2, 2, T, -1)

    kv = dot(rows_of(normed_one), kv_full[:, : 2 * head])
    put("k", 0, turn(kv[:, :head], factors))
    put("v", 0, kv[:, head:])
    for n in range(0, heads, 2):
        columns = slice(n * head, (n + 2) * head)
        pair = dot(rows_of(normed_one), q_w[:, :, :, columns].reshape(D, 2 * head))
        for j in (0, 1):
            put("q", (n + j) * head, turn(pair[:, j * head : (j + 1) * head], factors))
    results = [
        Local(
            here,
            [
                (side.at[x, core, :, column("k")], keys),
                (side.at[x, core, :, column("v")], values),
            ],
            21,
        )
    ]
    for r in range(S):
        rows, seen = slice(r * T, (r + 1) * T), slice(0, (r + 1) * T)
        keys_seen, values_seen = whole(side, "k")[seen], whole(side, "v")[seen]
        for n in range(heads):
            query = block(side, "q", r, n * head, head)
            scores = contract_last(query, keys_seen) * scale + bias[rows, seen].astype(f32)
            scores = jnp.exp(scores - jnp.max(scores, -1, keepdims=True))
            probs = (scores / jnp.sum(scores, -1, keepdims=True)).astype(bf16)
            side[r // 2, r % 2, :, column("attended", n * head, head)] = dot(
                probs, values_seen
            ).astype(bf16)
    spread_down.on_y()

    first_two = pl.ds(0, 2)
    row_bufs = (back_parts.at[first_two], back.from_core.at[first_two], back.chain.at[0])
    parts = RowSum(links, *row_bufs)

    def project(x_to):
        rows = side[x_to, :, :, column("attended")].reshape(two, HC)
        for n in range(0, D, HC):
            columns = slice(n, n + HC)
            total = dot(rows, o_w[:, :, columns].reshape(HC, HC))
            parts.parts[x_to, :, :, columns] = total.astype(bf16).reshape(2, T, HC)

    project(1 - x)
    parts.far()
    project(x)
    parts.near()
    parts.middle()
    spread_down.on_w()
    spreads[0].on_y()
    spreads[0].on_w()
    for m in range(1, Z):
        for a in (0, 1):
            ffn_in[a, m].wait()
        spreads[m].by_y()
        spreads[m].by_w()
    cot_line.arrived(0)
    cot_line.step(1)
    kept = Local(
        here, [(normed_one, normed_kept), (side.at[:, :, :, pl.ds(0, side_width)], side_kept)], 19
    )
    parts.arrive()

    def norm_two(rows):
        total = tok_g[s, rows].astype(f32) + parts.total(rows)
        residual[rows] = total
        inverse = lax.rsqrt(jnp.mean(total * total, -1, keepdims=True) + epsilon)
        normed[h, core, rows] = (total * inverse * gains[1:2]).astype(bf16)

    row_loop(T, 16, norm_two)
    normed_line = Line(links, lambda place: [normed.at[place, core]], h, Z, (1, 0))
    normed_line.step(0)
    beside = [links.pass_on(normed.at[h, core], (1, 0))]
    cot_line.arrived(1)
    cot_line.step(2)
    spreads[1].on_y()
    spreads[1].on_w()
    normed_line.arrived(0)
    normed_line.step(1)
    for m in range(2, Z):
        spreads[m].on_y()
        spreads[m].on_w()
    normed_line.arrived(1)
    normed_line.step(2)
    results[0].wait()
    kept_o.wait()
    kept.wait()
    for arrival in arriving:
        arrival.wait()
    for arrival in links.sent:
        arrival.wait_sent()

    slot = D // 2
    lane_is_low = lax.broadcasted_iota(jnp.int32, (two, lanes), 1) < lanes // 2

    def hidden_of(d):
        n = normed[d].reshape(two, D)
        c = cot[d].reshape(two, D)
        weights = down[...].reshape(FC, D)

        def units(first, width, gate_proj, up_proj, grad_inner):
            sig = jax.nn.sigmoid(gate_proj)
            silu = gate_proj * sig
            spot = pl.ds(pl.multiple_of(d // 2 * slot + first, lanes), width)
            hidden = (silu * up_proj).astype(bf16)[:, :width]
            o_w[pl.ds(d % 2 * (F // 2), F // 2), :, spot] = hidden.reshape(F // 2, rows_w, width)
            slope = sig * (1.0 + gate_proj * (1.0 - sig))
            return (grad_inner * up_proj * slope).astype(bf16), (grad_inner * silu).astype(bf16)

        for first in range(0, FC, 2 * lanes):
            width = min(2 * lanes, FC - first)
            rows = weights[first : first + width]
            if width % lanes:
                rows = jnp.concatenate([rows, rows[width - lanes // 2 :]], 0)
            grad_inner = contract_last(c, rows)
            for i in range(0, width, lanes):
                base = 2 * (first + i)
                columns = (slice(None),) * 6 + (slice(base, min(base + 2 * lanes, 2 * FC)),)
                proj = dot(n, both[columns].reshape(D, -1))
                part = slice(i, i + lanes)
                if i + lanes <= width:
                    grad_gate, grad_up = units(
                        first + i,
                        lanes,
                        proj[:, :lanes],
                        proj[:, lanes:],
                        grad_inner[:, part],
                    )
                    grad_both[d, :, base : base + lanes] = grad_gate
                    grad_both[d, :, base + lanes : base + 2 * lanes] = grad_up
                else:
                    mixed = proj
                    turned = pltpu.roll(mixed, lanes // 2, 1)
                    grad_gate, grad_up = units(
                        first + i,
                        lanes // 2,
                        jnp.where(lane_is_low, mixed, turned),
                        jnp.where(lane_is_low, turned, mixed),
                        grad_inner[:, part],
                    )
                    grad_both[d, :, base : base + lanes] = jnp.where(
                        lane_is_low, grad_gate, grad_up
                    )

    def back_of(d):
        for i in range(S):
            columns = slice(i * F * rows_w, (i + 1) * F * rows_w)
            total = contract_last(grad_both[d], both[i // 2, i % 2].reshape(-1, 2 * FC))
            back_parts[d, :, :, columns] = total.astype(bf16).reshape(2, T, -1)
        back.send_core(d)

    def out_of(d):
        spot = slice(d // 2 * slot, d // 2 * slot + FC)
        hidden = o_w[pl.ds(d % 2 * (F // 2), F // 2), :, spot].reshape(two, FC)
        for i in range(0, D, 512):
            columns = slice(i, i + 512)
            total = dot(hidden, down[:, :, :, :, columns].reshape(FC, 512))
            out_parts[d, :, :, columns] = total.astype(bf16).reshape(2, T, -1)
        out.send_core(d)

    for arrival in beside:
        arrival.wait()
    hidden_of(h)
    for line in (cot_line, normed_line):
        line.came(0)
    hidden_of(h ^ 1)
    for line in (cot_line, normed_line):
        line.came(1)
    hidden_of(h ^ 2)
    for line in (cot_line, normed_line):
        line.arrived(2)
    for line in (cot_line, normed_line):
        line.came(2)
    hidden_of(h ^ 3)
    back_of(3)
    back_of(0)
    back.stage(0, (3, 0))
    back_of(2)
    back_of(1)
    back.stage(0, (2, 1))
    for line in (cot_line, normed_line):
        line.finish()
    ffn = {}
    width = F * rows_w
    for c in (0, 1):
        for i in (0, 1):
            base = (2 * i + c) * width
            turned = normed[:, :, :, base : base + width].reshape(4 * two, width)
            for columns in [slice(n, min(n + 3 * lanes, 2 * FC)) for n in range(0, 2 * FC, 3 * lanes)]:
                total = contract_first(turned, grad_both[:, :, columns].reshape(4 * two, -1))
                both[i, c, :, :, :, :, columns] = total.astype(bf16).reshape(E, Z, 2, rows_w, -1)
        if c == 0:
            ffn["both", 0] = PieceByL(links, Natural(both.at[:, 0]), *bufs[4:6], w, w_masks)
            back.stage(1, (3, 0))
    ffn["both", 1] = PieceByW(links, Natural(both.at[:, 1]), *bufs[6:8], w, w_masks)
    for d in (3, 0, 2, 1):
        out_of(d)
    inner = [o_w[:, :, i * slot : i * slot + FC].reshape(2 * two, FC) for i in (0, 1)]
    for i in range(0, D, 256):
        columns = slice(i, i + 256)
        total = contract_first(inner[0], cot[0:2, :, :, columns].reshape(2 * two, 256))
        total += contract_first(inner[1], cot[2:4, :, :, columns].reshape(2 * two, 256))
        down[:, :, :, :, columns] = total.astype(bf16).reshape(1, W, 2, -1, 256)
        if i + 256 == cut:
            ffn["down_low"] = PieceByL(
                links, LeadFirst(down.at[:, :, :, :, low_half]), *bufs[0:2], w, w_masks
            )
    back.stage(1, (2, 1))
    back.stage(2, (3, 0))
    out.stage(0, (3, 0, 2, 1))

    cot_own, tok_own = normed.at[2, 0], normed.at[2, 1]
    own = Local(here, [(cot_in, cot_own), (tok, tok_own)], 23)
    gain_sums[...] = jnp.zeros_like(gain_sums)
    own.wait()
    back.arrive()

    def second_norm(rows):
        grad_normed = back.total(rows)
        grad, unit = norm_back(grad_normed, residual[rows], gains[1:2])
        grad = grad + cot_own[rows].astype(f32)
        grad_in[rows] = grad
        grad_row[s, rows] = grad.astype(bf16)
        gain_sums[1:2] += jnp.sum(grad_normed * unit, 0, keepdims=True)

    row_loop(T, 16, second_norm)
    row_x = links.pass_on(grad_row.at[s], (3, 0))
    row_c = links.pass_on(grad_row.at[s], (1, 0))

    last_two = pl.ds(2, 2)
    side = cot.at[first_two]
    normed_one = normed.at[first_two]
    grad_side = cot.at[last_two]
    loads = Local(
        here,
        [
            (o_kept, o_w),
            (side_kept, cot.at[first_two, :, :, pl.ds(0, side_width)]),
            (normed_kept, normed_one),
        ],
        25,
    )
    ffn["both", 1].middle()
    ffn["both", 0].middle()
    row_x.wait()
    row_cc = links.pass_on(grad_row.at[s ^ 3], (1, 0))
    out.stage(1, (3, 0, 2, 1))
    row_c.wait()
    row_cc.wait()
    loads.wait()
    per = 2 * head // rows_w
    for n in range(0, heads, 2):
        wo = o_w[n // 2 * per : (n // 2 + 1) * per].reshape(2 * head, D)
        pair = contract_last(rows_of(grad_row), wo).astype(bf16)
        side[:, :, :, column("grad", n * head, 2 * head)] = pair.reshape(2, 2, T, 2 * head)
    for i in range(0, D, HC):
        columns = slice(i, i + HC)
        grad_columns = grad_row[:, :, columns].reshape(row_len, HC)
        total = contract_first(whole(side, "attended"), grad_columns)
        o_w[:, :, columns] = total.astype(bf16).reshape(F, rows_w, HC)
    place_z, z_masks = f // 2, [(0, 2 * j) for j in range(FH)]
    o_view = LeadFirst(o_w.reshape(1, FH, 2, rows_w, D))
    o_piece = z_piece(links, o_view, *bufs[8:10], place_z, z_masks)
    ffn["down_low"].middle()
    grad_k[...] = jnp.zeros_like(grad_k)
    grad_v[...] = jnp.zeros_like(grad_v)
    factors = rotation(rows_of(tab))
    back_turn = (factors[0], -factors[1])
    for r in range(S):
        rows, seen = slice(r * T, (r + 1) * T), slice(0, (r + 1) * T)
        keys_seen, values_seen = whole(side, "k")[seen], whole(side, "v")[seen]
        for n in range(heads):
            query = block(side, "q", r, n * head, head)
            grad_att = block(side, "grad", r, n * head, head)
            scores = contract_last(query, keys_seen) * scale + bias[rows, seen].astype(f32)
            scores = jnp.exp(scores - jnp.max(scores, -1, keepdims=True))
            probs = scores / jnp.sum(scores, -1, keepdims=True)
            grad_probs = contract_last(grad_att, values_seen)
            delta = jnp.sum(probs * grad_probs, -1, keepdims=True)
            grad_scores = (probs * (grad_probs - delta)).astype(bf16)
            grad_q = dot(grad_scores, keys_seen) * scale
            grad_q = turn(grad_q, (back_turn[0][rows], back_turn[1][rows])).astype(bf16)
            grad_side[r // 2, r % 2, :, n * head : (n + 1) * head] = grad_q
            grad_k[seen] += contract_first(grad_scores, query)
            grad_v[seen] += contract_first(probs.astype(bf16), grad_att)
    grad_key = turn(grad_k[...] * scale, back_turn).astype(bf16)
    grad_side[:, :, :, HC : HC + head] = grad_key.reshape(2, 2, T, head)
    grad_side[:, :, :, HC + head : HC + 2 * head] = grad_v[...].astype(bf16).reshape(2, 2, T, head)
    grad_qkv = slice(0, HC + 2 * head)
    back.settle()
    row = RowSum(links, *row_bufs)
    for cx, go in ((1 - x, row.far), (x, row.near)):
        for i in range(S):
            total = contract_last(grad_side[cx, :, :, :HC].reshape(two, HC), q_w[i].reshape(-1, HC))
            total += contract_last(
                grad_side[cx, :, :, HC : HC + 2 * head].reshape(two, 2 * head),
                kv_w[i, :, :, : 2 * head].reshape(-1, 2 * head),
            )
            columns = slice(i * F * rows_w, (i + 1) * F * rows_w)
            row.parts[cx, :, :, columns] = total.astype(bf16).reshape(2, T, -1)
        go()
    row.middle()
    ffn["down_high"] = PieceByW(
        links, LeadFirst(down.at[:, :, :, :, high_half]), *bufs[2:4], w, w_masks
    )
    for i in (0, 1):
        ffn["both", i].last()
    owners = [
        links.start(both.at[x, core ^ a, e, h ^ (b // 2), l], both_own.at[t], (a, b))
        for a, b in group_masks
    ]
    mine = Local(here, [(both.at[x, core, e, h, l], both_own.at[t])], 28)
    out.stage(2, (3, 0))
    pieces = []
    q_view = q_w.reshape(S, FH, 2, rows_w, HC)
    kv_view = kv_w.reshape(S, FH, 2, rows_w, kv_w.shape[3])

    def q_piece(i):
        one = pl.ds(i, 1)
        spare = (bufs[10].at[one], bufs[11].at[:, one])
        return z_piece(links, LeadFirst(q_view.at[one]), *spare, place_z, z_masks)

    for i in range(S):
        columns = slice(i * F * rows_w, (i + 1) * F * rows_w)
        turned = normed_one[:, :, :, columns].reshape(row_len, -1)
        total = contract_first(turned, grad_side[:, :, :, grad_qkv].reshape(row_len, -1))
        total = total.astype(bf16)
        q_w[i] = total[:, :HC].reshape(F, rows_w, HC)
        kv_w[i, :, :, : 2 * head] = total[:, HC:].reshape(F, rows_w, 2 * head)
        pieces.append(q_piece(i))
    row.arrive()

    def first_norm(rows):
        grad_normed = row.total(rows)
        grad, unit = norm_back(grad_normed, tok_own[rows].astype(f32), gains[0:1])
        grad_in[rows] += grad
        gain_sums[0:1] += jnp.sum(grad_normed * unit, 0, keepdims=True)

    row_loop(T, 16, first_norm)
    results = [Local(here, [(grad_in, grad_tokens)], 29)]
    pick = jnp.where((place == lane) & (place < 2), 1.0, 0.0)
    columns = contract_first(gain_sums[...], pick).astype(bf16)
    kv_w[:, :, :, 2 * head :] = columns.reshape(S, F, rows_w, head)
    kv_row = RowSum(links, kv_w.reshape(2, 2, F * rows_w, kv_w.shape[3]), *bufs[12:14])
    kv_row.far()
    kv_row.near()
    kv_row.middle()
    o_piece.middle()
    pieces[0].middle()
    pieces[1].middle()
    ffn["down_high"].middle()
    o_piece.inner()
    pieces[2].middle()
    pieces[0].inner()
    pieces[3].middle()
    kv_row.arrive()

    def keep_kv(rows):
        kv_row.parts[x, core, rows] = kv_row.total(rows).astype(bf16)

    row_loop(F * rows_w, 16, keep_kv)
    kv_mine = LeadFirst(kv_view.at[pl.ds(s, 1)])
    kv_piece = z_piece(links, kv_mine, *bufs[14:16], place_z, z_masks)
    pieces[1].inner()
    pieces[2].inner()
    pieces[3].inner()
    kv_piece.middle()
    kv_piece.inner()

    grad_own = grad_both.reshape(Z, two // rows_w, rows_w, 2 * FC)
    for arrival in owners:
        arrival.wait()
    mine.wait()
    came = Local(
        here, [(both_own.at[pl.ds(2 * i, 2)], grad_own.at[i, pl.ds(0, 2)]) for i in range(Z)], 33
    )
    for piece in pieces:
        piece.last()
    for a in (1, 2, 3):
        links.start(q_view.at[s ^ a, place_z, l], q_own.at[s], (a, 0))
    q_own[s] = q_view[s, place_z, l]
    q_came = links.sent[-3:]

    def store_kv(i, rows, total):
        kv_sum[rows] = total

    kv_piece.last(store_kv)
    names = (wk_out, wv_out, gains_out)
    results.append(
        Local(here, [(kv_sum.at[:, pl.ds(i * head, head)], r) for i, r in enumerate(names)], 41)
    )

    def store_down(base):
        def store(i, rows, total):
            grad_down[rows, base : base + total.shape[1]] = total

        return store

    ffn["down_low"].last(store_down(0))
    ffn["down_high"].last(store_down(cut))
    results.append(Local(here, [(grad_down, down_out)], 30))

    def store_o(i, rows, total):
        o_sum[rows] = total

    o_piece.last(store_o)
    results.append(Local(here, [(o_sum, wo_out)], 31))
    out.arrive()

    out_rows = back_parts.at[3, 0]

    def finish_output(rows):
        out_rows[rows] = (residual[rows] + out.total(rows)).astype(bf16)

    row_loop(T, 16, finish_output)
    results.append(Local(here, [(out_rows, output)], 32))
    came.wait()
    results[0].wait()
    stores = [
        r.at[pl.ds(j * rows_w, rows_w), pl.ds(0, quarter)]
        for r in (residual, grad_in)
        for j in (0, 1)
    ]
    leaving = [None] * len(stores)
    count = 0
    for i, target in enumerate((gate_out, up_out)):
        units = []
        for at_h in range(Z):
            for c in (0, 1):
                block = grad_own[at_h, c].astype(f32)
                tiles = [
                    block[:, (2 * j + i) * lanes : (2 * j + i + 1) * lanes]
                    for j in range(whole_tiles)
                ]
                base = 2 * whole_tiles * lanes + i * (FC - whole_tiles * lanes)
                tiles.append(block[:, base : base + FC - whole_tiles * lanes])
                units.append(jnp.concatenate(tiles, 1))
        width = FC // W
        for at_x in (0, 1):
            for c in (0, 1):
                parts = [
                    units[2 * at_h + c][:, (2 * at_e + at_x) * width : (2 * at_e + at_x + 1) * width]
                    for at_e in range(E)
                    for at_h in range(Z)
                ]
                slot_now = count % len(stores)
                if leaving[slot_now] is not None:
                    leaving[slot_now].wait()
                stores[slot_now][...] = jnp.concatenate(parts, 1)
                columns = pl.ds((2 * at_x + c) * quarter, quarter)
                leaving[slot_now] = Local(
                    here, [(stores[slot_now], target.at[:, columns])], 37 + slot_now
                )
                count += 1
    for arrival in q_came:
        arrival.wait()
    for i in leaving:
        i.wait()
    q_rows = residual.at[pl.ds(0, rows_w)]
    for i in range(S):
        q_rows[:, i * HC : (i + 1) * HC] = q_own[i].astype(f32)
    results.append(Local(here, [(q_rows, wq_out)], 44))
    out.settle()
    for piece in [o_piece, kv_piece] + pieces:
        piece.settle()
    links.finish()
    assert links.count == copies, links.count
    for result in results[1:]:
        result.wait()


def hand_over_kernel(n, *refs):
    inputs, outputs, rooms, sems = refs[:n], refs[n : 2 * n], refs[2 * n : 3 * n], refs[3 * n]
    loads = [pltpu.make_async_copy(inputs[i], rooms[i], sems.at[i]) for i in range(n)]
    stores = [pltpu.make_async_copy(rooms[i], outputs[i], sems.at[n + i]) for i in range(n)]
    for load in loads:
        load.start()
    for load, store in zip(loads, stores):
        load.wait()
        store.start()
    for store in stores:
        store.wait()


def hand_over(arrays):
    n = len(arrays)
    anywhere = [pl.BlockSpec(memory_space=pl.ANY)] * n
    return pl.pallas_call(
        functools.partial(hand_over_kernel, n),
        out_shape=[shape(a.shape, a.dtype) for a in arrays],
        in_specs=anywhere,
        out_specs=anywhere,
        scratch_shapes=[pltpu.VMEM(a.shape, a.dtype) for a in arrays]
        + [pltpu.SemaphoreType.DMA((2 * n,))],
        compiler_params=pltpu.CompilerParams(vmem_limit_bytes=VMEM_LIMIT),
    )(*arrays)


def angle_tables(position_row, head_size):
    half_head = head_size // 2
    frequency = 10000.0 ** (-jnp.arange(half_head, dtype=f32) * 2.0 / head_size)
    phase_angle = position_row.astype(f32)[:, None] * frequency[None, :]
    return (jnp.cos(phase_angle), jnp.sin(phase_angle))


def per_device(
    S,
    F,
    tokens,
    segments,
    positions,
    gain_one,
    w_query,
    w_key,
    w_value,
    w_out,
    gain_two,
    w_gate,
    w_up,
    w_down,
    cotangent,
):
    T, D = tokens.shape[1:]
    head = w_key.shape[1]
    row_len = segments.shape[1]
    rows = w_query.shape[0]
    down_rows = w_down.shape[0]
    FF = w_gate.shape[1]
    FH, E = F // 2, F // 8
    W, TG = 2 * E, 2 * Z
    HC = w_query.shape[1] // S
    heads = HC // head
    FC = FF // TG

    gains = jnp.stack([gain_one, gain_two], 1)
    gains = jnp.concatenate([gains, jnp.zeros((rows, head - 2), bf16)], 1)
    KV = 3 * head
    table = jnp.concatenate(angle_tables(positions[0], head), 1)
    group = [pltpu.VMEM((Z, 2, T, D), bf16), pltpu.VMEM((Z, T, D), bf16)]
    group += [pltpu.VMEM((Z, T, D), bf16), pltpu.VMEM((T, D), bf16)]
    weight = pltpu.VMEM((2, 2, E, Z, 2, rows, 2 * FC), bf16)

    def natural_by_l(n):
        block = (n, rows, 2 * FC)
        return [pltpu.VMEM((2, E, *block), bf16), pltpu.VMEM((W - 1, *block), bf16)]

    outs = [
        ((T, D), bf16),
        ((T, head), bf16),
        ((T, head), bf16),
        ((T, D), f32),
        ((rows, FF), f32),
        ((rows, FF), f32),
        ((down_rows, D), f32),
        ((rows, D), f32),
        ((rows, D), f32),
        ((rows, head), f32),
        ((rows, head), f32),
        ((rows, head), f32),
        ((TG, rows, 2 * FC), bf16),
        ((2, 2, T, D), bf16),
        ((2, 2, T, 2 * HC + 2 * head), bf16),
        ((F, rows, D), bf16),
    ]
    copies = 111 + 12 * (FH - 1) + 19 * (W - 1) + 6 * (1 + (6 if FH == 4 else FH - 1))
    results = communicate(
        functools.partial(layer_kernel, FH, copies),
        (
            tokens[0],
            table,
            w_query,
            w_key,
            w_value,
            gains,
            w_out,
            w_gate,
            w_up,
            w_down,
            cotangent[0],
            segments,
        ),
        [shape(dims, kind) for dims, kind in outs],
        copies,
        0,
        in_vmem=[False] * 11 + [True],
        kept=45,
        scratch=[
            weight,
            pltpu.VMEM((1, W, 2, down_rows, D), bf16),
            pltpu.VMEM((S, F, rows, HC), bf16),
            pltpu.VMEM((S, F, rows, KV), bf16),
            pltpu.VMEM((F, rows, D), bf16),
            pltpu.VMEM((T, D), f32),
            pltpu.VMEM((T, D), f32),
            pltpu.VMEM((8, D), f32),
            pltpu.VMEM((8, D), f32),
            pltpu.VMEM((S, T, D), bf16),
            pltpu.VMEM((down_rows, D), f32),
            pltpu.VMEM((rows, D), f32),
            pltpu.VMEM((rows, KV), f32),
            pltpu.VMEM((S, rows, HC), bf16),
            *group,
            *group,
            pltpu.VMEM((Z, 2, T, D), bf16),
            pltpu.VMEM((Z, 2, T, D), bf16),
            pltpu.VMEM((Z, 2 * T, 2 * FC), bf16),
            pltpu.VMEM((S, T, head), f32),
            pltpu.VMEM((row_len, head), f32),
            pltpu.VMEM((row_len, head), f32),
            pltpu.VMEM((row_len, row_len), bf16),
            *by_l_scratch(1, W, down_rows, D // 2),
            *by_w_scratch(1, W, down_rows, D // 2),
            *natural_by_l(Z),
            *by_w_scratch(Z, W, rows, 2 * FC),
            *z_scratch(1, FH, rows, D),
            *z_scratch(S, FH, rows, HC),
            pltpu.VMEM((2, F * rows, KV), bf16),
            pltpu.VMEM((F * rows, KV), bf16),
            *z_scratch(1, FH, rows, KV),
        ],
    )
    output, keys, values, grad_tokens, gate, up, down, query, out, key, value, gains = hand_over(
        results[:12]
    )
    return (
        output[None],
        keys[None],
        values[None],
        grad_tokens[None],
        gains[:, 0],
        query,
        key,
        value,
        out,
        gains[:, 1],
        gate,
        up,
        down,
    )


def solution(mesh):
    token_spec = P("fsdp", "seq", None)
    flat, matrix = P(("seq", "fsdp")), P(("seq", "fsdp"), None)
    return jax.shard_map(
        functools.partial(per_device, mesh.shape["seq"], mesh.shape["fsdp"]),
        mesh=mesh,
        in_specs=(
            token_spec,
            P("fsdp", None),
            P("fsdp", "seq"),
            flat,
            matrix,
            matrix,
            matrix,
            matrix,
            flat,
            matrix,
            matrix,
            matrix,
            token_spec,
        ),
        out_specs=(
            token_spec,
            token_spec,
            token_spec,
            token_spec,
            flat,
            matrix,
            matrix,
            matrix,
            matrix,
            flat,
            matrix,
            matrix,
            matrix,
        ),
        check_vma=False,
    )
```

```python
import functools
import math

import jax
import jax.numpy as jnp
from jax import lax
from jax.experimental import pallas as pl
from jax.experimental.pallas import tpu as pltpu
from jax.sharding import PartitionSpec as P

epsilon = 1e-05
MESH = pl.DeviceIdType.MESH
Z = 4
VMEM_LIMIT = 64 * 2**20 - 2**18
bf16 = jnp.bfloat16
f32 = jnp.float32


def dot(left, right):
    return jnp.dot(left, right, preferred_element_type=f32)


def contract_last(left, right):
    return lax.dot_general(left, right, (((1,), (1,)), ((), ())), preferred_element_type=f32)


def contract_first(left, right):
    return lax.dot_general(left, right, (((0,), (0,)), ((), ())), preferred_element_type=f32)


class Arrival:
    def __init__(self, copy):
        self.copy, self.waited, self.left = copy, False, False

    def wait(self):
        if not self.waited:
            self.waited = True
            self.copy.wait_recv()

    def wait_sent(self):
        if not self.left:
            self.left = True
            self.copy.wait_send()


class Links:
    def __init__(self, send, recv):
        self.send, self.recv, self.sent, self.count = send, recv, [], 0
        self.s, self.f = lax.axis_index("seq"), lax.axis_index("fsdp")

    def greet(self, masks):
        barrier = pltpu.get_barrier_semaphore()
        for a, b in masks:
            pl.semaphore_signal(
                barrier, inc=1, device_id=(self.s ^ a, self.f ^ b), device_id_type=MESH
            )
        pl.semaphore_wait(barrier, len(masks))

    def copy(self, source, target, device):
        self.count += 1
        return pltpu.make_async_remote_copy(
            src_ref=source,
            dst_ref=target,
            send_sem=self.send.at[self.count - 1],
            recv_sem=self.recv.at[self.count - 1],
            device_id=device,
            device_id_type=MESH,
        )

    def start(self, source, target, mask):
        copy = self.copy(source, target, (self.s ^ mask[0], self.f ^ mask[1]))
        copy.start()
        self.sent.append(Arrival(copy))
        return self.sent[-1]

    def pass_on(self, block, mask):
        return self.start(block, block, mask)

    def finish(self):
        for arrival in self.sent:
            arrival.wait()
        for arrival in self.sent:
            arrival.wait_sent()


class Local:
    def __init__(self, sems, pairs, base=0):
        self.copies = [
            pltpu.make_async_copy(a, b, sems.at[base + i]) for i, (a, b) in enumerate(pairs)
        ]
        self.open = set(range(len(pairs)))
        for copy in self.copies:
            copy.start()

    def wait(self, *which):
        for i in which or sorted(self.open):
            self.open.discard(i)
            self.copies[i].wait()


def row_loop(rows, step, body):
    block_loop(1, rows, step, lambda i, part: body(part))


def block_loop(n, rows, step, body):
    if rows % step:
        for i in range(n):
            body(i, slice(0, rows))
        return
    steps = rows // step

    @pl.loop(0, n * steps)
    def _(k):
        body(k // steps, pl.ds(pl.multiple_of(lax.rem(k, steps) * step, step), step))


def communicate(
    body, args, outs, copies, collective_id, in_vmem=False, out_vmem=False, scratch=(), kept=1
):
    def specs(inside, n):
        inside = [inside] * n if isinstance(inside, bool) else inside
        return [pl.BlockSpec(memory_space=pltpu.VMEM if i else pl.ANY) for i in inside]

    return pl.pallas_call(
        body,
        out_shape=outs,
        in_specs=specs(in_vmem, len(args)),
        out_specs=specs(out_vmem, len(outs)),
        scratch_shapes=[
            pltpu.SemaphoreType.DMA((copies,)),
            pltpu.SemaphoreType.DMA((copies,)),
            pltpu.SemaphoreType.DMA((kept,)),
            *scratch,
        ],
        compiler_params=pltpu.CompilerParams(
            collective_id=collective_id, has_side_effects=True, vmem_limit_bytes=VMEM_LIMIT
        ),
    )(*args)


def shape(dims, kind=bf16):
    return jax.ShapeDtypeStruct(dims, kind)


class Line:
    def __init__(self, links, here, h, FH, forward):
        self.links, self.here, self.h, self.FH, self.forward = links, here, h, FH, forward
        self.right, self.left, self.pending = [], [], []
        self.settled = set()

    def step(self, j):
        h, FH = self.h, self.FH
        rights = [
            self.links.copy(block, block, (self.links.s, self.links.f + 2))
            for block in self.here(lax.max(h - j, 0))
        ]
        lefts = [
            self.links.copy(block, block, (self.links.s, self.links.f - 2))
            for block in self.here(lax.min(h + j, FH - 1))
        ]
        for i in range(len(rights)):

            @pl.when((h >= j) & (h < FH - 1))
            def _():
                rights[i].start()

            @pl.when((h + j < FH) & (h > 0))
            def _():
                lefts[i].start()

        self.right.append(rights)
        self.left.append(lefts)

    def arrived(self, j):
        h, FH = self.h, self.FH
        up = self.here(lax.max(h - 1 - j, 0))
        down = self.here(lax.min(h + 1 + j, FH - 1))
        for i in range(len(up)):
            for blocks, copies, there in (
                (up, self.right[j], h - 1 - j >= 0),
                (down, self.left[j], h + 1 + j < FH),
            ):
                a, b = self.forward
                on = self.links.copy(blocks[i], blocks[i], (self.links.s ^ a, self.links.f ^ b))
                self.pending.append((j, on, there))

                @pl.when(there)
                def _():
                    copies[i].wait_recv()
                    on.start()

    def came(self, j):
        self.settled.add(j)
        for step, on, there in self.pending:
            if step == j:

                @pl.when(there)
                def _():
                    on.wait_recv()

    def finish(self):
        h, FH = self.h, self.FH
        for j in range(FH - 1):
            if j not in self.settled:
                self.came(j)
        for _, on, there in self.pending:

            @pl.when(there)
            def _():
                on.wait_send()

        for j in range(FH - 1):
            for i in range(len(self.right[j])):

                @pl.when((h >= j) & (h < FH - 1))
                def _():
                    self.right[j][i].wait_send()

                @pl.when((h + j < FH) & (h > 0))
                def _():
                    self.left[j][i].wait_send()


def rows_of(ref):
    return ref[...].reshape(-1, ref.shape[-1])


def rotation(table):
    half = table.shape[-1] // 2
    swapped = pltpu.roll(table, half, 1)
    first = lax.broadcasted_iota(jnp.int32, table.shape, 1) < half
    return jnp.where(first, table, swapped), jnp.where(first, -swapped, table)


def turn(vector, factors):
    return vector * factors[0] + pltpu.roll(vector, vector.shape[-1] // 2, 1) * factors[1]


class RowSum:
    def __init__(self, links, parts, from_core, from_x):
        self.links, self.parts, self.from_core, self.from_x = links, parts, from_core, from_x
        self.x, self.core, self.sent = links.s // 2, links.s % 2, []

    def far(self):
        x, core = 1 - self.x, 1 - self.core
        self.to_far = self.links.start(self.parts.at[x, core], self.from_core.at[x], (1, 0))
        self.sent.append(self.to_far)

    def near(self):
        x, core = self.x, 1 - self.core
        self.to_near = self.links.start(self.parts.at[x, core], self.from_core.at[x], (1, 0))
        self.sent.append(self.to_near)

    def middle(self):
        self.to_far.wait()
        x, core = 1 - self.x, self.core

        def add(rows):
            total = self.parts[x, core, rows].astype(f32) + self.from_core[x, rows].astype(f32)
            self.parts[x, core, rows] = total.astype(bf16)

        row_loop(self.from_x.shape[0], 16, add)
        self.across = self.links.start(self.parts.at[x, core], self.from_x, (2, 0))
        self.sent.append(self.across)

    def arrive(self):
        self.to_near.wait()
        self.across.wait()

    def total(self, rows):
        return (
            self.parts[self.x, self.core, rows].astype(f32)
            + self.from_core[self.x, rows].astype(f32)
            + self.from_x[rows].astype(f32)
        )


class LineSum:
    def __init__(self, links, h, parts, from_core, chain, extra):
        self.links, self.h, self.parts = links, h, parts
        self.from_core, self.chain, self.extra = from_core, chain, extra
        self.core, self.T = links.s % 2, extra.shape[0]
        self.by_core, self.right, self.left, self.end = {}, {}, {}, {}
        s, f = links.s, links.f
        for d in range(Z):
            block = parts.at[d, self.core]
            self.right[d] = links.copy(block, chain.at[d], (s, f + 2))
            self.left[d] = links.copy(block, chain.at[d], (s, f - 2))
            self.end[d] = links.copy(block, extra, (s, f - 2))

    def send_core(self, d):
        self.by_core[d] = self.links.start(
            self.parts.at[d, 1 - self.core], self.from_core.at[d], (1, 0)
        )

    def add(self, d, chained):
        def add(rows):
            total = self.parts[d, self.core, rows].astype(f32)
            total += self.from_core[d, rows].astype(f32)
            if chained:
                total += self.chain[d, rows].astype(f32)
            self.parts[d, self.core, rows] = total.astype(bf16)

        row_loop(self.T, 16, add)

    def stage(self, k, places):
        h = self.h
        for d in places:
            self.by_core[d].wait()
            rightward, leftward = (h < d) & (h == k), (h > d) & (h == Z - 1 - k)

            @pl.when(rightward)
            def _():
                if k:
                    self.right[d].wait_recv()
                self.add(d, k > 0)
                self.right[d].start()

            @pl.when(leftward)
            def _():
                if k:
                    self.left[d].wait_recv()
                self.add(d, k > 0)

            @pl.when(leftward & (h > d + 1))
            def _():
                self.left[d].start()

            @pl.when(leftward & (h == d + 1))
            def _():
                self.end[d].start()

    def arrive(self):
        h = self.h
        for d in range(Z):
            self.by_core[d].wait()
            if d > 0:

                @pl.when(h == d)
                def _():
                    self.right[d].wait_recv()

            else:

                @pl.when(h == 0)
                def _():
                    self.chain[0] = jnp.zeros_like(self.chain[0])

            if d < Z - 1:

                @pl.when(h == d)
                def _():
                    self.end[d].wait_recv()

            else:

                @pl.when(h == Z - 1)
                def _():
                    self.extra[...] = jnp.zeros_like(self.extra)

    def total(self, rows):
        return (
            self.parts[self.h, self.core, rows].astype(f32)
            + self.from_core[self.h, rows].astype(f32)
            + self.chain[self.h, rows].astype(f32)
            + self.extra[rows].astype(f32)
        )

    def settle(self):
        h = self.h
        for d in range(Z):
            self.by_core[d].wait_sent()

            @pl.when(h < d)
            def _():
                self.right[d].wait_send()

            @pl.when(h > d + 1)
            def _():
                self.left[d].wait_send()

            @pl.when(h == d + 1)
            def _():
                self.end[d].wait_send()


class LeadFirst:
    def __init__(self, ref):
        self.ref, self.n, self.rows = ref, ref.shape[0], ref.shape[3]

    def half(self, l):
        return self.ref.at[:, :, l]

    def both(self, w):
        return self.ref.at[:, w]

    def part(self, w, l):
        return self.ref.at[:, w, l]

    def item(self, i, w, l):
        return self.ref.at[i, w, l]

    def got(self, ref, i, w):
        return ref.at[i, w]


class Natural:
    def __init__(self, ref):
        self.ref, self.n, self.rows = ref, ref.shape[2], ref.shape[4]

    def half(self, l):
        return self.ref.at[:, :, :, l]

    def both(self, w):
        return self.ref.at[w % 2, w // 2]

    def part(self, w, l):
        return self.ref.at[w % 2, w // 2, :, l]

    def item(self, i, w, l):
        return self.ref.at[w % 2, w // 2, i, l]

    def got(self, ref, i, w):
        return ref.at[w % 2, w // 2, i]


class PieceByL:
    def __init__(self, links, view, by_l, by_w, w, masks):
        self.links, self.view, self.by_l, self.by_w = links, view, by_l, by_w
        self.w, self.masks, self.l = w, masks, links.f % 2
        self.first = links.start(view.half(1 - self.l), by_l, (0, 1))

    def partial(self, i, w, rows):
        total = self.view.item(i, w, self.l)[rows].astype(f32)
        return total + self.view.got(self.by_l, i, w)[rows].astype(f32)

    def place(self, k, slot=None):
        w = self.w ^ k

        def add(i, rows):
            total = self.partial(i, w, rows)
            if slot is not None:
                total += self.by_w[slot, i, rows].astype(f32)
            self.view.item(i, w, self.l)[rows] = total.astype(bf16)

        block_loop(self.view.n, self.view.rows, 16, add)

    def middle(self):
        self.first.wait()
        self.second = []
        for k in range(1, len(self.masks)):
            self.place(k)
            block = self.view.part(self.w ^ k, self.l)
            self.second.append(self.links.start(block, self.by_w.at[k - 1], self.masks[k]))

    def arrive(self):
        for arrival in self.second:
            arrival.wait()

    def last(self, store=None):
        self.arrive()

        def add(i, rows):
            total = self.partial(i, self.w, rows)
            for k in self.slots():
                total += self.by_w[k, i, rows].astype(f32)
            if store is None:
                self.view.item(i, self.w, self.l)[rows] = total.astype(bf16)
            else:
                store(i, rows, total)

        block_loop(self.view.n, self.view.rows, 16, add)

    def slots(self):
        return range(len(self.masks) - 1)

    def inner(self):
        pass

    def settle(self):
        pass


class PieceAlongZ(PieceByL):
    def __init__(self, links, view, by_l, by_w, w, masks):
        super().__init__(links, view, by_l, by_w, w, masks)
        self.is_inner = (w == 1) | (w == 2)
        device = [(links.s ^ a, links.f ^ b) for a, b in masks]

        def copy(k, slot, to):
            return links.copy(view.part(w ^ k, self.l), by_w.at[slot], device[to])

        self.out = [copy(k, k - 1, 1) for k in (1, 2, 3)]
        self.over = [copy(3, 3, 3), copy(2, 3, 2)]
        self.beside = copy(1, 0, 1)

    def middle(self):
        self.first.wait()

        @pl.when(self.is_inner)
        def _():
            self.place(1)
            self.beside.start()

        @pl.when(jnp.logical_not(self.is_inner))
        def _():
            for k in (2, 3, 1):
                self.place(k)
                self.out[k - 1].start()

    def inner(self):
        @pl.when(self.is_inner)
        def _():
            for k, over in zip((3, 2), self.over):
                self.out[4 - k].wait_recv()
                self.place(k, 4 - k)
                over.start()

    def arrive(self):
        @pl.when(self.is_inner)
        def _():
            self.out[0].wait_recv()
            self.over[0].wait_recv()

        @pl.when(jnp.logical_not(self.is_inner))
        def _():
            self.beside.wait_recv()
            self.over[1].wait_recv()

    def slots(self):
        return (0, 3)

    def settle(self):
        @pl.when(self.is_inner)
        def _():
            for copy in [self.beside] + self.over:
                copy.wait_send()

        @pl.when(jnp.logical_not(self.is_inner))
        def _():
            for copy in self.out:
                copy.wait_send()


def z_piece(links, view, by_l, by_w, w, masks):
    kind = PieceAlongZ if len(masks) == 4 else PieceByL
    return kind(links, view, by_l, by_w, w, masks)


class PieceByW:
    def __init__(self, links, view, by_l, by_w, w, masks):
        self.links, self.view, self.by_l, self.by_w = links, view, by_l, by_w
        self.w, self.masks, self.l = w, masks, links.f % 2
        self.first = [
            links.start(view.both(w ^ k), by_w.at[k - 1], masks[k]) for k in range(1, len(masks))
        ]

    def partial(self, i, l, rows):
        total = self.view.item(i, self.w, l)[rows].astype(f32)
        for k in range(1, len(self.masks)):
            total += self.by_w[k - 1, i, l, rows].astype(f32)
        return total

    def middle(self):
        for arrival in self.first:
            arrival.wait()
        l = 1 - self.l

        def add(i, rows):
            self.view.item(i, self.w, l)[rows] = self.partial(i, l, rows).astype(bf16)

        block_loop(self.view.n, self.view.rows, 16, add)
        self.second = self.links.start(self.view.part(self.w, l), self.by_l, (0, 1))

    def last(self, store=None):
        self.second.wait()

        def add(i, rows):
            total = self.partial(i, self.l, rows) + self.by_l[i, rows].astype(f32)
            if store is None:
                self.view.item(i, self.w, self.l)[rows] = total.astype(bf16)
            else:
                store(i, rows, total)

        block_loop(self.view.n, self.view.rows, 16, add)


def by_l_scratch(n, W, rows, width):
    return [pltpu.VMEM((n, W, rows, width), bf16), pltpu.VMEM((W - 1, n, rows, width), bf16)]


def z_scratch(n, W, rows, width):
    slots = 4 if W == 4 else W - 1
    return [pltpu.VMEM((n, W, rows, width), bf16), pltpu.VMEM((slots, n, rows, width), bf16)]


def by_w_scratch(n, W, rows, width):
    return [pltpu.VMEM((n, rows, width), bf16), pltpu.VMEM((W - 1, n, 2, rows, width), bf16)]


def norm_back(grad_normed, inputs, gain):
    inverse = lax.rsqrt(jnp.mean(inputs * inputs, -1, keepdims=True) + epsilon)
    scaled = grad_normed * gain
    inner_sum = jnp.sum(scaled * inputs, -1, keepdims=True)
    grad = inverse * scaled - inputs * (inverse**3 * inner_sum / inputs.shape[-1])
    return grad, inputs * inverse


def layer_kernel(FH, copies, *refs):
    tok, wq_in, wk_in, wv_in, wo_in, gate_in, up_in, down_in, cot_in = refs[:9]
    segments, positions, gains_in = refs[9:12]
    output, keys, values, grad_tokens, gate_out, up_out, down_out = refs[12:19]
    wq_out, wo_out, wk_out, wv_out, gains_out = refs[19:24]
    both_own, normed_kept, side_kept, o_kept = refs[24:28]
    send, recv, here, both, down, q_w, kv_w, o_w = refs[28:36]
    residual, grad_in, gains, gain_sums, grad_row = refs[36:41]
    grad_down, o_sum, kv_sum, q_own = refs[41:45]
    back_bufs, out_bufs = refs[45:49], refs[49:53]
    normed, cot, grad_both, tab, grad_k, grad_v, bias, gain_block = refs[53:61]
    bufs = refs[61:]
    links = Links(send, recv)
    s, f = links.s, links.f
    x, core = s // 2, s % 2
    e, h, l = f // 8, (f // 2) % Z, f % 2
    t = 2 * h + core
    T, D = residual.shape
    S, F, rows_w, HC = q_w.shape
    row_len, head = grad_k.shape
    heads = HC // head
    E, FC = both.shape[2], both.shape[6] // 2
    W, TG = 2 * E, 2 * Z
    w = 2 * e + x
    two = 2 * T
    cut = D // 2
    scale = head ** (-0.5)
    group_masks = [(a, 2 * m) for m in range(Z) for a in (0, 1)][1:]
    w_masks = [(2 * (j % 2), 8 * (j // 2)) for j in range(W)]
    back = LineSum(links, h, *back_bufs)
    out = LineSum(links, h, *out_bufs)
    back_parts, out_parts = back.parts, out.parts
    tok_g = grad_row
    spots = {}
    for name, width in (("attended", HC), ("q", HC), ("k", head), ("v", head), ("grad", HC)):
        base = sum(n for _, n in spots.values())
        spots[name] = (base, width)
    side_width = spots["grad"][0]

    def column(name, first=0, width=None):
        base, full_width = spots[name]
        return pl.ds(base + first, width or full_width)

    def block(where, name, r, first=0, width=None):
        return where[r // 2, r % 2, :, column(name, first, width)]

    def to_x(ref, j):
        return ref.at[(w ^ j) % 2, :, (w ^ j) // 2]

    def whole(where, name, first=0, width=None):
        return where[:, :, :, column(name, first, width)].reshape(row_len, -1)

    links.greet(
        [(a, 0) for a in (1, 2, 3)]
        + [(0, 1)]
        + [(0, 2 * k) for k in range(1, FH)]
        + [(1, 2 * m) for m in range(1, Z)]
        + [mask for mask in w_masks if mask[0] and mask[1]]
    )
    place = lax.broadcasted_iota(jnp.int32, (8, head), 0)
    lane = lax.broadcasted_iota(jnp.int32, (8, head), 1)
    pick = jnp.where((place == lane) & (place < 2), 1.0, 0.0)
    row_at = lax.broadcasted_iota(jnp.int32, (8, rows_w), 0)
    both_gains = [jnp.broadcast_to(gains_in[i : i + 1].astype(f32), (8, rows_w)) for i in (0, 1)]
    gain_rows = jnp.where(row_at == 0, both_gains[0], jnp.where(row_at == 1, both_gains[1], 0.0))
    gain_block[...] = contract_first(gain_rows, pick).astype(bf16)
    local = Local(
        here,
        [
            (wq_in.at[:, pl.ds(pl.multiple_of(s * HC, HC), HC)], q_w.at[s, f]),
            (wk_in, kv_w.at[s, f, :, pl.ds(0, head)]),
            (wv_in, kv_w.at[s, f, :, pl.ds(head, head)]),
            (gain_block, kv_w.at[s, f, :, pl.ds(2 * head, head)]),
            (wo_in, o_w.at[f]),
            (tok, tok_g.at[s]),
            (down_in, down.at[0, w, l]),
            (cot_in, cot.at[h, core]),
        ],
    )
    first = [
        links.start(
            wq_in.at[:, pl.ds(pl.multiple_of((s ^ a) * HC, HC), HC)], q_w.at[s, f], (a, 0)
        )
        for a in (1, 2, 3)
    ]
    quarter = FC * TG // S
    natural = Local(
        here,
        [
            (r.at[:, pl.ds(i * quarter, quarter)], back_parts.at[i, j, pl.ds(0, rows_w), pl.ds(0, quarter)])
            for j, r in enumerate((gate_in, up_in))
            for i in range(S)
        ],
        9,
    )
    local.wait(1, 2, 3, 4)
    along_z = (f // 2, FH, (0, 1))
    kv_line = Line(links, lambda place: [kv_w.at[s, 2 * place + l]], *along_z)
    o_line = Line(links, lambda place: [o_w.at[2 * place + l]], *along_z)
    q_line = Line(links, lambda place: [q_w.at[:, 2 * place + l]], *along_z)
    kv_line.step(0)
    kv_y = links.pass_on(kv_w.at[s, f], (0, 1))
    o_line.step(0)
    needed = [links.pass_on(o_w.at[f], (0, 1))]
    local.wait(0)
    for arrival in first:
        arrival.wait()
    q_line.step(0)
    needed.append(links.pass_on(q_w.at[:, f], (0, 1)))
    at = jnp.broadcast_to(positions[...].astype(f32), (T, T))
    frequency = lax.broadcasted_iota(jnp.int32, (1, head), 1)
    frequency = lax.rem(frequency, head // 2).astype(f32) * (-2.0 / head * math.log(10000.0))
    angle = jnp.transpose(at)[:, :1] * jnp.exp(frequency)
    first_half = lax.broadcasted_iota(jnp.int32, (T, head), 1) < head // 2
    tab[s] = jnp.where(first_half, jnp.cos(angle), jnp.sin(angle))
    tok_x = links.start(tok, tok_g.at[s], (2, 0))
    needed.append(links.start(tok, tok_g.at[s], (1, 0)))
    needed += [links.pass_on(tab.at[s], (a, 0)) for a in (1, 2, 3)]
    ffn_in = {}
    lanes = 128
    whole_tiles = FC // lanes

    def blocks_of(ref, at_h, c):
        width = 2 * FC // W // 2
        parts = []
        for at_e in range(E):
            for at_x in (0, 1):
                base = (at_e * Z + at_h) * width
                parts.append(ref(2 * at_x + c)[:, base : base + width])
        return jnp.concatenate(parts, 1)

    def side_by_side(gate_units, up_units):
        tiles = []
        for j in range(whole_tiles):
            part = slice(j * lanes, (j + 1) * lanes)
            tiles += [gate_units[:, part], up_units[:, part]]
        rest = slice(whole_tiles * lanes, FC)
        return jnp.concatenate(tiles + [gate_units[:, rest], up_units[:, rest]], 1)

    def sent_blocks(at_h, c):
        return grad_both.at[at_h, pl.ds(pl.multiple_of(c * rows_w, rows_w), rows_w)]

    ids = jnp.broadcast_to(segments[...].astype(f32), (lanes, row_len))
    own_ids = jnp.transpose(ids)[:, :1]
    for r in range(S):
        rows = slice(r * T, (r + 1) * T)
        mine_at = lax.broadcasted_iota(jnp.int32, (T, row_len), 0) + r * T
        seen_at = lax.broadcasted_iota(jnp.int32, (T, row_len), 1)
        allowed = (seen_at <= mine_at) & (ids[:1] == own_ids[rows])
        bias[rows] = jnp.where(allowed, 0.0, -1e30).astype(bf16)
    natural.wait()
    columns_of = [
        [back_parts[i, j, :rows_w, :quarter].astype(f32) for i in range(S)] for j in (0, 1)
    ]
    for at_h in range(Z):
        for c in (0, 1):
            units = [blocks_of(lambda i: columns_of[j][i], at_h, c) for j in (0, 1)]
            grad_both[at_h, c * rows_w : (c + 1) * rows_w] = side_by_side(*units).astype(bf16)
    own_block = Local(here, [(sent_blocks(h, core), both.at[x, core, e, h, l])], 17)

    def to_group(m):
        for a in (0, 1):
            if (a, m) != (0, 0):
                place = (x, core, e, h, l)
                source = sent_blocks(h ^ m, core ^ a)
                ffn_in[a, m] = links.start(source, both.at[place], (a, 2 * m))

    arriving = []

    class Spread:
        def __init__(self, near, second_w, second_y):
            self.near, self.second_w, self.second_y = near, second_w, second_y

        def by_w(self):
            self.came_w = [links.pass_on(self.near, mask) for mask in w_masks[1:]]

        def by_y(self):
            self.came_y = links.pass_on(self.near, (0, 1))

        def on_w(self):
            self.came_y.wait()
            arriving.extend(links.pass_on(self.second_w, mask) for mask in w_masks[1:])

        def on_y(self):
            for j, arrival in enumerate(self.came_w):
                arrival.wait()
                arriving.append(links.pass_on(self.second_y(j + 1), (0, 1)))

    def spread_of(m):
        def second_y(j):
            return to_x(both, j).at[0, h ^ m, l]

        here_q = to_x(both, 0)
        return Spread(here_q.at[:, h ^ m, l], here_q.at[1, h ^ m, 1 - l], second_y)

    low_half, high_half = pl.ds(0, cut), pl.ds(cut, D - cut)
    spread_down = Spread(
        down.at[0, w, l],
        down.at[0, w, 1 - l, :, high_half],
        lambda j: down.at[0, w ^ j, l, :, low_half],
    )
    to_group(0)
    local.wait(6)
    spread_down.by_w()
    for j in range(FH - 1):
        for way in (kv_line, o_line, q_line):
            way.arrived(j)
            if j + 1 < FH - 1:
                way.step(j + 1)
        if j == 0:
            tok_x.wait()
            needed.append(links.pass_on(tok_g.at[s ^ 2], (1, 0)))
            own_block.wait()
            ffn_in[1, 0].wait()
            spreads = [spread_of(m) for m in range(Z)]
            spreads[0].by_w()
    kv_y.wait()
    kv_line.finish()
    kv_x = links.pass_on(kv_w.at[s], (2, 0))
    needed.append(links.pass_on(kv_w.at[s], (1, 0)))
    for m in range(1, Z):
        to_group(m)
    spread_down.by_y()
    spreads[0].by_y()
    cot_line = Line(links, lambda place: [cot.at[place, core]], h, Z, (1, 0))
    kv_x.wait()
    needed.append(links.pass_on(kv_w.at[s ^ 2], (1, 0)))
    for arrival in needed:
        arrival.wait()
    o_line.finish()
    q_line.finish()
    local.wait(5)
    kept_o = Local(here, [(o_w, o_kept)], 18)

    normed_one, side = out_parts.at[pl.ds(0, 2)], out_parts.at[pl.ds(2, 2)]
    kv_full = rows_of(kv_w)
    gains[...] = contract_last(pick.astype(bf16), kv_full[:, 2 * head :])

    def norm_one(i, rows):
        value = tok_g[i, rows].astype(f32)
        inverse = lax.rsqrt(jnp.mean(value * value, -1, keepdims=True) + epsilon)
        normed_one[i // 2, lax.rem(i, 2), rows] = (value * inverse * gains[0:1]).astype(bf16)

    block_loop(S, T, 16, norm_one)
    local.wait(7)
    cot_line.step(0)
    arriving.append(links.pass_on(cot.at[h, core], (1, 0)))
    factors = rotation(rows_of(tab))

    def put(name, first, value):
        columns = column(name, first, value.shape[1])
        side[:, :, :, columns] = value.astype(bf16).reshape(2, 2, T, -1)

    kv = dot(rows_of(normed_one), kv_full[:, : 2 * head])
    put("k", 0, turn(kv[:, :head], factors))
    put("v", 0, kv[:, head:])
    for n in range(0, heads, 2):
        columns = slice(n * head, (n + 2) * head)
        pair = dot(rows_of(normed_one), q_w[:, :, :, columns].reshape(D, 2 * head))
        for j in (0, 1):
            put("q", (n + j) * head, turn(pair[:, j * head : (j + 1) * head], factors))
    results = [
        Local(
            here,
            [
                (side.at[x, core, :, column("k")], keys),
                (side.at[x, core, :, column("v")], values),
            ],
            21,
        )
    ]
    for r in range(S):
        rows, seen = slice(r * T, (r + 1) * T), slice(0, (r + 1) * T)
        keys_seen, values_seen = whole(side, "k")[seen], whole(side, "v")[seen]
        for n in range(heads):
            query = block(side, "q", r, n * head, head)
            scores = contract_last(query, keys_seen) * scale + bias[rows, seen].astype(f32)
            scores = jnp.exp(scores - jnp.max(scores, -1, keepdims=True))
            probs = (scores / jnp.sum(scores, -1, keepdims=True)).astype(bf16)
            side[r // 2, r % 2, :, column("attended", n * head, head)] = dot(
                probs, values_seen
            ).astype(bf16)
    spread_down.on_y()

    first_two = pl.ds(0, 2)
    row_bufs = (back_parts.at[first_two], back.from_core.at[first_two], back.chain.at[0])
    parts = RowSum(links, *row_bufs)

    def project(x_to):
        rows = side[x_to, :, :, column("attended")].reshape(two, HC)
        for n in range(0, D, HC):
            columns = slice(n, n + HC)
            total = dot(rows, o_w[:, :, columns].reshape(HC, HC))
            parts.parts[x_to, :, :, columns] = total.astype(bf16).reshape(2, T, HC)

    project(1 - x)
    parts.far()
    project(x)
    parts.near()
    parts.middle()
    spread_down.on_w()
    spreads[0].on_y()
    spreads[0].on_w()
    for m in range(1, Z):
        for a in (0, 1):
            ffn_in[a, m].wait()
        spreads[m].by_y()
        spreads[m].by_w()
    cot_line.arrived(0)
    cot_line.step(1)
    kept = Local(
        here, [(normed_one, normed_kept), (side.at[:, :, :, pl.ds(0, side_width)], side_kept)], 19
    )
    parts.arrive()

    def norm_two(rows):
        total = tok_g[s, rows].astype(f32) + parts.total(rows)
        residual[rows] = total
        inverse = lax.rsqrt(jnp.mean(total * total, -1, keepdims=True) + epsilon)
        normed[h, core, rows] = (total * inverse * gains[1:2]).astype(bf16)

    row_loop(T, 16, norm_two)
    normed_line = Line(links, lambda place: [normed.at[place, core]], h, Z, (1, 0))
    normed_line.step(0)
    beside = [links.pass_on(normed.at[h, core], (1, 0))]
    cot_line.arrived(1)
    cot_line.step(2)
    spreads[1].on_y()
    spreads[1].on_w()
    normed_line.arrived(0)
    normed_line.step(1)
    for m in range(2, Z):
        spreads[m].on_y()
        spreads[m].on_w()
    normed_line.arrived(1)
    normed_line.step(2)
    results[0].wait()
    kept_o.wait()
    kept.wait()
    for arrival in arriving:
        arrival.wait()
    for arrival in links.sent:
        arrival.wait_sent()

    slot = D // 2
    lane_is_low = lax.broadcasted_iota(jnp.int32, (two, lanes), 1) < lanes // 2

    def hidden_of(d):
        n = normed[d].reshape(two, D)
        c = cot[d].reshape(two, D)
        weights = down[...].reshape(FC, D)

        def units(first, width, gate_proj, up_proj, grad_inner):
            sig = jax.nn.sigmoid(gate_proj)
            silu = gate_proj * sig
            spot = pl.ds(pl.multiple_of(d // 2 * slot + first, lanes), width)
            hidden = (silu * up_proj).astype(bf16)[:, :width]
            o_w[pl.ds(d % 2 * (F // 2), F // 2), :, spot] = hidden.reshape(F // 2, rows_w, width)
            slope = sig * (1.0 + gate_proj * (1.0 - sig))
            return (grad_inner * up_proj * slope).astype(bf16), (grad_inner * silu).astype(bf16)

        for first in range(0, FC, 2 * lanes):
            width = min(2 * lanes, FC - first)
            rows = weights[first : first + width]
            if width % lanes:
                rows = jnp.concatenate([rows, rows[width - lanes // 2 :]], 0)
            grad_inner = contract_last(c, rows)
            for i in range(0, width, lanes):
                base = 2 * (first + i)
                columns = (slice(None),) * 6 + (slice(base, min(base + 2 * lanes, 2 * FC)),)
                proj = dot(n, both[columns].reshape(D, -1))
                part = slice(i, i + lanes)
                if i + lanes <= width:
                    grad_gate, grad_up = units(
                        first + i,
                        lanes,
                        proj[:, :lanes],
                        proj[:, lanes:],
                        grad_inner[:, part],
                    )
                    grad_both[d, :, base : base + lanes] = grad_gate
                    grad_both[d, :, base + lanes : base + 2 * lanes] = grad_up
                else:
                    mixed = proj
                    turned = pltpu.roll(mixed, lanes // 2, 1)
                    grad_gate, grad_up = units(
                        first + i,
                        lanes // 2,
                        jnp.where(lane_is_low, mixed, turned),
                        jnp.where(lane_is_low, turned, mixed),
                        grad_inner[:, part],
                    )
                    grad_both[d, :, base : base + lanes] = jnp.where(
                        lane_is_low, grad_gate, grad_up
                    )

    def back_of(d):
        for i in range(S):
            columns = slice(i * F * rows_w, (i + 1) * F * rows_w)
            total = contract_last(grad_both[d], both[i // 2, i % 2].reshape(-1, 2 * FC))
            back_parts[d, :, :, columns] = total.astype(bf16).reshape(2, T, -1)
        back.send_core(d)

    def out_of(d):
        spot = slice(d // 2 * slot, d // 2 * slot + FC)
        hidden = o_w[pl.ds(d % 2 * (F // 2), F // 2), :, spot].reshape(two, FC)
        for i in range(0, D, 512):
            columns = slice(i, i + 512)
            total = dot(hidden, down[:, :, :, :, columns].reshape(FC, 512))
            out_parts[d, :, :, columns] = total.astype(bf16).reshape(2, T, -1)
        out.send_core(d)

    for arrival in beside:
        arrival.wait()
    hidden_of(h)
    for line in (cot_line, normed_line):
        line.came(0)
    hidden_of(h ^ 1)
    for line in (cot_line, normed_line):
        line.came(1)
    hidden_of(h ^ 2)
    for line in (cot_line, normed_line):
        line.arrived(2)
    for line in (cot_line, normed_line):
        line.came(2)
    hidden_of(h ^ 3)
    back_of(3)
    back_of(0)
    back.stage(0, (3, 0))
    back_of(2)
    back_of(1)
    back.stage(0, (2, 1))
    for line in (cot_line, normed_line):
        line.finish()
    ffn = {}
    width = F * rows_w
    for c in (0, 1):
        for i in (0, 1):
            base = (2 * i + c) * width
            turned = normed[:, :, :, base : base + width].reshape(4 * two, width)
            for columns in [slice(n, min(n + 3 * lanes, 2 * FC)) for n in range(0, 2 * FC, 3 * lanes)]:
                total = contract_first(turned, grad_both[:, :, columns].reshape(4 * two, -1))
                both[i, c, :, :, :, :, columns] = total.astype(bf16).reshape(E, Z, 2, rows_w, -1)
        if c == 0:
            ffn["both", 0] = PieceByL(links, Natural(both.at[:, 0]), *bufs[4:6], w, w_masks)
            back.stage(1, (3, 0))
    ffn["both", 1] = PieceByW(links, Natural(both.at[:, 1]), *bufs[6:8], w, w_masks)
    for d in (3, 0, 2, 1):
        out_of(d)
    quarters = [pl.ds(i * (cut // 2), cut // 2) for i in (0, 1)]
    inner = [o_w[:, :, i * slot : i * slot + FC].reshape(2 * two, FC) for i in (0, 1)]
    for i in range(0, D, 256):
        columns = slice(i, i + 256)
        total = contract_first(inner[0], cot[0:2, :, :, columns].reshape(2 * two, 256))
        total += contract_first(inner[1], cot[2:4, :, :, columns].reshape(2 * two, 256))
        down[:, :, :, :, columns] = total.astype(bf16).reshape(1, W, 2, -1, 256)
    def down_low(i):
        view = LeadFirst(down.at[:, :, :, :, quarters[i]])
        ffn["down_low", i] = PieceByL(
            links, view, bufs[0].at[:, :, :, quarters[i]], bufs[1].at[:, :, :, quarters[i]], w, w_masks
        )

    down_low(0)
    back.stage(1, (2, 1))
    back.stage(2, (3, 0))
    out.stage(0, (3, 0, 2, 1))

    cot_own, tok_own = normed.at[2, 0], normed.at[2, 1]
    own = Local(here, [(cot_in, cot_own), (tok, tok_own)], 23)
    gain_sums[...] = jnp.zeros_like(gain_sums)
    own.wait()
    back.arrive()

    def second_norm(rows):
        grad_normed = back.total(rows)
        grad, unit = norm_back(grad_normed, residual[rows], gains[1:2])
        grad = grad + cot_own[rows].astype(f32)
        grad_in[rows] = grad
        grad_row[s, rows] = grad.astype(bf16)
        gain_sums[1:2] += jnp.sum(grad_normed * unit, 0, keepdims=True)

    row_loop(T, 16, second_norm)
    row_x = links.pass_on(grad_row.at[s], (3, 0))
    row_c = links.pass_on(grad_row.at[s], (1, 0))

    last_two = pl.ds(2, 2)
    side = cot.at[first_two]
    normed_one = normed.at[first_two]
    grad_side = cot.at[last_two]
    loads = Local(
        here,
        [
            (o_kept, o_w),
            (side_kept, cot.at[first_two, :, :, pl.ds(0, side_width)]),
            (normed_kept, normed_one),
        ],
        25,
    )
    ffn["both", 1].middle()
    ffn["both", 0].middle()
    down_low(1)
    row_x.wait()
    row_cc = links.pass_on(grad_row.at[s ^ 3], (1, 0))
    out.stage(1, (3, 0))
    row_c.wait()
    row_cc.wait()
    loads.wait()
    per = 2 * head // rows_w
    for n in range(0, heads, 2):
        wo = o_w[n // 2 * per : (n // 2 + 1) * per].reshape(2 * head, D)
        pair = contract_last(rows_of(grad_row), wo).astype(bf16)
        side[:, :, :, column("grad", n * head, 2 * head)] = pair.reshape(2, 2, T, 2 * head)
    for i in range(0, D, HC):
        columns = slice(i, i + HC)
        grad_columns = grad_row[:, :, columns].reshape(row_len, HC)
        total = contract_first(whole(side, "attended"), grad_columns)
        o_w[:, :, columns] = total.astype(bf16).reshape(F, rows_w, HC)
    place_z, z_masks = f // 2, [(0, 2 * j) for j in range(FH)]
    o_view = LeadFirst(o_w.reshape(1, FH, 2, rows_w, D))
    o_piece = z_piece(links, o_view, *bufs[8:10], place_z, z_masks)

    owned = []

    def give(c):
        ffn["both", c].last()
        for source in (0, 1):
            for m in range(Z):
                if (source, m) != (c, 0):
                    copy = links.copy(
                        both.at[x, c, e, h ^ m, l], both_own.at[2 * h + source], (2 * x + c, f ^ (2 * m))
                    )
                    owned.append((c, source, copy))

                    @pl.when(core == source)
                    def _():
                        copy.start()

    give(1)
    grad_k[...] = jnp.zeros_like(grad_k)
    grad_v[...] = jnp.zeros_like(grad_v)
    factors = rotation(rows_of(tab))
    back_turn = (factors[0], -factors[1])
    for r in range(S):
        rows, seen = slice(r * T, (r + 1) * T), slice(0, (r + 1) * T)
        keys_seen, values_seen = whole(side, "k")[seen], whole(side, "v")[seen]
        for n in range(heads):
            query = block(side, "q", r, n * head, head)
            grad_att = block(side, "grad", r, n * head, head)
            scores = contract_last(query, keys_seen) * scale + bias[rows, seen].astype(f32)
            scores = jnp.exp(scores - jnp.max(scores, -1, keepdims=True))
            probs = scores / jnp.sum(scores, -1, keepdims=True)
            grad_probs = contract_last(grad_att, values_seen)
            delta = jnp.sum(probs * grad_probs, -1, keepdims=True)
            grad_scores = (probs * (grad_probs - delta)).astype(bf16)
            grad_q = dot(grad_scores, keys_seen) * scale
            grad_q = turn(grad_q, (back_turn[0][rows], back_turn[1][rows])).astype(bf16)
            grad_side[r // 2, r % 2, :, n * head : (n + 1) * head] = grad_q
            grad_k[seen] += contract_first(grad_scores, query)
            grad_v[seen] += contract_first(probs.astype(bf16), grad_att)
    grad_key = turn(grad_k[...] * scale, back_turn).astype(bf16)
    grad_side[:, :, :, HC : HC + head] = grad_key.reshape(2, 2, T, head)
    grad_side[:, :, :, HC + head : HC + 2 * head] = grad_v[...].astype(bf16).reshape(2, 2, T, head)
    grad_qkv = slice(0, HC + 2 * head)
    back.settle()
    row = RowSum(links, *row_bufs)
    for cx, go in ((1 - x, row.far), (x, row.near)):
        for i in range(S):
            total = contract_last(grad_side[cx, :, :, :HC].reshape(two, HC), q_w[i].reshape(-1, HC))
            total += contract_last(
                grad_side[cx, :, :, HC : HC + 2 * head].reshape(two, 2 * head),
                kv_w[i, :, :, : 2 * head].reshape(-1, 2 * head),
            )
            columns = slice(i * F * rows_w, (i + 1) * F * rows_w)
            row.parts[cx, :, :, columns] = total.astype(bf16).reshape(2, T, -1)
        go()
    row.middle()
    give(0)
    mine = Local(here, [(both.at[x, core, e, h, l], both_own.at[t])], 28)
    out.stage(1, (2, 1))
    out.stage(2, (3, 0))
    pieces = []
    q_view = q_w.reshape(S, FH, 2, rows_w, HC)
    kv_view = kv_w.reshape(S, FH, 2, rows_w, kv_w.shape[3])

    def q_piece(i):
        one = pl.ds(i, 1)
        spare = (bufs[10].at[one], bufs[11].at[:, one])
        return z_piece(links, LeadFirst(q_view.at[one]), *spare, place_z, z_masks)

    for i in range(S):
        columns = slice(i * F * rows_w, (i + 1) * F * rows_w)
        turned = normed_one[:, :, :, columns].reshape(row_len, -1)
        total = contract_first(turned, grad_side[:, :, :, grad_qkv].reshape(row_len, -1))
        total = total.astype(bf16)
        q_w[i] = total[:, :HC].reshape(F, rows_w, HC)
        kv_w[i, :, :, : 2 * head] = total[:, HC:].reshape(F, rows_w, 2 * head)
        pieces.append(q_piece(i))
    row.arrive()

    def first_norm(rows):
        grad_normed = row.total(rows)
        grad, unit = norm_back(grad_normed, tok_own[rows].astype(f32), gains[0:1])
        grad_in[rows] += grad
        gain_sums[0:1] += jnp.sum(grad_normed * unit, 0, keepdims=True)

    row_loop(T, 16, first_norm)
    results = [Local(here, [(grad_in, grad_tokens)], 29)]
    columns = contract_first(gain_sums[...], pick).astype(bf16)
    kv_w[:, :, :, 2 * head :] = columns.reshape(S, F, rows_w, head)
    kv_row = RowSum(links, kv_w.reshape(2, 2, F * rows_w, kv_w.shape[3]), *bufs[12:14])
    kv_row.far()
    kv_row.near()
    kv_row.middle()
    ffn["down_high"] = PieceByW(
        links, LeadFirst(down.at[:, :, :, :, high_half]), *bufs[2:4], w, w_masks
    )
    for i in (0, 1):
        ffn["down_low", i].middle()
    o_piece.middle()
    pieces[0].middle()
    pieces[1].middle()
    o_piece.inner()
    pieces[2].middle()
    pieces[0].inner()
    pieces[3].middle()
    kv_row.arrive()

    def keep_kv(rows):
        kv_row.parts[x, core, rows] = kv_row.total(rows).astype(bf16)

    row_loop(F * rows_w, 16, keep_kv)
    kv_mine = LeadFirst(kv_view.at[pl.ds(s, 1)])
    kv_piece = z_piece(links, kv_mine, *bufs[14:16], place_z, z_masks)
    pieces[1].inner()
    pieces[2].inner()
    pieces[3].inner()
    kv_piece.middle()
    ffn["down_high"].middle()
    kv_piece.inner()

    grad_own = grad_both.reshape(Z, two // rows_w, rows_w, 2 * FC)
    for c, source, copy in owned:

        @pl.when(core == c)
        def _():
            copy.wait_recv()

        @pl.when(core == source)
        def _():
            copy.wait_send()

    mine.wait()
    came = Local(
        here, [(both_own.at[pl.ds(2 * i, 2)], grad_own.at[i, pl.ds(0, 2)]) for i in range(Z)], 33
    )
    def store_down(base):
        def store(i, rows, total):
            grad_down[rows, base : base + total.shape[1]] = total

        return store

    for i in (0, 1):
        ffn["down_low", i].last(store_down(i * (cut // 2)))
    ffn["down_high"].last(store_down(cut))
    results.append(Local(here, [(grad_down, down_out)], 30))

    out.arrive()

    out_rows = back_parts.at[3, 0]

    def finish_output(rows):
        out_rows[rows] = (residual[rows] + out.total(rows)).astype(bf16)

    row_loop(T, 16, finish_output)
    results.append(Local(here, [(out_rows, output)], 32))
    came.wait()
    results[0].wait()
    stores = [
        r.at[pl.ds(j * rows_w, rows_w), pl.ds(0, quarter)]
        for r in (residual, grad_in)
        for j in (0, 1)
    ]
    leaving = [None] * len(stores)
    count = 0
    for i, target in enumerate((gate_out, up_out)):
        units = []
        for at_h in range(Z):
            for c in (0, 1):
                block = grad_own[at_h, c].astype(f32)
                tiles = [
                    block[:, (2 * j + i) * lanes : (2 * j + i + 1) * lanes]
                    for j in range(whole_tiles)
                ]
                base = 2 * whole_tiles * lanes + i * (FC - whole_tiles * lanes)
                tiles.append(block[:, base : base + FC - whole_tiles * lanes])
                units.append(jnp.concatenate(tiles, 1))
        width = FC // W
        for at_x in (0, 1):
            for c in (0, 1):
                parts = [
                    units[2 * at_h + c][:, (2 * at_e + at_x) * width : (2 * at_e + at_x + 1) * width]
                    for at_e in range(E)
                    for at_h in range(Z)
                ]
                slot_now = count % len(stores)
                if leaving[slot_now] is not None:
                    leaving[slot_now].wait()
                stores[slot_now][...] = jnp.concatenate(parts, 1)
                columns = pl.ds((2 * at_x + c) * quarter, quarter)
                leaving[slot_now] = Local(
                    here, [(stores[slot_now], target.at[:, columns])], 37 + slot_now
                )
                count += 1
    def store_o(i, rows, total):
        o_sum[rows] = total

    o_piece.last(store_o)
    results.append(Local(here, [(o_sum, wo_out)], 31))
    for piece in pieces:
        piece.last()
    for a in (1, 2, 3):
        links.start(q_view.at[s ^ a, place_z, l], q_own.at[s], (a, 0))
    q_own[s] = q_view[s, place_z, l]
    q_came = links.sent[-3:]

    def store_kv(i, rows, total):
        kv_sum[rows] = total

    kv_piece.last(store_kv)
    names = (wk_out, wv_out, gains_out)
    results.append(
        Local(here, [(kv_sum.at[:, pl.ds(i * head, head)], r) for i, r in enumerate(names)], 41)
    )

    for arrival in q_came:
        arrival.wait()
    for i in leaving:
        i.wait()
    q_rows = residual.at[pl.ds(0, rows_w)]
    for i in range(S):
        q_rows[:, i * HC : (i + 1) * HC] = q_own[i].astype(f32)
    results.append(Local(here, [(q_rows, wq_out)], 44))
    out.settle()
    for piece in [o_piece, kv_piece] + pieces:
        piece.settle()
    links.finish()
    assert links.count == copies, links.count
    for result in results[1:]:
        result.wait()


def hand_over_kernel(n, *refs):
    inputs, outputs, rooms, sems = refs[:n], refs[n : 2 * n], refs[2 * n : 3 * n], refs[3 * n]
    loads = [pltpu.make_async_copy(inputs[i], rooms[i], sems.at[i]) for i in range(n)]
    stores = [pltpu.make_async_copy(rooms[i], outputs[i], sems.at[n + i]) for i in range(n)]
    for load in loads:
        load.start()
    for load, store in zip(loads, stores):
        load.wait()
        store.start()
    for store in stores:
        store.wait()


def hand_over(arrays):
    n = len(arrays)
    anywhere = [pl.BlockSpec(memory_space=pl.ANY)] * n
    return pl.pallas_call(
        functools.partial(hand_over_kernel, n),
        out_shape=[shape(a.shape, a.dtype) for a in arrays],
        in_specs=anywhere,
        out_specs=anywhere,
        scratch_shapes=[pltpu.VMEM(a.shape, a.dtype) for a in arrays]
        + [pltpu.SemaphoreType.DMA((2 * n,))],
        compiler_params=pltpu.CompilerParams(vmem_limit_bytes=VMEM_LIMIT),
    )(*arrays)


def per_device(
    S,
    F,
    tokens,
    segments,
    positions,
    gain_one,
    w_query,
    w_key,
    w_value,
    w_out,
    gain_two,
    w_gate,
    w_up,
    w_down,
    cotangent,
):
    T, D = tokens.shape[1:]
    head = w_key.shape[1]
    row_len = segments.shape[1]
    rows = w_query.shape[0]
    down_rows = w_down.shape[0]
    FF = w_gate.shape[1]
    FH, E = F // 2, F // 8
    W, TG = 2 * E, 2 * Z
    HC = w_query.shape[1] // S
    heads = HC // head
    FC = FF // TG

    gains = jnp.stack([gain_one, gain_two])
    KV = 3 * head
    group = [pltpu.VMEM((Z, 2, T, D), bf16), pltpu.VMEM((Z, T, D), bf16)]
    group += [pltpu.VMEM((Z, T, D), bf16), pltpu.VMEM((T, D), bf16)]
    weight = pltpu.VMEM((2, 2, E, Z, 2, rows, 2 * FC), bf16)

    def natural_by_l(n):
        block = (n, rows, 2 * FC)
        return [pltpu.VMEM((2, E, *block), bf16), pltpu.VMEM((W - 1, *block), bf16)]

    outs = [
        ((T, D), bf16),
        ((T, head), bf16),
        ((T, head), bf16),
        ((T, D), f32),
        ((rows, FF), f32),
        ((rows, FF), f32),
        ((down_rows, D), f32),
        ((rows, D), f32),
        ((rows, D), f32),
        ((rows, head), f32),
        ((rows, head), f32),
        ((rows, head), f32),
        ((TG, rows, 2 * FC), bf16),
        ((2, 2, T, D), bf16),
        ((2, 2, T, 2 * HC + 2 * head), bf16),
        ((F, rows, D), bf16),
    ]
    copies = 119 + 12 * (FH - 1) + 20 * (W - 1) + 6 * (1 + (6 if FH == 4 else FH - 1))
    results = communicate(
        functools.partial(layer_kernel, FH, copies),
        (
            tokens[0],
            w_query,
            w_key,
            w_value,
            w_out,
            w_gate,
            w_up,
            w_down,
            cotangent[0],
            segments,
            positions,
            gains,
        ),
        [shape(dims, kind) for dims, kind in outs],
        copies,
        0,
        in_vmem=[False] * 9 + [True] * 3,
        kept=45,
        scratch=[
            weight,
            pltpu.VMEM((1, W, 2, down_rows, D), bf16),
            pltpu.VMEM((S, F, rows, HC), bf16),
            pltpu.VMEM((S, F, rows, KV), bf16),
            pltpu.VMEM((F, rows, D), bf16),
            pltpu.VMEM((T, D), f32),
            pltpu.VMEM((T, D), f32),
            pltpu.VMEM((8, D), f32),
            pltpu.VMEM((8, D), f32),
            pltpu.VMEM((S, T, D), bf16),
            pltpu.VMEM((down_rows, D), f32),
            pltpu.VMEM((rows, D), f32),
            pltpu.VMEM((rows, KV), f32),
            pltpu.VMEM((S, rows, HC), bf16),
            *group,
            *group,
            pltpu.VMEM((Z, 2, T, D), bf16),
            pltpu.VMEM((Z, 2, T, D), bf16),
            pltpu.VMEM((Z, 2 * T, 2 * FC), bf16),
            pltpu.VMEM((S, T, head), f32),
            pltpu.VMEM((row_len, head), f32),
            pltpu.VMEM((row_len, head), f32),
            pltpu.VMEM((row_len, row_len), bf16),
            pltpu.VMEM((rows, head), bf16),
            *by_l_scratch(1, W, down_rows, D // 2),
            *by_w_scratch(1, W, down_rows, D // 2),
            *natural_by_l(Z),
            *by_w_scratch(Z, W, rows, 2 * FC),
            *z_scratch(1, FH, rows, D),
            *z_scratch(S, FH, rows, HC),
            pltpu.VMEM((2, F * rows, KV), bf16),
            pltpu.VMEM((F * rows, KV), bf16),
            *z_scratch(1, FH, rows, KV),
        ],
    )
    output, keys, values, grad_tokens, gate, up, down, query, out, key, value, gains = hand_over(
        results[:12]
    )
    return (
        output[None],
        keys[None],
        values[None],
        grad_tokens[None],
        gains[:, 0],
        query,
        key,
        value,
        out,
        gains[:, 1],
        gate,
        up,
        down,
    )


def solution(mesh):
    token_spec = P("fsdp", "seq", None)
    flat, matrix = P(("seq", "fsdp")), P(("seq", "fsdp"), None)
    return jax.shard_map(
        functools.partial(per_device, mesh.shape["seq"], mesh.shape["fsdp"]),
        mesh=mesh,
        in_specs=(
            token_spec,
            P("fsdp", None),
            P("fsdp", "seq"),
            flat,
            matrix,
            matrix,
            matrix,
            matrix,
            flat,
            matrix,
            matrix,
            matrix,
            token_spec,
        ),
        out_specs=(
            token_spec,
            token_spec,
            token_spec,
            token_spec,
            flat,
            matrix,
            matrix,
            matrix,
            matrix,
            flat,
            matrix,
            matrix,
            matrix,
        ),
        check_vma=False,
    )
```

```python
import functools
import math

import jax
import jax.numpy as jnp
from jax import lax
from jax.experimental import pallas as pl
from jax.experimental.pallas import tpu as pltpu
from jax.sharding import PartitionSpec as P

epsilon = 1e-05
MESH = pl.DeviceIdType.MESH
Z = 4
VMEM_LIMIT = 64 * 2**20 - 2**18
bf16 = jnp.bfloat16
f32 = jnp.float32


def dot(left, right):
    return jnp.dot(left, right, preferred_element_type=f32)


def contract_last(left, right):
    return lax.dot_general(left, right, (((1,), (1,)), ((), ())), preferred_element_type=f32)


def contract_first(left, right):
    return lax.dot_general(left, right, (((0,), (0,)), ((), ())), preferred_element_type=f32)


class Arrival:
    def __init__(self, copy):
        self.copy, self.waited, self.left = copy, False, False

    def wait(self):
        if not self.waited:
            self.waited = True
            self.copy.wait_recv()

    def wait_sent(self):
        if not self.left:
            self.left = True
            self.copy.wait_send()


class Links:
    def __init__(self, send, recv):
        self.send, self.recv, self.sent, self.count = send, recv, [], 0
        self.s, self.f = lax.axis_index("seq"), lax.axis_index("fsdp")

    def greet(self, masks):
        barrier = pltpu.get_barrier_semaphore()
        for a, b in masks:
            pl.semaphore_signal(
                barrier, inc=1, device_id=(self.s ^ a, self.f ^ b), device_id_type=MESH
            )
        pl.semaphore_wait(barrier, len(masks))

    def copy(self, source, target, device):
        self.count += 1
        return pltpu.make_async_remote_copy(
            src_ref=source,
            dst_ref=target,
            send_sem=self.send.at[self.count - 1],
            recv_sem=self.recv.at[self.count - 1],
            device_id=device,
            device_id_type=MESH,
        )

    def start(self, source, target, mask):
        copy = self.copy(source, target, (self.s ^ mask[0], self.f ^ mask[1]))
        copy.start()
        self.sent.append(Arrival(copy))
        return self.sent[-1]

    def pass_on(self, block, mask):
        return self.start(block, block, mask)

    def finish(self):
        for arrival in self.sent:
            arrival.wait()
        for arrival in self.sent:
            arrival.wait_sent()


class Local:
    def __init__(self, sems, pairs, base=0):
        self.copies = [
            pltpu.make_async_copy(a, b, sems.at[base + i]) for i, (a, b) in enumerate(pairs)
        ]
        self.open = set(range(len(pairs)))
        for copy in self.copies:
            copy.start()

    def wait(self, *which):
        for i in which or sorted(self.open):
            self.open.discard(i)
            self.copies[i].wait()


def row_loop(rows, step, body):
    block_loop(1, rows, step, lambda i, part: body(part))


def block_loop(n, rows, step, body):
    if rows % step:
        for i in range(n):
            body(i, slice(0, rows))
        return
    steps = rows // step

    @pl.loop(0, n * steps)
    def _(k):
        body(k // steps, pl.ds(pl.multiple_of(lax.rem(k, steps) * step, step), step))


def communicate(
    body, args, outs, copies, collective_id, in_vmem=False, out_vmem=False, scratch=(), kept=1
):
    def specs(inside, n):
        inside = [inside] * n if isinstance(inside, bool) else inside
        return [pl.BlockSpec(memory_space=pltpu.VMEM if i else pl.ANY) for i in inside]

    return pl.pallas_call(
        body,
        out_shape=outs,
        in_specs=specs(in_vmem, len(args)),
        out_specs=specs(out_vmem, len(outs)),
        scratch_shapes=[
            pltpu.SemaphoreType.DMA((copies,)),
            pltpu.SemaphoreType.DMA((copies,)),
            pltpu.SemaphoreType.DMA((kept,)),
            *scratch,
        ],
        compiler_params=pltpu.CompilerParams(
            collective_id=collective_id, has_side_effects=True, vmem_limit_bytes=VMEM_LIMIT
        ),
    )(*args)


def shape(dims, kind=bf16):
    return jax.ShapeDtypeStruct(dims, kind)


class Line:
    def __init__(self, links, here, h, FH, forward):
        self.links, self.here, self.h, self.FH, self.forward = links, here, h, FH, forward
        self.right, self.left, self.pending = [], [], []
        self.settled = set()

    def step(self, j):
        h, FH = self.h, self.FH
        rights = [
            self.links.copy(block, block, (self.links.s, self.links.f + 2))
            for block in self.here(lax.max(h - j, 0))
        ]
        lefts = [
            self.links.copy(block, block, (self.links.s, self.links.f - 2))
            for block in self.here(lax.min(h + j, FH - 1))
        ]
        for i in range(len(rights)):

            @pl.when((h >= j) & (h < FH - 1))
            def _():
                rights[i].start()

            @pl.when((h + j < FH) & (h > 0))
            def _():
                lefts[i].start()

        self.right.append(rights)
        self.left.append(lefts)

    def arrived(self, j):
        h, FH = self.h, self.FH
        up = self.here(lax.max(h - 1 - j, 0))
        down = self.here(lax.min(h + 1 + j, FH - 1))
        for i in range(len(up)):
            for blocks, copies, there in (
                (up, self.right[j], h - 1 - j >= 0),
                (down, self.left[j], h + 1 + j < FH),
            ):
                a, b = self.forward
                on = self.links.copy(blocks[i], blocks[i], (self.links.s ^ a, self.links.f ^ b))
                self.pending.append((j, on, there))

                @pl.when(there)
                def _():
                    copies[i].wait_recv()
                    on.start()

    def came(self, j):
        self.settled.add(j)
        for step, on, there in self.pending:
            if step == j:

                @pl.when(there)
                def _():
                    on.wait_recv()

    def finish(self):
        h, FH = self.h, self.FH
        for j in range(FH - 1):
            if j not in self.settled:
                self.came(j)
        for _, on, there in self.pending:

            @pl.when(there)
            def _():
                on.wait_send()

        for j in range(FH - 1):
            for i in range(len(self.right[j])):

                @pl.when((h >= j) & (h < FH - 1))
                def _():
                    self.right[j][i].wait_send()

                @pl.when((h + j < FH) & (h > 0))
                def _():
                    self.left[j][i].wait_send()


def rows_of(ref):
    return ref[...].reshape(-1, ref.shape[-1])


def rotation(table):
    half = table.shape[-1] // 2
    swapped = pltpu.roll(table, half, 1)
    first = lax.broadcasted_iota(jnp.int32, table.shape, 1) < half
    return jnp.where(first, table, swapped), jnp.where(first, -swapped, table)


def turn(vector, factors):
    return vector * factors[0] + pltpu.roll(vector, vector.shape[-1] // 2, 1) * factors[1]


class RowSum:
    def __init__(self, links, parts, from_core, from_x):
        self.links, self.parts, self.from_core, self.from_x = links, parts, from_core, from_x
        self.x, self.core, self.sent = links.s // 2, links.s % 2, []

    def far(self):
        x, core = 1 - self.x, 1 - self.core
        self.to_far = self.links.start(self.parts.at[x, core], self.from_core.at[x], (1, 0))
        self.sent.append(self.to_far)

    def near(self):
        x, core = self.x, 1 - self.core
        self.to_near = self.links.start(self.parts.at[x, core], self.from_core.at[x], (1, 0))
        self.sent.append(self.to_near)

    def middle(self):
        self.to_far.wait()
        x, core = 1 - self.x, self.core

        def add(rows):
            total = self.parts[x, core, rows].astype(f32) + self.from_core[x, rows].astype(f32)
            self.parts[x, core, rows] = total.astype(bf16)

        row_loop(self.from_x.shape[0], 16, add)
        self.across = self.links.start(self.parts.at[x, core], self.from_x, (2, 0))
        self.sent.append(self.across)

    def arrive(self):
        self.to_near.wait()
        self.across.wait()

    def total(self, rows):
        return (
            self.parts[self.x, self.core, rows].astype(f32)
            + self.from_core[self.x, rows].astype(f32)
            + self.from_x[rows].astype(f32)
        )


class LineSum:
    def __init__(self, links, h, parts, from_core, chain, extra):
        self.links, self.h, self.parts = links, h, parts
        self.from_core, self.chain, self.extra = from_core, chain, extra
        self.core, self.T = links.s % 2, extra.shape[0]
        self.by_core, self.right, self.left, self.end = {}, {}, {}, {}
        s, f = links.s, links.f
        for d in range(Z):
            block = parts.at[d, self.core]
            self.right[d] = links.copy(block, chain.at[d], (s, f + 2))
            self.left[d] = links.copy(block, chain.at[d], (s, f - 2))
            self.end[d] = links.copy(block, extra, (s, f - 2))

    def send_core(self, d):
        self.by_core[d] = self.links.start(
            self.parts.at[d, 1 - self.core], self.from_core.at[d], (1, 0)
        )

    def add(self, d, chained):
        def add(rows):
            total = self.parts[d, self.core, rows].astype(f32)
            total += self.from_core[d, rows].astype(f32)
            if chained:
                total += self.chain[d, rows].astype(f32)
            self.parts[d, self.core, rows] = total.astype(bf16)

        row_loop(self.T, 16, add)

    def stage(self, k, places):
        h = self.h
        for d in places:
            self.by_core[d].wait()
            rightward, leftward = (h < d) & (h == k), (h > d) & (h == Z - 1 - k)

            @pl.when(rightward)
            def _():
                if k:
                    self.right[d].wait_recv()
                self.add(d, k > 0)
                self.right[d].start()

            @pl.when(leftward)
            def _():
                if k:
                    self.left[d].wait_recv()
                self.add(d, k > 0)

            @pl.when(leftward & (h > d + 1))
            def _():
                self.left[d].start()

            @pl.when(leftward & (h == d + 1))
            def _():
                self.end[d].start()

    def arrive(self):
        h = self.h
        for d in range(Z):
            self.by_core[d].wait()
            if d > 0:

                @pl.when(h == d)
                def _():
                    self.right[d].wait_recv()

            else:

                @pl.when(h == 0)
                def _():
                    self.chain[0] = jnp.zeros_like(self.chain[0])

            if d < Z - 1:

                @pl.when(h == d)
                def _():
                    self.end[d].wait_recv()

            else:

                @pl.when(h == Z - 1)
                def _():
                    self.extra[...] = jnp.zeros_like(self.extra)

    def total(self, rows):
        return (
            self.parts[self.h, self.core, rows].astype(f32)
            + self.from_core[self.h, rows].astype(f32)
            + self.chain[self.h, rows].astype(f32)
            + self.extra[rows].astype(f32)
        )

    def settle(self):
        h = self.h
        for d in range(Z):
            self.by_core[d].wait_sent()

            @pl.when(h < d)
            def _():
                self.right[d].wait_send()

            @pl.when(h > d + 1)
            def _():
                self.left[d].wait_send()

            @pl.when(h == d + 1)
            def _():
                self.end[d].wait_send()


class LeadFirst:
    def __init__(self, ref):
        self.ref, self.n, self.rows = ref, ref.shape[0], ref.shape[3]

    def half(self, l):
        return self.ref.at[:, :, l]

    def both(self, w):
        return self.ref.at[:, w]

    def part(self, w, l):
        return self.ref.at[:, w, l]

    def item(self, i, w, l):
        return self.ref.at[i, w, l]

    def got(self, ref, i, w):
        return ref.at[i, w]


class Natural:
    def __init__(self, ref):
        self.ref, self.n, self.rows = ref, ref.shape[2], ref.shape[4]

    def half(self, l):
        return self.ref.at[:, :, :, l]

    def both(self, w):
        return self.ref.at[w % 2, w // 2]

    def part(self, w, l):
        return self.ref.at[w % 2, w // 2, :, l]

    def item(self, i, w, l):
        return self.ref.at[w % 2, w // 2, i, l]

    def got(self, ref, i, w):
        return ref.at[w % 2, w // 2, i]


class PieceByL:
    def __init__(self, links, view, by_l, by_w, w, masks):
        self.links, self.view, self.by_l, self.by_w = links, view, by_l, by_w
        self.w, self.masks, self.l = w, masks, links.f % 2
        self.first = links.start(view.half(1 - self.l), by_l, (0, 1))

    def partial(self, i, w, rows):
        total = self.view.item(i, w, self.l)[rows].astype(f32)
        return total + self.view.got(self.by_l, i, w)[rows].astype(f32)

    def place(self, k, slot=None):
        w = self.w ^ k

        def add(i, rows):
            total = self.partial(i, w, rows)
            if slot is not None:
                total += self.by_w[slot, i, rows].astype(f32)
            self.view.item(i, w, self.l)[rows] = total.astype(bf16)

        block_loop(self.view.n, self.view.rows, 16, add)

    def middle(self):
        self.first.wait()
        self.second = []
        for k in range(1, len(self.masks)):
            self.place(k)
            block = self.view.part(self.w ^ k, self.l)
            self.second.append(self.links.start(block, self.by_w.at[k - 1], self.masks[k]))

    def arrive(self):
        for arrival in self.second:
            arrival.wait()

    def last(self, store=None):
        self.arrive()

        def add(i, rows):
            total = self.partial(i, self.w, rows)
            for k in self.slots():
                total += self.by_w[k, i, rows].astype(f32)
            if store is None:
                self.view.item(i, self.w, self.l)[rows] = total.astype(bf16)
            else:
                store(i, rows, total)

        block_loop(self.view.n, self.view.rows, 16, add)

    def slots(self):
        return range(len(self.masks) - 1)

    def inner(self):
        pass

    def settle(self):
        pass


class PieceAlongZ(PieceByL):
    def __init__(self, links, view, by_l, by_w, w, masks):
        super().__init__(links, view, by_l, by_w, w, masks)
        self.is_inner = (w == 1) | (w == 2)
        device = [(links.s ^ a, links.f ^ b) for a, b in masks]

        def copy(k, slot, to):
            return links.copy(view.part(w ^ k, self.l), by_w.at[slot], device[to])

        self.out = [copy(k, k - 1, 1) for k in (1, 2, 3)]
        self.over = [copy(3, 3, 3), copy(2, 3, 2)]
        self.beside = copy(1, 0, 1)

    def middle(self):
        self.first.wait()

        @pl.when(self.is_inner)
        def _():
            self.place(1)
            self.beside.start()

        @pl.when(jnp.logical_not(self.is_inner))
        def _():
            for k in (2, 3, 1):
                self.place(k)
                self.out[k - 1].start()

    def inner(self):
        @pl.when(self.is_inner)
        def _():
            for k, over in zip((3, 2), self.over):
                self.out[4 - k].wait_recv()
                self.place(k, 4 - k)
                over.start()

    def arrive(self):
        @pl.when(self.is_inner)
        def _():
            self.out[0].wait_recv()
            self.over[0].wait_recv()

        @pl.when(jnp.logical_not(self.is_inner))
        def _():
            self.beside.wait_recv()
            self.over[1].wait_recv()

    def slots(self):
        return (0, 3)

    def settle(self):
        @pl.when(self.is_inner)
        def _():
            for copy in [self.beside] + self.over:
                copy.wait_send()

        @pl.when(jnp.logical_not(self.is_inner))
        def _():
            for copy in self.out:
                copy.wait_send()


def z_piece(links, view, by_l, by_w, w, masks):
    kind = PieceAlongZ if len(masks) == 4 else PieceByL
    return kind(links, view, by_l, by_w, w, masks)


class PieceByW:
    def __init__(self, links, view, by_l, by_w, w, masks):
        self.links, self.view, self.by_l, self.by_w = links, view, by_l, by_w
        self.w, self.masks, self.l = w, masks, links.f % 2
        self.first = [
            links.start(view.both(w ^ k), by_w.at[k - 1], masks[k]) for k in range(1, len(masks))
        ]

    def partial(self, i, l, rows):
        total = self.view.item(i, self.w, l)[rows].astype(f32)
        for k in range(1, len(self.masks)):
            total += self.by_w[k - 1, i, l, rows].astype(f32)
        return total

    def middle(self):
        for arrival in self.first:
            arrival.wait()
        l = 1 - self.l

        def add(i, rows):
            self.view.item(i, self.w, l)[rows] = self.partial(i, l, rows).astype(bf16)

        block_loop(self.view.n, self.view.rows, 16, add)
        self.second = self.links.start(self.view.part(self.w, l), self.by_l, (0, 1))

    def last(self, store=None):
        self.second.wait()

        def add(i, rows):
            total = self.partial(i, self.l, rows) + self.by_l[i, rows].astype(f32)
            if store is None:
                self.view.item(i, self.w, self.l)[rows] = total.astype(bf16)
            else:
                store(i, rows, total)

        block_loop(self.view.n, self.view.rows, 16, add)


def by_l_scratch(n, W, rows, width):
    return [pltpu.VMEM((n, W, rows, width), bf16), pltpu.VMEM((W - 1, n, rows, width), bf16)]


def z_scratch(n, W, rows, width):
    slots = 4 if W == 4 else W - 1
    return [pltpu.VMEM((n, W, rows, width), bf16), pltpu.VMEM((slots, n, rows, width), bf16)]


def by_w_scratch(n, W, rows, width):
    return [pltpu.VMEM((n, rows, width), bf16), pltpu.VMEM((W - 1, n, 2, rows, width), bf16)]


def norm_back(grad_normed, inputs, gain):
    inverse = lax.rsqrt(jnp.mean(inputs * inputs, -1, keepdims=True) + epsilon)
    scaled = grad_normed * gain
    inner_sum = jnp.sum(scaled * inputs, -1, keepdims=True)
    grad = inverse * scaled - inputs * (inverse**3 * inner_sum / inputs.shape[-1])
    return grad, inputs * inverse


def layer_kernel(FH, copies, *refs):
    tok, wq_in, wk_in, wv_in, wo_in, gate_in, up_in, down_in, cot_in = refs[:9]
    segments, positions, gains_in = refs[9:12]
    output, keys, values, grad_tokens, gate_out, up_out, down_out = refs[12:19]
    wq_out, wo_out, wk_out, wv_out, gains_out = refs[19:24]
    both_own, normed_kept, side_kept, o_kept = refs[24:28]
    send, recv, here, both, down, q_w, kv_w, o_w = refs[28:36]
    residual, grad_in, gains, gain_sums, grad_row = refs[36:41]
    grad_down, o_sum, kv_sum, q_own = refs[41:45]
    back_bufs, out_bufs = refs[45:49], refs[49:53]
    normed, cot, grad_both, tab, grad_k, grad_v, bias, gain_block = refs[53:61]
    bufs = refs[61:]
    links = Links(send, recv)
    s, f = links.s, links.f
    x, core = s // 2, s % 2
    e, h, l = f // 8, (f // 2) % Z, f % 2
    t = 2 * h + core
    T, D = residual.shape
    S, F, rows_w, HC = q_w.shape
    row_len, head = grad_k.shape
    heads = HC // head
    E, FC = both.shape[2], both.shape[6] // 2
    W, TG = 2 * E, 2 * Z
    w = 2 * e + x
    two = 2 * T
    cut = D // 2
    scale = head ** (-0.5)
    group_masks = [(a, 2 * m) for m in range(Z) for a in (0, 1)][1:]
    w_masks = [(2 * (j % 2), 8 * (j // 2)) for j in range(W)]
    back = LineSum(links, h, *back_bufs)
    out = LineSum(links, h, *out_bufs)
    back_parts, out_parts = back.parts, out.parts
    tok_g = grad_row
    spots = {}
    for name, width in (("attended", HC), ("q", HC), ("k", head), ("v", head), ("grad", HC)):
        base = sum(n for _, n in spots.values())
        spots[name] = (base, width)
    side_width = spots["grad"][0]

    def column(name, first=0, width=None):
        base, full_width = spots[name]
        return pl.ds(base + first, width or full_width)

    def block(where, name, r, first=0, width=None):
        return where[r // 2, r % 2, :, column(name, first, width)]

    def to_x(ref, j):
        return ref.at[(w ^ j) % 2, :, (w ^ j) // 2]

    def whole(where, name, first=0, width=None):
        return where[:, :, :, column(name, first, width)].reshape(row_len, -1)

    links.greet(
        [(a, 0) for a in (1, 2, 3)]
        + [(0, 1)]
        + [(0, 2 * k) for k in range(1, FH)]
        + [(1, 2 * m) for m in range(1, Z)]
        + [mask for mask in w_masks if mask[0] and mask[1]]
    )
    place = lax.broadcasted_iota(jnp.int32, (8, head), 0)
    lane = lax.broadcasted_iota(jnp.int32, (8, head), 1)
    pick = jnp.where((place == lane) & (place < 2), 1.0, 0.0)
    row_at = lax.broadcasted_iota(jnp.int32, (8, rows_w), 0)
    both_gains = [jnp.broadcast_to(gains_in[i : i + 1].astype(f32), (8, rows_w)) for i in (0, 1)]
    gain_rows = jnp.where(row_at == 0, both_gains[0], jnp.where(row_at == 1, both_gains[1], 0.0))
    gain_block[...] = contract_first(gain_rows, pick).astype(bf16)
    local = Local(
        here,
        [
            (wq_in.at[:, pl.ds(pl.multiple_of(s * HC, HC), HC)], q_w.at[s, f]),
            (wk_in, kv_w.at[s, f, :, pl.ds(0, head)]),
            (wv_in, kv_w.at[s, f, :, pl.ds(head, head)]),
            (gain_block, kv_w.at[s, f, :, pl.ds(2 * head, head)]),
            (wo_in, o_w.at[f]),
            (tok, tok_g.at[s]),
            (down_in, down.at[0, w, l]),
            (cot_in, cot.at[h, core]),
        ],
    )
    first = [
        links.start(
            wq_in.at[:, pl.ds(pl.multiple_of((s ^ a) * HC, HC), HC)], q_w.at[s, f], (a, 0)
        )
        for a in (1, 2, 3)
    ]
    quarter = FC * TG // S
    natural = Local(
        here,
        [
            (r.at[:, pl.ds(i * quarter, quarter)], back_parts.at[i, j, pl.ds(0, rows_w), pl.ds(0, quarter)])
            for j, r in enumerate((gate_in, up_in))
            for i in range(S)
        ],
        9,
    )
    local.wait(1, 2, 3, 4)
    along_z = (f // 2, FH, (0, 1))
    kv_line = Line(links, lambda place: [kv_w.at[s, 2 * place + l]], *along_z)
    o_line = Line(links, lambda place: [o_w.at[2 * place + l]], *along_z)
    q_line = Line(links, lambda place: [q_w.at[:, 2 * place + l]], *along_z)
    kv_line.step(0)
    kv_y = links.pass_on(kv_w.at[s, f], (0, 1))
    o_line.step(0)
    needed = [links.pass_on(o_w.at[f], (0, 1))]
    local.wait(0)
    for arrival in first:
        arrival.wait()
    q_line.step(0)
    needed.append(links.pass_on(q_w.at[:, f], (0, 1)))
    at = jnp.broadcast_to(positions[...].astype(f32), (T, T))
    frequency = lax.broadcasted_iota(jnp.int32, (1, head), 1)
    frequency = lax.rem(frequency, head // 2).astype(f32) * (-2.0 / head * math.log(10000.0))
    angle = jnp.transpose(at)[:, :1] * jnp.exp(frequency)
    first_half = lax.broadcasted_iota(jnp.int32, (T, head), 1) < head // 2
    tab[s] = jnp.where(first_half, jnp.cos(angle), jnp.sin(angle))
    tok_x = links.start(tok, tok_g.at[s], (2, 0))
    needed.append(links.start(tok, tok_g.at[s], (1, 0)))
    needed += [links.pass_on(tab.at[s], (a, 0)) for a in (1, 2, 3)]
    ffn_in = {}
    lanes = 128
    whole_tiles = FC // lanes

    def blocks_of(ref, at_h, c):
        width = 2 * FC // W // 2
        parts = []
        for at_e in range(E):
            for at_x in (0, 1):
                base = (at_e * Z + at_h) * width
                parts.append(ref(2 * at_x + c)[:, base : base + width])
        return jnp.concatenate(parts, 1)

    def side_by_side(gate_units, up_units):
        tiles = []
        for j in range(whole_tiles):
            part = slice(j * lanes, (j + 1) * lanes)
            tiles += [gate_units[:, part], up_units[:, part]]
        rest = slice(whole_tiles * lanes, FC)
        return jnp.concatenate(tiles + [gate_units[:, rest], up_units[:, rest]], 1)

    def sent_blocks(at_h, c):
        return grad_both.at[at_h, pl.ds(pl.multiple_of(c * rows_w, rows_w), rows_w)]

    ids = jnp.broadcast_to(segments[...].astype(f32), (lanes, row_len))
    own_ids = jnp.transpose(ids)[:, :1]
    for r in range(S):
        rows = slice(r * T, (r + 1) * T)
        mine_at = lax.broadcasted_iota(jnp.int32, (T, row_len), 0) + r * T
        seen_at = lax.broadcasted_iota(jnp.int32, (T, row_len), 1)
        allowed = (seen_at <= mine_at) & (ids[:1] == own_ids[rows])
        bias[rows] = jnp.where(allowed, 0.0, -1e30).astype(bf16)
    natural.wait()
    columns_of = [
        [back_parts[i, j, :rows_w, :quarter].astype(f32) for i in range(S)] for j in (0, 1)
    ]
    for at_h in range(Z):
        for c in (0, 1):
            units = [blocks_of(lambda i: columns_of[j][i], at_h, c) for j in (0, 1)]
            grad_both[at_h, c * rows_w : (c + 1) * rows_w] = side_by_side(*units).astype(bf16)
    own_block = Local(here, [(sent_blocks(h, core), both.at[x, core, e, h, l])], 17)

    def to_group(m):
        for a in (0, 1):
            if (a, m) != (0, 0):
                place = (x, core, e, h, l)
                source = sent_blocks(h ^ m, core ^ a)
                ffn_in[a, m] = links.start(source, both.at[place], (a, 2 * m))

    arriving = []

    class Spread:
        def __init__(self, near, second_w, second_y):
            self.near, self.second_w, self.second_y = near, second_w, second_y

        def by_w(self):
            self.came_w = [links.pass_on(self.near, mask) for mask in w_masks[1:]]

        def by_y(self):
            self.came_y = links.pass_on(self.near, (0, 1))

        def on_w(self):
            self.came_y.wait()
            arriving.extend(links.pass_on(self.second_w, mask) for mask in w_masks[1:])

        def on_y(self):
            for j, arrival in enumerate(self.came_w):
                arrival.wait()
                arriving.append(links.pass_on(self.second_y(j + 1), (0, 1)))

    def spread_of(m):
        def second_y(j):
            return to_x(both, j).at[0, h ^ m, l]

        here_q = to_x(both, 0)
        return Spread(here_q.at[:, h ^ m, l], here_q.at[1, h ^ m, 1 - l], second_y)

    low_half, high_half = pl.ds(0, cut), pl.ds(cut, D - cut)
    spread_down = Spread(
        down.at[0, w, l],
        down.at[0, w, 1 - l, :, high_half],
        lambda j: down.at[0, w ^ j, l, :, low_half],
    )
    to_group(0)
    local.wait(6)
    spread_down.by_w()
    for j in range(FH - 1):
        for way in (kv_line, o_line, q_line):
            way.arrived(j)
            if j + 1 < FH - 1:
                way.step(j + 1)
        if j == 0:
            tok_x.wait()
            needed.append(links.pass_on(tok_g.at[s ^ 2], (1, 0)))
            own_block.wait()
            ffn_in[1, 0].wait()
            spreads = [spread_of(m) for m in range(Z)]
            spreads[0].by_w()
    kv_y.wait()
    kv_line.finish()
    kv_x = links.pass_on(kv_w.at[s], (2, 0))
    needed.append(links.pass_on(kv_w.at[s], (1, 0)))
    for m in range(1, Z):
        to_group(m)
    spread_down.by_y()
    spreads[0].by_y()
    cot_line = Line(links, lambda place: [cot.at[place, core]], h, Z, (1, 0))
    kv_x.wait()
    needed.append(links.pass_on(kv_w.at[s ^ 2], (1, 0)))
    for arrival in needed:
        arrival.wait()
    o_line.finish()
    q_line.finish()
    local.wait(5)
    kept_o = Local(here, [(o_w, o_kept)], 18)

    normed_one, side = out_parts.at[pl.ds(0, 2)], out_parts.at[pl.ds(2, 2)]
    kv_full = rows_of(kv_w)
    gains[...] = contract_last(pick.astype(bf16), kv_full[:, 2 * head :])

    def norm_one(i, rows):
        value = tok_g[i, rows].astype(f32)
        inverse = lax.rsqrt(jnp.mean(value * value, -1, keepdims=True) + epsilon)
        normed_one[i // 2, lax.rem(i, 2), rows] = (value * inverse * gains[0:1]).astype(bf16)

    block_loop(S, T, 16, norm_one)
    local.wait(7)
    cot_line.step(0)
    arriving.append(links.pass_on(cot.at[h, core], (1, 0)))
    factors = rotation(rows_of(tab))

    def put(name, first, value):
        columns = column(name, first, value.shape[1])
        side[:, :, :, columns] = value.astype(bf16).reshape(2, 2, T, -1)

    kv = dot(rows_of(normed_one), kv_full[:, : 2 * head])
    put("k", 0, turn(kv[:, :head], factors))
    put("v", 0, kv[:, head:])
    for n in range(0, heads, 2):
        columns = slice(n * head, (n + 2) * head)
        pair = dot(rows_of(normed_one), q_w[:, :, :, columns].reshape(D, 2 * head))
        for j in (0, 1):
            put("q", (n + j) * head, turn(pair[:, j * head : (j + 1) * head], factors))
    results = [
        Local(
            here,
            [
                (side.at[x, core, :, column("k")], keys),
                (side.at[x, core, :, column("v")], values),
            ],
            21,
        )
    ]
    for r in range(S):
        rows, seen = slice(r * T, (r + 1) * T), slice(0, (r + 1) * T)
        keys_seen, values_seen = whole(side, "k")[seen], whole(side, "v")[seen]
        for n in range(heads):
            query = block(side, "q", r, n * head, head)
            scores = contract_last(query, keys_seen) * scale + bias[rows, seen].astype(f32)
            scores = jnp.exp(scores - jnp.max(scores, -1, keepdims=True))
            probs = (scores / jnp.sum(scores, -1, keepdims=True)).astype(bf16)
            side[r // 2, r % 2, :, column("attended", n * head, head)] = dot(
                probs, values_seen
            ).astype(bf16)
    spread_down.on_y()

    first_two = pl.ds(0, 2)
    row_bufs = (back_parts.at[first_two], back.from_core.at[first_two], back.chain.at[0])
    parts = RowSum(links, *row_bufs)

    def project(x_to):
        rows = side[x_to, :, :, column("attended")].reshape(two, HC)
        for n in range(0, D, HC):
            columns = slice(n, n + HC)
            total = dot(rows, o_w[:, :, columns].reshape(HC, HC))
            parts.parts[x_to, :, :, columns] = total.astype(bf16).reshape(2, T, HC)

    project(1 - x)
    parts.far()
    project(x)
    parts.near()
    parts.middle()
    spread_down.on_w()
    spreads[0].on_y()
    spreads[0].on_w()
    for m in range(1, Z):
        for a in (0, 1):
            ffn_in[a, m].wait()
        spreads[m].by_y()
        spreads[m].by_w()
    cot_line.arrived(0)
    cot_line.step(1)
    kept = Local(
        here, [(normed_one, normed_kept), (side.at[:, :, :, pl.ds(0, side_width)], side_kept)], 19
    )
    parts.arrive()

    def norm_two(rows):
        total = tok_g[s, rows].astype(f32) + parts.total(rows)
        residual[rows] = total
        inverse = lax.rsqrt(jnp.mean(total * total, -1, keepdims=True) + epsilon)
        normed[h, core, rows] = (total * inverse * gains[1:2]).astype(bf16)

    row_loop(T, 16, norm_two)
    normed_line = Line(links, lambda place: [normed.at[place, core]], h, Z, (1, 0))
    normed_line.step(0)
    beside = [links.pass_on(normed.at[h, core], (1, 0))]
    cot_line.arrived(1)
    cot_line.step(2)
    spreads[1].on_y()
    spreads[1].on_w()
    normed_line.arrived(0)
    normed_line.step(1)
    for m in range(2, Z):
        spreads[m].on_y()
        spreads[m].on_w()
    normed_line.arrived(1)
    normed_line.step(2)
    results[0].wait()
    kept_o.wait()
    kept.wait()
    for arrival in arriving:
        arrival.wait()
    for arrival in links.sent:
        arrival.wait_sent()

    slot = D // 2
    lane_is_low = lax.broadcasted_iota(jnp.int32, (two, lanes), 1) < lanes // 2

    def hidden_of(d):
        n = normed[d].reshape(two, D)
        c = cot[d].reshape(two, D)
        weights = down[...].reshape(FC, D)

        def units(first, width, gate_proj, up_proj, grad_inner):
            sig = jax.nn.sigmoid(gate_proj)
            silu = gate_proj * sig
            spot = pl.ds(pl.multiple_of(d // 2 * slot + first, lanes), width)
            hidden = (silu * up_proj).astype(bf16)[:, :width]
            o_w[pl.ds(d % 2 * (F // 2), F // 2), :, spot] = hidden.reshape(F // 2, rows_w, width)
            slope = sig * (1.0 + gate_proj * (1.0 - sig))
            return (grad_inner * up_proj * slope).astype(bf16), (grad_inner * silu).astype(bf16)

        for first in range(0, FC, 2 * lanes):
            width = min(2 * lanes, FC - first)
            rows = weights[first : first + width]
            if width % lanes:
                rows = jnp.concatenate([rows, rows[width - lanes // 2 :]], 0)
            grad_inner = contract_last(c, rows)
            for i in range(0, width, lanes):
                base = 2 * (first + i)
                columns = (slice(None),) * 6 + (slice(base, min(base + 2 * lanes, 2 * FC)),)
                proj = dot(n, both[columns].reshape(D, -1))
                part = slice(i, i + lanes)
                if i + lanes <= width:
                    grad_gate, grad_up = units(
                        first + i,
                        lanes,
                        proj[:, :lanes],
                        proj[:, lanes:],
                        grad_inner[:, part],
                    )
                    grad_both[d, :, base : base + lanes] = grad_gate
                    grad_both[d, :, base + lanes : base + 2 * lanes] = grad_up
                else:
                    mixed = proj
                    turned = pltpu.roll(mixed, lanes // 2, 1)
                    grad_gate, grad_up = units(
                        first + i,
                        lanes // 2,
                        jnp.where(lane_is_low, mixed, turned),
                        jnp.where(lane_is_low, turned, mixed),
                        grad_inner[:, part],
                    )
                    grad_both[d, :, base : base + lanes] = jnp.where(
                        lane_is_low, grad_gate, grad_up
                    )

    def back_of(d):
        for i in range(S):
            columns = slice(i * F * rows_w, (i + 1) * F * rows_w)
            total = contract_last(grad_both[d], both[i // 2, i % 2].reshape(-1, 2 * FC))
            back_parts[d, :, :, columns] = total.astype(bf16).reshape(2, T, -1)
        back.send_core(d)

    def out_of(d):
        spot = slice(d // 2 * slot, d // 2 * slot + FC)
        hidden = o_w[pl.ds(d % 2 * (F // 2), F // 2), :, spot].reshape(two, FC)
        for i in range(0, D, 512):
            columns = slice(i, i + 512)
            total = dot(hidden, down[:, :, :, :, columns].reshape(FC, 512))
            out_parts[d, :, :, columns] = total.astype(bf16).reshape(2, T, -1)
        out.send_core(d)

    for arrival in beside:
        arrival.wait()
    hidden_of(h)
    for line in (cot_line, normed_line):
        line.came(0)
    hidden_of(h ^ 1)
    for line in (cot_line, normed_line):
        line.came(1)
    hidden_of(h ^ 2)
    for line in (cot_line, normed_line):
        line.arrived(2)
    for line in (cot_line, normed_line):
        line.came(2)
    hidden_of(h ^ 3)
    back_of(3)
    back_of(0)
    back.stage(0, (3, 0))
    back_of(2)
    back_of(1)
    back.stage(0, (2, 1))
    for line in (cot_line, normed_line):
        line.finish()
    ffn = {}
    width = F * rows_w
    for c in (0, 1):
        for i in (0, 1):
            base = (2 * i + c) * width
            turned = normed[:, :, :, base : base + width].reshape(4 * two, width)
            for columns in [slice(n, min(n + 3 * lanes, 2 * FC)) for n in range(0, 2 * FC, 3 * lanes)]:
                total = contract_first(turned, grad_both[:, :, columns].reshape(4 * two, -1))
                both[i, c, :, :, :, :, columns] = total.astype(bf16).reshape(E, Z, 2, rows_w, -1)
        if c == 0:
            ffn["both", 0] = PieceByL(links, Natural(both.at[:, 0]), *bufs[4:6], w, w_masks)
            back.stage(1, (3, 0))
    ffn["both", 1] = PieceByW(links, Natural(both.at[:, 1]), *bufs[6:8], w, w_masks)
    for d in (3, 0, 2, 1):
        out_of(d)
    quarters = [pl.ds(i * (cut // 2), cut // 2) for i in (0, 1)]
    inner = [o_w[:, :, i * slot : i * slot + FC].reshape(2 * two, FC) for i in (0, 1)]
    for i in range(0, D, 256):
        columns = slice(i, i + 256)
        total = contract_first(inner[0], cot[0:2, :, :, columns].reshape(2 * two, 256))
        total += contract_first(inner[1], cot[2:4, :, :, columns].reshape(2 * two, 256))
        down[:, :, :, :, columns] = total.astype(bf16).reshape(1, W, 2, -1, 256)
    def down_low(i):
        view = LeadFirst(down.at[:, :, :, :, quarters[i]])
        ffn["down_low", i] = PieceByL(
            links, view, bufs[0].at[:, :, :, quarters[i]], bufs[1].at[:, :, :, quarters[i]], w, w_masks
        )

    down_low(0)
    back.stage(1, (2, 1))
    back.stage(2, (3, 0))
    out.stage(0, (3, 0, 2, 1))

    cot_own, tok_own = normed.at[2, 0], normed.at[2, 1]
    own = Local(here, [(cot_in, cot_own), (tok, tok_own)], 23)
    gain_sums[...] = jnp.zeros_like(gain_sums)
    own.wait()
    back.arrive()

    def second_norm(rows):
        grad_normed = back.total(rows)
        grad, unit = norm_back(grad_normed, residual[rows], gains[1:2])
        grad = grad + cot_own[rows].astype(f32)
        grad_in[rows] = grad
        grad_row[s, rows] = grad.astype(bf16)
        gain_sums[1:2] += jnp.sum(grad_normed * unit, 0, keepdims=True)

    row_loop(T, 16, second_norm)
    row_x = links.pass_on(grad_row.at[s], (3, 0))
    row_c = links.pass_on(grad_row.at[s], (1, 0))

    last_two = pl.ds(2, 2)
    side = cot.at[first_two]
    normed_one = normed.at[first_two]
    grad_side = cot.at[last_two]
    loads = Local(
        here,
        [
            (o_kept, o_w),
            (side_kept, cot.at[first_two, :, :, pl.ds(0, side_width)]),
            (normed_kept, normed_one),
        ],
        25,
    )
    ffn["both", 1].middle()
    ffn["both", 0].middle()
    row_x.wait()
    row_cc = links.pass_on(grad_row.at[s ^ 3], (1, 0))
    out.stage(1, (3, 0))
    row_c.wait()
    row_cc.wait()
    loads.wait()
    per = 2 * head // rows_w
    for n in range(0, heads, 2):
        wo = o_w[n // 2 * per : (n // 2 + 1) * per].reshape(2 * head, D)
        pair = contract_last(rows_of(grad_row), wo).astype(bf16)
        side[:, :, :, column("grad", n * head, 2 * head)] = pair.reshape(2, 2, T, 2 * head)
    place_z, z_masks = f // 2, [(0, 2 * j) for j in range(FH)]
    o_whole, o_pieces = o_w.reshape(1, FH, 2, rows_w, D), []
    for i in range(0, D, HC):
        columns = slice(i, i + HC)
        grad_columns = grad_row[:, :, columns].reshape(row_len, HC)
        total = contract_first(whole(side, "attended"), grad_columns)
        o_w[:, :, columns] = total.astype(bf16).reshape(F, rows_w, HC)
        if (i + HC) % (D // 2) == 0:
            half = pl.ds(i + HC - D // 2, D // 2)
            view = LeadFirst(o_whole.at[:, :, :, :, half])
            spare = [r.at[:, :, :, half] for r in bufs[8:10]]
            o_pieces.append(z_piece(links, view, *spare, place_z, z_masks))

    owned = []

    def give(c):
        ffn["both", c].last()
        for source in (0, 1):
            for m in range(Z):
                if (source, m) != (c, 0):
                    copy = links.copy(
                        both.at[x, c, e, h ^ m, l], both_own.at[2 * h + source], (2 * x + c, f ^ (2 * m))
                    )
                    owned.append((c, source, copy))

                    @pl.when(core == source)
                    def _():
                        copy.start()

    give(1)
    grad_k[...] = jnp.zeros_like(grad_k)
    grad_v[...] = jnp.zeros_like(grad_v)
    factors = rotation(rows_of(tab))
    back_turn = (factors[0], -factors[1])
    for r in range(S):
        rows, seen = slice(r * T, (r + 1) * T), slice(0, (r + 1) * T)
        keys_seen, values_seen = whole(side, "k")[seen], whole(side, "v")[seen]
        for n in range(heads):
            query = block(side, "q", r, n * head, head)
            grad_att = block(side, "grad", r, n * head, head)
            scores = contract_last(query, keys_seen) * scale + bias[rows, seen].astype(f32)
            scores = jnp.exp(scores - jnp.max(scores, -1, keepdims=True))
            probs = scores / jnp.sum(scores, -1, keepdims=True)
            grad_probs = contract_last(grad_att, values_seen)
            delta = jnp.sum(probs * grad_probs, -1, keepdims=True)
            grad_scores = (probs * (grad_probs - delta)).astype(bf16)
            grad_q = dot(grad_scores, keys_seen) * scale
            grad_q = turn(grad_q, (back_turn[0][rows], back_turn[1][rows])).astype(bf16)
            grad_side[r // 2, r % 2, :, n * head : (n + 1) * head] = grad_q
            grad_k[seen] += contract_first(grad_scores, query)
            grad_v[seen] += contract_first(probs.astype(bf16), grad_att)
    grad_key = turn(grad_k[...] * scale, back_turn).astype(bf16)
    grad_side[:, :, :, HC : HC + head] = grad_key.reshape(2, 2, T, head)
    grad_side[:, :, :, HC + head : HC + 2 * head] = grad_v[...].astype(bf16).reshape(2, 2, T, head)
    grad_qkv = slice(0, HC + 2 * head)
    back.settle()
    row = RowSum(links, *row_bufs)
    for cx, go in ((1 - x, row.far), (x, row.near)):
        for i in range(S):
            total = contract_last(grad_side[cx, :, :, :HC].reshape(two, HC), q_w[i].reshape(-1, HC))
            total += contract_last(
                grad_side[cx, :, :, HC : HC + 2 * head].reshape(two, 2 * head),
                kv_w[i, :, :, : 2 * head].reshape(-1, 2 * head),
            )
            columns = slice(i * F * rows_w, (i + 1) * F * rows_w)
            row.parts[cx, :, :, columns] = total.astype(bf16).reshape(2, T, -1)
        go()
    row.middle()
    give(0)
    mine = Local(here, [(both.at[x, core, e, h, l], both_own.at[t])], 28)
    out.stage(1, (2, 1))
    out.stage(2, (3, 0))
    pieces = []
    q_view = q_w.reshape(S, FH, 2, rows_w, HC)
    kv_view = kv_w.reshape(S, FH, 2, rows_w, kv_w.shape[3])

    def q_piece(i):
        one = pl.ds(i, 1)
        spare = (bufs[10].at[one], bufs[11].at[:, one])
        return z_piece(links, LeadFirst(q_view.at[one]), *spare, place_z, z_masks)

    for i in range(S):
        columns = slice(i * F * rows_w, (i + 1) * F * rows_w)
        turned = normed_one[:, :, :, columns].reshape(row_len, -1)
        total = contract_first(turned, grad_side[:, :, :, grad_qkv].reshape(row_len, -1))
        total = total.astype(bf16)
        q_w[i] = total[:, :HC].reshape(F, rows_w, HC)
        kv_w[i, :, :, : 2 * head] = total[:, HC:].reshape(F, rows_w, 2 * head)
        pieces.append(q_piece(i))
    down_low(1)
    o_pieces[0].middle()
    row.arrive()

    def first_norm(rows):
        grad_normed = row.total(rows)
        grad, unit = norm_back(grad_normed, tok_own[rows].astype(f32), gains[0:1])
        grad_in[rows] += grad
        gain_sums[0:1] += jnp.sum(grad_normed * unit, 0, keepdims=True)

    row_loop(T, 16, first_norm)
    results = [Local(here, [(grad_in, grad_tokens)], 29)]
    columns = contract_first(gain_sums[...], pick).astype(bf16)
    kv_w[:, :, :, 2 * head :] = columns.reshape(S, F, rows_w, head)
    kv_row = RowSum(links, kv_w.reshape(2, 2, F * rows_w, kv_w.shape[3]), *bufs[12:14])
    kv_row.far()
    kv_row.near()
    kv_row.middle()
    ffn["down_high"] = PieceByW(
        links, LeadFirst(down.at[:, :, :, :, high_half]), *bufs[2:4], w, w_masks
    )
    ffn["down_low", 0].middle()
    o_pieces[1].middle()
    pieces[0].middle()
    pieces[1].middle()
    o_pieces[0].inner()
    o_pieces[1].inner()
    pieces[2].middle()
    pieces[0].inner()
    pieces[3].middle()
    kv_row.arrive()

    def keep_kv(rows):
        kv_row.parts[x, core, rows] = kv_row.total(rows).astype(bf16)

    row_loop(F * rows_w, 16, keep_kv)
    kv_mine = LeadFirst(kv_view.at[pl.ds(s, 1)])
    kv_piece = z_piece(links, kv_mine, *bufs[14:16], place_z, z_masks)
    pieces[1].inner()
    pieces[2].inner()
    pieces[3].inner()
    kv_piece.middle()
    ffn["down_high"].middle()
    kv_piece.inner()
    ffn["down_low", 1].middle()

    grad_own = grad_both.reshape(Z, two // rows_w, rows_w, 2 * FC)
    for c, source, copy in owned:

        @pl.when(core == c)
        def _():
            copy.wait_recv()

        @pl.when(core == source)
        def _():
            copy.wait_send()

    mine.wait()
    came = Local(
        here, [(both_own.at[pl.ds(2 * i, 2)], grad_own.at[i, pl.ds(0, 2)]) for i in range(Z)], 33
    )
    def store_down(base):
        def store(i, rows, total):
            grad_down[rows, base : base + total.shape[1]] = total

        return store

    for i in (0, 1):
        ffn["down_low", i].last(store_down(i * (cut // 2)))
    ffn["down_high"].last(store_down(cut))
    results.append(Local(here, [(grad_down, down_out)], 30))

    out.arrive()

    out_rows = back_parts.at[3, 0]

    def finish_output(rows):
        out_rows[rows] = (residual[rows] + out.total(rows)).astype(bf16)

    row_loop(T, 16, finish_output)
    results.append(Local(here, [(out_rows, output)], 32))
    came.wait()
    results[0].wait()
    stores = [
        r.at[pl.ds(j * rows_w, rows_w), pl.ds(0, quarter)]
        for r in (residual, grad_in)
        for j in (0, 1)
    ]
    leaving = [None] * len(stores)
    count = 0
    for i, target in enumerate((gate_out, up_out)):
        units = []
        for at_h in range(Z):
            for c in (0, 1):
                block = grad_own[at_h, c].astype(f32)
                tiles = [
                    block[:, (2 * j + i) * lanes : (2 * j + i + 1) * lanes]
                    for j in range(whole_tiles)
                ]
                base = 2 * whole_tiles * lanes + i * (FC - whole_tiles * lanes)
                tiles.append(block[:, base : base + FC - whole_tiles * lanes])
                units.append(jnp.concatenate(tiles, 1))
        width = FC // W
        for at_x in (0, 1):
            for c in (0, 1):
                parts = [
                    units[2 * at_h + c][:, (2 * at_e + at_x) * width : (2 * at_e + at_x + 1) * width]
                    for at_e in range(E)
                    for at_h in range(Z)
                ]
                slot_now = count % len(stores)
                if leaving[slot_now] is not None:
                    leaving[slot_now].wait()
                stores[slot_now][...] = jnp.concatenate(parts, 1)
                columns = pl.ds((2 * at_x + c) * quarter, quarter)
                leaving[slot_now] = Local(
                    here, [(stores[slot_now], target.at[:, columns])], 37 + slot_now
                )
                count += 1
    def store_o(base):
        def store(i, rows, total):
            o_sum[rows, base : base + D // 2] = total

        return store

    for i in (0, 1):
        o_pieces[i].last(store_o(i * D // 2))
    results.append(Local(here, [(o_sum, wo_out)], 31))
    for piece in pieces:
        piece.last()
    for a in (1, 2, 3):
        links.start(q_view.at[s ^ a, place_z, l], q_own.at[s], (a, 0))
    q_own[s] = q_view[s, place_z, l]
    q_came = links.sent[-3:]

    def store_kv(i, rows, total):
        kv_sum[rows] = total

    kv_piece.last(store_kv)
    names = (wk_out, wv_out, gains_out)
    results.append(
        Local(here, [(kv_sum.at[:, pl.ds(i * head, head)], r) for i, r in enumerate(names)], 41)
    )

    for arrival in q_came:
        arrival.wait()
    for i in leaving:
        i.wait()
    q_rows = residual.at[pl.ds(0, rows_w)]
    for i in range(S):
        q_rows[:, i * HC : (i + 1) * HC] = q_own[i].astype(f32)
    results.append(Local(here, [(q_rows, wq_out)], 44))
    out.settle()
    for piece in [*o_pieces, kv_piece, *pieces]:
        piece.settle()
    links.finish()
    assert links.count == copies, links.count
    for result in results[1:]:
        result.wait()


def hand_over_kernel(n, *refs):
    inputs, outputs, rooms, sems = refs[:n], refs[n : 2 * n], refs[2 * n : 3 * n], refs[3 * n]
    loads = [pltpu.make_async_copy(inputs[i], rooms[i], sems.at[i]) for i in range(n)]
    stores = [pltpu.make_async_copy(rooms[i], outputs[i], sems.at[n + i]) for i in range(n)]
    for load in loads:
        load.start()
    for load, store in zip(loads, stores):
        load.wait()
        store.start()
    for store in stores:
        store.wait()


def hand_over(arrays):
    n = len(arrays)
    anywhere = [pl.BlockSpec(memory_space=pl.ANY)] * n
    return pl.pallas_call(
        functools.partial(hand_over_kernel, n),
        out_shape=[shape(a.shape, a.dtype) for a in arrays],
        in_specs=anywhere,
        out_specs=anywhere,
        scratch_shapes=[pltpu.VMEM(a.shape, a.dtype) for a in arrays]
        + [pltpu.SemaphoreType.DMA((2 * n,))],
        compiler_params=pltpu.CompilerParams(vmem_limit_bytes=VMEM_LIMIT),
    )(*arrays)


def per_device(
    S,
    F,
    tokens,
    segments,
    positions,
    gain_one,
    w_query,
    w_key,
    w_value,
    w_out,
    gain_two,
    w_gate,
    w_up,
    w_down,
    cotangent,
):
    T, D = tokens.shape[1:]
    head = w_key.shape[1]
    row_len = segments.shape[1]
    rows = w_query.shape[0]
    down_rows = w_down.shape[0]
    FF = w_gate.shape[1]
    FH, E = F // 2, F // 8
    W, TG = 2 * E, 2 * Z
    HC = w_query.shape[1] // S
    heads = HC // head
    FC = FF // TG

    gains = jnp.stack([gain_one, gain_two])
    KV = 3 * head
    group = [pltpu.VMEM((Z, 2, T, D), bf16), pltpu.VMEM((Z, T, D), bf16)]
    group += [pltpu.VMEM((Z, T, D), bf16), pltpu.VMEM((T, D), bf16)]
    weight = pltpu.VMEM((2, 2, E, Z, 2, rows, 2 * FC), bf16)

    def natural_by_l(n):
        block = (n, rows, 2 * FC)
        return [pltpu.VMEM((2, E, *block), bf16), pltpu.VMEM((W - 1, *block), bf16)]

    outs = [
        ((T, D), bf16),
        ((T, head), bf16),
        ((T, head), bf16),
        ((T, D), f32),
        ((rows, FF), f32),
        ((rows, FF), f32),
        ((down_rows, D), f32),
        ((rows, D), f32),
        ((rows, D), f32),
        ((rows, head), f32),
        ((rows, head), f32),
        ((rows, head), f32),
        ((TG, rows, 2 * FC), bf16),
        ((2, 2, T, D), bf16),
        ((2, 2, T, 2 * HC + 2 * head), bf16),
        ((F, rows, D), bf16),
    ]
    copies = 119 + 12 * (FH - 1) + 20 * (W - 1) + 7 * (1 + (6 if FH == 4 else FH - 1))
    results = communicate(
        functools.partial(layer_kernel, FH, copies),
        (
            tokens[0],
            w_query,
            w_key,
            w_value,
            w_out,
            w_gate,
            w_up,
            w_down,
            cotangent[0],
            segments,
            positions,
            gains,
        ),
        [shape(dims, kind) for dims, kind in outs],
        copies,
        0,
        in_vmem=[False] * 9 + [True] * 3,
        kept=45,
        scratch=[
            weight,
            pltpu.VMEM((1, W, 2, down_rows, D), bf16),
            pltpu.VMEM((S, F, rows, HC), bf16),
            pltpu.VMEM((S, F, rows, KV), bf16),
            pltpu.VMEM((F, rows, D), bf16),
            pltpu.VMEM((T, D), f32),
            pltpu.VMEM((T, D), f32),
            pltpu.VMEM((8, D), f32),
            pltpu.VMEM((8, D), f32),
            pltpu.VMEM((S, T, D), bf16),
            pltpu.VMEM((down_rows, D), f32),
            pltpu.VMEM((rows, D), f32),
            pltpu.VMEM((rows, KV), f32),
            pltpu.VMEM((S, rows, HC), bf16),
            *group,
            *group,
            pltpu.VMEM((Z, 2, T, D), bf16),
            pltpu.VMEM((Z, 2, T, D), bf16),
            pltpu.VMEM((Z, 2 * T, 2 * FC), bf16),
            pltpu.VMEM((S, T, head), f32),
            pltpu.VMEM((row_len, head), f32),
            pltpu.VMEM((row_len, head), f32),
            pltpu.VMEM((row_len, row_len), bf16),
            pltpu.VMEM((rows, head), bf16),
            *by_l_scratch(1, W, down_rows, D // 2),
            *by_w_scratch(1, W, down_rows, D // 2),
            *natural_by_l(Z),
            *by_w_scratch(Z, W, rows, 2 * FC),
            *z_scratch(1, FH, rows, D),
            *z_scratch(S, FH, rows, HC),
            pltpu.VMEM((2, F * rows, KV), bf16),
            pltpu.VMEM((F * rows, KV), bf16),
            *z_scratch(1, FH, rows, KV),
        ],
    )
    output, keys, values, grad_tokens, gate, up, down, query, out, key, value, gains = hand_over(
        results[:12]
    )
    return (
        output[None],
        keys[None],
        values[None],
        grad_tokens[None],
        gains[:, 0],
        query,
        key,
        value,
        out,
        gains[:, 1],
        gate,
        up,
        down,
    )


def solution(mesh):
    token_spec = P("fsdp", "seq", None)
    flat, matrix = P(("seq", "fsdp")), P(("seq", "fsdp"), None)
    return jax.shard_map(
        functools.partial(per_device, mesh.shape["seq"], mesh.shape["fsdp"]),
        mesh=mesh,
        in_specs=(
            token_spec,
            P("fsdp", None),
            P("fsdp", "seq"),
            flat,
            matrix,
            matrix,
            matrix,
            matrix,
            flat,
            matrix,
            matrix,
            matrix,
            token_spec,
        ),
        out_specs=(
            token_spec,
            token_spec,
            token_spec,
            token_spec,
            flat,
            matrix,
            matrix,
            matrix,
            matrix,
            flat,
            matrix,
            matrix,
            matrix,
        ),
        check_vma=False,
    )
```
